32 devices in a mesh: dp: 4 (over y, core), mp: 8 (over z, x).
Axes of the slice: x: 2, y: 2, z: 4, core: 2. Of those that a mesh axis runs over, the one named last changes fastest.
Arguments:
- hidden_rows: bfloat16 [768, 2048], P('dp'), may hold values from -6 to 6
- w_query: bfloat16 [2048, 2048], P(None, 'mp'), may hold values from -0.125 to 0.125
- w_key: bfloat16 [2048, 1024], P(None, 'mp'), may hold values from -0.125 to 0.125
- w_value: bfloat16 [2048, 1024], P(None, 'mp'), may hold values from -0.125 to 0.125
- w_out: bfloat16 [2048, 2048], P('mp'), may hold values from -0.125 to 0.125
- q_gain: float32 [128], replicated, may hold values from 0.25 to 1.75
- k_gain: float32 [128], replicated, may hold values from 0.25 to 1.75
- prefix_kv: bfloat16 [192, 2048], P('dp', 'mp')
- cotangent: bfloat16 [768, 2048], P('dp', 'mp'), may hold values from -6 to 6
- prompt_len: int32 [4], replicated, may hold values from 1 to 64, 192 in all
- resp_prompt: int32 [8], P('dp'), may hold values from 0 to 3
- resp_len: int32 [8], P('dp'), may hold values from 32 to 96, as said below
Outputs:
- mixed: bfloat16 [768, 2048], P('dp', 'mp')
- grad_input: bfloat16 [768, 2048], P('dp', 'mp')
- grad_prefix: bfloat16 [192, 2048], P('dp', 'mp')
The draws below stay inside these ranges and needn't reach their ends.
Inputs may be any that keep to these rules, and one draw needn't show every extreme that they name: `prompt_len`: the lengths add up to 192; the longest is exactly 64. `resp_len`: some response of every draw has all 96 tokens live.
All inputs are finite; a program needn't handle non-finite values.
Results may differ from the reference program's by a relative error of at most 0.014.
The reference program's roundings to bfloat16 on the way count: a program that leaves them out, or rounds other values in their place, can miss the bound.
Values may be sent and summed in bfloat16 or wider, within the bound.
No kernel may reach another device: no remote copies, remote signals or barrier semaphores. Data moves between devices by JAX's collectives and lax.ppermute only.
A program may use at most 64 MiB of HBM per device.

```python
import math
import jax
import jax.numpy as jnp
import numpy as np
from jax import lax

D = 2048
QH = 16
KVH = 8
HD = 128
RLEN = 96
PROMPTS = 4
RESPONSES = 8
PREFIX_ROWS = 192
PREFIX_MOST = 64
N_MP = 8


def draw_prefix_kv(key, part):
    key = jax.random.fold_in(key, 5)
    values = jnp.clip(jax.random.normal(key, (PREFIX_ROWS, KVH * 2 * HD), jnp.float32), -6.0, 6.0)
    return values.astype(jnp.bfloat16)


def draw_resp_len(key, part):
    key = jax.random.fold_in(key, 11)
    lengths = jax.random.randint(key, (RESPONSES,), RLEN // 3, RLEN + 1)
    return lengths.at[0].set(RLEN)


def plant(result, stream_key, smallest, largest):
    dims = result.shape
    place = [jax.random.randint(jax.random.fold_in(stream_key, axis), (), 0, dims[axis]) for axis in range(len(dims))]
    result = result.at[tuple(place)].set(smallest)
    longest = dims.index(max(dims))
    place[longest] = (place[longest] + 1) % dims[longest]
    return result.at[tuple(place)].set(largest)


def shard_levels(key, shape, shards, least, high):
    loudness, own = 1.0, jax.random.fold_in(key, 6)
    for position, blocks in shards:
        steps = jnp.exp(jax.random.uniform(jax.random.fold_in(own, position), (blocks,), jnp.float32, least / len(shards), high / len(shards)))
        loudness = loudness * jnp.repeat(steps, shape[position] // blocks).reshape([-1 if axis == position else 1 for axis in range(len(shape))])
    return loudness


def split_up(amount, total, limit, lean):
    portions = [(1 << 20) // math.isqrt(grade ** lean) + 1 for grade in range(2, amount + 1)]
    surplus, counts = total - limit - (amount - 1), [1] * (amount - 1)
    while surplus > 0:
        movable = [i for i in range(amount - 1) if counts[i] < limit]
        pool, budget = sum([portions[i] for i in movable]), surplus
        for i in movable:
            more = min(limit - counts[i], max(1, budget * portions[i] // pool), surplus)
            counts[i] = counts[i] + more
            surplus = surplus - more
    return np.array([limit] + counts)


def ragged_sizes(key, amount, total, most, lean):
    if amount == 2:
        one = jax.random.randint(key, (), max(1, total - most), min(most, total - 1) + 1)
        return jnp.stack([one, total - one])
    sizes = jnp.asarray(split_up(amount, total, most, lean), jnp.int32)
    pairs = (amount - 1) // 2
    donor, taker = sizes[1:1 + 2 * pairs:2], sizes[2:2 + 2 * pairs:2]
    margin = jnp.minimum(donor - 1, most - taker)
    moved = jax.random.randint(jax.random.fold_in(key, 1), (pairs,), 0, 1 << 20) % (margin + 1)
    sizes = sizes.at[1:1 + 2 * pairs:2].set(donor - moved).at[2:2 + 2 * pairs:2].set(taker + moved)
    return sizes[jax.random.permutation(jax.random.fold_in(key, 2), amount)]


def noise(key, extent, scale, reach, cuts=(), kind=jnp.bfloat16):
    entries = scale * jax.random.normal(key, extent, jnp.float32)
    if cuts:
        entries = entries * shard_levels(key, extent, cuts, -0.22, 0.18)
    return jnp.clip(entries, -reach, reach).astype(kind)


def setup_inputs(seed: int = 0) -> dict:
    arg_keys = jax.random.split(jax.random.key(seed), 13)
    return {
        "hidden_rows": noise(arg_keys[0], (RESPONSES * RLEN, D), 1.0, 6.0, ((0, 4),)),
        "w_query": noise(arg_keys[1], (D, QH * HD), D ** -0.5, 0.125, ((1, 8),)),
        "w_key": noise(arg_keys[2], (D, KVH * HD), D ** -0.5, 0.125, ((1, 8),)),
        "w_value": noise(arg_keys[3], (D, KVH * HD), D ** -0.5, 0.125, ((1, 8),)),
        "w_out": noise(arg_keys[4], (QH * HD, D), (QH * HD) ** -0.5, 0.125, ((0, 8),)),
        "q_gain": jnp.clip(1.0 + 0.15 * jax.random.normal(arg_keys[5], (HD,), jnp.float32), 0.25, 1.75),
        "k_gain": jnp.clip(1.0 + 0.15 * jax.random.normal(arg_keys[6], (HD,), jnp.float32), 0.25, 1.75),
        "prefix_kv": draw_prefix_kv(jax.random.fold_in(arg_keys[12], 71), 0),
        "cotangent": noise(arg_keys[8], (RESPONSES * RLEN, D), 1.0, 6.0, ((0, 4), (1, 8))),
        "prompt_len": ragged_sizes(arg_keys[9], PROMPTS, PREFIX_ROWS, PREFIX_MOST, 2).astype(jnp.int32),
        "resp_prompt": plant(jax.random.randint(arg_keys[10], (RESPONSES,), 0, PROMPTS), jax.random.fold_in(arg_keys[10], 1), 0, PROMPTS - 1).astype(jnp.int32),
        "resp_len": draw_resp_len(jax.random.fold_in(arg_keys[12], 71), 0),
    }


EPS = 1e-06
NEG = -1e+30

def head_norm(hidden, gain):
    return hidden * lax.rsqrt(lax.optimization_barrier(jnp.mean(hidden * hidden, axis=-1, keepdims=True)) + EPS) * gain.astype(jnp.float32)

def mix(form, left, right):
    return jnp.einsum(form, left.astype(jnp.float32), right.astype(jnp.float32))

def prompt_of(lengths, count):
    ends = jnp.cumsum(lengths)
    positions = jnp.arange(count, dtype=jnp.int32)
    return lax.optimization_barrier(jnp.sum((positions[:, None] >= ends[None, :]).astype(jnp.int32), axis=1))

def attend(query, key, value, grad_heads, prompt, length, pre_k, pre_v, key_prompt):
    resp_len_slots, q_heads, head_size = query.shape
    kv_heads = key.shape[1]
    groups = q_heads // kv_heads
    scale = head_size ** (-0.5)
    q_group = query.reshape(resp_len_slots, kv_heads, groups, head_size)
    d_group = grad_heads.reshape(resp_len_slots, kv_heads, groups, head_size)
    pre_mask = (key_prompt == prompt)[None, None, None, :]
    places = jnp.arange(resp_len_slots, dtype=jnp.int32)
    own_mask = ((places[None, :] <= places[:, None]) & (places[None, :] < length))[None, None]
    s_pre = jnp.where(pre_mask, mix('tkgd,jkd->kgtj', q_group, pre_k) * scale, NEG)
    s_own = jnp.where(own_mask, mix('tkgd,ukd->kgtu', q_group, key) * scale, NEG)
    top = jnp.maximum(lax.optimization_barrier(jnp.max(s_pre, axis=-1)), lax.optimization_barrier(jnp.max(s_own, axis=-1)))
    e_pre = jnp.exp(s_pre - top[..., None])
    e_own = jnp.exp(s_own - top[..., None])
    total = lax.optimization_barrier(jnp.sum(e_pre, axis=-1)) + lax.optimization_barrier(jnp.sum(e_own, axis=-1))
    p_pre = (e_pre / total[..., None]).astype(jnp.bfloat16)
    p_own = (e_own / total[..., None]).astype(jnp.bfloat16)
    heads_out = mix('kgtj,jkd->tkgd', p_pre, pre_v) + mix('kgtu,ukd->tkgd', p_own, value)
    delta = jnp.transpose(lax.optimization_barrier(jnp.sum(d_group.astype(jnp.float32) * heads_out, axis=-1)), (1, 2, 0))
    dp_pre = mix('tkgd,jkd->kgtj', d_group, pre_v)
    dp_own = mix('tkgd,ukd->kgtu', d_group, value)
    ds_pre = (p_pre.astype(jnp.float32) * (dp_pre - delta[..., None])).astype(jnp.bfloat16)
    ds_own = (p_own.astype(jnp.float32) * (dp_own - delta[..., None])).astype(jnp.bfloat16)
    grad_query = scale * (mix('kgtj,jkd->tkgd', ds_pre, pre_k) + mix('kgtu,ukd->tkgd', ds_own, key))
    grad_key = scale * mix('kgtu,tkgd->ukd', ds_own, q_group)
    grad_value = mix('kgtu,tkgd->ukd', p_own, d_group)
    grad_pre_k = scale * mix('kgtj,tkgd->jkd', ds_pre, q_group)
    grad_pre_v = mix('kgtj,tkgd->jkd', p_pre, d_group)
    return (heads_out.reshape(resp_len_slots, q_heads, head_size), grad_query.reshape(resp_len_slots, q_heads, head_size), grad_key, grad_value, grad_pre_k, grad_pre_v)

def reference(hidden_rows, w_query, w_key, w_value, w_out, q_gain, k_gain, prefix_kv, cotangent, prompt_len, resp_prompt, resp_len):
    all_rows = RESPONSES * RLEN
    hq = jnp.dot(hidden_rows, w_query, preferred_element_type=jnp.float32).reshape(all_rows, QH, HD)
    hk = jnp.dot(hidden_rows, w_key, preferred_element_type=jnp.float32).reshape(all_rows, KVH, HD)
    qf, q_back = jax.vjp(lambda hidden: head_norm(hidden, q_gain), hq)
    kf, k_back = jax.vjp(lambda hidden: head_norm(hidden, k_gain), hk)
    vf = jnp.dot(hidden_rows, w_value, preferred_element_type=jnp.float32).reshape(all_rows, KVH, HD)
    query = qf.astype(jnp.bfloat16)
    key = kf.astype(jnp.bfloat16)
    value = vf.astype(jnp.bfloat16)
    prefix = prefix_kv.reshape(PREFIX_ROWS, KVH, 2, HD)
    pre_k = prefix[:, :, 0]
    pre_v = prefix[:, :, 1]
    key_prompt = prompt_of(prompt_len, PREFIX_ROWS)
    live = (jnp.arange(RLEN, dtype=jnp.int32)[None, :] < resp_len[:, None]).reshape(all_rows)
    masked = jnp.where(live[:, None], cotangent, jnp.zeros_like(cotangent))
    grad_heads = jnp.dot(masked, w_out.T, preferred_element_type=jnp.float32).astype(jnp.bfloat16).reshape(all_rows, QH, HD)

    def step(carry, item):
        q_one, k_one, v_one, d_one, prompt, length = item
        heads_out, grad_query, grad_key, grad_value, grad_pre_k, grad_pre_v = attend(q_one, k_one, v_one, d_one, prompt, length, pre_k, pre_v, key_prompt)
        return ((carry[0] + grad_pre_k, carry[1] + grad_pre_v), (heads_out, grad_query, grad_key, grad_value))
    start = (jnp.zeros((PREFIX_ROWS, KVH, HD), jnp.float32), jnp.zeros((PREFIX_ROWS, KVH, HD), jnp.float32))
    items = (query.reshape(RESPONSES, RLEN, QH, HD), key.reshape(RESPONSES, RLEN, KVH, HD), value.reshape(RESPONSES, RLEN, KVH, HD), grad_heads.reshape(RESPONSES, RLEN, QH, HD), resp_prompt, resp_len)
    (sum_k, sum_v), (heads_out, grad_query, grad_key, grad_value) = lax.scan(step, start, items)
    out_bf = heads_out.reshape(all_rows, QH * HD).astype(jnp.bfloat16)
    dhq = q_back(grad_query.reshape(all_rows, QH, HD))[0].astype(jnp.bfloat16).reshape(all_rows, QH * HD)
    dhk = k_back(grad_key.reshape(all_rows, KVH, HD))[0].astype(jnp.bfloat16).reshape(all_rows, KVH * HD)
    dv = grad_value.reshape(all_rows, KVH * HD).astype(jnp.bfloat16)
    q_cols = QH * HD // N_MP
    k_cols = KVH * HD // N_MP
    total_out = jnp.zeros((all_rows, D), jnp.float32)
    total_in = jnp.zeros((all_rows, D), jnp.float32)
    for group in range(N_MP):
        qs = slice(group * q_cols, (group + 1) * q_cols)
        ks = slice(group * k_cols, (group + 1) * k_cols)
        part_out = jnp.dot(out_bf[:, qs], w_out[qs], preferred_element_type=jnp.float32)
        total_out = total_out + part_out.astype(jnp.bfloat16).astype(jnp.float32)
        part_in = jnp.dot(dhq[:, qs], w_query[:, qs].T, preferred_element_type=jnp.float32) + jnp.dot(dhk[:, ks], w_key[:, ks].T, preferred_element_type=jnp.float32) + jnp.dot(dv[:, ks], w_value[:, ks].T, preferred_element_type=jnp.float32)
        total_in = total_in + part_in.astype(jnp.bfloat16).astype(jnp.float32)
    mixed = jnp.where(live[:, None], total_out, jnp.zeros_like(total_out)).astype(jnp.bfloat16)
    grad_input = total_in.astype(jnp.bfloat16)
    grad_prefix = jnp.stack([sum_k, sum_v], axis=2).reshape(PREFIX_ROWS, KVH * 2 * HD).astype(jnp.bfloat16)
    return (mixed, grad_input, grad_prefix)
```

```python
import jax
import jax.numpy as jnp
from jax import lax
from jax.sharding import PartitionSpec as P

EPS = 1e-06
NEG = -1e30


def head_norm(hidden, gain):
    return hidden * lax.rsqrt(jnp.mean(hidden * hidden, axis=-1, keepdims=True) + EPS) * gain


def mix(form, left, right):
    return jnp.einsum(form, left, right, preferred_element_type=jnp.float32)


def prompt_of(lengths, count):
    ends = jnp.cumsum(lengths)
    positions = jnp.arange(count, dtype=jnp.int32)
    return jnp.sum((positions[:, None] >= ends[None, :]).astype(jnp.int32), axis=1)


def pairs(axis_size, move):
    return [(i, move(i)) for i in range(axis_size)]


def gather_rows(block, axis):
    size = lax.axis_size(axis)
    if size > 8:
        return lax.all_gather(block, axis, axis=0, tiled=True)
    me = lax.axis_index(axis)
    whole = jnp.zeros((size,) + block.shape, block.dtype)
    for k in range(size):
        part = block
        if k:
            part = lax.ppermute(block, axis, pairs(size, lambda i: (i + k) % size))
        whole = lax.dynamic_update_index_in_dim(whole, part, (me - k) % size, 0)
    return whole.reshape((size * block.shape[0],) + block.shape[1:])


def scatter_rows(terms, axis):
    size = lax.axis_size(axis)
    if size > 8:
        return lax.psum_scatter(terms, axis, scatter_dimension=0, tiled=True)
    me = lax.axis_index(axis)
    rows = terms.shape[0] // size
    total = lax.dynamic_slice_in_dim(terms, me * rows, rows, 0)
    for k in range(1, size):
        part = lax.dynamic_slice_in_dim(terms, (me + k) % size * rows, rows, 0)
        total = total + lax.ppermute(part, axis, pairs(size, lambda i: (i + k) % size))
    return total


def gather_features(block, axis):
    size = lax.axis_size(axis)
    high = size // 2
    me = lax.axis_index(axis)
    hi, lo = me // 2, me % 2
    found = []
    for k in range(high):
        part = block
        if k:
            part = lax.ppermute(block, axis, pairs(size, lambda i: (i + 2 * k) % size))
        owner = (hi - k) % high * 2
        found.append((part, owner + lo))
        found.append((lax.ppermute(part, axis, pairs(size, lambda i: i ^ 1)), owner + 1 - lo))
    return found


def scatter_features(terms, axis):
    size = lax.axis_size(axis)
    high = size // 2
    me = lax.axis_index(axis)
    hi, lo = me // 2, me % 2
    width = terms.shape[1] // size

    def block(owner):
        return lax.dynamic_slice_in_dim(terms, owner * width, width, 1)

    halves = {}
    for k in [*range(1, high), 0]:
        owner = (hi + k) % high * 2
        swapped = lax.ppermute(block(owner + 1 - lo), axis, pairs(size, lambda i: i ^ 1))
        halves[k] = block(owner + lo).astype(jnp.float32) + swapped.astype(jnp.float32)
    total = halves[0]
    for k in range(1, high):
        sent = lax.ppermute(
            halves[k].astype(jnp.bfloat16), axis, pairs(size, lambda i: (i + 2 * k) % size)
        )
        total = total + sent.astype(jnp.float32)
    return total


def attend(query, key, value, grad_heads, prompt, length, pre_k, pre_v, key_prompt):
    slot_len, q_heads, head_size = query.shape
    kv_heads = key.shape[1]
    groups = q_heads // kv_heads
    scale = head_size ** (-0.5)
    q_group = query.reshape(slot_len, kv_heads, groups, head_size)
    d_group = grad_heads.reshape(slot_len, kv_heads, groups, head_size)
    pre_mask = (key_prompt == prompt)[None, None, None, :]
    places = jnp.arange(slot_len, dtype=jnp.int32)
    own_mask = ((places[None, :] <= places[:, None]) & (places[None, :] < length))[None, None]
    s_pre = jnp.where(pre_mask, mix("tkgd,jkd->kgtj", q_group, pre_k) * scale, NEG)
    s_own = jnp.where(own_mask, mix("tkgd,ukd->kgtu", q_group, key) * scale, NEG)
    top = jnp.maximum(jnp.max(s_pre, axis=-1), jnp.max(s_own, axis=-1))
    e_pre = jnp.exp(s_pre - top[..., None])
    e_own = jnp.exp(s_own - top[..., None])
    total = jnp.sum(e_pre, axis=-1) + jnp.sum(e_own, axis=-1)
    p_pre = (e_pre / total[..., None]).astype(jnp.bfloat16)
    p_own = (e_own / total[..., None]).astype(jnp.bfloat16)
    heads_out = mix("kgtj,jkd->tkgd", p_pre, pre_v) + mix("kgtu,ukd->tkgd", p_own, value)
    delta = jnp.transpose(jnp.sum(d_group.astype(jnp.float32) * heads_out, axis=-1), (1, 2, 0))
    dp_pre = mix("tkgd,jkd->kgtj", d_group, pre_v)
    dp_own = mix("tkgd,ukd->kgtu", d_group, value)
    ds_pre = (p_pre.astype(jnp.float32) * (dp_pre - delta[..., None])).astype(jnp.bfloat16)
    ds_own = (p_own.astype(jnp.float32) * (dp_own - delta[..., None])).astype(jnp.bfloat16)
    grad_query = scale * (mix("kgtj,jkd->tkgd", ds_pre, pre_k) + mix("kgtu,ukd->tkgd", ds_own, key))
    grad_key = scale * mix("kgtu,tkgd->ukd", ds_own, q_group)
    grad_value = mix("kgtu,tkgd->ukd", p_own, d_group)
    results = (
        heads_out.reshape(slot_len, q_heads, head_size),
        grad_query.reshape(slot_len, q_heads, head_size),
        grad_key,
        grad_value,
        top,
        total,
        delta,
    )
    grad_pre_k = scale * mix("kgtj,tkgd->jkd", ds_pre, q_group)
    grad_pre_v = mix("kgtj,tkgd->jkd", p_pre, d_group)
    return (results, (grad_pre_k, grad_pre_v))


def per_device(
    hidden_rows,
    w_query,
    w_key,
    w_value,
    w_out,
    q_gain,
    k_gain,
    prefix_kv,
    cotangent,
    prompt_len,
    resp_prompt,
    resp_len,
):
    row_count = hidden_rows.shape[0]
    head_size = q_gain.shape[0]
    slot_count = resp_len.shape[0]
    slot_len = row_count // slot_count
    q_heads = w_query.shape[1] // head_size
    kv_heads = w_key.shape[1] // head_size
    whole = gather_rows(prefix_kv, "dp")
    prefix_count = whole.shape[0]
    window = prefix_count // 3
    prefix = whole.reshape(prefix_count, kv_heads, 2, head_size)
    pre_k = prefix[:, :, 0]
    pre_v = prefix[:, :, 1]
    key_prompt = prompt_of(prompt_len, prefix_count)
    prompt_ends = jnp.cumsum(prompt_len)
    prompt_starts = jnp.minimum(prompt_ends - prompt_len, prefix_count - window)
    prompt_ids = jnp.arange(prompt_len.shape[0], dtype=jnp.int32)
    resp_start = jnp.sum(
        jnp.where(resp_prompt[:, None] == prompt_ids[None, :], prompt_starts[None, :], 0), axis=1
    )
    hq = jnp.dot(hidden_rows, w_query, preferred_element_type=jnp.float32).reshape(
        row_count, q_heads, head_size
    )
    hk = jnp.dot(hidden_rows, w_key, preferred_element_type=jnp.float32).reshape(
        row_count, kv_heads, head_size
    )
    qf, q_back = jax.vjp(lambda hidden: head_norm(hidden, q_gain), hq)
    kf, k_back = jax.vjp(lambda hidden: head_norm(hidden, k_gain), hk)
    vf = jnp.dot(hidden_rows, w_value, preferred_element_type=jnp.float32).reshape(
        row_count, kv_heads, head_size
    )
    query = qf.astype(jnp.bfloat16)
    key = kf.astype(jnp.bfloat16)
    value = vf.astype(jnp.bfloat16)
    live = (jnp.arange(slot_len, dtype=jnp.int32)[None, :] < resp_len[:, None]).reshape(row_count)
    masked = jnp.where(live[:, None], cotangent, jnp.zeros_like(cotangent))
    width = cotangent.shape[1]
    grad_heads = 0.0
    for part, owner in gather_features(masked, "mp"):
        grad_heads = grad_heads + lax.dot_general(
            part,
            lax.dynamic_slice_in_dim(w_out, owner * width, width, 1),
            (((1,), (1,)), ((), ())),
            preferred_element_type=jnp.float32,
        )
    grad_heads = grad_heads.astype(jnp.bfloat16).reshape(row_count, q_heads, head_size)
    items = (
        query.reshape(slot_count, slot_len, q_heads, head_size),
        key.reshape(slot_count, slot_len, kv_heads, head_size),
        value.reshape(slot_count, slot_len, kv_heads, head_size),
        grad_heads.reshape(slot_count, slot_len, q_heads, head_size),
        resp_prompt,
        resp_len,
        resp_start,
    )

    def windowed(item):
        q_one, k_one, v_one, d_one, prompt, length, first = item
        k_win = lax.dynamic_slice_in_dim(pre_k, first, window, 0)
        v_win = lax.dynamic_slice_in_dim(pre_v, first, window, 0)
        p_win = lax.dynamic_slice_in_dim(key_prompt, first, window, 0)
        return attend(q_one, k_one, v_one, d_one, prompt, length, k_win, v_win, p_win)

    def step_keys(carry, item):
        results, pre_terms = windowed(item)
        first = item[6]
        sum_k = lax.dynamic_update_slice_in_dim(
            carry[0], lax.dynamic_slice_in_dim(carry[0], first, window, 0) + pre_terms[0], first, 0
        )
        sum_v = lax.dynamic_update_slice_in_dim(
            carry[1], lax.dynamic_slice_in_dim(carry[1], first, window, 0) + pre_terms[1], first, 0
        )
        return ((sum_k, sum_v), results[:4])

    start = (
        jnp.zeros((prefix_count, kv_heads, head_size), jnp.float32),
        jnp.zeros((prefix_count, kv_heads, head_size), jnp.float32),
    )
    (sum_k, sum_v), (heads_out, grad_query, grad_key, grad_value) = lax.scan(
        step_keys, start, items
    )
    terms = jnp.stack([sum_k, sum_v], axis=2).reshape(prefix_count, kv_heads * 2 * head_size)
    grad_prefix = scatter_rows(terms, "dp").astype(jnp.bfloat16)
    out_bf = heads_out.reshape(row_count, q_heads * head_size).astype(jnp.bfloat16)
    part_out = jnp.dot(out_bf, w_out, preferred_element_type=jnp.float32).astype(jnp.bfloat16)
    summed = scatter_features(part_out, "mp")
    mixed = jnp.where(live[:, None], summed, jnp.zeros_like(summed)).astype(jnp.bfloat16)
    dhq = (
        q_back(grad_query.reshape(row_count, q_heads, head_size))[0]
        .astype(jnp.bfloat16)
        .reshape(row_count, q_heads * head_size)
    )
    dhk = (
        k_back(grad_key.reshape(row_count, kv_heads, head_size))[0]
        .astype(jnp.bfloat16)
        .reshape(row_count, kv_heads * head_size)
    )
    dv_rows = grad_value.reshape(row_count, kv_heads * head_size).astype(jnp.bfloat16)
    contract = (((1,), (1,)), ((), ()))
    part_in = (
        lax.dot_general(dhq, w_query, contract, preferred_element_type=jnp.float32)
        + lax.dot_general(dhk, w_key, contract, preferred_element_type=jnp.float32)
        + lax.dot_general(dv_rows, w_value, contract, preferred_element_type=jnp.float32)
    )
    grad_input = scatter_features(part_in.astype(jnp.bfloat16), "mp").astype(jnp.bfloat16)
    return (mixed, grad_input, grad_prefix)


def solution(mesh):
    in_specs = (
        P("dp", None),
        P(None, "mp"),
        P(None, "mp"),
        P(None, "mp"),
        P("mp", None),
        P(),
        P(),
        P("dp", "mp"),
        P("dp", "mp"),
        P(),
        P("dp"),
        P("dp"),
    )
    out_specs = (P("dp", "mp"), P("dp", "mp"), P("dp", "mp"))
    return jax.shard_map(
        per_device, mesh=mesh, in_specs=in_specs, out_specs=out_specs, check_vma=False
    )
```

```python
import functools

import jax
import jax.numpy as jnp
from jax import lax
from jax.experimental import pallas as pl
from jax.experimental.pallas import tpu as pltpu
from jax.sharding import PartitionSpec as P

EPS = 1e-06
NEG = -1e30
ROWS = 16
F32 = jnp.float32
BF16 = jnp.bfloat16
VMEM = pl.BlockSpec(memory_space=pltpu.VMEM)
SMEM = pl.BlockSpec(memory_space=pltpu.SMEM)


def dot(left, right):
    return jnp.dot(left, right, preferred_element_type=F32)


def dot_nt(left, right):
    return lax.dot_general(left, right, (((1,), (1,)), ((), ())), preferred_element_type=F32)


def dot_tn(left, right):
    return lax.dot_general(left, right, (((0,), (0,)), ((), ())), preferred_element_type=F32)


def inverse_root(hidden):
    return lax.rsqrt(jnp.mean(hidden * hidden, axis=-1, keepdims=True) + EPS)


def norm_back(hidden, gain, grad):
    root = inverse_root(hidden)
    unit = hidden * root
    scaled = grad * gain
    return root * (scaled - unit * jnp.mean(scaled * unit, axis=-1, keepdims=True))


def project_kernel(
    hid, w_q, w_k, w_v, q_gain, k_gain, query, key, value, hq, hk, sum_q, sum_k, sum_v
):
    step = pl.program_id(0)
    size = q_gain.shape[1]

    @pl.when(step == 0)
    def _():
        for total in (sum_q, sum_k, sum_v):
            total[...] = jnp.zeros_like(total)

    rows = hid[...]
    sum_q[...] += dot(rows, w_q[...])
    sum_k[...] += dot(rows, w_k[...])
    sum_v[...] += dot(rows, w_v[...])

    @pl.when(step == pl.num_programs(0) - 1)
    def _():
        hq[...] = sum_q[...]
        hk[...] = sum_k[...]
        value[...] = sum_v[...].astype(BF16)
        for total, gain, out in ((sum_q, q_gain, query), (sum_k, k_gain, key)):
            for at in range(0, total.shape[1], size):
                head = total[:, at : at + size]
                out[:, at : at + size] = (head * inverse_root(head) * gain[...]).astype(BF16)


def project(hidden, w_q, w_k, w_v, q_gain, k_gain):
    rows, depth = hidden.shape
    steps = 4
    part = depth // steps
    q_width, k_width = w_q.shape[1], w_k.shape[1]

    def whole(*shape):
        return pl.BlockSpec(shape, lambda i: (0,) * len(shape))

    def slab(width):
        return pl.BlockSpec((part, width), lambda i: (i, 0))

    return pl.pallas_call(
        project_kernel,
        grid=(steps,),
        in_specs=[
            pl.BlockSpec((rows, part), lambda i: (0, i)),
            slab(q_width),
            slab(k_width),
            slab(k_width),
            whole(*q_gain.shape),
            whole(*k_gain.shape),
        ],
        out_specs=[
            whole(rows, q_width),
            whole(rows, k_width),
            whole(rows, k_width),
            whole(rows, q_width),
            whole(rows, k_width),
        ],
        out_shape=[
            jax.ShapeDtypeStruct((rows, q_width), BF16),
            jax.ShapeDtypeStruct((rows, k_width), BF16),
            jax.ShapeDtypeStruct((rows, k_width), BF16),
            jax.ShapeDtypeStruct((rows, q_width), F32),
            jax.ShapeDtypeStruct((rows, k_width), F32),
        ],
        scratch_shapes=[
            pltpu.VMEM((rows, q_width), F32),
            pltpu.VMEM((rows, k_width), F32),
            pltpu.VMEM((rows, k_width), F32),
        ],
        compiler_params=pltpu.CompilerParams(vmem_limit_bytes=16 << 20),
        cost_estimate=pl.CostEstimate(
            flops=2 * rows * depth * (q_width + 2 * k_width),
            bytes_accessed=2 * depth * (rows + q_width + 2 * k_width),
            transcendentals=0,
        ),
    )(hidden, w_q, w_k, w_v, q_gain, k_gain)


def prompt_span(prompt_len, prompt):
    first, last = 0, 0
    end = 0
    for p in range(prompt_len.shape[0]):
        begin = end
        end = end + prompt_len[p]
        first = jnp.where(prompt == p, begin, first)
        last = jnp.where(prompt == p, end, last)
    return first, last


def window_rows(count):
    return min(count, count // 3 + ROWS)


def window_start(first, count):
    start = jnp.minimum(first // ROWS * ROWS, count - window_rows(count))
    return pl.multiple_of(start, ROWS)


def stacked(ref, rows, heads, size):
    return jnp.concatenate([ref[rows, a * size : (a + 1) * size] for a in heads], axis=0)


def forward_kernel(
    slots, size, prompt_len, resp_prompt, resp_len, owner,
    query, key, value, prefix, w_out,
    p_pre, p_own, heads_out, part, out_bf,
):
    count = prefix.shape[0]
    window = window_rows(count)
    slot_len = query.shape[0] // slots
    kv_heads = key.shape[1] // size
    groups = query.shape[1] // key.shape[1]
    scale = size ** (-0.5)
    for n in range(slots):
        first, last = prompt_span(prompt_len, resp_prompt[n])
        start = window_start(first, count)
        rows = slice(n * slot_len, (n + 1) * slot_len)
        for h in range(kv_heads):
            heads = range(h * groups, (h + 1) * groups)
            q = stacked(query, rows, heads, size)
            k_win = prefix[pl.ds(start, window), 2 * h * size : (2 * h + 1) * size]
            v_win = prefix[pl.ds(start, window), (2 * h + 1) * size : (2 * h + 2) * size]
            k_own = key[rows, h * size : (h + 1) * size]
            v_own = value[rows, h * size : (h + 1) * size]
            tall = groups * slot_len
            place = start + lax.broadcasted_iota(jnp.int32, (tall, window), 1)
            s_pre = jnp.where((place >= first) & (place < last), dot_nt(q, k_win) * scale, NEG)
            token = lax.broadcasted_iota(jnp.int32, (groups, slot_len, slot_len), 1)
            token = token.reshape(tall, slot_len)
            other = lax.broadcasted_iota(jnp.int32, (tall, slot_len), 1)
            s_own = jnp.where(
                (other <= token) & (other < resp_len[n]), dot_nt(q, k_own) * scale, NEG
            )
            top = jnp.maximum(
                jnp.max(s_pre, axis=-1, keepdims=True), jnp.max(s_own, axis=-1, keepdims=True)
            )
            e_pre = jnp.exp(s_pre - top)
            e_own = jnp.exp(s_own - top)
            total = jnp.sum(e_pre, axis=-1, keepdims=True) + jnp.sum(e_own, axis=-1, keepdims=True)
            b_pre = (e_pre / total).astype(BF16)
            b_own = (e_own / total).astype(BF16)
            p_pre[n, h] = b_pre
            p_own[n, h] = b_own
            out = dot(b_pre, v_win) + dot(b_own, v_own)
            for i, a in enumerate(heads):
                one = out[i * slot_len : (i + 1) * slot_len]
                heads_out[rows, a * size : (a + 1) * size] = one
                out_bf[rows, a * size : (a + 1) * size] = one.astype(BF16)
    width = part.shape[2]
    for b in range(part.shape[0]):
        at = pl.multiple_of(owner[b] * width, width)
        part[b] = dot(out_bf[...], w_out[:, pl.ds(at, width)]).astype(BF16)


def forward(prompt_len, resp_prompt, resp_len, owner, query, key, value, prefix, w_out, size):
    slots = resp_len.shape[0]
    rows, q_width = query.shape
    kv_heads = key.shape[1] // size
    tall = rows // slots * q_width // key.shape[1]
    window = window_rows(prefix.shape[0])
    blocks = owner.shape[0]
    return pl.pallas_call(
        functools.partial(forward_kernel, slots, size),
        in_specs=[SMEM] * 4 + [VMEM] * 5,
        out_specs=[VMEM] * 4,
        out_shape=[
            jax.ShapeDtypeStruct((slots, kv_heads, tall, window), BF16),
            jax.ShapeDtypeStruct((slots, kv_heads, tall, rows // slots), BF16),
            jax.ShapeDtypeStruct((rows, q_width), F32),
            jax.ShapeDtypeStruct((blocks, rows, w_out.shape[1] // blocks), BF16),
        ],
        scratch_shapes=[pltpu.VMEM((rows, q_width), BF16)],
        compiler_params=pltpu.CompilerParams(vmem_limit_bytes=vmem_room(prefix.shape[0])),
        cost_estimate=pl.CostEstimate(
            flops=2 * rows * q_width * (w_out.shape[1] + 2 * window + 2 * rows // slots),
            bytes_accessed=2 * w_out.size + 2 * rows * w_out.shape[1],
            transcendentals=slots * kv_heads * tall * window,
        ),
    )(prompt_len, resp_prompt, resp_len, owner, query, key, value, prefix, w_out)


def vmem_room(prefix_rows):
    return 48 << 20 if prefix_rows > 1024 else 20 << 20


def backward_kernel(
    slots, prompt_len, resp_prompt, resp_len, held, owner,
    cotangent, w_out, query, key, value, prefix, p_pre, p_own, heads_out, hq, hk,
    w_query, w_key, w_value, q_gain, k_gain,
    grad_prefix, part, dhq, dhk, dv,
):
    count = prefix.shape[0]
    window = window_rows(count)
    slot_len = query.shape[0] // slots
    size = q_gain.shape[1]
    kv_heads = key.shape[1] // size
    groups = query.shape[1] // key.shape[1]
    scale = size ** (-0.5)
    width = cotangent.shape[2]
    grad_heads = None
    for b in range(cotangent.shape[0]):
        at = pl.multiple_of(held[b] * width, width)
        term = dot_nt(cotangent[b], w_out[:, pl.ds(at, width)])
        grad_heads = term if b == 0 else grad_heads + term
    grad_prefix[...] = jnp.zeros_like(grad_prefix)
    for n in range(slots):
        first, _ = prompt_span(prompt_len, resp_prompt[n])
        start = window_start(first, count)
        rows = slice(n * slot_len, (n + 1) * slot_len)
        token = lax.broadcasted_iota(jnp.int32, (slot_len, size), 0)
        live = token < resp_len[n]
        for h in range(kv_heads):
            heads = range(h * groups, (h + 1) * groups)
            q = stacked(query, rows, heads, size)
            out = stacked(heads_out, rows, heads, size)
            g = jnp.concatenate(
                [
                    jnp.where(live, grad_heads[rows, a * size : (a + 1) * size], 0.0).astype(BF16)
                    for a in heads
                ],
                axis=0,
            )
            k_win = prefix[pl.ds(start, window), 2 * h * size : (2 * h + 1) * size]
            v_win = prefix[pl.ds(start, window), (2 * h + 1) * size : (2 * h + 2) * size]
            k_own = key[rows, h * size : (h + 1) * size]
            v_own = value[rows, h * size : (h + 1) * size]
            b_pre, b_own = p_pre[n, h], p_own[n, h]
            delta = jnp.sum(g.astype(F32) * out, axis=-1, keepdims=True)
            ds_pre = (b_pre.astype(F32) * (dot_nt(g, v_win) - delta)).astype(BF16)
            ds_own = (b_own.astype(F32) * (dot_nt(g, v_own) - delta)).astype(BF16)
            grad_q = scale * (dot(ds_pre, k_win) + dot(ds_own, k_own))
            for i, a in enumerate(heads):
                cols = slice(a * size, (a + 1) * size)
                one = grad_q[i * slot_len : (i + 1) * slot_len]
                dhq[rows, cols] = norm_back(hq[rows, cols], q_gain[...], one).astype(BF16)
            cols = slice(h * size, (h + 1) * size)
            grad_k = scale * dot_tn(ds_own, q)
            dhk[rows, cols] = norm_back(hk[rows, cols], k_gain[...], grad_k).astype(BF16)
            dv[rows, cols] = dot_tn(b_own, g).astype(BF16)
            k_cols = slice(2 * h * size, (2 * h + 1) * size)
            v_cols = slice((2 * h + 1) * size, (2 * h + 2) * size)
            grad_prefix[pl.ds(start, window), k_cols] += scale * dot_tn(ds_pre, q)
            grad_prefix[pl.ds(start, window), v_cols] += dot_tn(b_pre, g)
    for b in range(part.shape[0]):
        at = pl.multiple_of(owner[b] * part.shape[2], part.shape[2])
        cols = pl.ds(at, part.shape[2])
        part[b] = (
            dot_nt(dhq[...], w_query[cols, :])
            + dot_nt(dhk[...], w_key[cols, :])
            + dot_nt(dv[...], w_value[cols, :])
        ).astype(BF16)


def backward(prompt_len, resp_prompt, resp_len, held, owner, *arrays):
    cotangent, w_out, query, key, value, prefix = arrays[:6]
    slots = resp_len.shape[0]
    rows, q_width = query.shape
    depth = w_out.shape[1]
    blocks = owner.shape[0]
    window = window_rows(prefix.shape[0])
    return pl.pallas_call(
        functools.partial(backward_kernel, slots),
        in_specs=[SMEM] * 5 + [VMEM] * len(arrays),
        out_specs=[VMEM] * 2,
        out_shape=[
            jax.ShapeDtypeStruct(prefix.shape, F32),
            jax.ShapeDtypeStruct((blocks, rows, depth // blocks), BF16),
        ],
        scratch_shapes=[
            pltpu.VMEM((rows, q_width), BF16),
            pltpu.VMEM((rows, key.shape[1]), BF16),
            pltpu.VMEM((rows, key.shape[1]), BF16),
        ],
        compiler_params=pltpu.CompilerParams(vmem_limit_bytes=vmem_room(prefix.shape[0])),
        cost_estimate=pl.CostEstimate(
            flops=2 * rows * (2 * q_width + 2 * key.shape[1]) * depth
            + 10 * rows * q_width * (window + rows // slots),
            bytes_accessed=4 * w_out.size + 2 * depth * key.shape[1] * 2 + 4 * rows * depth,
            transcendentals=0,
        ),
    )(prompt_len, resp_prompt, resp_len, held, owner, *arrays)


def exchange(blocks, axis):
    return lax.all_to_all(blocks, axis, 0, 0, tiled=True)


def gather(block, axis):
    size = lax.axis_size(axis)
    if size > 8:
        return lax.all_gather(block, axis, axis=0)
    return exchange(jnp.broadcast_to(block[None], (size,) + block.shape), axis)


def per_device(
    hidden_rows,
    w_query,
    w_key,
    w_value,
    w_out,
    q_gain,
    k_gain,
    prefix_kv,
    cotangent,
    prompt_len,
    resp_prompt,
    resp_len,
):
    rows = hidden_rows.shape[0]
    size = q_gain.shape[0]
    slots = resp_len.shape[0]
    blocks = lax.axis_size("mp")
    order = jnp.arange(blocks, dtype=jnp.int32)
    q_gain, k_gain = q_gain[None], k_gain[None]
    prefix = gather(prefix_kv, "dp").reshape(-1, prefix_kv.shape[1])
    back = gather(cotangent, "mp")
    query, key, value, hq, hk = project(hidden_rows, w_query, w_key, w_value, q_gain, k_gain)
    p_pre, p_own, heads_out, part_out = forward(
        prompt_len, resp_prompt, resp_len, order, query, key, value, prefix, w_out, size
    )
    sent_out = exchange(part_out, "mp")
    grad_prefix, part_in = backward(
        prompt_len, resp_prompt, resp_len, order, order,
        back, w_out, query, key, value, prefix, p_pre, p_own, heads_out, hq, hk,
        w_query, w_key, w_value, q_gain, k_gain,
    )
    sent_in = exchange(part_in, "mp")
    if lax.axis_size("dp") > 8:
        grad_prefix = lax.psum_scatter(grad_prefix, "dp", scatter_dimension=0, tiled=True)
    else:
        grad_prefix = grad_prefix.reshape((-1,) + prefix_kv.shape)
        grad_prefix = jnp.sum(exchange(grad_prefix, "dp"), axis=0)
    live = jnp.arange(rows // slots, dtype=jnp.int32)[None, :] < resp_len[:, None]
    live = live.reshape(rows, 1)
    mixed = jnp.where(live, jnp.sum(sent_out.astype(F32), axis=0), 0.0).astype(BF16)
    grad_input = jnp.sum(sent_in.astype(F32), axis=0).astype(BF16)
    return mixed, grad_input, grad_prefix.astype(BF16)


def solution(mesh):
    in_specs = (
        P("dp", None),
        P(None, "mp"),
        P(None, "mp"),
        P(None, "mp"),
        P("mp", None),
        P(),
        P(),
        P("dp", "mp"),
        P("dp", "mp"),
        P(),
        P("dp"),
        P("dp"),
    )
    out_specs = (P("dp", "mp"), P("dp", "mp"), P("dp", "mp"))
    return jax.shard_map(
        per_device, mesh=mesh, in_specs=in_specs, out_specs=out_specs, check_vma=False
    )
```

```python
import functools

import jax
import jax.numpy as jnp
from jax import lax
from jax.experimental import pallas as pl
from jax.experimental.pallas import tpu as pltpu
from jax.sharding import PartitionSpec as P

EPS = 1e-06
NEG = -1e30
ROWS = 16
F32 = jnp.float32
BF16 = jnp.bfloat16
HBM = pl.BlockSpec(memory_space=pltpu.HBM)
PIECES = ((2, 1), (3, 0))


def dot(left, right):
    return jnp.dot(left, right, preferred_element_type=F32)


def dot_nt(left, right):
    return lax.dot_general(left, right, (((1,), (1,)), ((), ())), preferred_element_type=F32)


def dot_tn(left, right):
    return lax.dot_general(left, right, (((0,), (0,)), ((), ())), preferred_element_type=F32)


def inverse_root(hidden):
    return lax.rsqrt(jnp.mean(hidden * hidden, axis=-1, keepdims=True) + EPS)


def norm_back(hidden, gain, grad):
    root = inverse_root(hidden)
    unit = hidden * root
    scaled = grad * gain
    return root * (scaled - unit * jnp.mean(scaled * unit, axis=-1, keepdims=True))


class Copies:
    def __init__(self, sems):
        self.sems, self.count = sems, 0

    def start(self, source, target):
        copy = pltpu.make_async_copy(source, target, self.sems.at[self.count])
        self.count += 1
        copy.start()
        return copy


def wait(copies):
    for copy in copies:
        copy.wait()


def prompt_span(prompt_len, prompt):
    first, last = 0, 0
    end = 0
    for p in range(prompt_len.shape[0]):
        begin = end
        end = end + prompt_len[p]
        first = jnp.where(prompt == p, begin, first)
        last = jnp.where(prompt == p, end, last)
    return first, last


def window_rows(count):
    return min(count, count // 3 + ROWS)


def window_start(first, count):
    start = jnp.minimum(first // ROWS * ROWS, count - window_rows(count))
    return pl.multiple_of(start, ROWS)


def slot_rows(slots, rows, step):
    if slots == 1:
        return pl.ds(0, rows)
    at = lax.rem(lax.axis_index("dp") + step + slots, slots) * rows
    return pl.ds(pl.multiple_of(at, ROWS), rows)


def block_of(step, swapped, blocks):
    me = lax.axis_index("mp")
    low = lax.rem(me, 2)
    low = 1 - low if swapped else low
    return lax.rem(me // 2 + step + blocks // 2, blocks // 2) * 2 + low


def features(step, swapped, blocks, width):
    return pl.ds(pl.multiple_of(block_of(step, swapped, blocks) * width, width), width)


def stacked(ref, rows, heads, size):
    return jnp.concatenate([ref[rows, a * size : (a + 1) * size] for a in heads], axis=0)


def send_blocks(copies, make, blocks, width, sends, keeps, send_refs, keep_refs):
    started = []
    for piece, send, ref in zip(PIECES, sends, send_refs):
        for i, k in enumerate(piece):
            ref[i] = make(features(k, True, blocks, width))
            started.append(copies.start(ref.at[i], send.at[i]))
    for k, keep, ref in zip(sum(PIECES, ()), keeps, keep_refs):
        ref[...] = make(features(k, False, blocks, width))
        started.append(copies.start(ref, keep))
    return started


def forward_kernel(slots, blocks, *refs):
    refs = list(refs)

    def take(count):
        found, refs[:count] = refs[:count], []
        return found

    scalars = take(3)
    hidden, w_q, w_k, w_v, q_gain, k_gain, w_out = take(7)
    outs = 8 + 2 + blocks // 2
    prefix = take(len(refs) - 2 * outs - 7 - 3 - 3)
    results = take(8)
    sends, keeps = take(2), take(blocks // 2)
    saved = take(8)
    send_refs, keep_refs = take(2), take(blocks // 2)
    hidden_v, wq_v, wk_v, wv_v, qg_v, kg_v, wo_v = take(7)
    prompt_len, resp_prompt, resp_len = take(3)
    prefix_v, out_bf, sems = take(3)
    query, key, value, hq, hk, p_pre, p_own, heads_out = saved

    copies = Copies(sems)
    depth = hidden.shape[1]
    steps = 4
    part = depth // steps
    loads = []
    for i in range(steps):
        cut = pl.ds(i * part, part)
        loads.append(
            [copies.start(hidden.at[:, cut], hidden_v.at[:, cut])]
            + [
                copies.start(w.at[cut], v.at[cut])
                for w, v in ((w_q, wq_v), (w_k, wk_v), (w_v, wv_v))
            ]
        )
    small = [copies.start(q_gain, qg_v), copies.start(k_gain, kg_v)]
    for source, target in zip(scalars, (prompt_len, resp_prompt, resp_len)):
        small.append(copies.start(source, target))
    held = prefix[0].shape[0]
    for k, ref in enumerate(prefix):
        small.append(copies.start(ref, prefix_v.at[slot_rows(len(prefix), held, -k)]))
    load_out = copies.start(w_out, wo_v)

    sums = [None] * 3
    for i, load in enumerate(loads):
        wait(load)
        rows = hidden_v[:, i * part : (i + 1) * part]
        for j, v in enumerate((wq_v, wk_v, wv_v)):
            term = dot(rows, v[i * part : (i + 1) * part])
            sums[j] = term if i == 0 else sums[j] + term
    hq[...], hk[...] = sums[0], sums[1]
    value[...] = sums[2].astype(BF16)
    wait(small)
    size = qg_v.shape[1]
    for total, gain, out in ((sums[0], qg_v, query), (sums[1], kg_v, key)):
        for at in range(0, total.shape[1], size):
            head = total[:, at : at + size]
            out[:, at : at + size] = (head * inverse_root(head) * gain[...]).astype(BF16)
    stores = [copies.start(saved[i], results[i]) for i in range(5)]

    count = prefix_v.shape[0]
    window = window_rows(count)
    slot_len = query.shape[0] // slots
    kv_heads = key.shape[1] // size
    groups = query.shape[1] // key.shape[1]
    scale = size ** (-0.5)
    for n in range(slots):
        first, last = prompt_span(prompt_len, resp_prompt[n])
        start = window_start(first, count)
        rows = slice(n * slot_len, (n + 1) * slot_len)
        live = lax.broadcasted_iota(jnp.int32, (slot_len, size), 0) < resp_len[n]
        for h in range(kv_heads):
            heads = range(h * groups, (h + 1) * groups)
            q = stacked(query, rows, heads, size)
            k_win = prefix_v[pl.ds(start, window), 2 * h * size : (2 * h + 1) * size]
            v_win = prefix_v[pl.ds(start, window), (2 * h + 1) * size : (2 * h + 2) * size]
            k_own = key[rows, h * size : (h + 1) * size]
            v_own = value[rows, h * size : (h + 1) * size]
            tall = groups * slot_len
            place = start + lax.broadcasted_iota(jnp.int32, (tall, window), 1)
            s_pre = jnp.where((place >= first) & (place < last), dot_nt(q, k_win) * scale, NEG)
            token = lax.broadcasted_iota(jnp.int32, (groups, slot_len, slot_len), 1)
            token = token.reshape(tall, slot_len)
            other = lax.broadcasted_iota(jnp.int32, (tall, slot_len), 1)
            s_own = jnp.where(
                (other <= token) & (other < resp_len[n]), dot_nt(q, k_own) * scale, NEG
            )
            top = jnp.maximum(
                jnp.max(s_pre, axis=-1, keepdims=True), jnp.max(s_own, axis=-1, keepdims=True)
            )
            e_pre = jnp.exp(s_pre - top)
            e_own = jnp.exp(s_own - top)
            total = jnp.sum(e_pre, axis=-1, keepdims=True) + jnp.sum(e_own, axis=-1, keepdims=True)
            b_pre = (e_pre / total).astype(BF16)
            b_own = (e_own / total).astype(BF16)
            p_pre[n, h] = b_pre
            p_own[n, h] = b_own
            out = dot(b_pre, v_win) + dot(b_own, v_own)
            for i, a in enumerate(heads):
                one = out[i * slot_len : (i + 1) * slot_len]
                heads_out[rows, a * size : (a + 1) * size] = one
                out_bf[rows, a * size : (a + 1) * size] = jnp.where(live, one, 0.0).astype(BF16)
    stores += [copies.start(saved[i], results[i]) for i in range(5, 8)]
    load_out.wait()

    def make(cols):
        return dot(out_bf[...], wo_v[:, cols]).astype(BF16)

    width = depth // blocks
    stores += send_blocks(copies, make, blocks, width, sends, keeps, send_refs, keep_refs)
    wait(stores)


def block_shapes(blocks, rows, depth):
    width = depth // blocks
    shapes = [jax.ShapeDtypeStruct((len(piece), rows, width), BF16) for piece in PIECES]
    return shapes + [jax.ShapeDtypeStruct((rows, width), BF16)] * (blocks // 2)


def scratch(shapes):
    return [pltpu.VMEM(x.shape, x.dtype) for x in shapes]


def vmem_room(prefix_rows):
    return 48 << 20 if prefix_rows > 1024 else 24 << 20


def forward(blocks, scalars, hidden, w_q, w_k, w_v, q_gain, k_gain, w_out, prefix):
    slots = scalars[-1].shape[0]
    size = q_gain.shape[1]
    rows, depth = hidden.shape
    q_width, k_width = w_q.shape[1], w_k.shape[1]
    count = sum(x.shape[0] for x in prefix)
    window = window_rows(count)
    slot_len = rows // slots
    kv_heads, tall = k_width // size, slot_len * q_width // k_width
    results = [
        jax.ShapeDtypeStruct((rows, q_width), BF16),
        jax.ShapeDtypeStruct((rows, k_width), BF16),
        jax.ShapeDtypeStruct((rows, k_width), BF16),
        jax.ShapeDtypeStruct((rows, q_width), F32),
        jax.ShapeDtypeStruct((rows, k_width), F32),
        jax.ShapeDtypeStruct((slots, kv_heads, tall, window), BF16),
        jax.ShapeDtypeStruct((slots, kv_heads, tall, slot_len), BF16),
        jax.ShapeDtypeStruct((rows, q_width), F32),
    ]
    shapes = results + block_shapes(blocks, rows, depth)
    weights = [hidden, w_q, w_k, w_v, q_gain, k_gain, w_out]
    found = pl.pallas_call(
        functools.partial(forward_kernel, slots, blocks),
        in_specs=[HBM] * (3 + 7 + len(prefix)),
        out_specs=[HBM] * len(shapes),
        out_shape=shapes,
        scratch_shapes=scratch(shapes)
        + scratch(weights)
        + [pltpu.SMEM(x.shape, jnp.int32) for x in scalars]
        + [
            pltpu.VMEM((count, prefix[0].shape[1]), BF16),
            pltpu.VMEM((rows, q_width), BF16),
            pltpu.SemaphoreType.DMA((64,)),
        ],
        compiler_params=pltpu.CompilerParams(vmem_limit_bytes=vmem_room(count)),
        cost_estimate=pl.CostEstimate(
            flops=2 * rows * depth * (2 * q_width + 2 * k_width),
            bytes_accessed=2 * depth * (rows + 2 * q_width + 2 * k_width) + 2 * rows * depth,
            transcendentals=slots * kv_heads * tall * window,
        ),
    )(*scalars, *weights, *prefix)
    return found[:8], found[8:10], found[10:]


def backward_kernel(slots, blocks, *refs):
    refs = list(refs)

    def take(count):
        found, refs[:count] = refs[:count], []
        return found

    scalars = take(3)
    cotangent = take(blocks)
    weights = take(6)
    saved = take(8)
    outs = 2 + blocks // 2
    prefix = take((len(refs) - 2 * outs - blocks - 6 - 8 - 3 - 6) // 2)
    terms = take(len(prefix))
    sends, keeps = take(2), take(blocks // 2)
    send_refs, keep_refs = take(2), take(blocks // 2)
    cot_v = take(blocks)
    w_out, w_q, w_k, w_v, q_gain, k_gain = weights_v = take(6)
    query, key, value, hq, hk, p_pre, p_own, heads_out = saved_v = take(8)
    prompt_len, resp_prompt, resp_len = scalars_v = take(3)
    prefix_v, grad_prefix, dhq, dhk, dv, sems = take(6)

    copies = Copies(sems)
    load_out = copies.start(weights[0], w_out)
    load_cot = [copies.start(a, b) for a, b in zip(cotangent, cot_v)]
    small = [copies.start(a, b) for a, b in zip(scalars, scalars_v)]
    small += [copies.start(a, b) for a, b in zip(saved, saved_v)]
    held = prefix[0].shape[0]
    for k, ref in enumerate(prefix):
        small.append(copies.start(ref, prefix_v.at[slot_rows(len(prefix), held, -k)]))
    small += [copies.start(a, b) for a, b in zip(weights[4:], weights_v[4:])]
    load_in = [copies.start(a, b) for a, b in zip(weights[1:4], weights_v[1:4])]

    depth = w_out.shape[1]
    width = depth // blocks
    load_out.wait()
    grad_heads = None
    for b, ref in enumerate(cot_v):
        load_cot[b].wait()
        term = dot_nt(ref[...], w_out[:, features(-(b // 2), b % 2 == 1, blocks, width)])
        grad_heads = term if b == 0 else grad_heads + term
    grad_prefix[...] = jnp.zeros_like(grad_prefix)
    wait(small)

    count = prefix_v.shape[0]
    window = window_rows(count)
    slot_len = query.shape[0] // slots
    size = q_gain.shape[1]
    kv_heads = key.shape[1] // size
    groups = query.shape[1] // key.shape[1]
    scale = size ** (-0.5)
    for n in range(slots):
        first, _ = prompt_span(prompt_len, resp_prompt[n])
        start = window_start(first, count)
        rows = slice(n * slot_len, (n + 1) * slot_len)
        live = lax.broadcasted_iota(jnp.int32, (slot_len, size), 0) < resp_len[n]
        for h in range(kv_heads):
            heads = range(h * groups, (h + 1) * groups)
            q = stacked(query, rows, heads, size)
            out = stacked(heads_out, rows, heads, size)
            g = jnp.concatenate(
                [
                    jnp.where(live, grad_heads[rows, a * size : (a + 1) * size], 0.0).astype(BF16)
                    for a in heads
                ],
                axis=0,
            )
            k_win = prefix_v[pl.ds(start, window), 2 * h * size : (2 * h + 1) * size]
            v_win = prefix_v[pl.ds(start, window), (2 * h + 1) * size : (2 * h + 2) * size]
            k_own = key[rows, h * size : (h + 1) * size]
            v_own = value[rows, h * size : (h + 1) * size]
            b_pre, b_own = p_pre[n, h], p_own[n, h]
            delta = jnp.sum(g.astype(F32) * out, axis=-1, keepdims=True)
            ds_pre = (b_pre.astype(F32) * (dot_nt(g, v_win) - delta)).astype(BF16)
            ds_own = (b_own.astype(F32) * (dot_nt(g, v_own) - delta)).astype(BF16)
            grad_q = scale * (dot(ds_pre, k_win) + dot(ds_own, k_own))
            for i, a in enumerate(heads):
                cols = slice(a * size, (a + 1) * size)
                one = grad_q[i * slot_len : (i + 1) * slot_len]
                dhq[rows, cols] = norm_back(hq[rows, cols], q_gain[...], one).astype(BF16)
            cols = slice(h * size, (h + 1) * size)
            grad_k = scale * dot_tn(ds_own, q)
            dhk[rows, cols] = norm_back(hk[rows, cols], k_gain[...], grad_k).astype(BF16)
            dv[rows, cols] = dot_tn(b_own, g).astype(BF16)
            k_cols = slice(2 * h * size, (2 * h + 1) * size)
            v_cols = slice((2 * h + 1) * size, (2 * h + 2) * size)
            grad_prefix[pl.ds(start, window), k_cols] += scale * dot_tn(ds_pre, q)
            grad_prefix[pl.ds(start, window), v_cols] += dot_tn(b_pre, g)
    stores = [
        copies.start(grad_prefix.at[slot_rows(len(terms), held, k)], ref)
        for k, ref in enumerate(terms)
    ]
    wait(load_in)

    def make(cols):
        return (
            dot_nt(dhq[...], w_q[cols, :])
            + dot_nt(dhk[...], w_k[cols, :])
            + dot_nt(dv[...], w_v[cols, :])
        ).astype(BF16)

    stores += send_blocks(copies, make, blocks, width, sends, keeps, send_refs, keep_refs)
    wait(stores)


def backward(blocks, scalars, cotangent, weights, saved, prefix):
    slots = scalars[-1].shape[0]
    w_out, w_k = weights[0], weights[2]
    rows, q_width = saved[0].shape
    k_width = w_k.shape[1]
    depth = w_out.shape[1]
    count, kv_width = sum(x.shape[0] for x in prefix), prefix[0].shape[1]
    window = window_rows(count)
    shapes = block_shapes(blocks, rows, depth)
    found = pl.pallas_call(
        functools.partial(backward_kernel, slots, blocks),
        in_specs=[HBM] * (3 + blocks + 6 + 8 + len(prefix)),
        out_specs=[HBM] * (len(prefix) + len(shapes)),
        out_shape=[jax.ShapeDtypeStruct(x.shape, F32) for x in prefix] + shapes,
        scratch_shapes=scratch(shapes)
        + scratch(cotangent)
        + scratch(weights)
        + scratch(saved)
        + [pltpu.SMEM(x.shape, jnp.int32) for x in scalars]
        + [
            pltpu.VMEM((count, kv_width), BF16),
            pltpu.VMEM((count, kv_width), F32),
            pltpu.VMEM((rows, q_width), BF16),
            pltpu.VMEM((rows, k_width), BF16),
            pltpu.VMEM((rows, k_width), BF16),
            pltpu.SemaphoreType.DMA((64,)),
        ],
        compiler_params=pltpu.CompilerParams(vmem_limit_bytes=vmem_room(count)),
        cost_estimate=pl.CostEstimate(
            flops=2 * rows * (2 * q_width + 2 * k_width) * depth
            + 10 * rows * q_width * (window + rows // slots),
            bytes_accessed=4 * w_out.size + 2 * depth * k_width * 2 + 4 * rows * depth,
            transcendentals=0,
        ),
    )(*scalars, *cotangent, *weights, *saved, *prefix)
    cut = len(prefix)
    return found[:cut], found[cut : cut + 2], found[cut + 2 :]


def shift(block, axis, by):
    size = lax.axis_size(axis)
    return lax.ppermute(block, axis, [(i, (i + by) % size) for i in range(size)])


def swap(block):
    return lax.ppermute(block, "mp", [(i, i ^ 1) for i in range(lax.axis_size("mp"))])


def scatter_features(sends, keeps):
    kept = iter(keeps)
    parts = {}
    for piece, send in zip(PIECES, sends):
        got = swap(send)
        for i, k in enumerate(piece):
            both = next(kept).astype(F32) + got[i].astype(F32)
            parts[k] = shift(both.astype(BF16), "mp", 2 * k).astype(F32) if k else both
    total = parts[0]
    for k in sorted(parts)[1:]:
        total = total + parts[k]
    return total.astype(BF16)


def per_device(
    hidden_rows,
    w_query,
    w_key,
    w_value,
    w_out,
    q_gain,
    k_gain,
    prefix_kv,
    cotangent,
    prompt_len,
    resp_prompt,
    resp_len,
):
    blocks = lax.axis_size("mp")
    chips = lax.axis_size("dp")
    scalars = (prompt_len, resp_prompt, resp_len)
    q_gain, k_gain = q_gain[None], k_gain[None]
    if chips > 8:
        prefix = [lax.all_gather(prefix_kv, "dp", axis=0, tiled=True)]
    else:
        prefix = [prefix_kv] + [shift(prefix_kv, "dp", k) for k in range(1, chips)]
    back = [cotangent] + [shift(cotangent, "mp", 2 * k) for k in range(1, blocks // 2)]
    back = [x for one in back for x in (one, swap(one))]
    saved, sends, keeps = forward(
        blocks, scalars, hidden_rows, w_query, w_key, w_value, q_gain, k_gain, w_out, prefix
    )
    mixed = scatter_features(sends, keeps)
    weights = (w_out, w_query, w_key, w_value, q_gain, k_gain)
    terms, sends, keeps = backward(blocks, scalars, back, weights, saved, prefix)
    grad_input = scatter_features(sends, keeps)
    if chips > 8:
        grad_prefix = lax.psum_scatter(terms[0], "dp", scatter_dimension=0, tiled=True)
    else:
        grad_prefix = terms[0]
        for k in range(1, chips):
            grad_prefix = grad_prefix + shift(terms[k], "dp", k)
    return mixed, grad_input, grad_prefix.astype(BF16)


def solution(mesh):
    in_specs = (
        P("dp", None),
        P(None, "mp"),
        P(None, "mp"),
        P(None, "mp"),
        P("mp", None),
        P(),
        P(),
        P("dp", "mp"),
        P("dp", "mp"),
        P(),
        P("dp"),
        P("dp"),
    )
    out_specs = (P("dp", "mp"), P("dp", "mp"), P("dp", "mp"))
    return jax.shard_map(
        per_device, mesh=mesh, in_specs=in_specs, out_specs=out_specs, check_vma=False
    )
```

```python
import functools

import jax
import jax.numpy as jnp
from jax import lax
from jax.experimental import pallas as pl
from jax.experimental.pallas import tpu as pltpu
from jax.sharding import PartitionSpec as P

EPS = 1e-06
NEG = -1e30
ROWS = 16
F32 = jnp.float32
BF16 = jnp.bfloat16
HBM = pl.BlockSpec(memory_space=pltpu.HBM)
VMEM = pl.BlockSpec(memory_space=pltpu.VMEM)
PIECES = ((2, 1), (3, 0))


def dot(left, right):
    return jnp.dot(left, right, preferred_element_type=F32)


def dot_nt(left, right):
    return lax.dot_general(left, right, (((1,), (1,)), ((), ())), preferred_element_type=F32)


def dot_tn(left, right):
    return lax.dot_general(left, right, (((0,), (0,)), ((), ())), preferred_element_type=F32)


def inverse_root(hidden):
    return lax.rsqrt(jnp.mean(hidden * hidden, axis=-1, keepdims=True) + EPS)


def norm_back(hidden, gain, grad):
    root = inverse_root(hidden)
    unit = hidden * root
    scaled = grad * gain
    return root * (scaled - unit * jnp.mean(scaled * unit, axis=-1, keepdims=True))


class Copies:
    def __init__(self, sems):
        self.sems, self.count = sems, 0

    def start(self, source, target):
        copy = pltpu.make_async_copy(source, target, self.sems.at[self.count])
        self.count += 1
        copy.start()
        return copy


def wait(copies):
    for copy in copies:
        copy.wait()


def prompt_span(prompt_len, prompt):
    first, last = 0, 0
    end = 0
    for p in range(prompt_len.shape[0]):
        begin = end
        end = end + prompt_len[p]
        first = jnp.where(prompt == p, begin, first)
        last = jnp.where(prompt == p, end, last)
    return first, last


def window_rows(count):
    return min(count, count // 3 + ROWS)


def window_start(first, count):
    start = jnp.minimum(first // ROWS * ROWS, count - window_rows(count))
    return pl.multiple_of(start, ROWS)


def slot_rows(slots, rows, step):
    if slots == 1:
        return pl.ds(0, rows)
    at = lax.rem(lax.axis_index("dp") + step + slots, slots) * rows
    return pl.ds(pl.multiple_of(at, ROWS), rows)


def block_of(step, swapped, blocks):
    me = lax.axis_index("mp")
    low = lax.rem(me, 2)
    low = 1 - low if swapped else low
    return lax.rem(me // 2 + step + blocks // 2, blocks // 2) * 2 + low


def features(step, swapped, blocks, width):
    return pl.ds(pl.multiple_of(block_of(step, swapped, blocks) * width, width), width)


def stacked(ref, rows, heads, size):
    return jnp.concatenate([ref[rows, a * size : (a + 1) * size] for a in heads], axis=0)


def make_blocks(make, blocks, width, sends, keeps):
    for piece, send in zip(PIECES, sends):
        for i, k in enumerate(piece):
            send[i] = make(features(k, True, blocks, width))
    for k, keep in zip(sum(PIECES, ()), keeps):
        keep[...] = make(features(k, False, blocks, width))


def forward_kernel(slots, blocks, *refs):
    refs = list(refs)

    def take(count):
        found, refs[:count] = refs[:count], []
        return found

    scalars = take(3)
    hidden, w_q, w_k, w_v, q_gain, k_gain, w_out = take(7)
    prefix = take(len(refs) - 8 - 7 - 2 - blocks // 2 - 1 - 3 - 2)
    saved = take(8)
    wq_v, wk_v, wv_v, qg_v, kg_v, wo_v, prefix_v = take(7)
    sends, keeps = take(2), take(blocks // 2)
    (hidden_v,) = take(1)
    prompt_len, resp_prompt, resp_len = take(3)
    out_bf, sems = take(2)
    query, key, value, hq, hk, p_pre, p_own, heads_out = saved

    copies = Copies(sems)
    depth = hidden.shape[1]
    steps = 4
    part = depth // steps
    loads = []
    for i in range(steps):
        cut = pl.ds(i * part, part)
        loads.append(
            [copies.start(hidden.at[:, cut], hidden_v.at[:, cut])]
            + [
                copies.start(w.at[cut], v.at[cut])
                for w, v in ((w_q, wq_v), (w_k, wk_v), (w_v, wv_v))
            ]
        )
    small = [copies.start(q_gain, qg_v), copies.start(k_gain, kg_v)]
    for source, target in zip(scalars, (prompt_len, resp_prompt, resp_len)):
        small.append(copies.start(source, target))
    held = prefix[0].shape[0]
    small.append(copies.start(prefix[0], prefix_v.at[slot_rows(len(prefix), held, 0)]))
    load_out = copies.start(w_out, wo_v)

    sums = [None] * 3
    for i, load in enumerate(loads):
        wait(load)
        rows = hidden_v[:, i * part : (i + 1) * part]
        for j, v in enumerate((wq_v, wk_v, wv_v)):
            term = dot(rows, v[i * part : (i + 1) * part])
            sums[j] = term if i == 0 else sums[j] + term
    hq[...], hk[...] = sums[0], sums[1]
    value[...] = sums[2].astype(BF16)
    wait(small)
    for k, ref in enumerate(prefix[1:], 1):
        prefix_v[slot_rows(len(prefix), held, -k), :] = ref[...]
    size = qg_v.shape[1]
    for total, gain, out in ((sums[0], qg_v, query), (sums[1], kg_v, key)):
        for at in range(0, total.shape[1], size):
            head = total[:, at : at + size]
            out[:, at : at + size] = (head * inverse_root(head) * gain[...]).astype(BF16)

    count = prefix_v.shape[0]
    window = window_rows(count)
    slot_len = query.shape[0] // slots
    kv_heads = key.shape[1] // size
    groups = query.shape[1] // key.shape[1]
    scale = size ** (-0.5)
    for n in range(slots):
        first, last = prompt_span(prompt_len, resp_prompt[n])
        start = window_start(first, count)
        rows = slice(n * slot_len, (n + 1) * slot_len)
        live = lax.broadcasted_iota(jnp.int32, (slot_len, size), 0) < resp_len[n]
        for h in range(kv_heads):
            heads = range(h * groups, (h + 1) * groups)
            q = stacked(query, rows, heads, size)
            k_win = prefix_v[pl.ds(start, window), 2 * h * size : (2 * h + 1) * size]
            v_win = prefix_v[pl.ds(start, window), (2 * h + 1) * size : (2 * h + 2) * size]
            k_own = key[rows, h * size : (h + 1) * size]
            v_own = value[rows, h * size : (h + 1) * size]
            tall = groups * slot_len
            place = start + lax.broadcasted_iota(jnp.int32, (tall, window), 1)
            s_pre = jnp.where((place >= first) & (place < last), dot_nt(q, k_win) * scale, NEG)
            token = lax.broadcasted_iota(jnp.int32, (groups, slot_len, slot_len), 1)
            token = token.reshape(tall, slot_len)
            other = lax.broadcasted_iota(jnp.int32, (tall, slot_len), 1)
            s_own = jnp.where(
                (other <= token) & (other < resp_len[n]), dot_nt(q, k_own) * scale, NEG
            )
            top = jnp.maximum(
                jnp.max(s_pre, axis=-1, keepdims=True), jnp.max(s_own, axis=-1, keepdims=True)
            )
            e_pre = jnp.exp(s_pre - top)
            e_own = jnp.exp(s_own - top)
            total = jnp.sum(e_pre, axis=-1, keepdims=True) + jnp.sum(e_own, axis=-1, keepdims=True)
            b_pre = (e_pre / total).astype(BF16)
            b_own = (e_own / total).astype(BF16)
            p_pre[n, h] = b_pre
            p_own[n, h] = b_own
            out = dot(b_pre, v_win) + dot(b_own, v_own)
            for i, a in enumerate(heads):
                one = out[i * slot_len : (i + 1) * slot_len]
                heads_out[rows, a * size : (a + 1) * size] = one
                out_bf[rows, a * size : (a + 1) * size] = jnp.where(live, one, 0.0).astype(BF16)
    load_out.wait()

    def make(cols):
        return dot(out_bf[...], wo_v[:, cols]).astype(BF16)

    width = depth // blocks
    make_blocks(make, blocks, width, sends, keeps)


def block_shapes(blocks, rows, depth):
    width = depth // blocks
    return [((len(piece), rows, width), BF16) for piece in PIECES] + [
        ((rows, width), BF16)
    ] * (blocks // 2)


def in_vmem(shapes):
    return [pltpu.VMEM(*x) for x in shapes]


def held_in(space, arrays):
    return [pltpu.with_memory_space_constraint(x, space) for x in arrays]


def like(arrays):
    return [(x.shape, x.dtype) for x in arrays]


def vmem_room(prefix_rows):
    return 48 << 20 if prefix_rows > 1024 else 24 << 20


def forward(blocks, scalars, hidden, w_q, w_k, w_v, q_gain, k_gain, w_out, prefix):
    slots = scalars[-1].shape[0]
    size = q_gain.shape[1]
    rows, depth = hidden.shape
    q_width, k_width = w_q.shape[1], w_k.shape[1]
    count = sum(x.shape[0] for x in prefix)
    window = window_rows(count)
    slot_len = rows // slots
    kv_heads, tall = k_width // size, slot_len * q_width // k_width
    saved = [
        ((rows, q_width), BF16),
        ((rows, k_width), BF16),
        ((rows, k_width), BF16),
        ((rows, q_width), F32),
        ((rows, k_width), F32),
        ((slots, kv_heads, tall, window), BF16),
        ((slots, kv_heads, tall, slot_len), BF16),
        ((rows, q_width), F32),
    ]
    weights = [w_q, w_k, w_v, q_gain, k_gain, w_out]
    kept = saved + like(weights) + [((count, prefix[0].shape[1]), BF16)]
    sent = block_shapes(blocks, rows, depth)
    operands = [*scalars, hidden, *weights, prefix[0]]
    found = pl.pallas_call(
        functools.partial(forward_kernel, slots, blocks),
        in_specs=[HBM] * len(operands) + [VMEM] * (len(prefix) - 1),
        out_specs=[VMEM] * len(kept + sent),
        out_shape=in_vmem(kept + sent),
        scratch_shapes=[pltpu.VMEM(hidden.shape, hidden.dtype)]
        + [pltpu.SMEM(x.shape, jnp.int32) for x in scalars]
        + [pltpu.VMEM((rows, q_width), BF16), pltpu.SemaphoreType.DMA((64,))],
        compiler_params=pltpu.CompilerParams(vmem_limit_bytes=vmem_room(count)),
        cost_estimate=pl.CostEstimate(
            flops=2 * rows * depth * (2 * q_width + 2 * k_width),
            bytes_accessed=2 * depth * (rows + 2 * q_width + 2 * k_width) + 2 * rows * depth,
            transcendentals=slots * kv_heads * tall * window,
        ),
    )(*held_in(pltpu.HBM, operands), *held_in(pltpu.VMEM, prefix[1:]))
    found, sent = found[: len(kept)], found[len(kept) :]
    return found, sent[:2], sent[2:]


def backward_kernel(slots, blocks, *refs):
    refs = list(refs)

    def take(count):
        found, refs[:count] = refs[:count], []
        return found

    scalars = take(3)
    cotangent = take(blocks)
    query, key, value, hq, hk, p_pre, p_own, heads_out = take(8)
    w_q, w_k, w_v, q_gain, k_gain, w_out, prefix_v = take(7)
    terms = take(len(refs) - 2 - blocks // 2 - 1 - 3 - 5)
    sends, keeps = take(2), take(blocks // 2)
    (own,) = take(1)
    prompt_len, resp_prompt, resp_len = scalars_v = take(3)
    grad_prefix, dhq, dhk, dv, sems = take(5)

    copies = Copies(sems)
    load_own = copies.start(cotangent[0], own)
    small = [copies.start(a, b) for a, b in zip(scalars, scalars_v)]

    depth = w_out.shape[1]
    width = depth // blocks
    grad_heads = None
    load_own.wait()
    for b, ref in enumerate([own, *cotangent[1:]]):
        term = dot_nt(ref[...], w_out[:, features(-(b // 2), b % 2 == 1, blocks, width)])
        grad_heads = term if b == 0 else grad_heads + term
    grad_prefix[...] = jnp.zeros_like(grad_prefix)
    wait(small)

    count = prefix_v.shape[0]
    window = window_rows(count)
    slot_len = query.shape[0] // slots
    size = q_gain.shape[1]
    kv_heads = key.shape[1] // size
    groups = query.shape[1] // key.shape[1]
    scale = size ** (-0.5)
    for n in range(slots):
        first, _ = prompt_span(prompt_len, resp_prompt[n])
        start = window_start(first, count)
        rows = slice(n * slot_len, (n + 1) * slot_len)
        live = lax.broadcasted_iota(jnp.int32, (slot_len, size), 0) < resp_len[n]
        for h in range(kv_heads):
            heads = range(h * groups, (h + 1) * groups)
            q = stacked(query, rows, heads, size)
            out = stacked(heads_out, rows, heads, size)
            g = jnp.concatenate(
                [
                    jnp.where(live, grad_heads[rows, a * size : (a + 1) * size], 0.0).astype(BF16)
                    for a in heads
                ],
                axis=0,
            )
            k_win = prefix_v[pl.ds(start, window), 2 * h * size : (2 * h + 1) * size]
            v_win = prefix_v[pl.ds(start, window), (2 * h + 1) * size : (2 * h + 2) * size]
            k_own = key[rows, h * size : (h + 1) * size]
            v_own = value[rows, h * size : (h + 1) * size]
            b_pre, b_own = p_pre[n, h], p_own[n, h]
            delta = jnp.sum(g.astype(F32) * out, axis=-1, keepdims=True)
            ds_pre = (b_pre.astype(F32) * (dot_nt(g, v_win) - delta)).astype(BF16)
            ds_own = (b_own.astype(F32) * (dot_nt(g, v_own) - delta)).astype(BF16)
            grad_q = scale * (dot(ds_pre, k_win) + dot(ds_own, k_own))
            for i, a in enumerate(heads):
                cols = slice(a * size, (a + 1) * size)
                one = grad_q[i * slot_len : (i + 1) * slot_len]
                dhq[rows, cols] = norm_back(hq[rows, cols], q_gain[...], one).astype(BF16)
            cols = slice(h * size, (h + 1) * size)
            grad_k = scale * dot_tn(ds_own, q)
            dhk[rows, cols] = norm_back(hk[rows, cols], k_gain[...], grad_k).astype(BF16)
            dv[rows, cols] = dot_tn(b_own, g).astype(BF16)
            k_cols = slice(2 * h * size, (2 * h + 1) * size)
            v_cols = slice((2 * h + 1) * size, (2 * h + 2) * size)
            grad_prefix[pl.ds(start, window), k_cols] += scale * dot_tn(ds_pre, q)
            grad_prefix[pl.ds(start, window), v_cols] += dot_tn(b_pre, g)
    held = terms[0].shape[0]
    for k, ref in enumerate(terms):
        ref[...] = grad_prefix[slot_rows(len(terms), held, k), :]

    def make(cols):
        return (
            dot_nt(dhq[...], w_q[cols, :])
            + dot_nt(dhk[...], w_k[cols, :])
            + dot_nt(dv[...], w_v[cols, :])
        ).astype(BF16)

    make_blocks(make, blocks, width, sends, keeps)


def backward(blocks, scalars, cotangent, kept, prefix):
    slots = scalars[-1].shape[0]
    w_out, w_k = kept[13], kept[9]
    rows, q_width = kept[0].shape
    k_width = w_k.shape[1]
    depth = w_out.shape[1]
    count, kv_width = kept[14].shape
    sent = block_shapes(blocks, rows, depth)
    operands = [*scalars, cotangent[0]]
    results = [(x.shape, F32) for x in prefix] + sent
    found = pl.pallas_call(
        functools.partial(backward_kernel, slots, blocks),
        in_specs=[HBM] * len(operands) + [VMEM] * (blocks - 1 + len(kept)),
        out_specs=[VMEM] * len(results),
        out_shape=in_vmem(results),
        scratch_shapes=in_vmem(like(cotangent[:1]))
        + [pltpu.SMEM(x.shape, jnp.int32) for x in scalars]
        + [
            pltpu.VMEM((count, kv_width), F32),
            pltpu.VMEM((rows, q_width), BF16),
            pltpu.VMEM((rows, k_width), BF16),
            pltpu.VMEM((rows, k_width), BF16),
            pltpu.SemaphoreType.DMA((64,)),
        ],
        compiler_params=pltpu.CompilerParams(vmem_limit_bytes=vmem_room(count)),
        cost_estimate=pl.CostEstimate(
            flops=2 * rows * (2 * q_width + 2 * k_width) * depth
            + 10 * rows * q_width * (window_rows(count) + rows // slots),
            bytes_accessed=4 * rows * depth,
            transcendentals=0,
        ),
    )(*held_in(pltpu.HBM, operands), *held_in(pltpu.VMEM, [*cotangent[1:], *kept]))
    cut = len(prefix)
    return found[:cut], found[cut : cut + 2], found[cut + 2 :]


def shift(block, axis, by):
    size = lax.axis_size(axis)
    return lax.ppermute(block, axis, [(i, (i + by) % size) for i in range(size)])


def swap(block):
    return lax.ppermute(block, "mp", [(i, i ^ 1) for i in range(lax.axis_size("mp"))])


def scatter_features(sends, keeps):
    kept = iter(keeps)
    parts = {}
    for piece, send in zip(PIECES, sends):
        got = swap(send)
        for i, k in enumerate(piece):
            both = next(kept).astype(F32) + got[i].astype(F32)
            parts[k] = shift(both.astype(BF16), "mp", 2 * k).astype(F32) if k else both
    total = parts[0]
    for k in sorted(parts)[1:]:
        total = total + parts[k]
    return total.astype(BF16)


def per_device(
    hidden_rows,
    w_query,
    w_key,
    w_value,
    w_out,
    q_gain,
    k_gain,
    prefix_kv,
    cotangent,
    prompt_len,
    resp_prompt,
    resp_len,
):
    blocks = lax.axis_size("mp")
    chips = lax.axis_size("dp")
    scalars = (prompt_len, resp_prompt, resp_len)
    q_gain, k_gain = q_gain[None], k_gain[None]
    if chips > 8:
        prefix = [lax.all_gather(prefix_kv, "dp", axis=0, tiled=True)]
    else:
        prefix = [prefix_kv] + [shift(prefix_kv, "dp", k) for k in range(1, chips)]
    back = [cotangent] + [shift(cotangent, "mp", 2 * k) for k in range(1, blocks // 2)]
    back = [x for one in back for x in (one, swap(one))]
    kept, sends, keeps = forward(
        blocks, scalars, hidden_rows, w_query, w_key, w_value, q_gain, k_gain, w_out, prefix
    )
    mixed = scatter_features(sends, keeps)
    terms, sends, keeps = backward(blocks, scalars, back, kept, prefix)
    grad_input = scatter_features(sends, keeps)
    if chips > 8:
        grad_prefix = lax.psum_scatter(terms[0], "dp", scatter_dimension=0, tiled=True)
    else:
        grad_prefix = terms[0]
        for k in range(1, chips):
            grad_prefix = grad_prefix + shift(terms[k], "dp", k)
    return mixed, grad_input, grad_prefix.astype(BF16)


def solution(mesh):
    in_specs = (
        P("dp", None),
        P(None, "mp"),
        P(None, "mp"),
        P(None, "mp"),
        P("mp", None),
        P(),
        P(),
        P("dp", "mp"),
        P("dp", "mp"),
        P(),
        P("dp"),
        P("dp"),
    )
    out_specs = (P("dp", "mp"), P("dp", "mp"), P("dp", "mp"))
    return jax.shard_map(
        per_device, mesh=mesh, in_specs=in_specs, out_specs=out_specs, check_vma=False
    )
```

```python
import functools

import jax
import jax.numpy as jnp
from jax import lax
from jax.experimental import pallas as pl
from jax.experimental.pallas import tpu as pltpu
from jax.sharding import PartitionSpec as P

EPS = 1e-06
NEG = -1e30
ROWS = 16
F32 = jnp.float32
BF16 = jnp.bfloat16
HBM = pl.BlockSpec(memory_space=pltpu.HBM)
VMEM = pl.BlockSpec(memory_space=pltpu.VMEM)


def dot(left, right):
    return jnp.dot(left, right, preferred_element_type=F32)


def dot_nt(left, right):
    return lax.dot_general(left, right, (((1,), (1,)), ((), ())), preferred_element_type=F32)


def dot_tn(left, right):
    return lax.dot_general(left, right, (((0,), (0,)), ((), ())), preferred_element_type=F32)


def inverse_root(hidden):
    return lax.rsqrt(jnp.mean(hidden * hidden, axis=-1, keepdims=True) + EPS)


def norm_back(hidden, gain, grad):
    root = inverse_root(hidden)
    unit = hidden * root
    scaled = grad * gain
    return root * (scaled - unit * jnp.mean(scaled * unit, axis=-1, keepdims=True))


class Copies:
    def __init__(self, sems):
        self.sems, self.count = sems, 0

    def start(self, source, target):
        copy = pltpu.make_async_copy(source, target, self.sems.at[self.count])
        self.count += 1
        copy.start()
        return copy


def wait(copies):
    for copy in copies:
        copy.wait()


def prompt_span(prompt_len, prompt):
    first, last = 0, 0
    end = 0
    for p in range(prompt_len.shape[0]):
        begin = end
        end = end + prompt_len[p]
        first = jnp.where(prompt == p, begin, first)
        last = jnp.where(prompt == p, end, last)
    return first, last


def window_rows(count):
    return min(count, count // 3 + ROWS)


def window_start(first, count):
    start = jnp.minimum(first // ROWS * ROWS, count - window_rows(count))
    return pl.multiple_of(start, ROWS)


def slot_rows(slots, rows, step):
    if slots == 1:
        return pl.ds(0, rows)
    return pl.ds(pl.multiple_of((lax.axis_index("dp") ^ step) * rows, ROWS), rows)


def features(block, width):
    return pl.ds(pl.multiple_of(block * width, width), width)


def stacked(ref, rows, heads, size):
    return jnp.concatenate([ref[rows, a * size : (a + 1) * size] for a in heads], axis=0)


def make_blocks(make, sends, keep):
    low = lax.axis_index("mp") & 1
    width = keep.shape[-1]
    first = 0
    for send in sends:
        for i in range(send.shape[0]):
            send[i] = make(features((first + i) * 2 + 1 - low, width))
        first += send.shape[0]
    for i in range(keep.shape[0]):
        keep[i] = make(features(i * 2 + low, width))


def forward_kernel(slots, pieces, *refs):
    refs = list(refs)

    def take(count):
        found, refs[:count] = refs[:count], []
        return found

    scalars = take(3)
    hidden, w_q, w_k, w_v, q_gain, k_gain, w_out = take(7)
    prefix = take(len(refs) - 8 - 7 - pieces - 1 - 1 - 3 - 2)
    saved = take(8)
    wq_v, wk_v, wv_v, qg_v, kg_v, wo_v, prefix_v = take(7)
    *sends, keep = take(pieces + 1)
    (hidden_v,) = take(1)
    prompt_len, resp_prompt, resp_len = take(3)
    out_bf, sems = take(2)
    query, key, value, hq, hk, p_pre, p_own, heads_out = saved

    copies = Copies(sems)
    depth = hidden.shape[1]
    steps = 4
    part = depth // steps
    loads = []
    for i in range(steps):
        cut = pl.ds(i * part, part)
        loads.append(
            [copies.start(hidden.at[:, cut], hidden_v.at[:, cut])]
            + [
                copies.start(w.at[cut], v.at[cut])
                for w, v in ((w_q, wq_v), (w_k, wk_v), (w_v, wv_v))
            ]
        )
    small = [copies.start(q_gain, qg_v), copies.start(k_gain, kg_v)]
    for source, target in zip(scalars, (prompt_len, resp_prompt, resp_len)):
        small.append(copies.start(source, target))
    held = prefix[0].shape[0]
    small.append(copies.start(prefix[0], prefix_v.at[slot_rows(len(prefix), held, 0)]))
    load_out = copies.start(w_out, wo_v)

    sums = [None] * 3
    for i, load in enumerate(loads):
        wait(load)
        rows = hidden_v[:, i * part : (i + 1) * part]
        for j, v in enumerate((wq_v, wk_v, wv_v)):
            term = dot(rows, v[i * part : (i + 1) * part])
            sums[j] = term if i == 0 else sums[j] + term
    hq[...], hk[...] = sums[0], sums[1]
    value[...] = sums[2].astype(BF16)
    wait(small)
    for k, ref in enumerate(prefix[1:], 1):
        prefix_v[slot_rows(len(prefix), held, k), :] = ref[...]
    size = qg_v.shape[1]
    for total, gain, out in ((sums[0], qg_v, query), (sums[1], kg_v, key)):
        for at in range(0, total.shape[1], size):
            head = total[:, at : at + size]
            out[:, at : at + size] = (head * inverse_root(head) * gain[...]).astype(BF16)

    count = prefix_v.shape[0]
    window = window_rows(count)
    slot_len = query.shape[0] // slots
    kv_heads = key.shape[1] // size
    groups = query.shape[1] // key.shape[1]
    scale = size ** (-0.5)
    for n in range(slots):
        first, last = prompt_span(prompt_len, resp_prompt[n])
        start = window_start(first, count)
        rows = slice(n * slot_len, (n + 1) * slot_len)
        live = lax.broadcasted_iota(jnp.int32, (slot_len, size), 0) < resp_len[n]
        for h in range(kv_heads):
            heads = range(h * groups, (h + 1) * groups)
            q = stacked(query, rows, heads, size)
            k_win = prefix_v[pl.ds(start, window), 2 * h * size : (2 * h + 1) * size]
            v_win = prefix_v[pl.ds(start, window), (2 * h + 1) * size : (2 * h + 2) * size]
            k_own = key[rows, h * size : (h + 1) * size]
            v_own = value[rows, h * size : (h + 1) * size]
            tall = groups * slot_len
            place = start + lax.broadcasted_iota(jnp.int32, (tall, window), 1)
            s_pre = jnp.where((place >= first) & (place < last), dot_nt(q, k_win) * scale, NEG)
            token = lax.broadcasted_iota(jnp.int32, (groups, slot_len, slot_len), 1)
            token = token.reshape(tall, slot_len)
            other = lax.broadcasted_iota(jnp.int32, (tall, slot_len), 1)
            s_own = jnp.where(
                (other <= token) & (other < resp_len[n]), dot_nt(q, k_own) * scale, NEG
            )
            top = jnp.maximum(
                jnp.max(s_pre, axis=-1, keepdims=True), jnp.max(s_own, axis=-1, keepdims=True)
            )
            e_pre = jnp.exp(s_pre - top)
            e_own = jnp.exp(s_own - top)
            total = jnp.sum(e_pre, axis=-1, keepdims=True) + jnp.sum(e_own, axis=-1, keepdims=True)
            b_pre = (e_pre / total).astype(BF16)
            b_own = (e_own / total).astype(BF16)
            p_pre[n, h] = b_pre
            p_own[n, h] = b_own
            out = dot(b_pre, v_win) + dot(b_own, v_own)
            for i, a in enumerate(heads):
                one = out[i * slot_len : (i + 1) * slot_len]
                heads_out[rows, a * size : (a + 1) * size] = one
                out_bf[rows, a * size : (a + 1) * size] = jnp.where(live, one, 0.0).astype(BF16)
    load_out.wait()

    def make(cols):
        return dot(out_bf[...], wo_v[:, cols]).astype(BF16)

    make_blocks(make, sends, keep)


def block_shapes(blocks, pieces, rows, depth):
    width, tall = depth // blocks, blocks // 2
    return [((tall // pieces, rows, width), BF16)] * pieces + [((tall, rows, width), BF16)]


def in_vmem(shapes):
    return [pltpu.VMEM(*x) for x in shapes]


def held_in(space, arrays):
    return [pltpu.with_memory_space_constraint(x, space) for x in arrays]


def like(arrays):
    return [(x.shape, x.dtype) for x in arrays]


def vmem_room(prefix_rows):
    return 48 << 20 if prefix_rows > 1024 else 24 << 20


def forward(blocks, pieces, scalars, hidden, w_q, w_k, w_v, q_gain, k_gain, w_out, prefix):
    slots = scalars[-1].shape[0]
    size = q_gain.shape[1]
    rows, depth = hidden.shape
    q_width, k_width = w_q.shape[1], w_k.shape[1]
    count = sum(x.shape[0] for x in prefix)
    window = window_rows(count)
    slot_len = rows // slots
    kv_heads, tall = k_width // size, slot_len * q_width // k_width
    saved = [
        ((rows, q_width), BF16),
        ((rows, k_width), BF16),
        ((rows, k_width), BF16),
        ((rows, q_width), F32),
        ((rows, k_width), F32),
        ((slots, kv_heads, tall, window), BF16),
        ((slots, kv_heads, tall, slot_len), BF16),
        ((rows, q_width), F32),
    ]
    weights = [w_q, w_k, w_v, q_gain, k_gain, w_out]
    kept = saved + like(weights) + [((count, prefix[0].shape[1]), BF16)]
    sent = block_shapes(blocks, pieces, rows, depth)
    operands = [*scalars, hidden, *weights, prefix[0]]
    found = pl.pallas_call(
        functools.partial(forward_kernel, slots, pieces),
        in_specs=[HBM] * len(operands) + [VMEM] * (len(prefix) - 1),
        out_specs=[VMEM] * len(kept + sent),
        out_shape=in_vmem(kept + sent),
        scratch_shapes=[pltpu.VMEM(hidden.shape, hidden.dtype)]
        + [pltpu.SMEM(x.shape, jnp.int32) for x in scalars]
        + [pltpu.VMEM((rows, q_width), BF16), pltpu.SemaphoreType.DMA((64,))],
        compiler_params=pltpu.CompilerParams(vmem_limit_bytes=vmem_room(count)),
        cost_estimate=pl.CostEstimate(
            flops=2 * rows * depth * (2 * q_width + 2 * k_width),
            bytes_accessed=2 * depth * (rows + 2 * q_width + 2 * k_width) + 2 * rows * depth,
            transcendentals=slots * kv_heads * tall * window,
        ),
    )(*held_in(pltpu.HBM, operands), *held_in(pltpu.VMEM, prefix[1:]))
    return found[: len(kept)], found[len(kept) :]


def backward_kernel(slots, blocks, pieces, *refs):
    refs = list(refs)

    def take(count):
        found, refs[:count] = refs[:count], []
        return found

    scalars = take(3)
    cotangent = take(blocks)
    query, key, value, hq, hk, p_pre, p_own, heads_out = take(8)
    w_q, w_k, w_v, q_gain, k_gain, w_out, prefix_v = take(7)
    terms = take(len(refs) - pieces - 1 - 1 - 3 - 5)
    *sends, keep = take(pieces + 1)
    (own,) = take(1)
    prompt_len, resp_prompt, resp_len = scalars_v = take(3)
    grad_prefix, dhq, dhk, dv, sems = take(5)

    copies = Copies(sems)
    load_own = copies.start(cotangent[0], own)
    small = [copies.start(a, b) for a, b in zip(scalars, scalars_v)]

    width = own.shape[1]
    grad_heads = None
    load_own.wait()
    for b, ref in enumerate([own, *cotangent[1:]]):
        term = dot_nt(ref[...], w_out[:, features(lax.axis_index("mp") ^ b, width)])
        grad_heads = term if b == 0 else grad_heads + term
    grad_prefix[...] = jnp.zeros_like(grad_prefix)
    wait(small)

    count = prefix_v.shape[0]
    window = window_rows(count)
    slot_len = query.shape[0] // slots
    size = q_gain.shape[1]
    kv_heads = key.shape[1] // size
    groups = query.shape[1] // key.shape[1]
    scale = size ** (-0.5)
    for n in range(slots):
        first, _ = prompt_span(prompt_len, resp_prompt[n])
        start = window_start(first, count)
        rows = slice(n * slot_len, (n + 1) * slot_len)
        live = lax.broadcasted_iota(jnp.int32, (slot_len, size), 0) < resp_len[n]
        for h in range(kv_heads):
            heads = range(h * groups, (h + 1) * groups)
            q = stacked(query, rows, heads, size)
            out = stacked(heads_out, rows, heads, size)
            g = jnp.concatenate(
                [
                    jnp.where(live, grad_heads[rows, a * size : (a + 1) * size], 0.0).astype(BF16)
                    for a in heads
                ],
                axis=0,
            )
            k_win = prefix_v[pl.ds(start, window), 2 * h * size : (2 * h + 1) * size]
            v_win = prefix_v[pl.ds(start, window), (2 * h + 1) * size : (2 * h + 2) * size]
            k_own = key[rows, h * size : (h + 1) * size]
            v_own = value[rows, h * size : (h + 1) * size]
            b_pre, b_own = p_pre[n, h], p_own[n, h]
            delta = jnp.sum(g.astype(F32) * out, axis=-1, keepdims=True)
            ds_pre = (b_pre.astype(F32) * (dot_nt(g, v_win) - delta)).astype(BF16)
            ds_own = (b_own.astype(F32) * (dot_nt(g, v_own) - delta)).astype(BF16)
            grad_q = scale * (dot(ds_pre, k_win) + dot(ds_own, k_own))
            for i, a in enumerate(heads):
                cols = slice(a * size, (a + 1) * size)
                one = grad_q[i * slot_len : (i + 1) * slot_len]
                dhq[rows, cols] = norm_back(hq[rows, cols], q_gain[...], one).astype(BF16)
            cols = slice(h * size, (h + 1) * size)
            grad_k = scale * dot_tn(ds_own, q)
            dhk[rows, cols] = norm_back(hk[rows, cols], k_gain[...], grad_k).astype(BF16)
            dv[rows, cols] = dot_tn(b_own, g).astype(BF16)
            k_cols = slice(2 * h * size, (2 * h + 1) * size)
            v_cols = slice((2 * h + 1) * size, (2 * h + 2) * size)
            grad_prefix[pl.ds(start, window), k_cols] += scale * dot_tn(ds_pre, q)
            grad_prefix[pl.ds(start, window), v_cols] += dot_tn(b_pre, g)
    held = terms[0].shape[0]
    for k, ref in enumerate(terms):
        ref[...] = grad_prefix[slot_rows(len(terms), held, k), :]

    def make(cols):
        return (
            dot_nt(dhq[...], w_q[cols, :])
            + dot_nt(dhk[...], w_k[cols, :])
            + dot_nt(dv[...], w_v[cols, :])
        ).astype(BF16)

    make_blocks(make, sends, keep)


def backward(blocks, pieces, scalars, cotangent, kept, prefix):
    slots = scalars[-1].shape[0]
    w_out, w_k = kept[13], kept[9]
    rows, q_width = kept[0].shape
    k_width = w_k.shape[1]
    depth = w_out.shape[1]
    count, kv_width = kept[14].shape
    sent = block_shapes(blocks, pieces, rows, depth)
    operands = [*scalars, cotangent[0]]
    results = [(x.shape, F32) for x in prefix] + sent
    found = pl.pallas_call(
        functools.partial(backward_kernel, slots, blocks, pieces),
        in_specs=[HBM] * len(operands) + [VMEM] * (blocks - 1 + len(kept)),
        out_specs=[VMEM] * len(results),
        out_shape=in_vmem(results),
        scratch_shapes=in_vmem(like(cotangent[:1]))
        + [pltpu.SMEM(x.shape, jnp.int32) for x in scalars]
        + [
            pltpu.VMEM((count, kv_width), F32),
            pltpu.VMEM((rows, q_width), BF16),
            pltpu.VMEM((rows, k_width), BF16),
            pltpu.VMEM((rows, k_width), BF16),
            pltpu.SemaphoreType.DMA((64,)),
        ],
        compiler_params=pltpu.CompilerParams(vmem_limit_bytes=vmem_room(count)),
        cost_estimate=pl.CostEstimate(
            flops=2 * rows * (2 * q_width + 2 * k_width) * depth
            + 10 * rows * q_width * (window_rows(count) + rows // slots),
            bytes_accessed=4 * rows * depth,
            transcendentals=0,
        ),
    )(*held_in(pltpu.HBM, operands), *held_in(pltpu.VMEM, [*cotangent[1:], *kept]))
    return found[: len(prefix)], found[len(prefix) :]


def trade(block, axis, step):
    return lax.ppermute(block, axis, [(i, i ^ step) for i in range(lax.axis_size(axis))])


def after(value, *others):
    return lax.optimization_barrier((value, *others))[0]


def scatter_features(sends, keep):
    size = lax.axis_size("mp")
    got = [trade(send, "mp", 1) for send in sends]
    got = got[0] if len(got) == 1 else jnp.concatenate(got, axis=0)
    both = (keep.astype(F32) + got.astype(F32)).astype(BF16)
    groups = [list(range(low, size, 2)) for low in range(2)]
    terms = lax.all_to_all(both, "mp", 0, 0, axis_index_groups=groups, tiled=True)
    return jnp.sum(terms.astype(F32), axis=0).astype(BF16)


def per_device(
    hidden_rows,
    w_query,
    w_key,
    w_value,
    w_out,
    q_gain,
    k_gain,
    prefix_kv,
    cotangent,
    prompt_len,
    resp_prompt,
    resp_len,
):
    blocks = lax.axis_size("mp")
    chips = lax.axis_size("dp")
    scalars = (prompt_len, resp_prompt, resp_len)
    q_gain, k_gain = q_gain[None], k_gain[None]
    if chips > 8:
        prefix = [lax.all_gather(prefix_kv, "dp", axis=0, tiled=True)]
    else:
        prefix = [prefix_kv] + [trade(prefix_kv, "dp", k) for k in range(1, chips)]
    back = [cotangent, trade(cotangent, "mp", 1)]
    for z in range(2, blocks, 2):
        along = trade(cotangent, "mp", z)
        back += [along, trade(along, "mp", 1)]
    hidden_rows = after(hidden_rows, *back[2::2])
    kept, blocks_out = forward(
        blocks, 1, scalars, hidden_rows, w_query, w_key, w_value, q_gain, k_gain, w_out, prefix
    )
    mixed = scatter_features(blocks_out[:-1], blocks_out[-1])
    terms, blocks_in = backward(blocks, 2, scalars, back, kept, prefix)
    grad_input = scatter_features(blocks_in[:-1], blocks_in[-1])
    if chips > 8:
        grad_prefix = lax.psum_scatter(terms[0], "dp", scatter_dimension=0, tiled=True)
    else:
        grad_prefix = terms[0]
        for k in range(1, chips):
            grad_prefix = grad_prefix + trade(terms[k], "dp", k)
    return mixed, grad_input, grad_prefix.astype(BF16)


def solution(mesh):
    in_specs = (
        P("dp", None),
        P(None, "mp"),
        P(None, "mp"),
        P(None, "mp"),
        P("mp", None),
        P(),
        P(),
        P("dp", "mp"),
        P("dp", "mp"),
        P(),
        P("dp"),
        P("dp"),
    )
    out_specs = (P("dp", "mp"), P("dp", "mp"), P("dp", "mp"))
    return jax.shard_map(
        per_device, mesh=mesh, in_specs=in_specs, out_specs=out_specs, check_vma=False
    )
```

```python
import functools

import jax
import jax.numpy as jnp
from jax import lax
from jax.experimental import pallas as pl
from jax.experimental.pallas import tpu as pltpu
from jax.sharding import PartitionSpec as P

EPS = 1e-06
NEG = -1e30
ROWS = 16
HELD = ((0, 4), (2, 6), (1, 5), (3, 7))
OUT_SENT = ((2, 3, 6, 7),)
OUT_KEPT = ((0, 1, 4, 5),)
IN_SENT = ((3, 7), (1, 5))
IN_KEPT = ((2, 6), (0, 4))
F32 = jnp.float32
BF16 = jnp.bfloat16
HBM = pl.BlockSpec(memory_space=pltpu.HBM)
VMEM = pl.BlockSpec(memory_space=pltpu.VMEM)


def dot(left, right):
    return jnp.dot(left, right, preferred_element_type=F32)


def dot_nt(left, right):
    return lax.dot_general(left, right, (((1,), (1,)), ((), ())), preferred_element_type=F32)


def dot_tn(left, right):
    return lax.dot_general(left, right, (((0,), (0,)), ((), ())), preferred_element_type=F32)


def inverse_root(hidden):
    return lax.rsqrt(jnp.mean(hidden * hidden, axis=-1, keepdims=True) + EPS)


def norm_back(hidden, gain, grad):
    root = inverse_root(hidden)
    unit = hidden * root
    scaled = grad * gain
    return root * (scaled - unit * jnp.mean(scaled * unit, axis=-1, keepdims=True))


class Copies:
    def __init__(self, sems):
        self.sems, self.count = sems, 0

    def start(self, source, target):
        copy = pltpu.make_async_copy(source, target, self.sems.at[self.count])
        self.count += 1
        copy.start()
        return copy


def wait(copies):
    for copy in copies:
        copy.wait()


def prompt_span(prompt_len, prompt):
    first, last = 0, 0
    end = 0
    for p in range(prompt_len.shape[0]):
        begin = end
        end = end + prompt_len[p]
        first = jnp.where(prompt == p, begin, first)
        last = jnp.where(prompt == p, end, last)
    return first, last


def window_rows(count):
    return min(count, count // 3 + ROWS)


def window_start(first, count):
    start = jnp.minimum(first // ROWS * ROWS, count - window_rows(count))
    return pl.multiple_of(start, ROWS)


def slot_rows(slots, rows, step):
    if slots == 1:
        return pl.ds(0, rows)
    return pl.ds(pl.multiple_of((lax.axis_index("dp") ^ step) * rows, ROWS), rows)


def features(block, width):
    return pl.ds(pl.multiple_of(block * width, width), width)


def stacked(ref, rows, heads, size):
    return jnp.concatenate([ref[rows, a * size : (a + 1) * size] for a in heads], axis=0)


def make_blocks(make, names, refs):
    me = lax.axis_index("mp")
    for blocks, ref in zip(names, refs):
        for i, block in enumerate(blocks):
            ref[i] = make(features(me ^ block, ref.shape[-1]))


def forward_kernel(slots, names, *refs):
    refs = list(refs)

    def take(count):
        found, refs[:count] = refs[:count], []
        return found

    scalars = take(3)
    hidden, w_q, w_k, w_v, q_gain, k_gain, w_out = take(7)
    prefix = take(len(refs) - 8 - 7 - len(names) - 1 - 3 - 2)
    saved = take(8)
    wq_v, wk_v, wv_v, qg_v, kg_v, wo_v, prefix_v = take(7)
    parts = take(len(names))
    (hidden_v,) = take(1)
    prompt_len, resp_prompt, resp_len = take(3)
    out_bf, sems = take(2)
    query, key, value, hq, hk, p_pre, p_own, heads_out = saved

    copies = Copies(sems)
    depth = hidden.shape[1]
    steps = 4
    part = depth // steps
    loads = []
    for i in range(steps):
        cut = pl.ds(i * part, part)
        loads.append(
            [copies.start(hidden.at[:, cut], hidden_v.at[:, cut])]
            + [
                copies.start(w.at[cut], v.at[cut])
                for w, v in ((w_q, wq_v), (w_k, wk_v), (w_v, wv_v))
            ]
        )
    small = [copies.start(q_gain, qg_v), copies.start(k_gain, kg_v)]
    for source, target in zip(scalars, (prompt_len, resp_prompt, resp_len)):
        small.append(copies.start(source, target))
    held = prefix[0].shape[0]
    small.append(copies.start(prefix[0], prefix_v.at[slot_rows(len(prefix), held, 0)]))
    load_out = copies.start(w_out, wo_v)

    sums = [None] * 3
    for i, load in enumerate(loads):
        wait(load)
        rows = hidden_v[:, i * part : (i + 1) * part]
        for j, v in enumerate((wq_v, wk_v, wv_v)):
            term = dot(rows, v[i * part : (i + 1) * part])
            sums[j] = term if i == 0 else sums[j] + term
    hq[...], hk[...] = sums[0], sums[1]
    value[...] = sums[2].astype(BF16)
    wait(small)
    for k, ref in enumerate(prefix[1:], 1):
        prefix_v[slot_rows(len(prefix), held, k), :] = ref[...]
    size = qg_v.shape[1]
    for total, gain, out in ((sums[0], qg_v, query), (sums[1], kg_v, key)):
        for at in range(0, total.shape[1], size):
            head = total[:, at : at + size]
            out[:, at : at + size] = (head * inverse_root(head) * gain[...]).astype(BF16)

    count = prefix_v.shape[0]
    window = window_rows(count)
    slot_len = query.shape[0] // slots
    kv_heads = key.shape[1] // size
    groups = query.shape[1] // key.shape[1]
    scale = size ** (-0.5)
    for n in range(slots):
        first, last = prompt_span(prompt_len, resp_prompt[n])
        start = window_start(first, count)
        rows = slice(n * slot_len, (n + 1) * slot_len)
        live = lax.broadcasted_iota(jnp.int32, (slot_len, size), 0) < resp_len[n]
        for h in range(kv_heads):
            heads = range(h * groups, (h + 1) * groups)
            q = stacked(query, rows, heads, size)
            k_win = prefix_v[pl.ds(start, window), 2 * h * size : (2 * h + 1) * size]
            v_win = prefix_v[pl.ds(start, window), (2 * h + 1) * size : (2 * h + 2) * size]
            k_own = key[rows, h * size : (h + 1) * size]
            v_own = value[rows, h * size : (h + 1) * size]
            tall = groups * slot_len
            place = start + lax.broadcasted_iota(jnp.int32, (tall, window), 1)
            s_pre = jnp.where((place >= first) & (place < last), dot_nt(q, k_win) * scale, NEG)
            token = lax.broadcasted_iota(jnp.int32, (groups, slot_len, slot_len), 1)
            token = token.reshape(tall, slot_len)
            other = lax.broadcasted_iota(jnp.int32, (tall, slot_len), 1)
            s_own = jnp.where(
                (other <= token) & (other < resp_len[n]), dot_nt(q, k_own) * scale, NEG
            )
            top = jnp.maximum(
                jnp.max(s_pre, axis=-1, keepdims=True), jnp.max(s_own, axis=-1, keepdims=True)
            )
            e_pre = jnp.exp(s_pre - top)
            e_own = jnp.exp(s_own - top)
            total = jnp.sum(e_pre, axis=-1, keepdims=True) + jnp.sum(e_own, axis=-1, keepdims=True)
            b_pre = (e_pre / total).astype(BF16)
            b_own = (e_own / total).astype(BF16)
            p_pre[n, h] = b_pre
            p_own[n, h] = b_own
            out = dot(b_pre, v_win) + dot(b_own, v_own)
            for i, a in enumerate(heads):
                one = out[i * slot_len : (i + 1) * slot_len]
                heads_out[rows, a * size : (a + 1) * size] = one
                out_bf[rows, a * size : (a + 1) * size] = jnp.where(live, one, 0.0).astype(BF16)
    load_out.wait()

    def make(cols):
        return dot(out_bf[...], wo_v[:, cols]).astype(BF16)

    make_blocks(make, names, parts)


def block_shapes(names, rows, width):
    return [((len(blocks), rows, width), BF16) for blocks in names]


def in_vmem(shapes):
    return [pltpu.VMEM(*x) for x in shapes]


def held_in(space, arrays):
    return [pltpu.with_memory_space_constraint(x, space) for x in arrays]


def like(arrays):
    return [(x.shape, x.dtype) for x in arrays]


def vmem_room(prefix_rows):
    return 48 << 20 if prefix_rows > 1024 else 24 << 20


def forward(names, width, scalars, hidden, w_q, w_k, w_v, q_gain, k_gain, w_out, prefix):
    slots = scalars[-1].shape[0]
    size = q_gain.shape[1]
    rows, depth = hidden.shape
    q_width, k_width = w_q.shape[1], w_k.shape[1]
    count = sum(x.shape[0] for x in prefix)
    window = window_rows(count)
    slot_len = rows // slots
    kv_heads, tall = k_width // size, slot_len * q_width // k_width
    saved = [
        ((rows, q_width), BF16),
        ((rows, k_width), BF16),
        ((rows, k_width), BF16),
        ((rows, q_width), F32),
        ((rows, k_width), F32),
        ((slots, kv_heads, tall, window), BF16),
        ((slots, kv_heads, tall, slot_len), BF16),
        ((rows, q_width), F32),
    ]
    weights = [w_q, w_k, w_v, q_gain, k_gain, w_out]
    kept = saved + like(weights) + [((count, prefix[0].shape[1]), BF16)]
    sent = block_shapes(names, rows, width)
    operands = [*scalars, hidden, *weights, prefix[0]]
    found = pl.pallas_call(
        functools.partial(forward_kernel, slots, names),
        in_specs=[HBM] * len(operands) + [VMEM] * (len(prefix) - 1),
        out_specs=[VMEM] * len(kept + sent),
        out_shape=in_vmem(kept + sent),
        scratch_shapes=[pltpu.VMEM(hidden.shape, hidden.dtype)]
        + [pltpu.SMEM(x.shape, jnp.int32) for x in scalars]
        + [pltpu.VMEM((rows, q_width), BF16), pltpu.SemaphoreType.DMA((64,))],
        compiler_params=pltpu.CompilerParams(vmem_limit_bytes=vmem_room(count)),
        cost_estimate=pl.CostEstimate(
            flops=2 * rows * depth * (2 * q_width + 2 * k_width),
            bytes_accessed=2 * depth * (rows + 2 * q_width + 2 * k_width) + 2 * rows * depth,
            transcendentals=slots * kv_heads * tall * window,
        ),
    )(*held_in(pltpu.HBM, operands), *held_in(pltpu.VMEM, prefix[1:]))
    return found[: len(kept)], found[len(kept) :]


def backward_kernel(slots, names, *refs):
    refs = list(refs)

    def take(count):
        found, refs[:count] = refs[:count], []
        return found

    scalars = take(3)
    cotangent = take(len(HELD))
    query, key, value, hq, hk, p_pre, p_own, heads_out = take(8)
    w_q, w_k, w_v, q_gain, k_gain, w_out, prefix_v = take(7)
    terms = take(len(refs) - len(names) - 3 - 5)
    parts = take(len(names))
    prompt_len, resp_prompt, resp_len = scalars_v = take(3)
    grad_prefix, dhq, dhk, dv, sems = take(5)

    copies = Copies(sems)
    small = [copies.start(a, b) for a, b in zip(scalars, scalars_v)]

    width = cotangent[0].shape[2]
    me = lax.axis_index("mp")
    grad_heads = 0.0
    for blocks, ref in zip(HELD, cotangent):
        for i, block in enumerate(blocks):
            grad_heads += dot_nt(ref[i], w_out[:, features(me ^ block, width)])
    grad_prefix[...] = jnp.zeros_like(grad_prefix)
    wait(small)

    count = prefix_v.shape[0]
    window = window_rows(count)
    slot_len = query.shape[0] // slots
    size = q_gain.shape[1]
    kv_heads = key.shape[1] // size
    groups = query.shape[1] // key.shape[1]
    scale = size ** (-0.5)
    for n in range(slots):
        first, _ = prompt_span(prompt_len, resp_prompt[n])
        start = window_start(first, count)
        rows = slice(n * slot_len, (n + 1) * slot_len)
        live = lax.broadcasted_iota(jnp.int32, (slot_len, size), 0) < resp_len[n]
        for h in range(kv_heads):
            heads = range(h * groups, (h + 1) * groups)
            q = stacked(query, rows, heads, size)
            out = stacked(heads_out, rows, heads, size)
            g = jnp.concatenate(
                [
                    jnp.where(live, grad_heads[rows, a * size : (a + 1) * size], 0.0).astype(BF16)
                    for a in heads
                ],
                axis=0,
            )
            k_win = prefix_v[pl.ds(start, window), 2 * h * size : (2 * h + 1) * size]
            v_win = prefix_v[pl.ds(start, window), (2 * h + 1) * size : (2 * h + 2) * size]
            k_own = key[rows, h * size : (h + 1) * size]
            v_own = value[rows, h * size : (h + 1) * size]
            b_pre, b_own = p_pre[n, h], p_own[n, h]
            delta = jnp.sum(g.astype(F32) * out, axis=-1, keepdims=True)
            ds_pre = (b_pre.astype(F32) * (dot_nt(g, v_win) - delta)).astype(BF16)
            ds_own = (b_own.astype(F32) * (dot_nt(g, v_own) - delta)).astype(BF16)
            grad_q = scale * (dot(ds_pre, k_win) + dot(ds_own, k_own))
            for i, a in enumerate(heads):
                cols = slice(a * size, (a + 1) * size)
                one = grad_q[i * slot_len : (i + 1) * slot_len]
                dhq[rows, cols] = norm_back(hq[rows, cols], q_gain[...], one).astype(BF16)
            cols = slice(h * size, (h + 1) * size)
            grad_k = scale * dot_tn(ds_own, q)
            dhk[rows, cols] = norm_back(hk[rows, cols], k_gain[...], grad_k).astype(BF16)
            dv[rows, cols] = dot_tn(b_own, g).astype(BF16)
            k_cols = slice(2 * h * size, (2 * h + 1) * size)
            v_cols = slice((2 * h + 1) * size, (2 * h + 2) * size)
            grad_prefix[pl.ds(start, window), k_cols] += scale * dot_tn(ds_pre, q)
            grad_prefix[pl.ds(start, window), v_cols] += dot_tn(b_pre, g)
    held = terms[0].shape[0]
    for k, ref in enumerate(terms):
        ref[...] = grad_prefix[slot_rows(len(terms), held, k), :]

    def make(cols):
        return (
            dot_nt(dhq[...], w_q[cols, :])
            + dot_nt(dhk[...], w_k[cols, :])
            + dot_nt(dv[...], w_v[cols, :])
        ).astype(BF16)

    make_blocks(make, names, parts)


def backward(names, scalars, cotangent, kept, prefix):
    slots = scalars[-1].shape[0]
    w_out, w_k = kept[13], kept[9]
    rows, q_width = kept[0].shape
    k_width = w_k.shape[1]
    depth = w_out.shape[1]
    count, kv_width = kept[14].shape
    sent = block_shapes(names, rows, cotangent[0].shape[2])
    operands = list(scalars)
    results = [(x.shape, F32) for x in prefix] + sent
    found = pl.pallas_call(
        functools.partial(backward_kernel, slots, names),
        in_specs=[HBM] * len(operands) + [VMEM] * (len(cotangent) + len(kept)),
        out_specs=[VMEM] * len(results),
        out_shape=in_vmem(results),
        scratch_shapes=[pltpu.SMEM(x.shape, jnp.int32) for x in scalars]
        + [
            pltpu.VMEM((count, kv_width), F32),
            pltpu.VMEM((rows, q_width), BF16),
            pltpu.VMEM((rows, k_width), BF16),
            pltpu.VMEM((rows, k_width), BF16),
            pltpu.SemaphoreType.DMA((64,)),
        ],
        compiler_params=pltpu.CompilerParams(vmem_limit_bytes=vmem_room(count)),
        cost_estimate=pl.CostEstimate(
            flops=2 * rows * (2 * q_width + 2 * k_width) * depth
            + 10 * rows * q_width * (window_rows(count) + rows // slots),
            bytes_accessed=4 * rows * depth,
            transcendentals=0,
        ),
    )(*held_in(pltpu.HBM, operands), *held_in(pltpu.VMEM, [*cotangent, *kept]))
    return found[: len(prefix)], found[len(prefix) :]


def trade(block, axis, step):
    return lax.ppermute(block, axis, [(i, i ^ step) for i in range(lax.axis_size(axis))])


def after(value, *others):
    return lax.optimization_barrier((value, *others))[0]


def total(*terms):
    whole = terms[0].astype(F32)
    for term in terms[1:]:
        whole = whole + term.astype(F32)
    return whole.astype(BF16)


def sum_out(got, kept):
    sent, kept = total(kept[2:], got[2:]), total(kept[:2], got[:2])
    got = trade(sent, "mp", 4)
    sent, kept = total(kept[1], got[1]), total(kept[0], got[0])
    return total(kept, trade(sent, "mp", 1))


def sum_in(parts, gate):
    far, near, kept_far, kept = parts
    far = total(after(kept_far, gate), trade(far, "mp", 1))
    near = after(trade(near, "mp", 1), far)
    got = trade(far, "mp", 2)
    sent, kept = total(kept[1], near[1], got[1]), total(kept[0], near[0], got[0])
    return total(kept, trade(sent, "mp", 4)), near


def per_device(
    hidden_rows,
    w_query,
    w_key,
    w_value,
    w_out,
    q_gain,
    k_gain,
    prefix_kv,
    cotangent,
    prompt_len,
    resp_prompt,
    resp_len,
):
    chips = lax.axis_size("dp")
    scalars = (prompt_len, resp_prompt, resp_len)
    q_gain, k_gain = q_gain[None], k_gain[None]
    if chips > 8:
        prefix = [lax.all_gather(prefix_kv, "dp", axis=0, tiled=True)]
    else:
        prefix = [prefix_kv] + [trade(prefix_kv, "dp", k) for k in range(1, chips)]
    pair = jnp.stack([after(cotangent, *prefix[1:]), trade(cotangent, "mp", 4)])
    along = trade(pair, "mp", 2)
    back = [pair, along, trade(pair, "mp", 1), trade(along, "mp", 1)]
    kept, parts = forward(
        OUT_SENT + OUT_KEPT, cotangent.shape[1], scalars, after(hidden_rows, pair), w_query, w_key,
        w_value, q_gain, k_gain, w_out, prefix,
    )
    got, kept_out = trade(after(parts[0], along), "mp", 2), parts[1]
    terms, parts = backward(IN_SENT + IN_KEPT, scalars, back, kept, prefix)
    grad_input, near = sum_in(parts, got)
    mixed = sum_out(got, kept_out)
    terms = lax.optimization_barrier((*terms, near))[:-1]
    if chips > 8:
        grad_prefix = lax.psum_scatter(terms[0], "dp", scatter_dimension=0, tiled=True)
    else:
        grad_prefix = terms[0]
        for k in range(1, chips):
            grad_prefix = grad_prefix + trade(terms[k], "dp", k)
    return mixed, grad_input, grad_prefix.astype(BF16)


def solution(mesh):
    in_specs = (
        P("dp", None),
        P(None, "mp"),
        P(None, "mp"),
        P(None, "mp"),
        P("mp", None),
        P(),
        P(),
        P("dp", "mp"),
        P("dp", "mp"),
        P(),
        P("dp"),
        P("dp"),
    )
    out_specs = (P("dp", "mp"), P("dp", "mp"), P("dp", "mp"))
    return jax.shard_map(
        per_device, mesh=mesh, in_specs=in_specs, out_specs=out_specs, check_vma=False
    )
```

```python
import functools

import jax
import jax.numpy as jnp
from jax import lax
from jax.experimental import pallas as pl
from jax.experimental.pallas import tpu as pltpu
from jax.sharding import PartitionSpec as P

EPS = 1e-06
NEG = -1e30
ROWS = 16
HELD = ((0, 4), (2, 6), (1, 5), (3, 7))
OUT_SENT = ((2, 3, 6, 7),)
OUT_KEPT = ((0, 1, 4, 5),)
IN_SENT = ((3, 7), (1, 5))
IN_KEPT = ((2, 6), (0, 4))
F32 = jnp.float32
BF16 = jnp.bfloat16
HBM = pl.BlockSpec(memory_space=pltpu.HBM)
VMEM = pl.BlockSpec(memory_space=pltpu.VMEM)


def dot(left, right):
    return jnp.dot(left, right, preferred_element_type=F32)


def dot_nt(left, right):
    return lax.dot_general(left, right, (((1,), (1,)), ((), ())), preferred_element_type=F32)


def dot_tn(left, right):
    return lax.dot_general(left, right, (((0,), (0,)), ((), ())), preferred_element_type=F32)


def inverse_root(hidden):
    return lax.rsqrt(jnp.mean(hidden * hidden, axis=-1, keepdims=True) + EPS)


def norm_back(hidden, gain, grad):
    root = inverse_root(hidden)
    unit = hidden * root
    scaled = grad * gain
    return root * (scaled - unit * jnp.mean(scaled * unit, axis=-1, keepdims=True))


class Copies:
    def __init__(self, sems):
        self.sems, self.count = sems, 0

    def start(self, source, target):
        copy = pltpu.make_async_copy(source, target, self.sems.at[self.count])
        self.count += 1
        copy.start()
        return copy


def wait(copies):
    for copy in copies:
        copy.wait()


def prompt_span(prompt_len, prompt):
    first, last = 0, 0
    end = 0
    for p in range(prompt_len.shape[0]):
        begin = end
        end = end + prompt_len[p]
        first = jnp.where(prompt == p, begin, first)
        last = jnp.where(prompt == p, end, last)
    return first, last


def window_rows(count):
    return min(count, count // 3 + ROWS)


def window_start(first, count):
    start = jnp.minimum(first // ROWS * ROWS, count - window_rows(count))
    return pl.multiple_of(start, ROWS)


def slot_rows(slots, rows, step):
    if slots == 1:
        return pl.ds(0, rows)
    return pl.ds(pl.multiple_of((lax.axis_index("dp") ^ step) * rows, ROWS), rows)


def features(block, width):
    return pl.ds(pl.multiple_of(block * width, width), width)


def stacked(ref, rows, heads, size):
    return jnp.concatenate([ref[rows, a * size : (a + 1) * size] for a in heads], axis=0)


def make_blocks(make, names, refs):
    me = lax.axis_index("mp")
    for blocks, ref in zip(names, refs):
        for i, block in enumerate(blocks):
            ref[i] = make(features(me ^ block, ref.shape[-1]))


def forward_kernel(slots, names, *refs):
    refs = list(refs)

    def take(count):
        found, refs[:count] = refs[:count], []
        return found

    scalars = take(3)
    hidden, w_q, w_k, w_v, q_gain, k_gain, w_out = take(7)
    prefix = take(len(refs) - 8 - 7 - len(names) - 1 - 3 - 2)
    saved = take(8)
    wq_v, wk_v, wv_v, qg_v, kg_v, wo_v, prefix_v = take(7)
    parts = take(len(names))
    (hidden_v,) = take(1)
    prompt_len, resp_prompt, resp_len = take(3)
    out_bf, sems = take(2)
    query, key, value, hq, hk, p_pre, p_own, heads_out = saved

    copies = Copies(sems)
    depth = hidden.shape[1]
    steps = 4
    part = depth // steps
    loads = []
    for i in range(steps):
        cut = pl.ds(i * part, part)
        loads.append(
            [copies.start(hidden.at[:, cut], hidden_v.at[:, cut])]
            + [
                copies.start(w.at[cut], v.at[cut])
                for w, v in ((w_q, wq_v), (w_k, wk_v), (w_v, wv_v))
            ]
        )
    small = [copies.start(q_gain, qg_v), copies.start(k_gain, kg_v)]
    for source, target in zip(scalars, (prompt_len, resp_prompt, resp_len)):
        small.append(copies.start(source, target))
    held = prefix[0].shape[0]
    small.append(copies.start(prefix[0], prefix_v.at[slot_rows(len(prefix), held, 0)]))
    load_out = copies.start(w_out, wo_v)

    sums = [None] * 3
    for i, load in enumerate(loads):
        wait(load)
        rows = hidden_v[:, i * part : (i + 1) * part]
        for j, v in enumerate((wq_v, wk_v, wv_v)):
            term = dot(rows, v[i * part : (i + 1) * part])
            sums[j] = term if i == 0 else sums[j] + term
    hq[...], hk[...] = sums[0], sums[1]
    value[...] = sums[2].astype(BF16)
    wait(small)
    for k, ref in enumerate(prefix[1:], 1):
        prefix_v[slot_rows(len(prefix), held, k), :] = ref[...]
    size = qg_v.shape[1]
    for total, gain, out in ((sums[0], qg_v, query), (sums[1], kg_v, key)):
        for at in range(0, total.shape[1], size):
            head = total[:, at : at + size]
            out[:, at : at + size] = (head * inverse_root(head) * gain[...]).astype(BF16)

    count = prefix_v.shape[0]
    window = window_rows(count)
    slot_len = query.shape[0] // slots
    kv_heads = key.shape[1] // size
    groups = query.shape[1] // key.shape[1]
    scale = size ** (-0.5)
    for n in range(slots):
        first, last = prompt_span(prompt_len, resp_prompt[n])
        start = window_start(first, count)
        rows = slice(n * slot_len, (n + 1) * slot_len)
        live = lax.broadcasted_iota(jnp.int32, (slot_len, size), 0) < resp_len[n]
        for h in range(kv_heads):
            heads = range(h * groups, (h + 1) * groups)
            q = stacked(query, rows, heads, size)
            k_win = prefix_v[pl.ds(start, window), 2 * h * size : (2 * h + 1) * size]
            v_win = prefix_v[pl.ds(start, window), (2 * h + 1) * size : (2 * h + 2) * size]
            k_own = key[rows, h * size : (h + 1) * size]
            v_own = value[rows, h * size : (h + 1) * size]
            tall = groups * slot_len
            place = start + lax.broadcasted_iota(jnp.int32, (tall, window), 1)
            s_pre = jnp.where((place >= first) & (place < last), dot_nt(q, k_win) * scale, NEG)
            token = lax.broadcasted_iota(jnp.int32, (groups, slot_len, slot_len), 1)
            token = token.reshape(tall, slot_len)
            other = lax.broadcasted_iota(jnp.int32, (tall, slot_len), 1)
            s_own = jnp.where(
                (other <= token) & (other < resp_len[n]), dot_nt(q, k_own) * scale, NEG
            )
            top = jnp.maximum(
                jnp.max(s_pre, axis=-1, keepdims=True), jnp.max(s_own, axis=-1, keepdims=True)
            )
            e_pre = jnp.exp(s_pre - top)
            e_own = jnp.exp(s_own - top)
            total = jnp.sum(e_pre, axis=-1, keepdims=True) + jnp.sum(e_own, axis=-1, keepdims=True)
            b_pre = (e_pre / total).astype(BF16)
            b_own = (e_own / total).astype(BF16)
            p_pre[n, h] = b_pre
            p_own[n, h] = b_own
            out = dot(b_pre, v_win) + dot(b_own, v_own)
            for i, a in enumerate(heads):
                one = out[i * slot_len : (i + 1) * slot_len]
                heads_out[rows, a * size : (a + 1) * size] = one
                out_bf[rows, a * size : (a + 1) * size] = jnp.where(live, one, 0.0).astype(BF16)
    load_out.wait()

    def make(cols):
        return dot(out_bf[...], wo_v[:, cols]).astype(BF16)

    make_blocks(make, names, parts)


def block_shapes(names, rows, width):
    return [((len(blocks), rows, width), BF16) for blocks in names]


def in_vmem(shapes):
    return [pltpu.VMEM(*x) for x in shapes]


def held_in(space, arrays):
    return [pltpu.with_memory_space_constraint(x, space) for x in arrays]


def like(arrays):
    return [(x.shape, x.dtype) for x in arrays]


def vmem_room(prefix_rows):
    return 48 << 20 if prefix_rows > 1024 else 24 << 20


def forward(names, width, scalars, hidden, w_q, w_k, w_v, q_gain, k_gain, w_out, prefix):
    slots = scalars[-1].shape[0]
    size = q_gain.shape[1]
    rows, depth = hidden.shape
    q_width, k_width = w_q.shape[1], w_k.shape[1]
    count = sum(x.shape[0] for x in prefix)
    window = window_rows(count)
    slot_len = rows // slots
    kv_heads, tall = k_width // size, slot_len * q_width // k_width
    saved = [
        ((rows, q_width), BF16),
        ((rows, k_width), BF16),
        ((rows, k_width), BF16),
        ((rows, q_width), F32),
        ((rows, k_width), F32),
        ((slots, kv_heads, tall, window), BF16),
        ((slots, kv_heads, tall, slot_len), BF16),
        ((rows, q_width), F32),
    ]
    weights = [w_q, w_k, w_v, q_gain, k_gain, w_out]
    kept = saved + like(weights) + [((count, prefix[0].shape[1]), BF16)]
    sent = block_shapes(names, rows, width)
    operands = [*scalars, hidden, *weights, prefix[0]]
    found = pl.pallas_call(
        functools.partial(forward_kernel, slots, names),
        in_specs=[HBM] * len(operands) + [VMEM] * (len(prefix) - 1),
        out_specs=[VMEM] * len(kept + sent),
        out_shape=in_vmem(kept + sent),
        scratch_shapes=[pltpu.VMEM(hidden.shape, hidden.dtype)]
        + [pltpu.SMEM(x.shape, jnp.int32) for x in scalars]
        + [pltpu.VMEM((rows, q_width), BF16), pltpu.SemaphoreType.DMA((64,))],
        compiler_params=pltpu.CompilerParams(vmem_limit_bytes=vmem_room(count)),
        cost_estimate=pl.CostEstimate(
            flops=2 * rows * depth * (2 * q_width + 2 * k_width),
            bytes_accessed=2 * depth * (rows + 2 * q_width + 2 * k_width) + 2 * rows * depth,
            transcendentals=slots * kv_heads * tall * window,
        ),
    )(*held_in(pltpu.HBM, operands), *held_in(pltpu.VMEM, prefix[1:]))
    return found[: len(kept)], found[len(kept) :]


def backward_kernel(slots, names, *refs):
    refs = list(refs)

    def take(count):
        found, refs[:count] = refs[:count], []
        return found

    scalars = take(3)
    cotangent = take(len(HELD))
    query, key, value, hq, hk, p_pre, p_own, heads_out = take(8)
    w_q, w_k, w_v, q_gain, k_gain, w_out, prefix_v = take(7)
    terms = take(len(refs) - len(names) - 3 - 5)
    parts = take(len(names))
    prompt_len, resp_prompt, resp_len = scalars_v = take(3)
    grad_prefix, dhq, dhk, dv, sems = take(5)

    copies = Copies(sems)
    small = [copies.start(a, b) for a, b in zip(scalars, scalars_v)]

    width = cotangent[0].shape[2]
    me = lax.axis_index("mp")
    grad_heads = 0.0
    for blocks, ref in zip(HELD, cotangent):
        for i, block in enumerate(blocks):
            grad_heads += dot_nt(ref[i], w_out[:, features(me ^ block, width)])
    grad_prefix[...] = jnp.zeros_like(grad_prefix)
    wait(small)

    count = prefix_v.shape[0]
    window = window_rows(count)
    slot_len = query.shape[0] // slots
    size = q_gain.shape[1]
    kv_heads = key.shape[1] // size
    groups = query.shape[1] // key.shape[1]
    scale = size ** (-0.5)
    for n in range(slots):
        first, _ = prompt_span(prompt_len, resp_prompt[n])
        start = window_start(first, count)
        rows = slice(n * slot_len, (n + 1) * slot_len)
        live = lax.broadcasted_iota(jnp.int32, (slot_len, size), 0) < resp_len[n]
        for h in range(kv_heads):
            heads = range(h * groups, (h + 1) * groups)
            q = stacked(query, rows, heads, size)
            out = stacked(heads_out, rows, heads, size)
            g = jnp.concatenate(
                [
                    jnp.where(live, grad_heads[rows, a * size : (a + 1) * size], 0.0).astype(BF16)
                    for a in heads
                ],
                axis=0,
            )
            k_win = prefix_v[pl.ds(start, window), 2 * h * size : (2 * h + 1) * size]
            v_win = prefix_v[pl.ds(start, window), (2 * h + 1) * size : (2 * h + 2) * size]
            k_own = key[rows, h * size : (h + 1) * size]
            v_own = value[rows, h * size : (h + 1) * size]
            b_pre, b_own = p_pre[n, h], p_own[n, h]
            delta = jnp.sum(g.astype(F32) * out, axis=-1, keepdims=True)
            ds_pre = (b_pre.astype(F32) * (dot_nt(g, v_win) - delta)).astype(BF16)
            ds_own = (b_own.astype(F32) * (dot_nt(g, v_own) - delta)).astype(BF16)
            grad_q = scale * (dot(ds_pre, k_win) + dot(ds_own, k_own))
            for i, a in enumerate(heads):
                cols = slice(a * size, (a + 1) * size)
                one = grad_q[i * slot_len : (i + 1) * slot_len]
                dhq[rows, cols] = norm_back(hq[rows, cols], q_gain[...], one).astype(BF16)
            cols = slice(h * size, (h + 1) * size)
            grad_k = scale * dot_tn(ds_own, q)
            dhk[rows, cols] = norm_back(hk[rows, cols], k_gain[...], grad_k).astype(BF16)
            dv[rows, cols] = dot_tn(b_own, g).astype(BF16)
            k_cols = slice(2 * h * size, (2 * h + 1) * size)
            v_cols = slice((2 * h + 1) * size, (2 * h + 2) * size)
            grad_prefix[pl.ds(start, window), k_cols] += scale * dot_tn(ds_pre, q)
            grad_prefix[pl.ds(start, window), v_cols] += dot_tn(b_pre, g)
    held = terms[0].shape[0]
    for k, ref in enumerate(terms):
        ref[...] = grad_prefix[slot_rows(len(terms), held, k), :]

    def make(cols):
        return (
            dot_nt(dhq[...], w_q[cols, :])
            + dot_nt(dhk[...], w_k[cols, :])
            + dot_nt(dv[...], w_v[cols, :])
        ).astype(BF16)

    make_blocks(make, names, parts)


def backward(names, scalars, cotangent, kept, prefix):
    slots = scalars[-1].shape[0]
    w_out, w_k = kept[13], kept[9]
    rows, q_width = kept[0].shape
    k_width = w_k.shape[1]
    depth = w_out.shape[1]
    count, kv_width = kept[14].shape
    sent = block_shapes(names, rows, cotangent[0].shape[2])
    operands = list(scalars)
    results = [(x.shape, F32) for x in prefix] + sent
    found = pl.pallas_call(
        functools.partial(backward_kernel, slots, names),
        in_specs=[HBM] * len(operands) + [VMEM] * (len(cotangent) + len(kept)),
        out_specs=[VMEM] * len(results),
        out_shape=in_vmem(results),
        scratch_shapes=[pltpu.SMEM(x.shape, jnp.int32) for x in scalars]
        + [
            pltpu.VMEM((count, kv_width), F32),
            pltpu.VMEM((rows, q_width), BF16),
            pltpu.VMEM((rows, k_width), BF16),
            pltpu.VMEM((rows, k_width), BF16),
            pltpu.SemaphoreType.DMA((64,)),
        ],
        compiler_params=pltpu.CompilerParams(vmem_limit_bytes=vmem_room(count)),
        cost_estimate=pl.CostEstimate(
            flops=2 * rows * (2 * q_width + 2 * k_width) * depth
            + 10 * rows * q_width * (window_rows(count) + rows // slots),
            bytes_accessed=4 * rows * depth,
            transcendentals=0,
        ),
    )(*held_in(pltpu.HBM, operands), *held_in(pltpu.VMEM, [*cotangent, *kept]))
    return found[: len(prefix)], found[len(prefix) :]


def trade(block, axis, step):
    return lax.ppermute(block, axis, [(i, i ^ step) for i in range(lax.axis_size(axis))])


def after(value, *others):
    return lax.optimization_barrier((value, *others))[0]


def total(*terms):
    whole = terms[0].astype(F32)
    for term in terms[1:]:
        whole = whole + term.astype(F32)
    return whole.astype(BF16)


def sum_all(sent_out, kept_out, parts):
    far, near, kept_far, kept = parts
    got = trade(sent_out, "mp", 2)
    sent_out, kept_out = total(kept_out[2:], got[2:]), total(kept_out[:2], got[:2])
    far = total(after(kept_far, sent_out), trade(far, "mp", 1))
    near = after(trade(near, "mp", 1), far)
    got_out = trade(sent_out, "mp", 4)
    got = trade(far, "mp", 2)
    sent, kept = total(kept[1], near[1], got[1]), total(kept[0], near[0], got[0])
    kept_out = after(kept_out, sent)
    sent_out, kept_out = total(kept_out[1], got_out[1]), total(kept_out[0], got_out[0])
    mixed = total(kept_out, trade(sent_out, "mp", 1))
    return mixed, total(kept, trade(sent, "mp", 4)), sent, sent_out


def per_device(
    hidden_rows,
    w_query,
    w_key,
    w_value,
    w_out,
    q_gain,
    k_gain,
    prefix_kv,
    cotangent,
    prompt_len,
    resp_prompt,
    resp_len,
):
    chips = lax.axis_size("dp")
    scalars = (prompt_len, resp_prompt, resp_len)
    q_gain, k_gain = q_gain[None], k_gain[None]
    if chips > 8:
        prefix = [lax.all_gather(prefix_kv, "dp", axis=0, tiled=True)]
    else:
        prefix = [prefix_kv] + [trade(prefix_kv, "dp", k) for k in range(1, chips)]
    pair = jnp.stack([after(cotangent, *prefix[1:]), trade(cotangent, "mp", 4)])
    along = trade(pair, "mp", 2)
    kept, (sent, kept_out) = forward(
        OUT_SENT + OUT_KEPT, cotangent.shape[1], scalars, after(hidden_rows, pair), w_query, w_key,
        w_value, q_gain, k_gain, w_out, prefix,
    )
    across = trade(pair, "mp", 1)
    back = [pair, along, across, trade(after(along, kept_out, across), "mp", 1)]
    sent = after(sent, along)
    terms, parts = backward(IN_SENT + IN_KEPT, scalars, back, kept, prefix)
    mixed, grad_input, near, last = sum_all(sent, kept_out, parts)
    terms = lax.optimization_barrier((*terms, near))[:-1]
    if chips > 8:
        grad_prefix = lax.psum_scatter(terms[0], "dp", scatter_dimension=0, tiled=True)
    else:
        grad_prefix = after(terms[0], last)
        for k in range(1, chips):
            grad_prefix = grad_prefix + trade(terms[k], "dp", k)
    return mixed, grad_input, grad_prefix.astype(BF16)


def solution(mesh):
    in_specs = (
        P("dp", None),
        P(None, "mp"),
        P(None, "mp"),
        P(None, "mp"),
        P("mp", None),
        P(),
        P(),
        P("dp", "mp"),
        P("dp", "mp"),
        P(),
        P("dp"),
        P("dp"),
    )
    out_specs = (P("dp", "mp"), P("dp", "mp"), P("dp", "mp"))
    return jax.shard_map(
        per_device, mesh=mesh, in_specs=in_specs, out_specs=out_specs, check_vma=False
    )
```

```python
import functools

import jax
import jax.numpy as jnp
from jax import lax
from jax.experimental import pallas as pl
from jax.experimental.pallas import tpu as pltpu
from jax.sharding import PartitionSpec as P

EPS = 1e-06
NEG = -1e30
ROWS = 16
HELD = ((0,), (2,), (4,), (6,), (1,), (3,), (5,), (7,))
OUT = ((6, 7), (2, 3), (4, 5), (0, 1))
TERMS = ((1, 3), (0, 2))
IN = ((7,), (5,), (3, 1), (6,), (4,), (2,), (0,))
F32 = jnp.float32
BF16 = jnp.bfloat16
HBM = pl.BlockSpec(memory_space=pltpu.HBM)
SMEM = pl.BlockSpec(memory_space=pltpu.SMEM)
VMEM = pl.BlockSpec(memory_space=pltpu.VMEM)


def dot(left, right):
    return jnp.dot(left, right, preferred_element_type=F32)


def dot_nt(left, right):
    return lax.dot_general(left, right, (((1,), (1,)), ((), ())), preferred_element_type=F32)


def dot_tn(left, right):
    return lax.dot_general(left, right, (((0,), (0,)), ((), ())), preferred_element_type=F32)


def inverse_root(hidden):
    return lax.rsqrt(jnp.mean(hidden * hidden, axis=-1, keepdims=True) + EPS)


def norm_back(hidden, gain, grad):
    root = inverse_root(hidden)
    unit = hidden * root
    scaled = grad * gain
    return root * (scaled - unit * jnp.mean(scaled * unit, axis=-1, keepdims=True))


class Copies:
    def __init__(self, sems):
        self.sems, self.count = sems, 0

    def start(self, source, target):
        copy = pltpu.make_async_copy(source, target, self.sems.at[self.count])
        self.count += 1
        copy.start()
        return copy


def wait(copies):
    for copy in copies:
        copy.wait()


def prompt_span(prompt_len, prompt):
    first, last = 0, 0
    end = 0
    for p in range(prompt_len.shape[0]):
        begin = end
        end = end + prompt_len[p]
        first = jnp.where(prompt == p, begin, first)
        last = jnp.where(prompt == p, end, last)
    return first, last


def window_rows(count):
    return min(count, count // 3 + ROWS)


def window_start(first, count):
    start = jnp.minimum(first // ROWS * ROWS, count - window_rows(count))
    return pl.multiple_of(start, ROWS)


def slot_rows(slots, rows, step):
    if slots == 1:
        return pl.ds(0, rows)
    return pl.ds(pl.multiple_of((lax.axis_index("dp") ^ step) * rows, ROWS), rows)


def features(block, width):
    return pl.ds(pl.multiple_of(block * width, width), width)


def stacked(ref, rows, heads, size):
    return jnp.concatenate([ref[rows, a * size : (a + 1) * size] for a in heads], axis=0)


def make_blocks(make, names, refs):
    me = lax.axis_index("mp")
    for blocks, ref in zip(names, refs):
        for i, block in enumerate(blocks):
            ref[i] = make(features(me ^ block, ref.shape[-1]))


def taker(refs):
    refs = list(refs)

    def take(count):
        found, refs[:count] = refs[:count], []
        return found

    return take, refs


def project_kernel(*refs):
    take, _ = taker(refs)
    scalars = take(3)
    hidden, w_q, w_k, w_v, q_gain, k_gain, w_out, prefix, own = take(9)
    scalars_v = take(3)
    query, key, value, hq, hk = take(5)
    wq_v, wk_v, wv_v, qg_v, kg_v, wo_v, prefix_v, own_v = take(8)
    hidden_v, sems = take(2)

    copies = Copies(sems)
    depth = hidden.shape[1]
    steps = 4
    part = depth // steps
    loads = []
    for i in range(steps):
        cut = pl.ds(i * part, part)
        loads.append(
            [copies.start(hidden.at[:, cut], hidden_v.at[:, cut])]
            + [
                copies.start(w.at[cut], v.at[cut])
                for w, v in ((w_q, wq_v), (w_k, wk_v), (w_v, wv_v))
            ]
        )
    small = [copies.start(q_gain, qg_v), copies.start(k_gain, kg_v)]
    small += [copies.start(source, target) for source, target in zip(scalars, scalars_v)]
    small += [copies.start(prefix, prefix_v), copies.start(w_out, wo_v), copies.start(own, own_v)]

    sums = [None] * 3
    for i, load in enumerate(loads):
        wait(load)
        rows = hidden_v[:, i * part : (i + 1) * part]
        for j, v in enumerate((wq_v, wk_v, wv_v)):
            term = dot(rows, v[i * part : (i + 1) * part])
            sums[j] = term if i == 0 else sums[j] + term
    hq[...], hk[...] = sums[0], sums[1]
    value[...] = sums[2].astype(BF16)
    wait(small)
    size = qg_v.shape[1]
    for whole, gain, out in ((sums[0], qg_v, query), (sums[1], kg_v, key)):
        for at in range(0, whole.shape[1], size):
            head = whole[:, at : at + size]
            out[:, at : at + size] = (head * inverse_root(head) * gain[...]).astype(BF16)


def project(scalars, hidden, w_q, w_k, w_v, q_gain, k_gain, w_out, prefix, own):
    rows, depth = hidden.shape
    q_width, k_width = w_q.shape[1], w_k.shape[1]
    weights = [w_q, w_k, w_v, q_gain, k_gain, w_out, prefix, own]
    operands = [*scalars, hidden, *weights]
    kept = [
        ((rows, q_width), BF16),
        ((rows, k_width), BF16),
        ((rows, k_width), BF16),
        ((rows, q_width), F32),
        ((rows, k_width), F32),
    ] + like(weights)
    found = pl.pallas_call(
        project_kernel,
        in_specs=[HBM] * len(operands),
        out_specs=[SMEM] * 3 + [VMEM] * len(kept),
        out_shape=[pltpu.SMEM(x.shape, jnp.int32) for x in scalars] + in_vmem(kept),
        scratch_shapes=[pltpu.VMEM(hidden.shape, hidden.dtype), pltpu.SemaphoreType.DMA((32,))],
        compiler_params=pltpu.CompilerParams(vmem_limit_bytes=vmem_room(prefix.shape[0])),
        cost_estimate=lasting(2.6),
    )(*held_in(pltpu.HBM, operands))
    return found[:3], found[3:8], found[8:14], found[14], found[15]


def forward_kernel(slots, names, *refs):
    take, rest = taker(refs)
    prompt_len, resp_prompt, resp_len = take(3)
    query, key, value, wo_v = take(4)
    prefix = take(len(rest) - 4 - len(names) - 1)
    p_pre, p_own, heads_out, prefix_v = take(4)
    parts = take(len(names))
    (out_bf,) = take(1)

    held = prefix[0].shape[0]
    for k, ref in enumerate(prefix):
        prefix_v[slot_rows(len(prefix), held, k), :] = ref[...]
    size = heads_out.shape[1] * p_own.shape[3] // p_own.shape[2] // p_own.shape[1]
    count = prefix_v.shape[0]
    window = window_rows(count)
    slot_len = query.shape[0] // slots
    kv_heads = key.shape[1] // size
    groups = query.shape[1] // key.shape[1]
    scale = size ** (-0.5)
    for n in range(slots):
        first, last = prompt_span(prompt_len, resp_prompt[n])
        start = window_start(first, count)
        rows = slice(n * slot_len, (n + 1) * slot_len)
        live = lax.broadcasted_iota(jnp.int32, (slot_len, size), 0) < resp_len[n]
        for h in range(kv_heads):
            heads = range(h * groups, (h + 1) * groups)
            q = stacked(query, rows, heads, size)
            k_win = prefix_v[pl.ds(start, window), 2 * h * size : (2 * h + 1) * size]
            v_win = prefix_v[pl.ds(start, window), (2 * h + 1) * size : (2 * h + 2) * size]
            k_own = key[rows, h * size : (h + 1) * size]
            v_own = value[rows, h * size : (h + 1) * size]
            tall = groups * slot_len
            place = start + lax.broadcasted_iota(jnp.int32, (tall, window), 1)
            s_pre = jnp.where((place >= first) & (place < last), dot_nt(q, k_win) * scale, NEG)
            token = lax.broadcasted_iota(jnp.int32, (groups, slot_len, slot_len), 1)
            token = token.reshape(tall, slot_len)
            other = lax.broadcasted_iota(jnp.int32, (tall, slot_len), 1)
            s_own = jnp.where(
                (other <= token) & (other < resp_len[n]), dot_nt(q, k_own) * scale, NEG
            )
            top = jnp.maximum(
                jnp.max(s_pre, axis=-1, keepdims=True), jnp.max(s_own, axis=-1, keepdims=True)
            )
            e_pre = jnp.exp(s_pre - top)
            e_own = jnp.exp(s_own - top)
            total = jnp.sum(e_pre, axis=-1, keepdims=True) + jnp.sum(e_own, axis=-1, keepdims=True)
            b_pre = (e_pre / total).astype(BF16)
            b_own = (e_own / total).astype(BF16)
            p_pre[n, h] = b_pre
            p_own[n, h] = b_own
            out = dot(b_pre, v_win) + dot(b_own, v_own)
            for i, a in enumerate(heads):
                one = out[i * slot_len : (i + 1) * slot_len]
                heads_out[rows, a * size : (a + 1) * size] = one
                out_bf[rows, a * size : (a + 1) * size] = jnp.where(live, one, 0.0).astype(BF16)

    def make(cols):
        return dot(out_bf[...], wo_v[:, cols]).astype(BF16)

    make_blocks(make, names, parts)


def block_shapes(names, rows, width):
    return [((len(blocks), rows, width), BF16) for blocks in names]


def in_vmem(shapes):
    return [pltpu.VMEM(*x) for x in shapes]


def held_in(space, arrays):
    return [pltpu.with_memory_space_constraint(x, space) for x in arrays]


def lasting(us):
    return pl.CostEstimate(flops=int(us * 1.15e9), bytes_accessed=0, transcendentals=0)


def like(arrays):
    return [(x.shape, x.dtype) for x in arrays]


def vmem_room(prefix_rows):
    return 48 << 20 if prefix_rows > 1024 else 24 << 20


def forward(names, width, size, scalars, query, key, value, w_out, prefix):
    slots = scalars[-1].shape[0]
    rows, q_width = query.shape
    k_width = key.shape[1]
    count = sum(x.shape[0] for x in prefix)
    window = window_rows(count)
    slot_len = rows // slots
    kv_heads, tall = k_width // size, slot_len * q_width // k_width
    results = [
        ((slots, kv_heads, tall, window), BF16),
        ((slots, kv_heads, tall, slot_len), BF16),
        ((rows, q_width), F32),
        ((count, prefix[0].shape[1]), BF16),
    ] + block_shapes(names, rows, width)
    operands = [query, key, value, w_out, *prefix]
    found = pl.pallas_call(
        functools.partial(forward_kernel, slots, names),
        in_specs=[SMEM] * 3 + [VMEM] * len(operands),
        out_specs=[VMEM] * len(results),
        out_shape=in_vmem(results),
        scratch_shapes=[pltpu.VMEM((rows, q_width), BF16)],
        compiler_params=pltpu.CompilerParams(vmem_limit_bytes=vmem_room(count)),
        cost_estimate=lasting(1.7),
    )(*held_in(pltpu.SMEM, scalars), *held_in(pltpu.VMEM, operands))
    return found[:4], found[4:]


def backward_kernel(slots, names, *refs):
    take, rest = taker(refs)
    prompt_len, resp_prompt, resp_len = take(3)
    cotangent = take(len(HELD))
    query, key, value, hq, hk = take(5)
    w_q, w_k, w_v, q_gain, k_gain, w_out = take(6)
    p_pre, p_own, heads_out, prefix_v = take(4)
    terms = take(len(rest) - len(names) - 4)
    parts = take(len(names))
    grad_prefix, dhq, dhk, dv = take(4)

    width = cotangent[0].shape[2]
    me = lax.axis_index("mp")
    grad_heads = 0.0
    for blocks, ref in zip(HELD, cotangent):
        for i, block in enumerate(blocks):
            grad_heads += dot_nt(ref[i], w_out[:, features(me ^ block, width)])
    grad_prefix[...] = jnp.zeros_like(grad_prefix)

    count = prefix_v.shape[0]
    window = window_rows(count)
    slot_len = query.shape[0] // slots
    size = q_gain.shape[1]
    kv_heads = key.shape[1] // size
    groups = query.shape[1] // key.shape[1]
    scale = size ** (-0.5)
    for n in range(slots):
        first, _ = prompt_span(prompt_len, resp_prompt[n])
        start = window_start(first, count)
        rows = slice(n * slot_len, (n + 1) * slot_len)
        live = lax.broadcasted_iota(jnp.int32, (slot_len, size), 0) < resp_len[n]
        for h in range(kv_heads):
            heads = range(h * groups, (h + 1) * groups)
            q = stacked(query, rows, heads, size)
            out = stacked(heads_out, rows, heads, size)
            g = jnp.concatenate(
                [
                    jnp.where(live, grad_heads[rows, a * size : (a + 1) * size], 0.0).astype(BF16)
                    for a in heads
                ],
                axis=0,
            )
            k_win = prefix_v[pl.ds(start, window), 2 * h * size : (2 * h + 1) * size]
            v_win = prefix_v[pl.ds(start, window), (2 * h + 1) * size : (2 * h + 2) * size]
            k_own = key[rows, h * size : (h + 1) * size]
            v_own = value[rows, h * size : (h + 1) * size]
            b_pre, b_own = p_pre[n, h], p_own[n, h]
            delta = jnp.sum(g.astype(F32) * out, axis=-1, keepdims=True)
            ds_pre = (b_pre.astype(F32) * (dot_nt(g, v_win) - delta)).astype(BF16)
            ds_own = (b_own.astype(F32) * (dot_nt(g, v_own) - delta)).astype(BF16)
            grad_q = scale * (dot(ds_pre, k_win) + dot(ds_own, k_own))
            for i, a in enumerate(heads):
                cols = slice(a * size, (a + 1) * size)
                one = grad_q[i * slot_len : (i + 1) * slot_len]
                dhq[rows, cols] = norm_back(hq[rows, cols], q_gain[...], one).astype(BF16)
            cols = slice(h * size, (h + 1) * size)
            grad_k = scale * dot_tn(ds_own, q)
            dhk[rows, cols] = norm_back(hk[rows, cols], k_gain[...], grad_k).astype(BF16)
            dv[rows, cols] = dot_tn(b_own, g).astype(BF16)
            k_cols = slice(2 * h * size, (2 * h + 1) * size)
            v_cols = slice((2 * h + 1) * size, (2 * h + 2) * size)
            grad_prefix[pl.ds(start, window), k_cols] += scale * dot_tn(ds_pre, q)
            grad_prefix[pl.ds(start, window), v_cols] += dot_tn(b_pre, g)
    chips = prefix_v.shape[0] // terms[0].shape[1] if len(terms) > 1 else 1
    for ref, steps in zip(terms, TERMS if len(terms) > 1 else ((0,),)):
        for i, step in enumerate(steps):
            ref[i] = grad_prefix[slot_rows(chips, ref.shape[1], step), :]

    def make(cols):
        return (
            dot_nt(dhq[...], w_q[cols, :])
            + dot_nt(dhk[...], w_k[cols, :])
            + dot_nt(dv[...], w_v[cols, :])
        ).astype(BF16)

    make_blocks(make, names, parts)


def backward(names, scalars, cotangent, kept, terms):
    slots = scalars[-1].shape[0]
    query, key, w_out, prefix = kept[0], kept[1], kept[10], kept[14]
    rows, q_width = query.shape
    k_width, depth = key.shape[1], w_out.shape[1]
    count, kv_width = prefix.shape
    results = [(x, F32) for x in terms] + block_shapes(names, rows, cotangent[0].shape[2])
    found = pl.pallas_call(
        functools.partial(backward_kernel, slots, names),
        in_specs=[SMEM] * 3 + [VMEM] * (len(cotangent) + len(kept)),
        out_specs=[VMEM] * len(results),
        out_shape=in_vmem(results),
        scratch_shapes=[
            pltpu.VMEM((count, kv_width), F32),
            pltpu.VMEM((rows, q_width), BF16),
            pltpu.VMEM((rows, k_width), BF16),
            pltpu.VMEM((rows, k_width), BF16),
        ],
        compiler_params=pltpu.CompilerParams(vmem_limit_bytes=vmem_room(count)),
        cost_estimate=lasting(3.5),
    )(*held_in(pltpu.SMEM, scalars), *held_in(pltpu.VMEM, [*cotangent, *kept]))
    return found[: len(terms)], found[len(terms) :]


def last_kernel(counts, *refs):
    take, rest = taker(refs)
    groups = [take(len(count)) for count in counts]
    results = take(len(counts))
    stage = take(len(counts))
    (sems,) = take(1)
    copies = Copies(sems)
    stores = []
    for count, group, result, ref in zip(counts, groups, results, stage):
        whole = 0.0
        for i, term in zip(count, group):
            whole = whole + term[i].astype(F32)
        ref[...] = whole.astype(BF16)
        stores.append(copies.start(ref, result))
    wait(stores)


def last_sums(groups):
    arrays = [array for group in groups for array, _ in group]
    shapes = [jax.ShapeDtypeStruct(group[0][0].shape[1:], BF16) for group in groups]
    return pl.pallas_call(
        functools.partial(last_kernel, [[i for _, i in group] for group in groups]),
        in_specs=[VMEM] * len(arrays),
        out_specs=[HBM] * len(groups),
        out_shape=shapes,
        scratch_shapes=in_vmem(like(shapes)) + [pltpu.SemaphoreType.DMA((len(groups),))],
        compiler_params=pltpu.CompilerParams(vmem_limit_bytes=vmem_room(0)),
        cost_estimate=lasting(0.9),
    )(*held_in(pltpu.VMEM, arrays))


def trade(block, axis, step):
    return lax.ppermute(block, axis, [(i, i ^ step) for i in range(lax.axis_size(axis))])


def after(value, *others):
    return lax.optimization_barrier((value, *others))[0]


def total(*terms):
    whole = terms[0].astype(F32)
    for term in terms[1:]:
        whole = whole + term.astype(F32)
    return whole.astype(BF16)


def per_device(
    hidden_rows,
    w_query,
    w_key,
    w_value,
    w_out,
    q_gain,
    k_gain,
    prefix_kv,
    cotangent,
    prompt_len,
    resp_prompt,
    resp_len,
):
    chips = lax.axis_size("dp")
    scalars = (prompt_len, resp_prompt, resp_len)
    q_gain, k_gain = q_gain[None], k_gain[None]
    own = cotangent[None]
    far = trade(own, "mp", 4)
    near = trade(own, "mp", 2)
    if chips == 4:
        others = [trade(prefix_kv, "dp", k) for k in range(1, chips)]
    else:
        prefix_kv, others = lax.all_gather(prefix_kv, "dp", axis=0, tiled=True), []
    far = after(far, *others)
    both = trade(far, "mp", 2)
    own_x, near_x, far_x = [trade(x, "mp", 1) for x in (own, near, far)]
    scalars, projected, weights, prefix, own = project(
        scalars, after(hidden_rows, far), w_query, w_key, w_value, q_gain, k_gain, w_out,
        prefix_kv, own,
    )
    both_x = trade(after(both, projected[0]), "mp", 1)
    probed, parts = forward(
        OUT, cotangent.shape[1], q_gain.shape[1], scalars, after(projected[0], both),
        *projected[1:3], weights[5], [prefix, *others],
    )
    back = [own, near, far, both, own_x, near_x, far_x, both_x]
    shape = prefix_kv.shape
    terms = [(1, *shape)] if chips != 4 else [(len(steps), *shape) for steps in TERMS]
    terms, grads = backward(IN, scalars, back, [*projected, *weights, *probed], terms)

    out_a, out_b, kept_a, kept_b = parts
    got_a = trade(out_a, "mp", 2)
    out_a = total(kept_a, got_a)
    got_out = trade(out_a, "mp", 4)
    in_7, in_5, in_31, in_6, in_4, in_2, in_0 = grads
    got_7 = trade(in_7, "mp", 1)
    got_5 = trade(in_5, "mp", 1)
    in_6 = total(after(in_6, out_a), got_7)
    got_6 = trade(in_6, "mp", 2)
    got_31 = trade(after(in_31, in_6), "mp", 1)
    got_b = trade(after(out_b, in_6), "mp", 2)
    in_4 = total(in_4, got_5, got_6)
    got_4 = trade(in_4, "mp", 4)
    got_2 = trade(total(in_2, got_31[:1]), "mp", 2)
    got_x = trade(total(after(kept_b, in_4)[1:], got_b[1:], got_out[1:]), "mp", 1)
    groups = [
        [(kept_b, 0), (got_b, 0), (got_out, 0), (got_x, 0)],
        [(in_0, 0), (got_31, 1), (got_2, 0), (got_4, 0)],
    ]
    if chips == 4:
        got = trade(after(terms[0], in_4), "dp", 1)
        sent = terms[1][1:] + got[1:]
        groups.append([(terms[1], 0), (got, 0), (trade(sent, "dp", 2), 0)])
        return last_sums(groups)
    grad_prefix = lax.psum_scatter(terms[0][0], "dp", scatter_dimension=0, tiled=True)
    return *last_sums(groups), grad_prefix.astype(BF16)


def solution(mesh):
    in_specs = (
        P("dp", None),
        P(None, "mp"),
        P(None, "mp"),
        P(None, "mp"),
        P("mp", None),
        P(),
        P(),
        P("dp", "mp"),
        P("dp", "mp"),
        P(),
        P("dp"),
        P("dp"),
    )
    out_specs = (P("dp", "mp"), P("dp", "mp"), P("dp", "mp"))
    return jax.shard_map(
        per_device, mesh=mesh, in_specs=in_specs, out_specs=out_specs, check_vma=False
    )
```

```python
import functools

import jax
import jax.numpy as jnp
from jax import lax
from jax.experimental import pallas as pl
from jax.experimental.pallas import tpu as pltpu
from jax.sharding import PartitionSpec as P

EPS = 1e-06
NEG = -1e30
ROWS = 16
HELD = ((0,), (2,), (4,), (6,), (1,), (3,), (5,), (7,))
OUT = ((6, 7), (2, 3), (4, 5), (0, 1))
TERMS = ((0,), (1,), (2,), (3,))
IN = ((7,), (5,), (3, 1), (6,), (4,), (2,), (0,))
F32 = jnp.float32
BF16 = jnp.bfloat16
HBM = pl.BlockSpec(memory_space=pltpu.HBM)
SMEM = pl.BlockSpec(memory_space=pltpu.SMEM)
VMEM = pl.BlockSpec(memory_space=pltpu.VMEM)


def dot(left, right):
    return jnp.dot(left, right, preferred_element_type=F32)


def dot_nt(left, right):
    return lax.dot_general(left, right, (((1,), (1,)), ((), ())), preferred_element_type=F32)


def dot_tn(left, right):
    return lax.dot_general(left, right, (((0,), (0,)), ((), ())), preferred_element_type=F32)


def inverse_root(hidden):
    return lax.rsqrt(jnp.mean(hidden * hidden, axis=-1, keepdims=True) + EPS)


def norm_back(hidden, gain, grad):
    root = inverse_root(hidden)
    unit = hidden * root
    scaled = grad * gain
    return root * (scaled - unit * jnp.mean(scaled * unit, axis=-1, keepdims=True))


class Copies:
    def __init__(self, sems):
        self.sems, self.count = sems, 0

    def start(self, source, target):
        copy = pltpu.make_async_copy(source, target, self.sems.at[self.count])
        self.count += 1
        copy.start()
        return copy


def wait(copies):
    for copy in copies:
        copy.wait()


def prompt_span(prompt_len, prompt):
    first, last = 0, 0
    end = 0
    for p in range(prompt_len.shape[0]):
        begin = end
        end = end + prompt_len[p]
        first = jnp.where(prompt == p, begin, first)
        last = jnp.where(prompt == p, end, last)
    return first, last


def window_rows(count):
    return min(count, count // 3 + ROWS)


def window_start(first, count):
    start = jnp.minimum(first // ROWS * ROWS, count - window_rows(count))
    return pl.multiple_of(start, ROWS)


def slot_rows(slots, rows, step):
    if slots == 1:
        return pl.ds(0, rows)
    return pl.ds(pl.multiple_of((lax.axis_index("dp") ^ step) * rows, ROWS), rows)


def features(block, width):
    return pl.ds(pl.multiple_of(block * width, width), width)


def stacked(ref, rows, heads, size):
    return jnp.concatenate([ref[rows, a * size : (a + 1) * size] for a in heads], axis=0)


def make_blocks(make, names, refs):
    me = lax.axis_index("mp")
    for blocks, ref in zip(names, refs):
        for i, block in enumerate(blocks):
            ref[i] = make(features(me ^ block, ref.shape[-1]))


def taker(refs):
    refs = list(refs)

    def take(count):
        found, refs[:count] = refs[:count], []
        return found

    return take, refs


def project_kernel(*refs):
    take, _ = taker(refs)
    scalars = take(3)
    hidden, w_q, w_k, w_v, q_gain, k_gain, w_out, prefix, own = take(9)
    scalars_v = take(3)
    query, key, value, hq, hk = take(5)
    wq_v, wk_v, wv_v, qg_v, kg_v, wo_v, prefix_v, own_v = take(8)
    hidden_v, sems = take(2)

    copies = Copies(sems)
    depth = hidden.shape[1]
    steps = 4
    part = depth // steps
    loads = []
    for i in range(steps):
        cut = pl.ds(i * part, part)
        loads.append(
            [copies.start(hidden.at[:, cut], hidden_v.at[:, cut])]
            + [
                copies.start(w.at[cut], v.at[cut])
                for w, v in ((w_q, wq_v), (w_k, wk_v), (w_v, wv_v))
            ]
        )
    small = [copies.start(q_gain, qg_v), copies.start(k_gain, kg_v)]
    small += [copies.start(source, target) for source, target in zip(scalars, scalars_v)]
    small += [copies.start(prefix, prefix_v), copies.start(w_out, wo_v), copies.start(own, own_v)]

    sums = [None] * 3
    for i, load in enumerate(loads):
        wait(load)
        rows = hidden_v[:, i * part : (i + 1) * part]
        for j, v in enumerate((wq_v, wk_v, wv_v)):
            term = dot(rows, v[i * part : (i + 1) * part])
            sums[j] = term if i == 0 else sums[j] + term
    hq[...], hk[...] = sums[0], sums[1]
    value[...] = sums[2].astype(BF16)
    wait(small)
    size = qg_v.shape[1]
    for whole, gain, out in ((sums[0], qg_v, query), (sums[1], kg_v, key)):
        for at in range(0, whole.shape[1], size):
            head = whole[:, at : at + size]
            out[:, at : at + size] = (head * inverse_root(head) * gain[...]).astype(BF16)


def project(scalars, hidden, w_q, w_k, w_v, q_gain, k_gain, w_out, prefix, own):
    rows, depth = hidden.shape
    q_width, k_width = w_q.shape[1], w_k.shape[1]
    weights = [w_q, w_k, w_v, q_gain, k_gain, w_out, prefix, own]
    operands = [*scalars, hidden, *weights]
    kept = [
        ((rows, q_width), BF16),
        ((rows, k_width), BF16),
        ((rows, k_width), BF16),
        ((rows, q_width), F32),
        ((rows, k_width), F32),
    ] + like(weights)
    found = pl.pallas_call(
        project_kernel,
        in_specs=[HBM] * len(operands),
        out_specs=[SMEM] * 3 + [VMEM] * len(kept),
        out_shape=[pltpu.SMEM(x.shape, jnp.int32) for x in scalars] + in_vmem(kept),
        scratch_shapes=[pltpu.VMEM(hidden.shape, hidden.dtype), pltpu.SemaphoreType.DMA((32,))],
        compiler_params=pltpu.CompilerParams(vmem_limit_bytes=vmem_room(prefix.shape[0])),
        cost_estimate=lasting(2.6),
    )(*held_in(pltpu.HBM, operands))
    return found[:3], found[3:8], found[8:14], found[14], found[15]


def forward_kernel(slots, names, *refs):
    take, rest = taker(refs)
    prompt_len, resp_prompt, resp_len = take(3)
    query, key, value, wo_v = take(4)
    prefix = take(len(rest) - 4 - len(names) - 1)
    p_pre, p_own, heads_out, prefix_v = take(4)
    parts = take(len(names))
    (out_bf,) = take(1)

    held = prefix[0].shape[0]
    for k, ref in enumerate(prefix):
        prefix_v[slot_rows(len(prefix), held, k), :] = ref[...]
    size = heads_out.shape[1] * p_own.shape[3] // p_own.shape[2] // p_own.shape[1]
    count = prefix_v.shape[0]
    window = window_rows(count)
    slot_len = query.shape[0] // slots
    kv_heads = key.shape[1] // size
    groups = query.shape[1] // key.shape[1]
    scale = size ** (-0.5)
    for n in range(slots):
        first, last = prompt_span(prompt_len, resp_prompt[n])
        start = window_start(first, count)
        rows = slice(n * slot_len, (n + 1) * slot_len)
        live = lax.broadcasted_iota(jnp.int32, (slot_len, size), 0) < resp_len[n]
        for h in range(kv_heads):
            heads = range(h * groups, (h + 1) * groups)
            q = stacked(query, rows, heads, size)
            k_win = prefix_v[pl.ds(start, window), 2 * h * size : (2 * h + 1) * size]
            v_win = prefix_v[pl.ds(start, window), (2 * h + 1) * size : (2 * h + 2) * size]
            k_own = key[rows, h * size : (h + 1) * size]
            v_own = value[rows, h * size : (h + 1) * size]
            tall = groups * slot_len
            place = start + lax.broadcasted_iota(jnp.int32, (tall, window), 1)
            s_pre = jnp.where((place >= first) & (place < last), dot_nt(q, k_win) * scale, NEG)
            token = lax.broadcasted_iota(jnp.int32, (groups, slot_len, slot_len), 1)
            token = token.reshape(tall, slot_len)
            other = lax.broadcasted_iota(jnp.int32, (tall, slot_len), 1)
            s_own = jnp.where(
                (other <= token) & (other < resp_len[n]), dot_nt(q, k_own) * scale, NEG
            )
            top = jnp.maximum(
                jnp.max(s_pre, axis=-1, keepdims=True), jnp.max(s_own, axis=-1, keepdims=True)
            )
            e_pre = jnp.exp(s_pre - top)
            e_own = jnp.exp(s_own - top)
            total = jnp.sum(e_pre, axis=-1, keepdims=True) + jnp.sum(e_own, axis=-1, keepdims=True)
            b_pre = (e_pre / total).astype(BF16)
            b_own = (e_own / total).astype(BF16)
            p_pre[n, h] = b_pre
            p_own[n, h] = b_own
            out = dot(b_pre, v_win) + dot(b_own, v_own)
            for i, a in enumerate(heads):
                one = out[i * slot_len : (i + 1) * slot_len]
                heads_out[rows, a * size : (a + 1) * size] = one
                out_bf[rows, a * size : (a + 1) * size] = jnp.where(live, one, 0.0).astype(BF16)

    def make(cols):
        return dot(out_bf[...], wo_v[:, cols]).astype(BF16)

    make_blocks(make, names, parts)


def block_shapes(names, rows, width):
    return [((len(blocks), rows, width), BF16) for blocks in names]


def in_vmem(shapes):
    return [pltpu.VMEM(*x) for x in shapes]


def held_in(space, arrays):
    return [pltpu.with_memory_space_constraint(x, space) for x in arrays]


def lasting(us):
    return pl.CostEstimate(flops=int(us * 1.15e9), bytes_accessed=0, transcendentals=0)


def like(arrays):
    return [(x.shape, x.dtype) for x in arrays]


def vmem_room(prefix_rows):
    return 48 << 20 if prefix_rows > 1024 else 24 << 20


def forward(names, width, size, scalars, query, key, value, w_out, prefix):
    slots = scalars[-1].shape[0]
    rows, q_width = query.shape
    k_width = key.shape[1]
    count = sum(x.shape[0] for x in prefix)
    window = window_rows(count)
    slot_len = rows // slots
    kv_heads, tall = k_width // size, slot_len * q_width // k_width
    results = [
        ((slots, kv_heads, tall, window), BF16),
        ((slots, kv_heads, tall, slot_len), BF16),
        ((rows, q_width), F32),
        ((count, prefix[0].shape[1]), BF16),
    ] + block_shapes(names, rows, width)
    operands = [query, key, value, w_out, *prefix]
    found = pl.pallas_call(
        functools.partial(forward_kernel, slots, names),
        in_specs=[SMEM] * 3 + [VMEM] * len(operands),
        out_specs=[VMEM] * len(results),
        out_shape=in_vmem(results),
        scratch_shapes=[pltpu.VMEM((rows, q_width), BF16)],
        compiler_params=pltpu.CompilerParams(vmem_limit_bytes=vmem_room(count)),
        cost_estimate=lasting(1.7),
    )(*held_in(pltpu.SMEM, scalars), *held_in(pltpu.VMEM, operands))
    return found[:4], found[4:]


def backward_kernel(slots, names, *refs):
    take, rest = taker(refs)
    prompt_len, resp_prompt, resp_len = take(3)
    cotangent = take(len(HELD))
    query, key, value, hq, hk = take(5)
    w_q, w_k, w_v, q_gain, k_gain, w_out = take(6)
    p_pre, p_own, heads_out, prefix_v = take(4)
    terms = take(len(rest) - len(names) - 4)
    parts = take(len(names))
    grad_prefix, dhq, dhk, dv = take(4)

    width = cotangent[0].shape[2]
    me = lax.axis_index("mp")
    grad_heads = 0.0
    for blocks, ref in zip(HELD, cotangent):
        for i, block in enumerate(blocks):
            grad_heads += dot_nt(ref[i], w_out[:, features(me ^ block, width)])
    grad_prefix[...] = jnp.zeros_like(grad_prefix)

    count = prefix_v.shape[0]
    window = window_rows(count)
    slot_len = query.shape[0] // slots
    size = q_gain.shape[1]
    kv_heads = key.shape[1] // size
    groups = query.shape[1] // key.shape[1]
    scale = size ** (-0.5)
    for n in range(slots):
        first, _ = prompt_span(prompt_len, resp_prompt[n])
        start = window_start(first, count)
        rows = slice(n * slot_len, (n + 1) * slot_len)
        live = lax.broadcasted_iota(jnp.int32, (slot_len, size), 0) < resp_len[n]
        for h in range(kv_heads):
            heads = range(h * groups, (h + 1) * groups)
            q = stacked(query, rows, heads, size)
            out = stacked(heads_out, rows, heads, size)
            g = jnp.concatenate(
                [
                    jnp.where(live, grad_heads[rows, a * size : (a + 1) * size], 0.0).astype(BF16)
                    for a in heads
                ],
                axis=0,
            )
            k_win = prefix_v[pl.ds(start, window), 2 * h * size : (2 * h + 1) * size]
            v_win = prefix_v[pl.ds(start, window), (2 * h + 1) * size : (2 * h + 2) * size]
            k_own = key[rows, h * size : (h + 1) * size]
            v_own = value[rows, h * size : (h + 1) * size]
            b_pre, b_own = p_pre[n, h], p_own[n, h]
            delta = jnp.sum(g.astype(F32) * out, axis=-1, keepdims=True)
            ds_pre = (b_pre.astype(F32) * (dot_nt(g, v_win) - delta)).astype(BF16)
            ds_own = (b_own.astype(F32) * (dot_nt(g, v_own) - delta)).astype(BF16)
            grad_q = scale * (dot(ds_pre, k_win) + dot(ds_own, k_own))
            for i, a in enumerate(heads):
                cols = slice(a * size, (a + 1) * size)
                one = grad_q[i * slot_len : (i + 1) * slot_len]
                dhq[rows, cols] = norm_back(hq[rows, cols], q_gain[...], one).astype(BF16)
            cols = slice(h * size, (h + 1) * size)
            grad_k = scale * dot_tn(ds_own, q)
            dhk[rows, cols] = norm_back(hk[rows, cols], k_gain[...], grad_k).astype(BF16)
            dv[rows, cols] = dot_tn(b_own, g).astype(BF16)
            k_cols = slice(2 * h * size, (2 * h + 1) * size)
            v_cols = slice((2 * h + 1) * size, (2 * h + 2) * size)
            grad_prefix[pl.ds(start, window), k_cols] += scale * dot_tn(ds_pre, q)
            grad_prefix[pl.ds(start, window), v_cols] += dot_tn(b_pre, g)
    chips = prefix_v.shape[0] // terms[0].shape[1] if len(terms) > 1 else 1
    for ref, steps in zip(terms, TERMS if len(terms) > 1 else ((0,),)):
        for i, step in enumerate(steps):
            ref[i] = grad_prefix[slot_rows(chips, ref.shape[1], step), :]

    def make(cols):
        return (
            dot_nt(dhq[...], w_q[cols, :])
            + dot_nt(dhk[...], w_k[cols, :])
            + dot_nt(dv[...], w_v[cols, :])
        ).astype(BF16)

    make_blocks(make, names, parts)


def backward(names, scalars, cotangent, kept, terms):
    slots = scalars[-1].shape[0]
    query, key, w_out, prefix = kept[0], kept[1], kept[10], kept[14]
    rows, q_width = query.shape
    k_width, depth = key.shape[1], w_out.shape[1]
    count, kv_width = prefix.shape
    results = [(x, F32) for x in terms] + block_shapes(names, rows, cotangent[0].shape[2])
    found = pl.pallas_call(
        functools.partial(backward_kernel, slots, names),
        in_specs=[SMEM] * 3 + [VMEM] * (len(cotangent) + len(kept)),
        out_specs=[VMEM] * len(results),
        out_shape=in_vmem(results),
        scratch_shapes=[
            pltpu.VMEM((count, kv_width), F32),
            pltpu.VMEM((rows, q_width), BF16),
            pltpu.VMEM((rows, k_width), BF16),
            pltpu.VMEM((rows, k_width), BF16),
        ],
        compiler_params=pltpu.CompilerParams(vmem_limit_bytes=vmem_room(count)),
        cost_estimate=lasting(3.5),
    )(*held_in(pltpu.SMEM, scalars), *held_in(pltpu.VMEM, [*cotangent, *kept]))
    return found[: len(terms)], found[len(terms) :]


def last_kernel(counts, *refs):
    take, rest = taker(refs)
    groups = [take(len(count)) for count in counts]
    results = take(len(counts))
    stage = take(len(counts))
    (sems,) = take(1)
    copies = Copies(sems)
    stores = []
    for count, group, result, ref in zip(counts, groups, results, stage):
        whole = 0.0
        for i, term in zip(count, group):
            whole = whole + term[i].astype(F32)
        ref[...] = whole.astype(BF16)
        stores.append(copies.start(ref, result))
    wait(stores)


def last_sums(groups):
    arrays = [array for group in groups for array, _ in group]
    shapes = [jax.ShapeDtypeStruct(group[0][0].shape[1:], BF16) for group in groups]
    return pl.pallas_call(
        functools.partial(last_kernel, [[i for _, i in group] for group in groups]),
        in_specs=[VMEM] * len(arrays),
        out_specs=[HBM] * len(groups),
        out_shape=shapes,
        scratch_shapes=in_vmem(like(shapes)) + [pltpu.SemaphoreType.DMA((len(groups),))],
        compiler_params=pltpu.CompilerParams(vmem_limit_bytes=vmem_room(0)),
        cost_estimate=lasting(0.9),
    )(*held_in(pltpu.VMEM, arrays))


def trade(name, block, axis, step):
    with jax.named_scope(name):
        return lax.ppermute(block, axis, [(i, i ^ step) for i in range(lax.axis_size(axis))])


def after(value, *others):
    return lax.optimization_barrier((value, *others))[0]


def total(*terms):
    whole = terms[0].astype(F32)
    for term in terms[1:]:
        whole = whole + term.astype(F32)
    return whole.astype(BF16)


def per_device(
    hidden_rows,
    w_query,
    w_key,
    w_value,
    w_out,
    q_gain,
    k_gain,
    prefix_kv,
    cotangent,
    prompt_len,
    resp_prompt,
    resp_len,
):
    chips = lax.axis_size("dp")
    scalars = (prompt_len, resp_prompt, resp_len)
    q_gain, k_gain = q_gain[None], k_gain[None]
    own = cotangent[None]
    far = trade("gather_far", own, "mp", 4)
    near = trade("gather_near", own, "mp", 2)
    if chips == 4:
        others = [trade("gather_prefix", prefix_kv, "dp", k) for k in range(1, chips)]
    else:
        prefix_kv, others = lax.all_gather(prefix_kv, "dp", axis=0, tiled=True), []
    far = after(far, *others)
    both = trade("gather_both", far, "mp", 2)
    far_x = trade("gather_far_x", far, "mp", 1)
    own_x = trade("gather_own_x", own, "mp", 1)
    near_x = trade("gather_near_x", near, "mp", 1)
    scalars, projected, weights, prefix, own = project(
        scalars, after(hidden_rows, far), w_query, w_key, w_value, q_gain, k_gain, w_out,
        prefix_kv, own,
    )
    both_x = trade("gather_both_x", after(both, projected[0], near_x), "mp", 1)
    probed, parts = forward(
        OUT, cotangent.shape[1], q_gain.shape[1], scalars, *projected[:3], weights[5],
        [prefix, *others],
    )
    back = [own, near, far, both, own_x, near_x, far_x, both_x]
    shape = prefix_kv.shape
    terms = [(1, *shape)] * (4 if chips == 4 else 1)
    terms, grads = backward(IN, scalars, back, [*projected, *weights, *probed], terms)

    out_a, out_b, kept_a, kept_b = parts
    got_a = trade("out_a", out_a, "mp", 2)
    got_b = trade("out_b", after(out_b, far_x), "mp", 2)
    out_a = total(kept_a, got_a)
    got_out = trade("out_mid", out_a, "mp", 4)
    in_7, in_5, in_31, in_6, in_4, in_2, in_0 = grads
    got_7 = trade("in_7", in_7, "mp", 1)
    in_6 = total(after(in_6, out_a), got_7)
    got_5 = trade("in_5", after(in_5, in_6), "mp", 1)
    got_6 = trade("in_6", in_6, "mp", 2)
    got_31 = trade("in_31", after(in_31, in_6), "mp", 1)
    in_4 = total(after(in_4, got_b, got_out), got_5, got_6)
    got_4 = trade("in_4", in_4, "mp", 4)
    in_2 = total(in_2, got_31[:1])
    got_2 = trade("in_2", in_2, "mp", 2)
    got_x = trade("out_x", total(after(kept_b, in_4)[1:], got_b[1:], got_out[1:]), "mp", 1)
    groups = [
        [(kept_b, 0), (got_b, 0), (got_out, 0), (got_x, 0)],
        [(in_0, 0), (got_31, 1), (got_2, 0), (got_4, 0)],
    ]
    if chips == 4:
        sent = after(tuple(terms[1:]), in_2)
        sums = [terms[0]] + [trade("grad_prefix", sent[k - 1], "dp", k) for k in range(1, chips)]
        groups.append([(term, 0) for term in sums])
        return last_sums(groups)
    grad_prefix = lax.psum_scatter(terms[0][0], "dp", scatter_dimension=0, tiled=True)
    return *last_sums(groups), grad_prefix.astype(BF16)


def solution(mesh):
    in_specs = (
        P("dp", None),
        P(None, "mp"),
        P(None, "mp"),
        P(None, "mp"),
        P("mp", None),
        P(),
        P(),
        P("dp", "mp"),
        P("dp", "mp"),
        P(),
        P("dp"),
        P("dp"),
    )
    out_specs = (P("dp", "mp"), P("dp", "mp"), P("dp", "mp"))
    return jax.shard_map(
        per_device, mesh=mesh, in_specs=in_specs, out_specs=out_specs, check_vma=False
    )
```

```python
import functools

import jax
import jax.numpy as jnp
from jax import lax
from jax.experimental import pallas as pl
from jax.experimental.pallas import tpu as pltpu
from jax.sharding import PartitionSpec as P

EPS = 1e-06
NEG = -1e30
ROWS = 16
HELD = ((0,), (2,), (4,), (6,), (1,), (3,), (5,), (7,))
OUT = ((6, 7), (2, 3), (4, 5), (0, 1))
TERMS = ((0,), (1,), (2,), (3,))
IN = ((7,), (5,), (3, 1), (6,), (4,), (2,), (0,))
F32 = jnp.float32
BF16 = jnp.bfloat16
HBM = pl.BlockSpec(memory_space=pltpu.HBM)
SMEM = pl.BlockSpec(memory_space=pltpu.SMEM)
VMEM = pl.BlockSpec(memory_space=pltpu.VMEM)


def dot(left, right):
    return jnp.dot(left, right, preferred_element_type=F32)


def dot_nt(left, right):
    return lax.dot_general(left, right, (((1,), (1,)), ((), ())), preferred_element_type=F32)


def dot_tn(left, right):
    return lax.dot_general(left, right, (((0,), (0,)), ((), ())), preferred_element_type=F32)


def inverse_root(hidden):
    return lax.rsqrt(jnp.mean(hidden * hidden, axis=-1, keepdims=True) + EPS)


def norm_back(hidden, gain, grad):
    root = inverse_root(hidden)
    unit = hidden * root
    scaled = grad * gain
    return root * (scaled - unit * jnp.mean(scaled * unit, axis=-1, keepdims=True))


class Copies:
    def __init__(self, sems):
        self.sems, self.count = sems, 0

    def start(self, source, target):
        copy = pltpu.make_async_copy(source, target, self.sems.at[self.count])
        self.count += 1
        copy.start()
        return copy


def wait(copies):
    for copy in copies:
        copy.wait()


def prompt_span(prompt_len, prompt):
    first, last = 0, 0
    end = 0
    for p in range(prompt_len.shape[0]):
        begin = end
        end = end + prompt_len[p]
        first = jnp.where(prompt == p, begin, first)
        last = jnp.where(prompt == p, end, last)
    return first, last


def window_rows(count):
    return min(count, count // 3 + ROWS)


def window_start(first, count):
    start = jnp.minimum(first // ROWS * ROWS, count - window_rows(count))
    return pl.multiple_of(start, ROWS)


def slot_rows(slots, rows, step):
    if slots == 1:
        return pl.ds(0, rows)
    return pl.ds(pl.multiple_of((lax.axis_index("dp") ^ step) * rows, ROWS), rows)


def features(block, width):
    return pl.ds(pl.multiple_of(block * width, width), width)


def stacked(ref, rows, heads, size):
    return jnp.concatenate([ref[rows, a * size : (a + 1) * size] for a in heads], axis=0)


def make_blocks(make, names, refs):
    me = lax.axis_index("mp")
    for blocks, ref in zip(names, refs):
        for i, block in enumerate(blocks):
            ref[i] = make(features(me ^ block, ref.shape[-1]))


def taker(refs):
    refs = list(refs)

    def take(count):
        found, refs[:count] = refs[:count], []
        return found

    return take, refs


def project_kernel(*refs):
    take, _ = taker(refs)
    scalars = take(3)
    hidden, w_q, w_k, w_v, q_gain, k_gain, w_out, prefix, own = take(9)
    scalars_v = take(3)
    query, key, value, hq, hk = take(5)
    wq_v, wk_v, wv_v, qg_v, kg_v, wo_v, prefix_v, own_v = take(8)
    hidden_v, sems = take(2)

    copies = Copies(sems)
    depth = hidden.shape[1]
    steps = 4
    part = depth // steps
    loads = []
    for i in range(steps):
        cut = pl.ds(i * part, part)
        loads.append(
            [copies.start(hidden.at[:, cut], hidden_v.at[:, cut])]
            + [
                copies.start(w.at[cut], v.at[cut])
                for w, v in ((w_q, wq_v), (w_k, wk_v), (w_v, wv_v))
            ]
        )
    small = [copies.start(q_gain, qg_v), copies.start(k_gain, kg_v)]
    small += [copies.start(source, target) for source, target in zip(scalars, scalars_v)]
    small += [copies.start(prefix, prefix_v), copies.start(w_out, wo_v), copies.start(own, own_v)]

    sums = [None] * 3
    for i, load in enumerate(loads):
        wait(load)
        rows = hidden_v[:, i * part : (i + 1) * part]
        for j, v in enumerate((wq_v, wk_v, wv_v)):
            term = dot(rows, v[i * part : (i + 1) * part])
            sums[j] = term if i == 0 else sums[j] + term
    hq[...], hk[...] = sums[0], sums[1]
    value[...] = sums[2].astype(BF16)
    wait(small)
    size = qg_v.shape[1]
    for whole, gain, out in ((sums[0], qg_v, query), (sums[1], kg_v, key)):
        for at in range(0, whole.shape[1], size):
            head = whole[:, at : at + size]
            out[:, at : at + size] = (head * inverse_root(head) * gain[...]).astype(BF16)


def project(scalars, hidden, w_q, w_k, w_v, q_gain, k_gain, w_out, prefix, own):
    rows, depth = hidden.shape
    q_width, k_width = w_q.shape[1], w_k.shape[1]
    weights = [w_q, w_k, w_v, q_gain, k_gain, w_out, prefix, own]
    operands = [*scalars, hidden, *weights]
    kept = [
        ((rows, q_width), BF16),
        ((rows, k_width), BF16),
        ((rows, k_width), BF16),
        ((rows, q_width), F32),
        ((rows, k_width), F32),
    ] + like(weights)
    found = pl.pallas_call(
        project_kernel,
        in_specs=[HBM] * len(operands),
        out_specs=[SMEM] * 3 + [VMEM] * len(kept),
        out_shape=[pltpu.SMEM(x.shape, jnp.int32) for x in scalars] + in_vmem(kept),
        scratch_shapes=[pltpu.VMEM(hidden.shape, hidden.dtype), pltpu.SemaphoreType.DMA((32,))],
        compiler_params=pltpu.CompilerParams(vmem_limit_bytes=vmem_room(prefix.shape[0])),
        cost_estimate=lasting(2.6),
    )(*held_in(pltpu.HBM, operands))
    return found[:3], found[3:8], found[8:14], found[14], found[15]


def forward_kernel(slots, names, *refs):
    take, rest = taker(refs)
    prompt_len, resp_prompt, resp_len = take(3)
    query, key, value, wo_v = take(4)
    prefix = take(len(rest) - 4 - len(names) - 1)
    p_pre, p_own, heads_out, prefix_v = take(4)
    parts = take(len(names))
    (out_bf,) = take(1)

    held = prefix[0].shape[0]
    for k, ref in enumerate(prefix):
        prefix_v[slot_rows(len(prefix), held, k), :] = ref[...]
    size = heads_out.shape[1] * p_own.shape[3] // p_own.shape[2] // p_own.shape[1]
    count = prefix_v.shape[0]
    window = window_rows(count)
    slot_len = query.shape[0] // slots
    kv_heads = key.shape[1] // size
    groups = query.shape[1] // key.shape[1]
    scale = size ** (-0.5)
    for n in range(slots):
        first, last = prompt_span(prompt_len, resp_prompt[n])
        start = window_start(first, count)
        rows = slice(n * slot_len, (n + 1) * slot_len)
        live = lax.broadcasted_iota(jnp.int32, (slot_len, size), 0) < resp_len[n]
        for h in range(kv_heads):
            heads = range(h * groups, (h + 1) * groups)
            q = stacked(query, rows, heads, size)
            k_win = prefix_v[pl.ds(start, window), 2 * h * size : (2 * h + 1) * size]
            v_win = prefix_v[pl.ds(start, window), (2 * h + 1) * size : (2 * h + 2) * size]
            k_own = key[rows, h * size : (h + 1) * size]
            v_own = value[rows, h * size : (h + 1) * size]
            tall = groups * slot_len
            place = start + lax.broadcasted_iota(jnp.int32, (tall, window), 1)
            s_pre = jnp.where((place >= first) & (place < last), dot_nt(q, k_win) * scale, NEG)
            token = lax.broadcasted_iota(jnp.int32, (groups, slot_len, slot_len), 1)
            token = token.reshape(tall, slot_len)
            other = lax.broadcasted_iota(jnp.int32, (tall, slot_len), 1)
            s_own = jnp.where(
                (other <= token) & (other < resp_len[n]), dot_nt(q, k_own) * scale, NEG
            )
            top = jnp.maximum(
                jnp.max(s_pre, axis=-1, keepdims=True), jnp.max(s_own, axis=-1, keepdims=True)
            )
            e_pre = jnp.exp(s_pre - top)
            e_own = jnp.exp(s_own - top)
            total = jnp.sum(e_pre, axis=-1, keepdims=True) + jnp.sum(e_own, axis=-1, keepdims=True)
            b_pre = (e_pre / total).astype(BF16)
            b_own = (e_own / total).astype(BF16)
            p_pre[n, h] = b_pre
            p_own[n, h] = b_own
            out = dot(b_pre, v_win) + dot(b_own, v_own)
            for i, a in enumerate(heads):
                one = out[i * slot_len : (i + 1) * slot_len]
                heads_out[rows, a * size : (a + 1) * size] = one
                out_bf[rows, a * size : (a + 1) * size] = jnp.where(live, one, 0.0).astype(BF16)

    def make(cols):
        return dot(out_bf[...], wo_v[:, cols]).astype(BF16)

    make_blocks(make, names, parts)


def block_shapes(names, rows, width):
    return [((len(blocks), rows, width), BF16) for blocks in names]


def in_vmem(shapes):
    return [pltpu.VMEM(*x) for x in shapes]


def held_in(space, arrays):
    return [pltpu.with_memory_space_constraint(x, space) for x in arrays]


def lasting(us):
    return pl.CostEstimate(flops=int(us * 1.15e9), bytes_accessed=0, transcendentals=0)


def like(arrays):
    return [(x.shape, x.dtype) for x in arrays]


def vmem_room(prefix_rows):
    return 48 << 20 if prefix_rows > 1024 else 24 << 20


def forward(names, width, size, scalars, query, key, value, w_out, prefix):
    slots = scalars[-1].shape[0]
    rows, q_width = query.shape
    k_width = key.shape[1]
    count = sum(x.shape[0] for x in prefix)
    window = window_rows(count)
    slot_len = rows // slots
    kv_heads, tall = k_width // size, slot_len * q_width // k_width
    results = [
        ((slots, kv_heads, tall, window), BF16),
        ((slots, kv_heads, tall, slot_len), BF16),
        ((rows, q_width), F32),
        ((count, prefix[0].shape[1]), BF16),
    ] + block_shapes(names, rows, width)
    operands = [query, key, value, w_out, *prefix]
    found = pl.pallas_call(
        functools.partial(forward_kernel, slots, names),
        in_specs=[SMEM] * 3 + [VMEM] * len(operands),
        out_specs=[VMEM] * len(results),
        out_shape=in_vmem(results),
        scratch_shapes=[pltpu.VMEM((rows, q_width), BF16)],
        compiler_params=pltpu.CompilerParams(vmem_limit_bytes=vmem_room(count)),
        cost_estimate=lasting(1.7),
    )(*held_in(pltpu.SMEM, scalars), *held_in(pltpu.VMEM, operands))
    return found[:4], found[4:]


def backward_kernel(slots, names, *refs):
    take, rest = taker(refs)
    prompt_len, resp_prompt, resp_len = take(3)
    cotangent = take(len(HELD))
    query, key, value, hq, hk = take(5)
    w_q, w_k, w_v, q_gain, k_gain, w_out = take(6)
    p_pre, p_own, heads_out, prefix_v = take(4)
    terms = take(len(rest) - len(names) - 4)
    parts = take(len(names))
    grad_prefix, dhq, dhk, dv = take(4)

    width = cotangent[0].shape[2]
    me = lax.axis_index("mp")
    grad_heads = 0.0
    for blocks, ref in zip(HELD, cotangent):
        for i, block in enumerate(blocks):
            grad_heads += dot_nt(ref[i], w_out[:, features(me ^ block, width)])
    grad_prefix[...] = jnp.zeros_like(grad_prefix)

    count = prefix_v.shape[0]
    window = window_rows(count)
    slot_len = query.shape[0] // slots
    size = q_gain.shape[1]
    kv_heads = key.shape[1] // size
    groups = query.shape[1] // key.shape[1]
    scale = size ** (-0.5)
    for n in range(slots):
        first, _ = prompt_span(prompt_len, resp_prompt[n])
        start = window_start(first, count)
        rows = slice(n * slot_len, (n + 1) * slot_len)
        live = lax.broadcasted_iota(jnp.int32, (slot_len, size), 0) < resp_len[n]
        for h in range(kv_heads):
            heads = range(h * groups, (h + 1) * groups)
            q = stacked(query, rows, heads, size)
            out = stacked(heads_out, rows, heads, size)
            g = jnp.concatenate(
                [
                    jnp.where(live, grad_heads[rows, a * size : (a + 1) * size], 0.0).astype(BF16)
                    for a in heads
                ],
                axis=0,
            )
            k_win = prefix_v[pl.ds(start, window), 2 * h * size : (2 * h + 1) * size]
            v_win = prefix_v[pl.ds(start, window), (2 * h + 1) * size : (2 * h + 2) * size]
            k_own = key[rows, h * size : (h + 1) * size]
            v_own = value[rows, h * size : (h + 1) * size]
            b_pre, b_own = p_pre[n, h], p_own[n, h]
            delta = jnp.sum(g.astype(F32) * out, axis=-1, keepdims=True)
            ds_pre = (b_pre.astype(F32) * (dot_nt(g, v_win) - delta)).astype(BF16)
            ds_own = (b_own.astype(F32) * (dot_nt(g, v_own) - delta)).astype(BF16)
            grad_q = scale * (dot(ds_pre, k_win) + dot(ds_own, k_own))
            for i, a in enumerate(heads):
                cols = slice(a * size, (a + 1) * size)
                one = grad_q[i * slot_len : (i + 1) * slot_len]
                dhq[rows, cols] = norm_back(hq[rows, cols], q_gain[...], one).astype(BF16)
            cols = slice(h * size, (h + 1) * size)
            grad_k = scale * dot_tn(ds_own, q)
            dhk[rows, cols] = norm_back(hk[rows, cols], k_gain[...], grad_k).astype(BF16)
            dv[rows, cols] = dot_tn(b_own, g).astype(BF16)
            k_cols = slice(2 * h * size, (2 * h + 1) * size)
            v_cols = slice((2 * h + 1) * size, (2 * h + 2) * size)
            grad_prefix[pl.ds(start, window), k_cols] += scale * dot_tn(ds_pre, q)
            grad_prefix[pl.ds(start, window), v_cols] += dot_tn(b_pre, g)
    chips = prefix_v.shape[0] // terms[0].shape[1] if len(terms) > 1 else 1
    for ref, steps in zip(terms, TERMS if len(terms) > 1 else ((0,),)):
        for i, step in enumerate(steps):
            ref[i] = grad_prefix[slot_rows(chips, ref.shape[1], step), :]

    def make(cols):
        return (
            dot_nt(dhq[...], w_q[cols, :])
            + dot_nt(dhk[...], w_k[cols, :])
            + dot_nt(dv[...], w_v[cols, :])
        ).astype(BF16)

    make_blocks(make, names, parts)


def backward(names, scalars, cotangent, kept, terms):
    slots = scalars[-1].shape[0]
    query, key, w_out, prefix = kept[0], kept[1], kept[10], kept[14]
    rows, q_width = query.shape
    k_width, depth = key.shape[1], w_out.shape[1]
    count, kv_width = prefix.shape
    results = [(x, F32) for x in terms] + block_shapes(names, rows, cotangent[0].shape[2])
    found = pl.pallas_call(
        functools.partial(backward_kernel, slots, names),
        in_specs=[SMEM] * 3 + [VMEM] * (len(cotangent) + len(kept)),
        out_specs=[VMEM] * len(results),
        out_shape=in_vmem(results),
        scratch_shapes=[
            pltpu.VMEM((count, kv_width), F32),
            pltpu.VMEM((rows, q_width), BF16),
            pltpu.VMEM((rows, k_width), BF16),
            pltpu.VMEM((rows, k_width), BF16),
        ],
        compiler_params=pltpu.CompilerParams(vmem_limit_bytes=vmem_room(count)),
        cost_estimate=lasting(3.5),
    )(*held_in(pltpu.SMEM, scalars), *held_in(pltpu.VMEM, [*cotangent, *kept]))
    return found[: len(terms)], found[len(terms) :]


def last_kernel(counts, *refs):
    take, rest = taker(refs)
    groups = [take(len(count)) for count in counts]
    results = take(len(counts))
    stage = take(len(counts))
    (sems,) = take(1)
    copies = Copies(sems)
    stores = []
    for count, group, result, ref in zip(counts, groups, results, stage):
        whole = 0.0
        for i, term in zip(count, group):
            whole = whole + term[i].astype(F32)
        ref[...] = whole.astype(BF16)
        stores.append(copies.start(ref, result))
    wait(stores)


def last_sums(groups):
    arrays = [array for group in groups for array, _ in group]
    shapes = [jax.ShapeDtypeStruct(group[0][0].shape[1:], BF16) for group in groups]
    return pl.pallas_call(
        functools.partial(last_kernel, [[i for _, i in group] for group in groups]),
        in_specs=[VMEM] * len(arrays),
        out_specs=[HBM] * len(groups),
        out_shape=shapes,
        scratch_shapes=in_vmem(like(shapes)) + [pltpu.SemaphoreType.DMA((len(groups),))],
        compiler_params=pltpu.CompilerParams(vmem_limit_bytes=vmem_room(0)),
        cost_estimate=lasting(0.9),
    )(*held_in(pltpu.VMEM, arrays))


def trade(name, block, axis, step):
    with jax.named_scope(name):
        return lax.ppermute(block, axis, [(i, i ^ step) for i in range(lax.axis_size(axis))])


def after(value, *others):
    return lax.optimization_barrier((value, *others))[0]


def total(*terms):
    whole = terms[0].astype(F32)
    for term in terms[1:]:
        whole = whole + term.astype(F32)
    return whole.astype(BF16)


def per_device(
    hidden_rows,
    w_query,
    w_key,
    w_value,
    w_out,
    q_gain,
    k_gain,
    prefix_kv,
    cotangent,
    prompt_len,
    resp_prompt,
    resp_len,
):
    chips = lax.axis_size("dp")
    scalars = (prompt_len, resp_prompt, resp_len)
    q_gain, k_gain = q_gain[None], k_gain[None]
    own = cotangent[None]
    far = trade("gather_far", own, "mp", 4)
    near = trade("gather_near", own, "mp", 2)
    if chips == 4:
        others = [trade("gather_prefix", prefix_kv, "dp", k) for k in range(1, chips)]
    else:
        prefix_kv, others = lax.all_gather(prefix_kv, "dp", axis=0, tiled=True), []
    far = after(far, *others)
    both = trade("gather_both", far, "mp", 2)
    far_x = trade("gather_far_x", far, "mp", 1)
    own_x = trade("gather_own_x", own, "mp", 1)
    near_x = trade("gather_near_x", near, "mp", 1)
    scalars, projected, weights, prefix, own = project(
        scalars, after(hidden_rows, far), w_query, w_key, w_value, q_gain, k_gain, w_out,
        prefix_kv, own,
    )
    both_x = trade("gather_both_x", after(both, projected[0]), "mp", 1)
    probed, parts = forward(
        OUT, cotangent.shape[1], q_gain.shape[1], scalars, *projected[:3], weights[5],
        [prefix, *others],
    )
    back = [own, near, far, both, own_x, near_x, far_x, both_x]
    shape = prefix_kv.shape
    terms = [(1, *shape)] * (4 if chips == 4 else 1)
    terms, grads = backward(IN, scalars, back, [*projected, *weights, *probed], terms)

    out_a, out_b, kept_a, kept_b = parts
    got_a = trade("out_a", out_a, "mp", 2)
    got_b = trade("out_b", after(out_b, far_x), "mp", 2)
    out_a = total(kept_a, got_a)
    got_out = trade("out_mid", out_a, "mp", 4)
    in_7, in_5, in_31, in_6, in_4, in_2, in_0 = grads
    got_7 = trade("in_7", in_7, "mp", 1)
    in_6 = total(after(in_6, out_a), got_7)
    got_5 = trade("in_5", after(in_5, in_6), "mp", 1)
    got_6 = trade("in_6", in_6, "mp", 2)
    got_31 = trade("in_31", after(in_31, in_6), "mp", 1)
    in_4 = total(after(in_4, got_b), got_5, got_6)
    got_4 = trade("in_4", in_4, "mp", 4)
    sums = list(terms)
    if chips == 4:
        sent = after(tuple(terms[1:]), in_4)
        sums[1:] = [trade("grad_prefix", sent[k - 1], "dp", k) for k in range(1, chips)]
    in_2 = total(after(in_2, *sums), got_31[:1])
    got_2 = trade("in_2", in_2, "mp", 2)
    got_x = trade("out_x", total(kept_b[1:], got_b[1:], got_out[1:]), "mp", 1)
    groups = [
        [(kept_b, 0), (got_b, 0), (got_out, 0), (got_x, 0)],
        [(in_0, 0), (got_31, 1), (got_2, 0), (got_4, 0)],
    ]
    if chips == 4:
        groups.append([(term, 0) for term in sums])
        return last_sums(groups)
    grad_prefix = lax.psum_scatter(terms[0][0], "dp", scatter_dimension=0, tiled=True)
    return *last_sums(groups), grad_prefix.astype(BF16)


def solution(mesh):
    in_specs = (
        P("dp", None),
        P(None, "mp"),
        P(None, "mp"),
        P(None, "mp"),
        P("mp", None),
        P(),
        P(),
        P("dp", "mp"),
        P("dp", "mp"),
        P(),
        P("dp"),
        P("dp"),
    )
    out_specs = (P("dp", "mp"), P("dp", "mp"), P("dp", "mp"))
    return jax.shard_map(
        per_device, mesh=mesh, in_specs=in_specs, out_specs=out_specs, check_vma=False
    )
```

```python
import functools

import jax
import jax.numpy as jnp
from jax import lax
from jax.experimental import pallas as pl
from jax.experimental.pallas import tpu as pltpu
from jax.sharding import PartitionSpec as P

EPS = 1e-06
NEG = -1e30
ROWS = 16
HELD = ((0,), (2,), (4,), (6,), (1,), (3,), (5,), (7,))
OUT = ((6, 7), (2, 3), (4, 5), (0, 1))
TERMS = ((1, 3), (0, 2))
IN = ((7,), (5,), (3, 1), (6,), (4,), (2,), (0,))
F32 = jnp.float32
BF16 = jnp.bfloat16
HBM = pl.BlockSpec(memory_space=pltpu.HBM)
SMEM = pl.BlockSpec(memory_space=pltpu.SMEM)
VMEM = pl.BlockSpec(memory_space=pltpu.VMEM)


def dot(left, right):
    return jnp.dot(left, right, preferred_element_type=F32)


def dot_nt(left, right):
    return lax.dot_general(left, right, (((1,), (1,)), ((), ())), preferred_element_type=F32)


def dot_tn(left, right):
    return lax.dot_general(left, right, (((0,), (0,)), ((), ())), preferred_element_type=F32)


def inverse_root(hidden):
    return lax.rsqrt(jnp.mean(hidden * hidden, axis=-1, keepdims=True) + EPS)


def norm_back(hidden, gain, grad):
    root = inverse_root(hidden)
    unit = hidden * root
    scaled = grad * gain
    return root * (scaled - unit * jnp.mean(scaled * unit, axis=-1, keepdims=True))


class Copies:
    def __init__(self, sems):
        self.sems, self.count = sems, 0

    def start(self, source, target):
        copy = pltpu.make_async_copy(source, target, self.sems.at[self.count])
        self.count += 1
        copy.start()
        return copy


def wait(copies):
    for copy in copies:
        copy.wait()


def prompt_span(prompt_len, prompt):
    first, last = 0, 0
    end = 0
    for p in range(prompt_len.shape[0]):
        begin = end
        end = end + prompt_len[p]
        first = jnp.where(prompt == p, begin, first)
        last = jnp.where(prompt == p, end, last)
    return first, last


def window_rows(count):
    return min(count, count // 3 + ROWS)


def window_start(first, count):
    start = jnp.minimum(first // ROWS * ROWS, count - window_rows(count))
    return pl.multiple_of(start, ROWS)


def slot_rows(slots, rows, step):
    if slots == 1:
        return pl.ds(0, rows)
    return pl.ds(pl.multiple_of((lax.axis_index("dp") ^ step) * rows, ROWS), rows)


def features(block, width):
    return pl.ds(pl.multiple_of(block * width, width), width)


def stacked(ref, rows, heads, size):
    return jnp.concatenate([ref[rows, a * size : (a + 1) * size] for a in heads], axis=0)


def make_blocks(make, names, refs):
    me = lax.axis_index("mp")
    for blocks, ref in zip(names, refs):
        for i, block in enumerate(blocks):
            ref[i] = make(features(me ^ block, ref.shape[-1]))


def taker(refs):
    refs = list(refs)

    def take(count):
        found, refs[:count] = refs[:count], []
        return found

    return take, refs


def project_kernel(*refs):
    take, _ = taker(refs)
    scalars = take(3)
    hidden, w_q, w_k, w_v, q_gain, k_gain, w_out, prefix, own = take(9)
    scalars_v = take(3)
    query, key, value, hq, hk = take(5)
    wq_v, wk_v, wv_v, qg_v, kg_v, wo_v, prefix_v, own_v = take(8)
    hidden_v, sems = take(2)

    copies = Copies(sems)
    depth = hidden.shape[1]
    steps = 4
    part = depth // steps
    loads = []
    for i in range(steps):
        cut = pl.ds(i * part, part)
        loads.append(
            [copies.start(hidden.at[:, cut], hidden_v.at[:, cut])]
            + [
                copies.start(w.at[cut], v.at[cut])
                for w, v in ((w_q, wq_v), (w_k, wk_v), (w_v, wv_v))
            ]
        )
    small = [copies.start(q_gain, qg_v), copies.start(k_gain, kg_v)]
    small += [copies.start(source, target) for source, target in zip(scalars, scalars_v)]
    small += [copies.start(prefix, prefix_v), copies.start(w_out, wo_v), copies.start(own, own_v)]

    sums = [None] * 3
    for i, load in enumerate(loads):
        wait(load)
        rows = hidden_v[:, i * part : (i + 1) * part]
        for j, v in enumerate((wq_v, wk_v, wv_v)):
            term = dot(rows, v[i * part : (i + 1) * part])
            sums[j] = term if i == 0 else sums[j] + term
    hq[...], hk[...] = sums[0], sums[1]
    value[...] = sums[2].astype(BF16)
    wait(small)
    size = qg_v.shape[1]
    for whole, gain, out in ((sums[0], qg_v, query), (sums[1], kg_v, key)):
        for at in range(0, whole.shape[1], size):
            head = whole[:, at : at + size]
            out[:, at : at + size] = (head * inverse_root(head) * gain[...]).astype(BF16)


def project(scalars, hidden, w_q, w_k, w_v, q_gain, k_gain, w_out, prefix, own):
    rows, depth = hidden.shape
    q_width, k_width = w_q.shape[1], w_k.shape[1]
    weights = [w_q, w_k, w_v, q_gain, k_gain, w_out, prefix, own]
    operands = [*scalars, hidden, *weights]
    kept = [
        ((rows, q_width), BF16),
        ((rows, k_width), BF16),
        ((rows, k_width), BF16),
        ((rows, q_width), F32),
        ((rows, k_width), F32),
    ] + like(weights)
    found = pl.pallas_call(
        project_kernel,
        in_specs=[HBM] * len(operands),
        out_specs=[SMEM] * 3 + [VMEM] * len(kept),
        out_shape=[pltpu.SMEM(x.shape, jnp.int32) for x in scalars] + in_vmem(kept),
        scratch_shapes=[pltpu.VMEM(hidden.shape, hidden.dtype), pltpu.SemaphoreType.DMA((32,))],
        compiler_params=pltpu.CompilerParams(vmem_limit_bytes=vmem_room(prefix.shape[0])),
        cost_estimate=lasting(2.6),
    )(*held_in(pltpu.HBM, operands))
    return found[:3], found[3:8], found[8:14], found[14], found[15]


def forward_kernel(slots, names, *refs):
    take, rest = taker(refs)
    prompt_len, resp_prompt, resp_len = take(3)
    query, key, value, wo_v = take(4)
    prefix = take(len(rest) - 4 - len(names) - 1)
    p_pre, p_own, heads_out, prefix_v = take(4)
    parts = take(len(names))
    (out_bf,) = take(1)

    held = prefix[0].shape[0]
    for k, ref in enumerate(prefix):
        prefix_v[slot_rows(len(prefix), held, k), :] = ref[...]
    size = heads_out.shape[1] * p_own.shape[3] // p_own.shape[2] // p_own.shape[1]
    count = prefix_v.shape[0]
    window = window_rows(count)
    slot_len = query.shape[0] // slots
    kv_heads = key.shape[1] // size
    groups = query.shape[1] // key.shape[1]
    scale = size ** (-0.5)
    for n in range(slots):
        first, last = prompt_span(prompt_len, resp_prompt[n])
        start = window_start(first, count)
        rows = slice(n * slot_len, (n + 1) * slot_len)
        live = lax.broadcasted_iota(jnp.int32, (slot_len, size), 0) < resp_len[n]
        for h in range(kv_heads):
            heads = range(h * groups, (h + 1) * groups)
            q = stacked(query, rows, heads, size)
            k_win = prefix_v[pl.ds(start, window), 2 * h * size : (2 * h + 1) * size]
            v_win = prefix_v[pl.ds(start, window), (2 * h + 1) * size : (2 * h + 2) * size]
            k_own = key[rows, h * size : (h + 1) * size]
            v_own = value[rows, h * size : (h + 1) * size]
            tall = groups * slot_len
            place = start + lax.broadcasted_iota(jnp.int32, (tall, window), 1)
            s_pre = jnp.where((place >= first) & (place < last), dot_nt(q, k_win) * scale, NEG)
            token = lax.broadcasted_iota(jnp.int32, (groups, slot_len, slot_len), 1)
            token = token.reshape(tall, slot_len)
            other = lax.broadcasted_iota(jnp.int32, (tall, slot_len), 1)
            s_own = jnp.where(
                (other <= token) & (other < resp_len[n]), dot_nt(q, k_own) * scale, NEG
            )
            top = jnp.maximum(
                jnp.max(s_pre, axis=-1, keepdims=True), jnp.max(s_own, axis=-1, keepdims=True)
            )
            e_pre = jnp.exp(s_pre - top)
            e_own = jnp.exp(s_own - top)
            total = jnp.sum(e_pre, axis=-1, keepdims=True) + jnp.sum(e_own, axis=-1, keepdims=True)
            b_pre = (e_pre / total).astype(BF16)
            b_own = (e_own / total).astype(BF16)
            p_pre[n, h] = b_pre
            p_own[n, h] = b_own
            out = dot(b_pre, v_win) + dot(b_own, v_own)
            for i, a in enumerate(heads):
                one = out[i * slot_len : (i + 1) * slot_len]
                heads_out[rows, a * size : (a + 1) * size] = one
                out_bf[rows, a * size : (a + 1) * size] = jnp.where(live, one, 0.0).astype(BF16)

    def make(cols):
        return dot(out_bf[...], wo_v[:, cols]).astype(BF16)

    make_blocks(make, names, parts)


def block_shapes(names, rows, width):
    return [((len(blocks), rows, width), BF16) for blocks in names]


def in_vmem(shapes):
    return [pltpu.VMEM(*x) for x in shapes]


def held_in(space, arrays):
    return [pltpu.with_memory_space_constraint(x, space) for x in arrays]


def lasting(us):
    return pl.CostEstimate(flops=int(us * 1.15e9), bytes_accessed=0, transcendentals=0)


def like(arrays):
    return [(x.shape, x.dtype) for x in arrays]


def vmem_room(prefix_rows):
    return 48 << 20 if prefix_rows > 1024 else 24 << 20


def forward(names, width, size, scalars, query, key, value, w_out, prefix):
    slots = scalars[-1].shape[0]
    rows, q_width = query.shape
    k_width = key.shape[1]
    count = sum(x.shape[0] for x in prefix)
    window = window_rows(count)
    slot_len = rows // slots
    kv_heads, tall = k_width // size, slot_len * q_width // k_width
    results = [
        ((slots, kv_heads, tall, window), BF16),
        ((slots, kv_heads, tall, slot_len), BF16),
        ((rows, q_width), F32),
        ((count, prefix[0].shape[1]), BF16),
    ] + block_shapes(names, rows, width)
    operands = [query, key, value, w_out, *prefix]
    found = pl.pallas_call(
        functools.partial(forward_kernel, slots, names),
        in_specs=[SMEM] * 3 + [VMEM] * len(operands),
        out_specs=[VMEM] * len(results),
        out_shape=in_vmem(results),
        scratch_shapes=[pltpu.VMEM((rows, q_width), BF16)],
        compiler_params=pltpu.CompilerParams(vmem_limit_bytes=vmem_room(count)),
        cost_estimate=lasting(1.7),
    )(*held_in(pltpu.SMEM, scalars), *held_in(pltpu.VMEM, operands))
    return found[:4], found[4:]


def backward_kernel(slots, names, *refs):
    take, rest = taker(refs)
    prompt_len, resp_prompt, resp_len = take(3)
    cotangent = take(len(HELD))
    query, key, value, hq, hk = take(5)
    w_q, w_k, w_v, q_gain, k_gain, w_out = take(6)
    p_pre, p_own, heads_out, prefix_v = take(4)
    terms = take(len(rest) - len(names) - 4)
    parts = take(len(names))
    grad_prefix, dhq, dhk, dv = take(4)

    width = cotangent[0].shape[2]
    me = lax.axis_index("mp")
    grad_heads = 0.0
    for blocks, ref in zip(HELD, cotangent):
        for i, block in enumerate(blocks):
            grad_heads += dot_nt(ref[i], w_out[:, features(me ^ block, width)])
    grad_prefix[...] = jnp.zeros_like(grad_prefix)

    count = prefix_v.shape[0]
    window = window_rows(count)
    slot_len = query.shape[0] // slots
    size = q_gain.shape[1]
    kv_heads = key.shape[1] // size
    groups = query.shape[1] // key.shape[1]
    scale = size ** (-0.5)
    for n in range(slots):
        first, _ = prompt_span(prompt_len, resp_prompt[n])
        start = window_start(first, count)
        rows = slice(n * slot_len, (n + 1) * slot_len)
        live = lax.broadcasted_iota(jnp.int32, (slot_len, size), 0) < resp_len[n]
        for h in range(kv_heads):
            heads = range(h * groups, (h + 1) * groups)
            q = stacked(query, rows, heads, size)
            out = stacked(heads_out, rows, heads, size)
            g = jnp.concatenate(
                [
                    jnp.where(live, grad_heads[rows, a * size : (a + 1) * size], 0.0).astype(BF16)
                    for a in heads
                ],
                axis=0,
            )
            k_win = prefix_v[pl.ds(start, window), 2 * h * size : (2 * h + 1) * size]
            v_win = prefix_v[pl.ds(start, window), (2 * h + 1) * size : (2 * h + 2) * size]
            k_own = key[rows, h * size : (h + 1) * size]
            v_own = value[rows, h * size : (h + 1) * size]
            b_pre, b_own = p_pre[n, h], p_own[n, h]
            delta = jnp.sum(g.astype(F32) * out, axis=-1, keepdims=True)
            ds_pre = (b_pre.astype(F32) * (dot_nt(g, v_win) - delta)).astype(BF16)
            ds_own = (b_own.astype(F32) * (dot_nt(g, v_own) - delta)).astype(BF16)
            grad_q = scale * (dot(ds_pre, k_win) + dot(ds_own, k_own))
            for i, a in enumerate(heads):
                cols = slice(a * size, (a + 1) * size)
                one = grad_q[i * slot_len : (i + 1) * slot_len]
                dhq[rows, cols] = norm_back(hq[rows, cols], q_gain[...], one).astype(BF16)
            cols = slice(h * size, (h + 1) * size)
            grad_k = scale * dot_tn(ds_own, q)
            dhk[rows, cols] = norm_back(hk[rows, cols], k_gain[...], grad_k).astype(BF16)
            dv[rows, cols] = dot_tn(b_own, g).astype(BF16)
            k_cols = slice(2 * h * size, (2 * h + 1) * size)
            v_cols = slice((2 * h + 1) * size, (2 * h + 2) * size)
            grad_prefix[pl.ds(start, window), k_cols] += scale * dot_tn(ds_pre, q)
            grad_prefix[pl.ds(start, window), v_cols] += dot_tn(b_pre, g)
    chips = prefix_v.shape[0] // terms[0].shape[1] if len(terms) > 1 else 1
    for ref, steps in zip(terms, TERMS if len(terms) > 1 else ((0,),)):
        for i, step in enumerate(steps):
            ref[i] = grad_prefix[slot_rows(chips, ref.shape[1], step), :]

    def make(cols):
        return (
            dot_nt(dhq[...], w_q[cols, :])
            + dot_nt(dhk[...], w_k[cols, :])
            + dot_nt(dv[...], w_v[cols, :])
        ).astype(BF16)

    make_blocks(make, names, parts)


def backward(names, scalars, cotangent, kept, terms):
    slots = scalars[-1].shape[0]
    query, key, w_out, prefix = kept[0], kept[1], kept[10], kept[14]
    rows, q_width = query.shape
    k_width, depth = key.shape[1], w_out.shape[1]
    count, kv_width = prefix.shape
    results = [(x, F32) for x in terms] + block_shapes(names, rows, cotangent[0].shape[2])
    found = pl.pallas_call(
        functools.partial(backward_kernel, slots, names),
        in_specs=[SMEM] * 3 + [VMEM] * (len(cotangent) + len(kept)),
        out_specs=[VMEM] * len(results),
        out_shape=in_vmem(results),
        scratch_shapes=[
            pltpu.VMEM((count, kv_width), F32),
            pltpu.VMEM((rows, q_width), BF16),
            pltpu.VMEM((rows, k_width), BF16),
            pltpu.VMEM((rows, k_width), BF16),
        ],
        compiler_params=pltpu.CompilerParams(vmem_limit_bytes=vmem_room(count)),
        cost_estimate=lasting(3.5),
    )(*held_in(pltpu.SMEM, scalars), *held_in(pltpu.VMEM, [*cotangent, *kept]))
    return found[: len(terms)], found[len(terms) :]


def last_kernel(counts, *refs):
    take, rest = taker(refs)
    groups = [take(len(count)) for count in counts]
    results = take(len(counts))
    stage = take(len(counts))
    (sems,) = take(1)
    copies = Copies(sems)
    stores = []
    for count, group, result, ref in zip(counts, groups, results, stage):
        whole = 0.0
        for i, term in zip(count, group):
            whole = whole + term[i].astype(F32)
        ref[...] = whole.astype(BF16)
        stores.append(copies.start(ref, result))
    wait(stores)


def last_sums(groups):
    arrays = [array for group in groups for array, _ in group]
    shapes = [jax.ShapeDtypeStruct(group[0][0].shape[1:], BF16) for group in groups]
    return pl.pallas_call(
        functools.partial(last_kernel, [[i for _, i in group] for group in groups]),
        in_specs=[VMEM] * len(arrays),
        out_specs=[HBM] * len(groups),
        out_shape=shapes,
        scratch_shapes=in_vmem(like(shapes)) + [pltpu.SemaphoreType.DMA((len(groups),))],
        compiler_params=pltpu.CompilerParams(vmem_limit_bytes=vmem_room(0)),
        cost_estimate=lasting(0.9),
    )(*held_in(pltpu.VMEM, arrays))


def trade(name, block, axis, step):
    with jax.named_scope(name):
        return lax.ppermute(block, axis, [(i, i ^ step) for i in range(lax.axis_size(axis))])


def after(value, *others):
    return lax.optimization_barrier((value, *others))[0]


def total(*terms):
    whole = terms[0].astype(F32)
    for term in terms[1:]:
        whole = whole + term.astype(F32)
    return whole.astype(BF16)


def per_device(
    hidden_rows,
    w_query,
    w_key,
    w_value,
    w_out,
    q_gain,
    k_gain,
    prefix_kv,
    cotangent,
    prompt_len,
    resp_prompt,
    resp_len,
):
    chips = lax.axis_size("dp")
    scalars = (prompt_len, resp_prompt, resp_len)
    q_gain, k_gain = q_gain[None], k_gain[None]
    own = cotangent[None]
    far = trade("gather_far", own, "mp", 4)
    near = trade("gather_near", own, "mp", 2)
    if chips == 4:
        others = [trade("gather_prefix", prefix_kv, "dp", k) for k in range(1, chips)]
    else:
        prefix_kv, others = lax.all_gather(prefix_kv, "dp", axis=0, tiled=True), []
    far = after(far, *others)
    both = trade("gather_both", far, "mp", 2)
    far_x = trade("gather_far_x", far, "mp", 1)
    own_x = trade("gather_own_x", own, "mp", 1)
    near_x = trade("gather_near_x", near, "mp", 1)
    scalars, projected, weights, prefix, own = project(
        scalars, after(hidden_rows, far), w_query, w_key, w_value, q_gain, k_gain, w_out,
        prefix_kv, own,
    )
    both_x = trade("gather_both_x", after(both, projected[0]), "mp", 1)
    probed, parts = forward(
        OUT, cotangent.shape[1], q_gain.shape[1], scalars, *projected[:3], weights[5],
        [prefix, *others],
    )
    back = [own, near, far, both, own_x, near_x, far_x, both_x]
    shape = prefix_kv.shape
    terms = [(1, *shape)] if chips != 4 else [(len(steps), *shape) for steps in TERMS]
    terms, grads = backward(IN, scalars, back, [*projected, *weights, *probed], terms)

    out_a, out_b, kept_a, kept_b = parts
    got_a = trade("out_a", out_a, "mp", 2)
    got_b = trade("out_b", after(out_b, far_x), "mp", 2)
    out_a = total(kept_a, got_a)
    got_out = trade("out_mid", out_a, "mp", 4)
    in_7, in_5, in_31, in_6, in_4, in_2, in_0 = grads
    got_7 = trade("in_7", in_7, "mp", 1)
    in_6 = total(after(in_6, out_a), got_7)
    got_5 = trade("in_5", after(in_5, in_6), "mp", 1)
    got_6 = trade("in_6", in_6, "mp", 2)
    got_31 = trade("in_31", after(in_31, in_6), "mp", 1)
    in_4 = total(after(in_4, got_b), got_5, got_6)
    got_4 = trade("in_4", in_4, "mp", 4)
    in_2 = total(in_2, got_31[:1])
    got_2 = trade("in_2", in_2, "mp", 2)
    got_x = trade("out_x", total(after(kept_b, in_4)[1:], got_b[1:], got_out[1:]), "mp", 1)
    groups = [
        [(kept_b, 0), (got_b, 0), (got_out, 0), (got_x, 0)],
        [(in_0, 0), (got_31, 1), (got_2, 0), (got_4, 0)],
    ]
    if chips == 4:
        got = trade("grad_prefix", after(terms[0], in_4), "dp", 1)
        sent = terms[1][1:] + got[1:]
        last = trade("grad_prefix", sent, "dp", 2)
        groups.append([(terms[1], 0), (got, 0), (last, 0)])
        return last_sums(groups)
    grad_prefix = lax.psum_scatter(terms[0][0], "dp", scatter_dimension=0, tiled=True)
    return *last_sums(groups), grad_prefix.astype(BF16)


def solution(mesh):
    in_specs = (
        P("dp", None),
        P(None, "mp"),
        P(None, "mp"),
        P(None, "mp"),
        P("mp", None),
        P(),
        P(),
        P("dp", "mp"),
        P("dp", "mp"),
        P(),
        P("dp"),
        P("dp"),
    )
    out_specs = (P("dp", "mp"), P("dp", "mp"), P("dp", "mp"))
    return jax.shard_map(
        per_device, mesh=mesh, in_specs=in_specs, out_specs=out_specs, check_vma=False
    )
```

```python
import functools

import jax
import jax.numpy as jnp
from jax import lax
from jax.experimental import pallas as pl
from jax.experimental.pallas import tpu as pltpu
from jax.sharding import PartitionSpec as P

EPS = 1e-06
NEG = -1e30
ROWS = 16
HELD = ((0,), (2,), (4,), (6,), (1,), (3,), (5,), (7,))
OUT = ((6, 7), (2, 3), (4, 5), (0, 1))
TERMS = ((1, 3), (0, 2))
IN = ((7,), (5,), (3, 1), (6,), (4,), (2,), (0,))
F32 = jnp.float32
BF16 = jnp.bfloat16
HBM = pl.BlockSpec(memory_space=pltpu.HBM)
SMEM = pl.BlockSpec(memory_space=pltpu.SMEM)
VMEM = pl.BlockSpec(memory_space=pltpu.VMEM)


def dot(left, right):
    return jnp.dot(left, right, preferred_element_type=F32)


def dot_nt(left, right):
    return lax.dot_general(left, right, (((1,), (1,)), ((), ())), preferred_element_type=F32)


def dot_tn(left, right):
    return lax.dot_general(left, right, (((0,), (0,)), ((), ())), preferred_element_type=F32)


def inverse_root(hidden):
    return lax.rsqrt(jnp.mean(hidden * hidden, axis=-1, keepdims=True) + EPS)


def norm_back(hidden, gain, grad):
    root = inverse_root(hidden)
    unit = hidden * root
    scaled = grad * gain
    return root * (scaled - unit * jnp.mean(scaled * unit, axis=-1, keepdims=True))


class Copies:
    def __init__(self, sems):
        self.sems, self.count = sems, 0

    def start(self, source, target):
        copy = pltpu.make_async_copy(source, target, self.sems.at[self.count])
        self.count += 1
        copy.start()
        return copy


def wait(copies):
    for copy in copies:
        copy.wait()


def prompt_span(prompt_len, prompt):
    first, last = 0, 0
    end = 0
    for p in range(prompt_len.shape[0]):
        begin = end
        end = end + prompt_len[p]
        first = jnp.where(prompt == p, begin, first)
        last = jnp.where(prompt == p, end, last)
    return first, last


def window_rows(count):
    return min(count, count // 3 + ROWS)


def window_start(first, count):
    start = jnp.minimum(first // ROWS * ROWS, count - window_rows(count))
    return pl.multiple_of(start, ROWS)


def slot_rows(slots, rows, step):
    if slots == 1:
        return pl.ds(0, rows)
    return pl.ds(pl.multiple_of((lax.axis_index("dp") ^ step) * rows, ROWS), rows)


def features(block, width):
    return pl.ds(pl.multiple_of(block * width, width), width)


def stacked(ref, rows, heads, size):
    return jnp.concatenate([ref[rows, a * size : (a + 1) * size] for a in heads], axis=0)


def make_blocks(make, names, refs):
    me = lax.axis_index("mp")
    for blocks, ref in zip(names, refs):
        for i, block in enumerate(blocks):
            ref[i] = make(features(me ^ block, ref.shape[-1]))


def taker(refs):
    refs = list(refs)

    def take(count):
        found, refs[:count] = refs[:count], []
        return found

    return take, refs


def project_kernel(*refs):
    take, _ = taker(refs)
    scalars = take(3)
    hidden, w_q, w_k, w_v, q_gain, k_gain, w_out, prefix, own = take(9)
    scalars_v = take(3)
    query, key, value, hq, hk = take(5)
    wq_v, wk_v, wv_v, qg_v, kg_v, wo_v, prefix_v, own_v = take(8)
    hidden_v, sems = take(2)

    copies = Copies(sems)
    depth = hidden.shape[1]
    steps = 4
    part = depth // steps
    loads = []
    for i in range(steps):
        cut = pl.ds(i * part, part)
        loads.append(
            [copies.start(hidden.at[:, cut], hidden_v.at[:, cut])]
            + [
                copies.start(w.at[cut], v.at[cut])
                for w, v in ((w_q, wq_v), (w_k, wk_v), (w_v, wv_v))
            ]
        )
    small = [copies.start(q_gain, qg_v), copies.start(k_gain, kg_v)]
    small += [copies.start(source, target) for source, target in zip(scalars, scalars_v)]
    small += [copies.start(prefix, prefix_v), copies.start(w_out, wo_v), copies.start(own, own_v)]

    sums = [None] * 3
    for i, load in enumerate(loads):
        wait(load)
        rows = hidden_v[:, i * part : (i + 1) * part]
        for j, v in enumerate((wq_v, wk_v, wv_v)):
            term = dot(rows, v[i * part : (i + 1) * part])
            sums[j] = term if i == 0 else sums[j] + term
    hq[...], hk[...] = sums[0], sums[1]
    value[...] = sums[2].astype(BF16)
    wait(small)
    size = qg_v.shape[1]
    for whole, gain, out in ((sums[0], qg_v, query), (sums[1], kg_v, key)):
        for at in range(0, whole.shape[1], size):
            head = whole[:, at : at + size]
            out[:, at : at + size] = (head * inverse_root(head) * gain[...]).astype(BF16)


def project(scalars, hidden, w_q, w_k, w_v, q_gain, k_gain, w_out, prefix, own):
    rows, depth = hidden.shape
    q_width, k_width = w_q.shape[1], w_k.shape[1]
    weights = [w_q, w_k, w_v, q_gain, k_gain, w_out, prefix, own]
    operands = [*scalars, hidden, *weights]
    kept = [
        ((rows, q_width), BF16),
        ((rows, k_width), BF16),
        ((rows, k_width), BF16),
        ((rows, q_width), F32),
        ((rows, k_width), F32),
    ] + like(weights)
    found = pl.pallas_call(
        project_kernel,
        in_specs=[HBM] * len(operands),
        out_specs=[SMEM] * 3 + [VMEM] * len(kept),
        out_shape=[pltpu.SMEM(x.shape, jnp.int32) for x in scalars] + in_vmem(kept),
        scratch_shapes=[pltpu.VMEM(hidden.shape, hidden.dtype), pltpu.SemaphoreType.DMA((32,))],
        compiler_params=pltpu.CompilerParams(vmem_limit_bytes=vmem_room(prefix.shape[0])),
        cost_estimate=lasting(2.6),
    )(*held_in(pltpu.HBM, operands))
    return found[:3], found[3:8], found[8:14], found[14], found[15]


def forward_kernel(slots, names, *refs):
    take, rest = taker(refs)
    prompt_len, resp_prompt, resp_len = take(3)
    query, key, value, wo_v = take(4)
    prefix = take(len(rest) - 4 - len(names) - 1)
    p_pre, p_own, heads_out, prefix_v = take(4)
    parts = take(len(names))
    (out_bf,) = take(1)

    held = prefix[0].shape[0]
    for k, ref in enumerate(prefix):
        prefix_v[slot_rows(len(prefix), held, k), :] = ref[...]
    size = heads_out.shape[1] * p_own.shape[3] // p_own.shape[2] // p_own.shape[1]
    count = prefix_v.shape[0]
    window = window_rows(count)
    slot_len = query.shape[0] // slots
    kv_heads = key.shape[1] // size
    groups = query.shape[1] // key.shape[1]
    scale = size ** (-0.5)
    for n in range(slots):
        first, last = prompt_span(prompt_len, resp_prompt[n])
        start = window_start(first, count)
        rows = slice(n * slot_len, (n + 1) * slot_len)
        live = lax.broadcasted_iota(jnp.int32, (slot_len, size), 0) < resp_len[n]
        for h in range(kv_heads):
            heads = range(h * groups, (h + 1) * groups)
            q = stacked(query, rows, heads, size)
            k_win = prefix_v[pl.ds(start, window), 2 * h * size : (2 * h + 1) * size]
            v_win = prefix_v[pl.ds(start, window), (2 * h + 1) * size : (2 * h + 2) * size]
            k_own = key[rows, h * size : (h + 1) * size]
            v_own = value[rows, h * size : (h + 1) * size]
            tall = groups * slot_len
            place = start + lax.broadcasted_iota(jnp.int32, (tall, window), 1)
            s_pre = jnp.where((place >= first) & (place < last), dot_nt(q, k_win) * scale, NEG)
            token = lax.broadcasted_iota(jnp.int32, (groups, slot_len, slot_len), 1)
            token = token.reshape(tall, slot_len)
            other = lax.broadcasted_iota(jnp.int32, (tall, slot_len), 1)
            s_own = jnp.where(
                (other <= token) & (other < resp_len[n]), dot_nt(q, k_own) * scale, NEG
            )
            top = jnp.maximum(
                jnp.max(s_pre, axis=-1, keepdims=True), jnp.max(s_own, axis=-1, keepdims=True)
            )
            e_pre = jnp.exp(s_pre - top)
            e_own = jnp.exp(s_own - top)
            total = jnp.sum(e_pre, axis=-1, keepdims=True) + jnp.sum(e_own, axis=-1, keepdims=True)
            b_pre = (e_pre / total).astype(BF16)
            b_own = (e_own / total).astype(BF16)
            p_pre[n, h] = b_pre
            p_own[n, h] = b_own
            out = dot(b_pre, v_win) + dot(b_own, v_own)
            for i, a in enumerate(heads):
                one = out[i * slot_len : (i + 1) * slot_len]
                heads_out[rows, a * size : (a + 1) * size] = one
                out_bf[rows, a * size : (a + 1) * size] = jnp.where(live, one, 0.0).astype(BF16)

    def make(cols):
        return dot(out_bf[...], wo_v[:, cols]).astype(BF16)

    make_blocks(make, names, parts)


def block_shapes(names, rows, width):
    return [((len(blocks), rows, width), BF16) for blocks in names]


def in_vmem(shapes):
    return [pltpu.VMEM(*x) for x in shapes]


def held_in(space, arrays):
    return [pltpu.with_memory_space_constraint(x, space) for x in arrays]


def lasting(us):
    return pl.CostEstimate(flops=int(us * 1.15e9), bytes_accessed=0, transcendentals=0)


def like(arrays):
    return [(x.shape, x.dtype) for x in arrays]


def vmem_room(prefix_rows):
    return 48 << 20 if prefix_rows > 1024 else 24 << 20


def forward(names, width, size, scalars, query, key, value, w_out, prefix):
    slots = scalars[-1].shape[0]
    rows, q_width = query.shape
    k_width = key.shape[1]
    count = sum(x.shape[0] for x in prefix)
    window = window_rows(count)
    slot_len = rows // slots
    kv_heads, tall = k_width // size, slot_len * q_width // k_width
    results = [
        ((slots, kv_heads, tall, window), BF16),
        ((slots, kv_heads, tall, slot_len), BF16),
        ((rows, q_width), F32),
        ((count, prefix[0].shape[1]), BF16),
    ] + block_shapes(names, rows, width)
    operands = [query, key, value, w_out, *prefix]
    found = pl.pallas_call(
        functools.partial(forward_kernel, slots, names),
        in_specs=[SMEM] * 3 + [VMEM] * len(operands),
        out_specs=[VMEM] * len(results),
        out_shape=in_vmem(results),
        scratch_shapes=[pltpu.VMEM((rows, q_width), BF16)],
        compiler_params=pltpu.CompilerParams(vmem_limit_bytes=vmem_room(count)),
        cost_estimate=lasting(1.7),
    )(*held_in(pltpu.SMEM, scalars), *held_in(pltpu.VMEM, operands))
    return found[:4], found[4:]


def backward_kernel(slots, names, *refs):
    take, rest = taker(refs)
    prompt_len, resp_prompt, resp_len = take(3)
    cotangent = take(len(HELD))
    query, key, value, hq, hk = take(5)
    w_q, w_k, w_v, q_gain, k_gain, w_out = take(6)
    p_pre, p_own, heads_out, prefix_v = take(4)
    terms = take(len(rest) - len(names) - 4)
    parts = take(len(names))
    grad_prefix, dhq, dhk, dv = take(4)

    width = cotangent[0].shape[2]
    me = lax.axis_index("mp")
    grad_heads = 0.0
    for blocks, ref in zip(HELD, cotangent):
        for i, block in enumerate(blocks):
            grad_heads += dot_nt(ref[i], w_out[:, features(me ^ block, width)])
    grad_prefix[...] = jnp.zeros_like(grad_prefix)

    count = prefix_v.shape[0]
    window = window_rows(count)
    slot_len = query.shape[0] // slots
    size = q_gain.shape[1]
    kv_heads = key.shape[1] // size
    groups = query.shape[1] // key.shape[1]
    scale = size ** (-0.5)
    for n in range(slots):
        first, _ = prompt_span(prompt_len, resp_prompt[n])
        start = window_start(first, count)
        rows = slice(n * slot_len, (n + 1) * slot_len)
        live = lax.broadcasted_iota(jnp.int32, (slot_len, size), 0) < resp_len[n]
        for h in range(kv_heads):
            heads = range(h * groups, (h + 1) * groups)
            q = stacked(query, rows, heads, size)
            out = stacked(heads_out, rows, heads, size)
            g = jnp.concatenate(
                [
                    jnp.where(live, grad_heads[rows, a * size : (a + 1) * size], 0.0).astype(BF16)
                    for a in heads
                ],
                axis=0,
            )
            k_win = prefix_v[pl.ds(start, window), 2 * h * size : (2 * h + 1) * size]
            v_win = prefix_v[pl.ds(start, window), (2 * h + 1) * size : (2 * h + 2) * size]
            k_own = key[rows, h * size : (h + 1) * size]
            v_own = value[rows, h * size : (h + 1) * size]
            b_pre, b_own = p_pre[n, h], p_own[n, h]
            delta = jnp.sum(g.astype(F32) * out, axis=-1, keepdims=True)
            ds_pre = (b_pre.astype(F32) * (dot_nt(g, v_win) - delta)).astype(BF16)
            ds_own = (b_own.astype(F32) * (dot_nt(g, v_own) - delta)).astype(BF16)
            grad_q = scale * (dot(ds_pre, k_win) + dot(ds_own, k_own))
            for i, a in enumerate(heads):
                cols = slice(a * size, (a + 1) * size)
                one = grad_q[i * slot_len : (i + 1) * slot_len]
                dhq[rows, cols] = norm_back(hq[rows, cols], q_gain[...], one).astype(BF16)
            cols = slice(h * size, (h + 1) * size)
            grad_k = scale * dot_tn(ds_own, q)
            dhk[rows, cols] = norm_back(hk[rows, cols], k_gain[...], grad_k).astype(BF16)
            dv[rows, cols] = dot_tn(b_own, g).astype(BF16)
            k_cols = slice(2 * h * size, (2 * h + 1) * size)
            v_cols = slice((2 * h + 1) * size, (2 * h + 2) * size)
            grad_prefix[pl.ds(start, window), k_cols] += scale * dot_tn(ds_pre, q)
            grad_prefix[pl.ds(start, window), v_cols] += dot_tn(b_pre, g)
    chips = prefix_v.shape[0] // terms[0].shape[1] if len(terms) > 1 else 1
    for ref, steps in zip(terms, TERMS if len(terms) > 1 else ((0,),)):
        for i, step in enumerate(steps):
            ref[i] = grad_prefix[slot_rows(chips, ref.shape[1], step), :]

    def make(cols):
        return (
            dot_nt(dhq[...], w_q[cols, :])
            + dot_nt(dhk[...], w_k[cols, :])
            + dot_nt(dv[...], w_v[cols, :])
        ).astype(BF16)

    make_blocks(make, names, parts)


def backward(names, scalars, cotangent, kept, terms):
    slots = scalars[-1].shape[0]
    query, key, w_out, prefix = kept[0], kept[1], kept[10], kept[14]
    rows, q_width = query.shape
    k_width, depth = key.shape[1], w_out.shape[1]
    count, kv_width = prefix.shape
    results = [(x, F32) for x in terms] + block_shapes(names, rows, cotangent[0].shape[2])
    found = pl.pallas_call(
        functools.partial(backward_kernel, slots, names),
        in_specs=[SMEM] * 3 + [VMEM] * (len(cotangent) + len(kept)),
        out_specs=[VMEM] * len(results),
        out_shape=in_vmem(results),
        scratch_shapes=[
            pltpu.VMEM((count, kv_width), F32),
            pltpu.VMEM((rows, q_width), BF16),
            pltpu.VMEM((rows, k_width), BF16),
            pltpu.VMEM((rows, k_width), BF16),
        ],
        compiler_params=pltpu.CompilerParams(vmem_limit_bytes=vmem_room(count)),
        cost_estimate=lasting(3.5),
    )(*held_in(pltpu.SMEM, scalars), *held_in(pltpu.VMEM, [*cotangent, *kept]))
    return found[: len(terms)], found[len(terms) :]


def last_kernel(counts, *refs):
    take, rest = taker(refs)
    groups = [take(len(count)) for count in counts]
    results = take(len(counts))
    stage = take(len(counts))
    (sems,) = take(1)
    copies = Copies(sems)
    stores = []
    for count, group, result, ref in zip(counts, groups, results, stage):
        whole = 0.0
        for i, term in zip(count, group):
            whole = whole + term[i].astype(F32)
        ref[...] = whole.astype(BF16)
        stores.append(copies.start(ref, result))
    wait(stores)


def last_sums(groups):
    arrays = [array for group in groups for array, _ in group]
    shapes = [jax.ShapeDtypeStruct(group[0][0].shape[1:], BF16) for group in groups]
    return pl.pallas_call(
        functools.partial(last_kernel, [[i for _, i in group] for group in groups]),
        in_specs=[VMEM] * len(arrays),
        out_specs=[HBM] * len(groups),
        out_shape=shapes,
        scratch_shapes=in_vmem(like(shapes)) + [pltpu.SemaphoreType.DMA((len(groups),))],
        compiler_params=pltpu.CompilerParams(vmem_limit_bytes=vmem_room(0)),
        cost_estimate=lasting(0.9),
    )(*held_in(pltpu.VMEM, arrays))


def trade(name, block, axis, step):
    with jax.named_scope(name):
        return lax.ppermute(block, axis, [(i, i ^ step) for i in range(lax.axis_size(axis))])


def after(value, *others):
    return lax.optimization_barrier((value, *others))[0]


def total(*terms):
    whole = terms[0].astype(F32)
    for term in terms[1:]:
        whole = whole + term.astype(F32)
    return whole.astype(BF16)


def per_device(
    hidden_rows,
    w_query,
    w_key,
    w_value,
    w_out,
    q_gain,
    k_gain,
    prefix_kv,
    cotangent,
    prompt_len,
    resp_prompt,
    resp_len,
):
    chips = lax.axis_size("dp")
    scalars = (prompt_len, resp_prompt, resp_len)
    q_gain, k_gain = q_gain[None], k_gain[None]
    own = cotangent[None]
    far = trade("gather_far", own, "mp", 4)
    near = trade("gather_near", own, "mp", 2)
    if chips == 4:
        others = [trade("gather_prefix", prefix_kv, "dp", k) for k in range(1, chips)]
    else:
        prefix_kv, others = lax.all_gather(prefix_kv, "dp", axis=0, tiled=True), []
    far = after(far, *others)
    both = trade("gather_both", far, "mp", 2)
    far_x = trade("gather_far_x", far, "mp", 1)
    own_x = trade("gather_own_x", own, "mp", 1)
    near_x = trade("gather_near_x", near, "mp", 1)
    scalars, projected, weights, prefix, own = project(
        scalars, after(hidden_rows, far), w_query, w_key, w_value, q_gain, k_gain, w_out,
        prefix_kv, own,
    )
    both_x = trade("gather_both_x", after(both, projected[0]), "mp", 1)
    probed, parts = forward(
        OUT, cotangent.shape[1], q_gain.shape[1], scalars, *projected[:3], weights[5],
        [prefix, *others],
    )
    back = [own, near, far, both, own_x, near_x, far_x, both_x]
    shape = prefix_kv.shape
    terms = [(1, *shape)] if chips != 4 else [(len(steps), *shape) for steps in TERMS]
    terms, grads = backward(IN, scalars, back, [*projected, *weights, *probed], terms)

    out_a, out_b, kept_a, kept_b = parts
    got_a = trade("out_a", out_a, "mp", 2)
    got_b = trade("out_b", after(out_b, far_x), "mp", 2)
    out_a = total(kept_a, got_a)
    got_out = trade("out_mid", out_a, "mp", 4)
    in_7, in_5, in_31, in_6, in_4, in_2, in_0 = grads
    got_7 = trade("in_7", in_7, "mp", 1)
    in_6 = total(after(in_6, out_a), got_7)
    got_5 = trade("in_5", after(in_5, in_6), "mp", 1)
    got_6 = trade("in_6", in_6, "mp", 2)
    got_31 = trade("in_31", after(in_31, in_6), "mp", 1)
    in_4 = total(after(in_4, got_b, got_out), got_5, got_6)
    got_4 = trade("in_4", in_4, "mp", 4)
    in_2 = total(in_2, got_31[:1])
    got_2 = trade("in_2", in_2, "mp", 2)
    got_x = trade("out_x", total(after(kept_b, in_4)[1:], got_b[1:], got_out[1:]), "mp", 1)
    groups = [
        [(kept_b, 0), (got_b, 0), (got_out, 0), (got_x, 0)],
        [(in_0, 0), (got_31, 1), (got_2, 0), (got_4, 0)],
    ]
    if chips == 4:
        got = trade("grad_prefix", after(terms[0], in_4), "dp", 1)
        sent = terms[1][1:] + got[1:]
        last = trade("grad_prefix", sent, "dp", 2)
        groups.append([(terms[1], 0), (got, 0), (last, 0)])
        return last_sums(groups)
    grad_prefix = lax.psum_scatter(terms[0][0], "dp", scatter_dimension=0, tiled=True)
    return *last_sums(groups), grad_prefix.astype(BF16)


def solution(mesh):
    in_specs = (
        P("dp", None),
        P(None, "mp"),
        P(None, "mp"),
        P(None, "mp"),
        P("mp", None),
        P(),
        P(),
        P("dp", "mp"),
        P("dp", "mp"),
        P(),
        P("dp"),
        P("dp"),
    )
    out_specs = (P("dp", "mp"), P("dp", "mp"), P("dp", "mp"))
    return jax.shard_map(
        per_device, mesh=mesh, in_specs=in_specs, out_specs=out_specs, check_vma=False
    )
```

```python
import functools

import jax
import jax.numpy as jnp
from jax import lax
from jax.experimental import pallas as pl
from jax.experimental.pallas import tpu as pltpu
from jax.sharding import PartitionSpec as P

EPS = 1e-06
NEG = -1e30
ROWS = 16
HELD = ((0,), (4, 2), (6,), (1,), (5, 3), (7,))
OUT = ((6, 7), (2, 3), (4, 5), (0, 1))
TERMS = ((1, 3), (0, 2))
IN = ((7,), (5,), (3, 1), (6,), (4,), (2,), (0,))
F32 = jnp.float32
BF16 = jnp.bfloat16
HBM = pl.BlockSpec(memory_space=pltpu.HBM)
SMEM = pl.BlockSpec(memory_space=pltpu.SMEM)
VMEM = pl.BlockSpec(memory_space=pltpu.VMEM)


def dot(left, right):
    return jnp.dot(left, right, preferred_element_type=F32)


def dot_nt(left, right):
    return lax.dot_general(left, right, (((1,), (1,)), ((), ())), preferred_element_type=F32)


def dot_tn(left, right):
    return lax.dot_general(left, right, (((0,), (0,)), ((), ())), preferred_element_type=F32)


def inverse_root(hidden):
    return lax.rsqrt(jnp.mean(hidden * hidden, axis=-1, keepdims=True) + EPS)


def norm_back(hidden, gain, grad):
    root = inverse_root(hidden)
    unit = hidden * root
    scaled = grad * gain
    return root * (scaled - unit * jnp.mean(scaled * unit, axis=-1, keepdims=True))


class Copies:
    def __init__(self, sems):
        self.sems, self.count = sems, 0

    def start(self, source, target):
        copy = pltpu.make_async_copy(source, target, self.sems.at[self.count])
        self.count += 1
        copy.start()
        return copy


def wait(copies):
    for copy in copies:
        copy.wait()


def prompt_span(prompt_len, prompt):
    first, last = 0, 0
    end = 0
    for p in range(prompt_len.shape[0]):
        begin = end
        end = end + prompt_len[p]
        first = jnp.where(prompt == p, begin, first)
        last = jnp.where(prompt == p, end, last)
    return first, last


def window_rows(count):
    return min(count, count // 3 + ROWS)


def window_start(first, count):
    start = jnp.minimum(first // ROWS * ROWS, count - window_rows(count))
    return pl.multiple_of(start, ROWS)


def slot_rows(slots, rows, step):
    if slots == 1:
        return pl.ds(0, rows)
    return pl.ds(pl.multiple_of((lax.axis_index("dp") ^ step) * rows, ROWS), rows)


def features(block, width):
    return pl.ds(pl.multiple_of(block * width, width), width)


def stacked(ref, rows, heads, size):
    return jnp.concatenate([ref[rows, a * size : (a + 1) * size] for a in heads], axis=0)


def make_blocks(make, names, refs):
    me = lax.axis_index("mp")
    for blocks, ref in zip(names, refs):
        for i, block in enumerate(blocks):
            ref[i] = make(features(me ^ block, ref.shape[-1]))


def taker(refs):
    refs = list(refs)

    def take(count):
        found, refs[:count] = refs[:count], []
        return found

    return take, refs


def project_kernel(*refs):
    take, _ = taker(refs)
    scalars = take(3)
    hidden, w_q, w_k, w_v, q_gain, k_gain, w_out, prefix, own = take(9)
    scalars_v = take(3)
    query, key, value, hq, hk = take(5)
    wq_v, wk_v, wv_v, qg_v, kg_v, wo_v, prefix_v, own_v = take(8)
    hidden_v, sems = take(2)

    copies = Copies(sems)
    depth = hidden.shape[1]
    steps = 4
    part = depth // steps
    loads = []
    for i in range(steps):
        cut = pl.ds(i * part, part)
        loads.append(
            [copies.start(hidden.at[:, cut], hidden_v.at[:, cut])]
            + [
                copies.start(w.at[cut], v.at[cut])
                for w, v in ((w_q, wq_v), (w_k, wk_v), (w_v, wv_v))
            ]
        )
    small = [copies.start(q_gain, qg_v), copies.start(k_gain, kg_v)]
    small += [copies.start(source, target) for source, target in zip(scalars, scalars_v)]
    small += [copies.start(prefix, prefix_v), copies.start(w_out, wo_v), copies.start(own, own_v)]

    sums = [None] * 3
    for i, load in enumerate(loads):
        wait(load)
        rows = hidden_v[:, i * part : (i + 1) * part]
        for j, v in enumerate((wq_v, wk_v, wv_v)):
            term = dot(rows, v[i * part : (i + 1) * part])
            sums[j] = term if i == 0 else sums[j] + term
    hq[...], hk[...] = sums[0], sums[1]
    value[...] = sums[2].astype(BF16)
    wait(small)
    size = qg_v.shape[1]
    for whole, gain, out in ((sums[0], qg_v, query), (sums[1], kg_v, key)):
        for at in range(0, whole.shape[1], size):
            head = whole[:, at : at + size]
            out[:, at : at + size] = (head * inverse_root(head) * gain[...]).astype(BF16)


def project(scalars, hidden, w_q, w_k, w_v, q_gain, k_gain, w_out, prefix, own):
    rows, depth = hidden.shape
    q_width, k_width = w_q.shape[1], w_k.shape[1]
    weights = [w_q, w_k, w_v, q_gain, k_gain, w_out, prefix, own]
    operands = [*scalars, hidden, *weights]
    kept = [
        ((rows, q_width), BF16),
        ((rows, k_width), BF16),
        ((rows, k_width), BF16),
        ((rows, q_width), F32),
        ((rows, k_width), F32),
    ] + like(weights)
    found = pl.pallas_call(
        project_kernel,
        in_specs=[HBM] * len(operands),
        out_specs=[SMEM] * 3 + [VMEM] * len(kept),
        out_shape=[pltpu.SMEM(x.shape, jnp.int32) for x in scalars] + in_vmem(kept),
        scratch_shapes=[pltpu.VMEM(hidden.shape, hidden.dtype), pltpu.SemaphoreType.DMA((32,))],
        compiler_params=pltpu.CompilerParams(vmem_limit_bytes=vmem_room(prefix.shape[0])),
        cost_estimate=lasting(2.6),
    )(*held_in(pltpu.HBM, operands))
    return found[:3], found[3:8], found[8:14], found[14], found[15]


def forward_kernel(slots, names, *refs):
    take, rest = taker(refs)
    prompt_len, resp_prompt, resp_len = take(3)
    query, key, value, wo_v = take(4)
    prefix = take(len(rest) - 4 - len(names) - 1)
    p_pre, p_own, heads_out, prefix_v = take(4)
    parts = take(len(names))
    (out_bf,) = take(1)

    held = prefix[0].shape[0]
    for k, ref in enumerate(prefix):
        prefix_v[slot_rows(len(prefix), held, k), :] = ref[...]
    size = heads_out.shape[1] * p_own.shape[3] // p_own.shape[2] // p_own.shape[1]
    count = prefix_v.shape[0]
    window = window_rows(count)
    slot_len = query.shape[0] // slots
    kv_heads = key.shape[1] // size
    groups = query.shape[1] // key.shape[1]
    scale = size ** (-0.5)
    for n in range(slots):
        first, last = prompt_span(prompt_len, resp_prompt[n])
        start = window_start(first, count)
        rows = slice(n * slot_len, (n + 1) * slot_len)
        live = lax.broadcasted_iota(jnp.int32, (slot_len, size), 0) < resp_len[n]
        for h in range(kv_heads):
            heads = range(h * groups, (h + 1) * groups)
            q = stacked(query, rows, heads, size)
            k_win = prefix_v[pl.ds(start, window), 2 * h * size : (2 * h + 1) * size]
            v_win = prefix_v[pl.ds(start, window), (2 * h + 1) * size : (2 * h + 2) * size]
            k_own = key[rows, h * size : (h + 1) * size]
            v_own = value[rows, h * size : (h + 1) * size]
            tall = groups * slot_len
            place = start + lax.broadcasted_iota(jnp.int32, (tall, window), 1)
            s_pre = jnp.where((place >= first) & (place < last), dot_nt(q, k_win) * scale, NEG)
            token = lax.broadcasted_iota(jnp.int32, (groups, slot_len, slot_len), 1)
            token = token.reshape(tall, slot_len)
            other = lax.broadcasted_iota(jnp.int32, (tall, slot_len), 1)
            s_own = jnp.where(
                (other <= token) & (other < resp_len[n]), dot_nt(q, k_own) * scale, NEG
            )
            top = jnp.maximum(
                jnp.max(s_pre, axis=-1, keepdims=True), jnp.max(s_own, axis=-1, keepdims=True)
            )
            e_pre = jnp.exp(s_pre - top)
            e_own = jnp.exp(s_own - top)
            total = jnp.sum(e_pre, axis=-1, keepdims=True) + jnp.sum(e_own, axis=-1, keepdims=True)
            b_pre = (e_pre / total).astype(BF16)
            b_own = (e_own / total).astype(BF16)
            p_pre[n, h] = b_pre
            p_own[n, h] = b_own
            out = dot(b_pre, v_win) + dot(b_own, v_own)
            for i, a in enumerate(heads):
                one = out[i * slot_len : (i + 1) * slot_len]
                heads_out[rows, a * size : (a + 1) * size] = one
                out_bf[rows, a * size : (a + 1) * size] = jnp.where(live, one, 0.0).astype(BF16)

    def make(cols):
        return dot(out_bf[...], wo_v[:, cols]).astype(BF16)

    make_blocks(make, names, parts)


def block_shapes(names, rows, width):
    return [((len(blocks), rows, width), BF16) for blocks in names]


def in_vmem(shapes):
    return [pltpu.VMEM(*x) for x in shapes]


def held_in(space, arrays):
    return [pltpu.with_memory_space_constraint(x, space) for x in arrays]


def lasting(us):
    return pl.CostEstimate(flops=int(us * 1.15e9), bytes_accessed=0, transcendentals=0)


def like(arrays):
    return [(x.shape, x.dtype) for x in arrays]


def vmem_room(prefix_rows):
    return 48 << 20 if prefix_rows > 1024 else 24 << 20


def forward(names, width, size, scalars, query, key, value, w_out, prefix):
    slots = scalars[-1].shape[0]
    rows, q_width = query.shape
    k_width = key.shape[1]
    count = sum(x.shape[0] for x in prefix)
    window = window_rows(count)
    slot_len = rows // slots
    kv_heads, tall = k_width // size, slot_len * q_width // k_width
    results = [
        ((slots, kv_heads, tall, window), BF16),
        ((slots, kv_heads, tall, slot_len), BF16),
        ((rows, q_width), F32),
        ((count, prefix[0].shape[1]), BF16),
    ] + block_shapes(names, rows, width)
    operands = [query, key, value, w_out, *prefix]
    found = pl.pallas_call(
        functools.partial(forward_kernel, slots, names),
        in_specs=[SMEM] * 3 + [VMEM] * len(operands),
        out_specs=[VMEM] * len(results),
        out_shape=in_vmem(results),
        scratch_shapes=[pltpu.VMEM((rows, q_width), BF16)],
        compiler_params=pltpu.CompilerParams(vmem_limit_bytes=vmem_room(count)),
        cost_estimate=lasting(1.7),
    )(*held_in(pltpu.SMEM, scalars), *held_in(pltpu.VMEM, operands))
    return found[:4], found[4:]


def backward_kernel(slots, names, *refs):
    take, rest = taker(refs)
    prompt_len, resp_prompt, resp_len = take(3)
    cotangent = take(len(HELD))
    query, key, value, hq, hk = take(5)
    w_q, w_k, w_v, q_gain, k_gain, w_out = take(6)
    p_pre, p_own, heads_out, prefix_v = take(4)
    terms = take(len(rest) - len(names) - 4)
    parts = take(len(names))
    grad_prefix, dhq, dhk, dv = take(4)

    width = cotangent[0].shape[2]
    me = lax.axis_index("mp")
    grad_heads = 0.0
    for blocks, ref in zip(HELD, cotangent):
        for i, block in enumerate(blocks):
            grad_heads += dot_nt(ref[i], w_out[:, features(me ^ block, width)])
    grad_prefix[...] = jnp.zeros_like(grad_prefix)

    count = prefix_v.shape[0]
    window = window_rows(count)
    slot_len = query.shape[0] // slots
    size = q_gain.shape[1]
    kv_heads = key.shape[1] // size
    groups = query.shape[1] // key.shape[1]
    scale = size ** (-0.5)
    for n in range(slots):
        first, _ = prompt_span(prompt_len, resp_prompt[n])
        start = window_start(first, count)
        rows = slice(n * slot_len, (n + 1) * slot_len)
        live = lax.broadcasted_iota(jnp.int32, (slot_len, size), 0) < resp_len[n]
        for h in range(kv_heads):
            heads = range(h * groups, (h + 1) * groups)
            q = stacked(query, rows, heads, size)
            out = stacked(heads_out, rows, heads, size)
            g = jnp.concatenate(
                [
                    jnp.where(live, grad_heads[rows, a * size : (a + 1) * size], 0.0).astype(BF16)
                    for a in heads
                ],
                axis=0,
            )
            k_win = prefix_v[pl.ds(start, window), 2 * h * size : (2 * h + 1) * size]
            v_win = prefix_v[pl.ds(start, window), (2 * h + 1) * size : (2 * h + 2) * size]
            k_own = key[rows, h * size : (h + 1) * size]
            v_own = value[rows, h * size : (h + 1) * size]
            b_pre, b_own = p_pre[n, h], p_own[n, h]
            delta = jnp.sum(g.astype(F32) * out, axis=-1, keepdims=True)
            ds_pre = (b_pre.astype(F32) * (dot_nt(g, v_win) - delta)).astype(BF16)
            ds_own = (b_own.astype(F32) * (dot_nt(g, v_own) - delta)).astype(BF16)
            grad_q = scale * (dot(ds_pre, k_win) + dot(ds_own, k_own))
            for i, a in enumerate(heads):
                cols = slice(a * size, (a + 1) * size)
                one = grad_q[i * slot_len : (i + 1) * slot_len]
                dhq[rows, cols] = norm_back(hq[rows, cols], q_gain[...], one).astype(BF16)
            cols = slice(h * size, (h + 1) * size)
            grad_k = scale * dot_tn(ds_own, q)
            dhk[rows, cols] = norm_back(hk[rows, cols], k_gain[...], grad_k).astype(BF16)
            dv[rows, cols] = dot_tn(b_own, g).astype(BF16)
            k_cols = slice(2 * h * size, (2 * h + 1) * size)
            v_cols = slice((2 * h + 1) * size, (2 * h + 2) * size)
            grad_prefix[pl.ds(start, window), k_cols] += scale * dot_tn(ds_pre, q)
            grad_prefix[pl.ds(start, window), v_cols] += dot_tn(b_pre, g)
    chips = prefix_v.shape[0] // terms[0].shape[1] if len(terms) > 1 else 1
    for ref, steps in zip(terms, TERMS if len(terms) > 1 else ((0,),)):
        for i, step in enumerate(steps):
            ref[i] = grad_prefix[slot_rows(chips, ref.shape[1], step), :]

    def make(cols):
        return (
            dot_nt(dhq[...], w_q[cols, :])
            + dot_nt(dhk[...], w_k[cols, :])
            + dot_nt(dv[...], w_v[cols, :])
        ).astype(BF16)

    make_blocks(make, names, parts)


def backward(names, scalars, cotangent, kept, terms):
    slots = scalars[-1].shape[0]
    query, key, w_out, prefix = kept[0], kept[1], kept[10], kept[14]
    rows, q_width = query.shape
    k_width, depth = key.shape[1], w_out.shape[1]
    count, kv_width = prefix.shape
    results = [(x, F32) for x in terms] + block_shapes(names, rows, cotangent[0].shape[2])
    found = pl.pallas_call(
        functools.partial(backward_kernel, slots, names),
        in_specs=[SMEM] * 3 + [VMEM] * (len(cotangent) + len(kept)),
        out_specs=[VMEM] * len(results),
        out_shape=in_vmem(results),
        scratch_shapes=[
            pltpu.VMEM((count, kv_width), F32),
            pltpu.VMEM((rows, q_width), BF16),
            pltpu.VMEM((rows, k_width), BF16),
            pltpu.VMEM((rows, k_width), BF16),
        ],
        compiler_params=pltpu.CompilerParams(vmem_limit_bytes=vmem_room(count)),
        cost_estimate=lasting(3.5),
    )(*held_in(pltpu.SMEM, scalars), *held_in(pltpu.VMEM, [*cotangent, *kept]))
    return found[: len(terms)], found[len(terms) :]


def last_kernel(counts, *refs):
    take, rest = taker(refs)
    groups = [take(len(count)) for count in counts]
    results = take(len(counts))
    stage = take(len(counts))
    (sems,) = take(1)
    copies = Copies(sems)
    stores = []
    for count, group, result, ref in zip(counts, groups, results, stage):
        whole = 0.0
        for i, term in zip(count, group):
            whole = whole + term[i].astype(F32)
        ref[...] = whole.astype(BF16)
        stores.append(copies.start(ref, result))
    wait(stores)


def last_sums(groups):
    arrays = [array for group in groups for array, _ in group]
    shapes = [jax.ShapeDtypeStruct(group[0][0].shape[1:], BF16) for group in groups]
    return pl.pallas_call(
        functools.partial(last_kernel, [[i for _, i in group] for group in groups]),
        in_specs=[VMEM] * len(arrays),
        out_specs=[HBM] * len(groups),
        out_shape=shapes,
        scratch_shapes=in_vmem(like(shapes)) + [pltpu.SemaphoreType.DMA((len(groups),))],
        compiler_params=pltpu.CompilerParams(vmem_limit_bytes=vmem_room(0)),
        cost_estimate=lasting(0.9),
    )(*held_in(pltpu.VMEM, arrays))


def trade(name, block, axis, step):
    with jax.named_scope(name):
        return lax.ppermute(block, axis, [(i, i ^ step) for i in range(lax.axis_size(axis))])


def after(value, *others):
    return lax.optimization_barrier((value, *others))[0]


def total(*terms):
    whole = terms[0].astype(F32)
    for term in terms[1:]:
        whole = whole + term.astype(F32)
    return whole.astype(BF16)


def per_device(
    hidden_rows,
    w_query,
    w_key,
    w_value,
    w_out,
    q_gain,
    k_gain,
    prefix_kv,
    cotangent,
    prompt_len,
    resp_prompt,
    resp_len,
):
    chips = lax.axis_size("dp")
    scalars = (prompt_len, resp_prompt, resp_len)
    q_gain, k_gain = q_gain[None], k_gain[None]
    own = cotangent[None]
    far = trade("gather_far", own, "mp", 4)
    near = trade("gather_near", own, "mp", 2)
    if chips == 4:
        others = [trade("gather_prefix", prefix_kv, "dp", k) for k in range(1, chips)]
    else:
        prefix_kv, others = lax.all_gather(prefix_kv, "dp", axis=0, tiled=True), []
    far = after(far, *others)
    both = trade("gather_both", far, "mp", 2)
    pair = jnp.concatenate([far, near])
    pair_x = trade("gather_pair_x", pair, "mp", 1)
    own_x = trade("gather_own_x", own, "mp", 1)
    scalars, projected, weights, prefix, own = project(
        scalars, after(hidden_rows, far), w_query, w_key, w_value, q_gain, k_gain, w_out,
        prefix_kv, own,
    )
    both_x = trade("gather_both_x", after(both, projected[0]), "mp", 1)
    probed, parts = forward(
        OUT, cotangent.shape[1], q_gain.shape[1], scalars, *projected[:3], weights[5],
        [prefix, *others],
    )
    back = [own, pair, both, own_x, pair_x, both_x]
    shape = prefix_kv.shape
    terms = [(1, *shape)] if chips != 4 else [(len(steps), *shape) for steps in TERMS]
    terms, grads = backward(IN, scalars, back, [*projected, *weights, *probed], terms)

    out_a, out_b, kept_a, kept_b = parts
    got_a = trade("out_a", out_a, "mp", 2)
    got_b = trade("out_b", after(out_b, pair_x), "mp", 2)
    out_a = total(kept_a, got_a)
    got_out = trade("out_mid", out_a, "mp", 4)
    in_7, in_5, in_31, in_6, in_4, in_2, in_0 = grads
    got_7 = trade("in_7", in_7, "mp", 1)
    in_6 = total(after(in_6, out_a), got_7)
    got_5 = trade("in_5", after(in_5, in_6), "mp", 1)
    got_6 = trade("in_6", in_6, "mp", 2)
    got_31 = trade("in_31", after(in_31, in_6), "mp", 1)
    in_4 = total(after(in_4, got_b, got_out), got_5, got_6)
    got_4 = trade("in_4", in_4, "mp", 4)
    in_2 = total(in_2, got_31[:1])
    got_2 = trade("in_2", in_2, "mp", 2)
    got_x = trade("out_x", total(after(kept_b, in_4)[1:], got_b[1:], got_out[1:]), "mp", 1)
    groups = [
        [(kept_b, 0), (got_b, 0), (got_out, 0), (got_x, 0)],
        [(in_0, 0), (got_31, 1), (got_2, 0), (got_4, 0)],
    ]
    if chips == 4:
        got = trade("grad_prefix", after(terms[0], in_4), "dp", 1)
        sent = terms[1][1:] + got[1:]
        last = trade("grad_prefix", sent, "dp", 2)
        groups.append([(terms[1], 0), (got, 0), (last, 0)])
        return last_sums(groups)
    grad_prefix = lax.psum_scatter(terms[0][0], "dp", scatter_dimension=0, tiled=True)
    return *last_sums(groups), grad_prefix.astype(BF16)


def solution(mesh):
    in_specs = (
        P("dp", None),
        P(None, "mp"),
        P(None, "mp"),
        P(None, "mp"),
        P("mp", None),
        P(),
        P(),
        P("dp", "mp"),
        P("dp", "mp"),
        P(),
        P("dp"),
        P("dp"),
    )
    out_specs = (P("dp", "mp"), P("dp", "mp"), P("dp", "mp"))
    return jax.shard_map(
        per_device, mesh=mesh, in_specs=in_specs, out_specs=out_specs, check_vma=False
    )
```

```python
import functools

import jax
import jax.numpy as jnp
from jax import lax
from jax.experimental import pallas as pl
from jax.experimental.pallas import tpu as pltpu
from jax.sharding import PartitionSpec as P

EPS = 1e-06
NEG = -1e30
ROWS = 16
HELD = ((0,), (4, 2), (6,), (1,), (5, 3), (7,))
OUT = ((6, 7), (2, 3), (4, 5), (0, 1))
TERMS = ((1, 3), (0, 2))
IN = ((7,), (5,), (3, 1), (6,), (4,), (2,), (0,))
F32 = jnp.float32
BF16 = jnp.bfloat16
HBM = pl.BlockSpec(memory_space=pltpu.HBM)
SMEM = pl.BlockSpec(memory_space=pltpu.SMEM)
VMEM = pl.BlockSpec(memory_space=pltpu.VMEM)


def dot(left, right):
    return jnp.dot(left, right, preferred_element_type=F32)


def dot_nt(left, right):
    return lax.dot_general(left, right, (((1,), (1,)), ((), ())), preferred_element_type=F32)


def dot_tn(left, right):
    return lax.dot_general(left, right, (((0,), (0,)), ((), ())), preferred_element_type=F32)


def inverse_root(hidden):
    return lax.rsqrt(jnp.mean(hidden * hidden, axis=-1, keepdims=True) + EPS)


def norm_back(hidden, gain, grad):
    root = inverse_root(hidden)
    unit = hidden * root
    scaled = grad * gain
    return root * (scaled - unit * jnp.mean(scaled * unit, axis=-1, keepdims=True))


class Copies:
    def __init__(self, sems):
        self.sems, self.count = sems, 0

    def start(self, source, target):
        copy = pltpu.make_async_copy(source, target, self.sems.at[self.count])
        self.count += 1
        copy.start()
        return copy


def wait(copies):
    for copy in copies:
        copy.wait()


def prompt_span(prompt_len, prompt):
    first, last = 0, 0
    end = 0
    for p in range(prompt_len.shape[0]):
        begin = end
        end = end + prompt_len[p]
        first = jnp.where(prompt == p, begin, first)
        last = jnp.where(prompt == p, end, last)
    return first, last


def window_rows(count):
    return min(count, count // 3 + ROWS)


def window_start(first, count):
    start = jnp.minimum(first // ROWS * ROWS, count - window_rows(count))
    return pl.multiple_of(start, ROWS)


def slot_rows(slots, rows, step):
    if slots == 1:
        return pl.ds(0, rows)
    return pl.ds(pl.multiple_of((lax.axis_index("dp") ^ step) * rows, ROWS), rows)


def features(block, width):
    return pl.ds(pl.multiple_of(block * width, width), width)


def stacked(ref, rows, heads, size):
    return jnp.concatenate([ref[rows, a * size : (a + 1) * size] for a in heads], axis=0)


def make_blocks(make, names, refs):
    me = lax.axis_index("mp")
    for blocks, ref in zip(names, refs):
        for i, block in enumerate(blocks):
            ref[i] = make(features(me ^ block, ref.shape[-1]))


def taker(refs):
    refs = list(refs)

    def take(count):
        found, refs[:count] = refs[:count], []
        return found

    return take, refs


def project_kernel(*refs):
    take, _ = taker(refs)
    scalars = take(3)
    hidden, w_q, w_k, w_v, q_gain, k_gain, w_out, prefix, own = take(9)
    scalars_v = take(3)
    query, key, value, hq, hk = take(5)
    wq_v, wk_v, wv_v, qg_v, kg_v, wo_v, prefix_v, own_v = take(8)
    hidden_v, sems = take(2)

    copies = Copies(sems)
    depth = hidden.shape[1]
    steps = 4
    part = depth // steps
    loads = []
    for i in range(steps):
        cut = pl.ds(i * part, part)
        loads.append(
            [copies.start(hidden.at[:, cut], hidden_v.at[:, cut])]
            + [
                copies.start(w.at[cut], v.at[cut])
                for w, v in ((w_q, wq_v), (w_k, wk_v), (w_v, wv_v))
            ]
        )
    small = [copies.start(q_gain, qg_v), copies.start(k_gain, kg_v)]
    small += [copies.start(source, target) for source, target in zip(scalars, scalars_v)]
    small += [copies.start(prefix, prefix_v), copies.start(w_out, wo_v), copies.start(own, own_v)]

    sums = [None] * 3
    for i, load in enumerate(loads):
        wait(load)
        rows = hidden_v[:, i * part : (i + 1) * part]
        for j, v in enumerate((wq_v, wk_v, wv_v)):
            term = dot(rows, v[i * part : (i + 1) * part])
            sums[j] = term if i == 0 else sums[j] + term
    hq[...], hk[...] = sums[0], sums[1]
    value[...] = sums[2].astype(BF16)
    wait(small)
    size = qg_v.shape[1]
    for whole, gain, out in ((sums[0], qg_v, query), (sums[1], kg_v, key)):
        for at in range(0, whole.shape[1], size):
            head = whole[:, at : at + size]
            out[:, at : at + size] = (head * inverse_root(head) * gain[...]).astype(BF16)


def project(scalars, hidden, w_q, w_k, w_v, q_gain, k_gain, w_out, prefix, own):
    rows, depth = hidden.shape
    q_width, k_width = w_q.shape[1], w_k.shape[1]
    weights = [w_q, w_k, w_v, q_gain, k_gain, w_out, prefix, own]
    operands = [*scalars, hidden, *weights]
    kept = [
        ((rows, q_width), BF16),
        ((rows, k_width), BF16),
        ((rows, k_width), BF16),
        ((rows, q_width), F32),
        ((rows, k_width), F32),
    ] + like(weights)
    found = pl.pallas_call(
        project_kernel,
        in_specs=[HBM] * len(operands),
        out_specs=[SMEM] * 3 + [VMEM] * len(kept),
        out_shape=[pltpu.SMEM(x.shape, jnp.int32) for x in scalars] + in_vmem(kept),
        scratch_shapes=[pltpu.VMEM(hidden.shape, hidden.dtype), pltpu.SemaphoreType.DMA((32,))],
        compiler_params=pltpu.CompilerParams(vmem_limit_bytes=vmem_room(prefix.shape[0])),
        cost_estimate=lasting(2.6),
    )(*held_in(pltpu.HBM, operands))
    return found[:3], found[3:8], found[8:14], found[14], found[15]


def forward_kernel(slots, names, *refs):
    take, rest = taker(refs)
    prompt_len, resp_prompt, resp_len = take(3)
    query, key, value, wo_v = take(4)
    prefix = take(len(rest) - 4 - len(names) - 1)
    p_pre, p_own, heads_out, prefix_v = take(4)
    parts = take(len(names))
    (out_bf,) = take(1)

    held = prefix[0].shape[0]
    for k, ref in enumerate(prefix):
        prefix_v[slot_rows(len(prefix), held, k), :] = ref[...]
    size = heads_out.shape[1] * p_own.shape[3] // p_own.shape[2] // p_own.shape[1]
    count = prefix_v.shape[0]
    window = window_rows(count)
    slot_len = query.shape[0] // slots
    kv_heads = key.shape[1] // size
    groups = query.shape[1] // key.shape[1]
    scale = size ** (-0.5)
    for n in range(slots):
        first, last = prompt_span(prompt_len, resp_prompt[n])
        start = window_start(first, count)
        rows = slice(n * slot_len, (n + 1) * slot_len)
        live = lax.broadcasted_iota(jnp.int32, (slot_len, size), 0) < resp_len[n]
        for h in range(kv_heads):
            heads = range(h * groups, (h + 1) * groups)
            q = stacked(query, rows, heads, size)
            k_win = prefix_v[pl.ds(start, window), 2 * h * size : (2 * h + 1) * size]
            v_win = prefix_v[pl.ds(start, window), (2 * h + 1) * size : (2 * h + 2) * size]
            k_own = key[rows, h * size : (h + 1) * size]
            v_own = value[rows, h * size : (h + 1) * size]
            tall = groups * slot_len
            place = start + lax.broadcasted_iota(jnp.int32, (tall, window), 1)
            s_pre = jnp.where((place >= first) & (place < last), dot_nt(q, k_win) * scale, NEG)
            token = lax.broadcasted_iota(jnp.int32, (groups, slot_len, slot_len), 1)
            token = token.reshape(tall, slot_len)
            other = lax.broadcasted_iota(jnp.int32, (tall, slot_len), 1)
            s_own = jnp.where(
                (other <= token) & (other < resp_len[n]), dot_nt(q, k_own) * scale, NEG
            )
            top = jnp.maximum(
                jnp.max(s_pre, axis=-1, keepdims=True), jnp.max(s_own, axis=-1, keepdims=True)
            )
            e_pre = jnp.exp(s_pre - top)
            e_own = jnp.exp(s_own - top)
            total = jnp.sum(e_pre, axis=-1, keepdims=True) + jnp.sum(e_own, axis=-1, keepdims=True)
            b_pre = (e_pre / total).astype(BF16)
            b_own = (e_own / total).astype(BF16)
            p_pre[n, h] = b_pre
            p_own[n, h] = b_own
            out = dot(b_pre, v_win) + dot(b_own, v_own)
            for i, a in enumerate(heads):
                one = out[i * slot_len : (i + 1) * slot_len]
                heads_out[rows, a * size : (a + 1) * size] = one
                out_bf[rows, a * size : (a + 1) * size] = jnp.where(live, one, 0.0).astype(BF16)

    def make(cols):
        return dot(out_bf[...], wo_v[:, cols]).astype(BF16)

    make_blocks(make, names, parts)


def block_shapes(names, rows, width):
    return [((len(blocks), rows, width), BF16) for blocks in names]


def in_vmem(shapes):
    return [pltpu.VMEM(*x) for x in shapes]


def held_in(space, arrays):
    return [pltpu.with_memory_space_constraint(x, space) for x in arrays]


def lasting(us):
    return pl.CostEstimate(flops=int(us * 1.15e9), bytes_accessed=0, transcendentals=0)


def like(arrays):
    return [(x.shape, x.dtype) for x in arrays]


def vmem_room(prefix_rows):
    return 48 << 20 if prefix_rows > 1024 else 24 << 20


def forward(names, width, size, scalars, query, key, value, w_out, prefix):
    slots = scalars[-1].shape[0]
    rows, q_width = query.shape
    k_width = key.shape[1]
    count = sum(x.shape[0] for x in prefix)
    window = window_rows(count)
    slot_len = rows // slots
    kv_heads, tall = k_width // size, slot_len * q_width // k_width
    results = [
        ((slots, kv_heads, tall, window), BF16),
        ((slots, kv_heads, tall, slot_len), BF16),
        ((rows, q_width), F32),
        ((count, prefix[0].shape[1]), BF16),
    ] + block_shapes(names, rows, width)
    operands = [query, key, value, w_out, *prefix]
    found = pl.pallas_call(
        functools.partial(forward_kernel, slots, names),
        in_specs=[SMEM] * 3 + [VMEM] * len(operands),
        out_specs=[VMEM] * len(results),
        out_shape=in_vmem(results),
        scratch_shapes=[pltpu.VMEM((rows, q_width), BF16)],
        compiler_params=pltpu.CompilerParams(vmem_limit_bytes=vmem_room(count)),
        cost_estimate=lasting(1.7),
    )(*held_in(pltpu.SMEM, scalars), *held_in(pltpu.VMEM, operands))
    return found[:4], found[4:]


def backward_kernel(slots, names, *refs):
    take, rest = taker(refs)
    prompt_len, resp_prompt, resp_len = take(3)
    cotangent = take(len(HELD))
    query, key, value, hq, hk = take(5)
    w_q, w_k, w_v, q_gain, k_gain, w_out = take(6)
    p_pre, p_own, heads_out, prefix_v = take(4)
    terms = take(len(rest) - len(names) - 4)
    parts = take(len(names))
    grad_prefix, dhq, dhk, dv = take(4)

    width = cotangent[0].shape[2]
    me = lax.axis_index("mp")
    grad_heads = 0.0
    for blocks, ref in zip(HELD, cotangent):
        for i, block in enumerate(blocks):
            grad_heads += dot_nt(ref[i], w_out[:, features(me ^ block, width)])
    grad_prefix[...] = jnp.zeros_like(grad_prefix)

    count = prefix_v.shape[0]
    window = window_rows(count)
    slot_len = query.shape[0] // slots
    size = q_gain.shape[1]
    kv_heads = key.shape[1] // size
    groups = query.shape[1] // key.shape[1]
    scale = size ** (-0.5)
    for n in range(slots):
        first, _ = prompt_span(prompt_len, resp_prompt[n])
        start = window_start(first, count)
        rows = slice(n * slot_len, (n + 1) * slot_len)
        live = lax.broadcasted_iota(jnp.int32, (slot_len, size), 0) < resp_len[n]
        for h in range(kv_heads):
            heads = range(h * groups, (h + 1) * groups)
            q = stacked(query, rows, heads, size)
            out = stacked(heads_out, rows, heads, size)
            g = jnp.concatenate(
                [
                    jnp.where(live, grad_heads[rows, a * size : (a + 1) * size], 0.0).astype(BF16)
                    for a in heads
                ],
                axis=0,
            )
            k_win = prefix_v[pl.ds(start, window), 2 * h * size : (2 * h + 1) * size]
            v_win = prefix_v[pl.ds(start, window), (2 * h + 1) * size : (2 * h + 2) * size]
            k_own = key[rows, h * size : (h + 1) * size]
            v_own = value[rows, h * size : (h + 1) * size]
            b_pre, b_own = p_pre[n, h], p_own[n, h]
            delta = jnp.sum(g.astype(F32) * out, axis=-1, keepdims=True)
            ds_pre = (b_pre.astype(F32) * (dot_nt(g, v_win) - delta)).astype(BF16)
            ds_own = (b_own.astype(F32) * (dot_nt(g, v_own) - delta)).astype(BF16)
            grad_q = scale * (dot(ds_pre, k_win) + dot(ds_own, k_own))
            for i, a in enumerate(heads):
                cols = slice(a * size, (a + 1) * size)
                one = grad_q[i * slot_len : (i + 1) * slot_len]
                dhq[rows, cols] = norm_back(hq[rows, cols], q_gain[...], one).astype(BF16)
            cols = slice(h * size, (h + 1) * size)
            grad_k = scale * dot_tn(ds_own, q)
            dhk[rows, cols] = norm_back(hk[rows, cols], k_gain[...], grad_k).astype(BF16)
            dv[rows, cols] = dot_tn(b_own, g).astype(BF16)
            k_cols = slice(2 * h * size, (2 * h + 1) * size)
            v_cols = slice((2 * h + 1) * size, (2 * h + 2) * size)
            grad_prefix[pl.ds(start, window), k_cols] += scale * dot_tn(ds_pre, q)
            grad_prefix[pl.ds(start, window), v_cols] += dot_tn(b_pre, g)
    chips = prefix_v.shape[0] // terms[0].shape[1] if len(terms) > 1 else 1
    for ref, steps in zip(terms, TERMS if len(terms) > 1 else ((0,),)):
        for i, step in enumerate(steps):
            ref[i] = grad_prefix[slot_rows(chips, ref.shape[1], step), :]

    def make(cols):
        return (
            dot_nt(dhq[...], w_q[cols, :])
            + dot_nt(dhk[...], w_k[cols, :])
            + dot_nt(dv[...], w_v[cols, :])
        ).astype(BF16)

    make_blocks(make, names, parts)


def backward(names, scalars, cotangent, kept, terms):
    slots = scalars[-1].shape[0]
    query, key, w_out, prefix = kept[0], kept[1], kept[10], kept[14]
    rows, q_width = query.shape
    k_width, depth = key.shape[1], w_out.shape[1]
    count, kv_width = prefix.shape
    results = [(x, F32) for x in terms] + block_shapes(names, rows, cotangent[0].shape[2])
    found = pl.pallas_call(
        functools.partial(backward_kernel, slots, names),
        in_specs=[SMEM] * 3 + [VMEM] * (len(cotangent) + len(kept)),
        out_specs=[VMEM] * len(results),
        out_shape=in_vmem(results),
        scratch_shapes=[
            pltpu.VMEM((count, kv_width), F32),
            pltpu.VMEM((rows, q_width), BF16),
            pltpu.VMEM((rows, k_width), BF16),
            pltpu.VMEM((rows, k_width), BF16),
        ],
        compiler_params=pltpu.CompilerParams(vmem_limit_bytes=vmem_room(count)),
        cost_estimate=lasting(3.5),
    )(*held_in(pltpu.SMEM, scalars), *held_in(pltpu.VMEM, [*cotangent, *kept]))
    return found[: len(terms)], found[len(terms) :]


def last_kernel(counts, *refs):
    take, rest = taker(refs)
    groups = [take(len(count)) for count in counts]
    results = take(len(counts))
    stage = take(len(counts))
    (sems,) = take(1)
    copies = Copies(sems)
    stores = []
    for count, group, result, ref in zip(counts, groups, results, stage):
        whole = 0.0
        for i, term in zip(count, group):
            whole = whole + term[i].astype(F32)
        ref[...] = whole.astype(BF16)
        stores.append(copies.start(ref, result))
    wait(stores)


def last_sums(groups):
    arrays = [array for group in groups for array, _ in group]
    shapes = [jax.ShapeDtypeStruct(group[0][0].shape[1:], BF16) for group in groups]
    return pl.pallas_call(
        functools.partial(last_kernel, [[i for _, i in group] for group in groups]),
        in_specs=[VMEM] * len(arrays),
        out_specs=[HBM] * len(groups),
        out_shape=shapes,
        scratch_shapes=in_vmem(like(shapes)) + [pltpu.SemaphoreType.DMA((len(groups),))],
        compiler_params=pltpu.CompilerParams(vmem_limit_bytes=vmem_room(0)),
        cost_estimate=lasting(0.9),
    )(*held_in(pltpu.VMEM, arrays))


def trade(name, block, axis, step):
    with jax.named_scope(name):
        return lax.ppermute(block, axis, [(i, i ^ step) for i in range(lax.axis_size(axis))])


def after(value, *others):
    return lax.optimization_barrier((value, *others))[0]


def total(*terms):
    whole = terms[0].astype(F32)
    for term in terms[1:]:
        whole = whole + term.astype(F32)
    return whole.astype(BF16)


def per_device(
    hidden_rows,
    w_query,
    w_key,
    w_value,
    w_out,
    q_gain,
    k_gain,
    prefix_kv,
    cotangent,
    prompt_len,
    resp_prompt,
    resp_len,
):
    chips = lax.axis_size("dp")
    scalars = (prompt_len, resp_prompt, resp_len)
    q_gain, k_gain = q_gain[None], k_gain[None]
    own = cotangent[None]
    far = trade("gather_far", own, "mp", 4)
    near = trade("gather_near", own, "mp", 2)
    if chips == 4:
        others = [trade("gather_prefix", prefix_kv, "dp", k) for k in range(1, chips)]
    else:
        prefix_kv, others = lax.all_gather(prefix_kv, "dp", axis=0, tiled=True), []
    far = after(far, *others)
    both = trade("gather_both", far, "mp", 2)
    pair = jnp.concatenate([far, near])
    pair_x = trade("gather_pair_x", pair, "mp", 1)
    own_x = trade("gather_own_x", own, "mp", 1)
    scalars, projected, weights, prefix, own = project(
        scalars, after(hidden_rows, far), w_query, w_key, w_value, q_gain, k_gain, w_out,
        prefix_kv, own,
    )
    both_x = trade("gather_both_x", after(both, projected[0]), "mp", 1)
    probed, parts = forward(
        OUT, cotangent.shape[1], q_gain.shape[1], scalars, *projected[:3], weights[5],
        [prefix, *others],
    )
    back = [own, pair, both, own_x, pair_x, both_x]
    shape = prefix_kv.shape
    terms = [(1, *shape)] if chips != 4 else [(len(steps), *shape) for steps in TERMS]
    terms, grads = backward(IN, scalars, back, [*projected, *weights, *probed], terms)

    out_a, out_b, kept_a, kept_b = parts
    got_a = trade("out_a", out_a, "mp", 2)
    got_b = trade("out_b", after(out_b, pair_x), "mp", 2)
    out_a = total(kept_a, got_a)
    got_out = trade("out_mid", out_a, "mp", 4)
    in_7, in_5, in_31, in_6, in_4, in_2, in_0 = grads
    got_7 = trade("in_7", in_7, "mp", 1)
    in_6 = total(after(in_6, out_a), got_7)
    got_5 = trade("in_5", after(in_5, in_6), "mp", 1)
    got_6 = trade("in_6", in_6, "mp", 2)
    got_31 = trade("in_31", after(in_31, in_6), "mp", 1)
    if chips == 4:
        got = trade("grad_prefix_core", after(terms[0], in_6), "dp", 1)
        got_31 = after(got_31, got)
    in_4 = total(after(in_4, got_b, got_out), got_5, got_6)
    got_4 = trade("in_4", in_4, "mp", 4)
    in_2 = total(in_2, got_31[:1])
    got_2 = trade("in_2", in_2, "mp", 2)
    got_x = trade("out_x", total(after(kept_b, in_4)[1:], got_b[1:], got_out[1:]), "mp", 1)
    groups = [
        [(kept_b, 0), (got_b, 0), (got_out, 0), (got_x, 0)],
        [(in_0, 0), (got_31, 1), (got_2, 0), (got_4, 0)],
    ]
    if chips == 4:
        sent = terms[1][1:] + got[1:]
        last = trade("grad_prefix_y", sent, "dp", 2)
        groups.append([(terms[1], 0), (got, 0), (last, 0)])
        return last_sums(groups)
    grad_prefix = lax.psum_scatter(terms[0][0], "dp", scatter_dimension=0, tiled=True)
    return *last_sums(groups), grad_prefix.astype(BF16)


def solution(mesh):
    in_specs = (
        P("dp", None),
        P(None, "mp"),
        P(None, "mp"),
        P(None, "mp"),
        P("mp", None),
        P(),
        P(),
        P("dp", "mp"),
        P("dp", "mp"),
        P(),
        P("dp"),
        P("dp"),
    )
    out_specs = (P("dp", "mp"), P("dp", "mp"), P("dp", "mp"))
    return jax.shard_map(
        per_device, mesh=mesh, in_specs=in_specs, out_specs=out_specs, check_vma=False
    )
```

```python
import functools

import jax
import jax.numpy as jnp
from jax import lax
from jax.experimental import pallas as pl
from jax.experimental.pallas import tpu as pltpu
from jax.sharding import PartitionSpec as P

EPS = 1e-06
NEG = -1e30
ROWS = 16
HELD = ((0,), (4, 2), (6,), (1,), (5, 3), (7,))
OUT = ((6, 7), (2, 3), (4, 5), (0, 1))
TERMS = ((1, 3), (0, 2))
IN = ((7, 5), (3,), (1,), (6,), (4,), (2,), (0,))
F32 = jnp.float32
BF16 = jnp.bfloat16
HBM = pl.BlockSpec(memory_space=pltpu.HBM)
SMEM = pl.BlockSpec(memory_space=pltpu.SMEM)
VMEM = pl.BlockSpec(memory_space=pltpu.VMEM)


def dot(left, right):
    return jnp.dot(left, right, preferred_element_type=F32)


def dot_nt(left, right):
    return lax.dot_general(left, right, (((1,), (1,)), ((), ())), preferred_element_type=F32)


def dot_tn(left, right):
    return lax.dot_general(left, right, (((0,), (0,)), ((), ())), preferred_element_type=F32)


def inverse_root(hidden):
    return lax.rsqrt(jnp.mean(hidden * hidden, axis=-1, keepdims=True) + EPS)


def norm_back(hidden, gain, grad):
    root = inverse_root(hidden)
    unit = hidden * root
    scaled = grad * gain
    return root * (scaled - unit * jnp.mean(scaled * unit, axis=-1, keepdims=True))


class Copies:
    def __init__(self, sems):
        self.sems, self.count = sems, 0

    def start(self, source, target):
        copy = pltpu.make_async_copy(source, target, self.sems.at[self.count])
        self.count += 1
        copy.start()
        return copy


def wait(copies):
    for copy in copies:
        copy.wait()


def prompt_span(prompt_len, prompt):
    first, last = 0, 0
    end = 0
    for p in range(prompt_len.shape[0]):
        begin = end
        end = end + prompt_len[p]
        first = jnp.where(prompt == p, begin, first)
        last = jnp.where(prompt == p, end, last)
    return first, last


def window_rows(count):
    return min(count, count // 3 + ROWS)


def window_start(first, count):
    start = jnp.minimum(first // ROWS * ROWS, count - window_rows(count))
    return pl.multiple_of(start, ROWS)


def slot_rows(slots, rows, step):
    if slots == 1:
        return pl.ds(0, rows)
    return pl.ds(pl.multiple_of((lax.axis_index("dp") ^ step) * rows, ROWS), rows)


def features(block, width):
    return pl.ds(pl.multiple_of(block * width, width), width)


def stacked(ref, rows, heads, size):
    return jnp.concatenate([ref[rows, a * size : (a + 1) * size] for a in heads], axis=0)


def make_blocks(make, names, refs):
    me = lax.axis_index("mp")
    for blocks, ref in zip(names, refs):
        for i, block in enumerate(blocks):
            ref[i] = make(features(me ^ block, ref.shape[-1]))


def taker(refs):
    refs = list(refs)

    def take(count):
        found, refs[:count] = refs[:count], []
        return found

    return take, refs


def project_kernel(*refs):
    take, _ = taker(refs)
    scalars = take(3)
    hidden, w_q, w_k, w_v, q_gain, k_gain, w_out, prefix, own = take(9)
    scalars_v = take(3)
    query, key, value, hq, hk = take(5)
    wq_v, wk_v, wv_v, qg_v, kg_v, wo_v, prefix_v, own_v = take(8)
    hidden_v, sems = take(2)

    copies = Copies(sems)
    half = hidden.shape[1] // 2
    halves = [pl.ds(0, half), pl.ds(half, half)]
    load_q = [
        [copies.start(hidden.at[:, cut], hidden_v.at[:, cut]), copies.start(w_q.at[cut], wq_v.at[cut])]
        for cut in halves
    ]
    load_kv = [copies.start(w_k, wk_v), copies.start(w_v, wv_v)]
    small = [copies.start(q_gain, qg_v), copies.start(k_gain, kg_v)]
    small += [copies.start(source, target) for source, target in zip(scalars, scalars_v)]
    small += [copies.start(prefix, prefix_v), copies.start(w_out, wo_v), copies.start(own, own_v)]

    sums = [0.0]
    for cut, load in zip(halves, load_q):
        wait(load)
        sums[0] += dot(hidden_v[:, cut], wq_v[cut, :])
    for load, w in zip(load_kv, (wk_v, wv_v)):
        load.wait()
        sums.append(dot(hidden_v[...], w[...]))
    hq[...], hk[...] = sums[0], sums[1]
    value[...] = sums[2].astype(BF16)
    wait(small)
    size = qg_v.shape[1]
    for whole, gain, out in ((sums[0], qg_v, query), (sums[1], kg_v, key)):
        for at in range(0, whole.shape[1], size):
            head = whole[:, at : at + size]
            out[:, at : at + size] = (head * inverse_root(head) * gain[...]).astype(BF16)


def project(scalars, hidden, w_q, w_k, w_v, q_gain, k_gain, w_out, prefix, own):
    rows, depth = hidden.shape
    q_width, k_width = w_q.shape[1], w_k.shape[1]
    weights = [w_q, w_k, w_v, q_gain, k_gain, w_out, prefix, own]
    operands = [*scalars, hidden, *weights]
    kept = [
        ((rows, q_width), BF16),
        ((rows, k_width), BF16),
        ((rows, k_width), BF16),
        ((rows, q_width), F32),
        ((rows, k_width), F32),
    ] + like(weights)
    found = pl.pallas_call(
        project_kernel,
        in_specs=[HBM] * len(operands),
        out_specs=[SMEM] * 3 + [VMEM] * len(kept),
        out_shape=[pltpu.SMEM(x.shape, jnp.int32) for x in scalars] + in_vmem(kept),
        scratch_shapes=[pltpu.VMEM(hidden.shape, hidden.dtype), pltpu.SemaphoreType.DMA((32,))],
        compiler_params=pltpu.CompilerParams(vmem_limit_bytes=vmem_room(prefix.shape[0])),
        cost_estimate=lasting(2.6),
    )(*held_in(pltpu.HBM, operands))
    return found[:3], found[3:8], found[8:14], found[14], found[15]


def forward_kernel(slots, names, *refs):
    take, rest = taker(refs)
    prompt_len, resp_prompt, resp_len = take(3)
    query, key, value, wo_v = take(4)
    prefix = take(len(rest) - 4 - len(names) - 1)
    p_pre, p_own, heads_out, prefix_v = take(4)
    parts = take(len(names))
    (out_bf,) = take(1)

    held = prefix[0].shape[0]
    for k, ref in enumerate(prefix):
        prefix_v[slot_rows(len(prefix), held, k), :] = ref[...]
    size = heads_out.shape[1] * p_own.shape[3] // p_own.shape[2] // p_own.shape[1]
    count = prefix_v.shape[0]
    window = window_rows(count)
    slot_len = query.shape[0] // slots
    kv_heads = key.shape[1] // size
    groups = query.shape[1] // key.shape[1]
    scale = size ** (-0.5)
    for n in range(slots):
        first, last = prompt_span(prompt_len, resp_prompt[n])
        start = window_start(first, count)
        rows = slice(n * slot_len, (n + 1) * slot_len)
        live = lax.broadcasted_iota(jnp.int32, (slot_len, size), 0) < resp_len[n]
        for h in range(kv_heads):
            heads = range(h * groups, (h + 1) * groups)
            q = stacked(query, rows, heads, size)
            k_win = prefix_v[pl.ds(start, window), 2 * h * size : (2 * h + 1) * size]
            v_win = prefix_v[pl.ds(start, window), (2 * h + 1) * size : (2 * h + 2) * size]
            k_own = key[rows, h * size : (h + 1) * size]
            v_own = value[rows, h * size : (h + 1) * size]
            tall = groups * slot_len
            place = start + lax.broadcasted_iota(jnp.int32, (tall, window), 1)
            s_pre = jnp.where((place >= first) & (place < last), dot_nt(q, k_win) * scale, NEG)
            token = lax.broadcasted_iota(jnp.int32, (groups, slot_len, slot_len), 1)
            token = token.reshape(tall, slot_len)
            other = lax.broadcasted_iota(jnp.int32, (tall, slot_len), 1)
            s_own = jnp.where(
                (other <= token) & (other < resp_len[n]), dot_nt(q, k_own) * scale, NEG
            )
            top = jnp.maximum(
                jnp.max(s_pre, axis=-1, keepdims=True), jnp.max(s_own, axis=-1, keepdims=True)
            )
            e_pre = jnp.exp(s_pre - top)
            e_own = jnp.exp(s_own - top)
            total = jnp.sum(e_pre, axis=-1, keepdims=True) + jnp.sum(e_own, axis=-1, keepdims=True)
            b_pre = (e_pre / total).astype(BF16)
            b_own = (e_own / total).astype(BF16)
            p_pre[n, h] = b_pre
            p_own[n, h] = b_own
            out = dot(b_pre, v_win) + dot(b_own, v_own)
            for i, a in enumerate(heads):
                one = out[i * slot_len : (i + 1) * slot_len]
                heads_out[rows, a * size : (a + 1) * size] = one
                out_bf[rows, a * size : (a + 1) * size] = jnp.where(live, one, 0.0).astype(BF16)

    def make(cols):
        return dot(out_bf[...], wo_v[:, cols]).astype(BF16)

    make_blocks(make, names, parts)


def block_shapes(names, rows, width):
    return [((len(blocks), rows, width), BF16) for blocks in names]


def in_vmem(shapes):
    return [pltpu.VMEM(*x) for x in shapes]


def held_in(space, arrays):
    return [pltpu.with_memory_space_constraint(x, space) for x in arrays]


def lasting(us):
    return pl.CostEstimate(flops=int(us * 1.15e9), bytes_accessed=0, transcendentals=0)


def like(arrays):
    return [(x.shape, x.dtype) for x in arrays]


def vmem_room(prefix_rows):
    return 48 << 20 if prefix_rows > 1024 else 24 << 20


def forward(names, width, size, scalars, query, key, value, w_out, prefix):
    slots = scalars[-1].shape[0]
    rows, q_width = query.shape
    k_width = key.shape[1]
    count = sum(x.shape[0] for x in prefix)
    window = window_rows(count)
    slot_len = rows // slots
    kv_heads, tall = k_width // size, slot_len * q_width // k_width
    results = [
        ((slots, kv_heads, tall, window), BF16),
        ((slots, kv_heads, tall, slot_len), BF16),
        ((rows, q_width), F32),
        ((count, prefix[0].shape[1]), BF16),
    ] + block_shapes(names, rows, width)
    operands = [query, key, value, w_out, *prefix]
    found = pl.pallas_call(
        functools.partial(forward_kernel, slots, names),
        in_specs=[SMEM] * 3 + [VMEM] * len(operands),
        out_specs=[VMEM] * len(results),
        out_shape=in_vmem(results),
        scratch_shapes=[pltpu.VMEM((rows, q_width), BF16)],
        compiler_params=pltpu.CompilerParams(vmem_limit_bytes=vmem_room(count)),
        cost_estimate=lasting(1.7),
    )(*held_in(pltpu.SMEM, scalars), *held_in(pltpu.VMEM, operands))
    return found[:4], found[4:]


def backward_kernel(slots, names, *refs):
    take, rest = taker(refs)
    prompt_len, resp_prompt, resp_len = take(3)
    cotangent = take(len(HELD))
    query, key, value, hq, hk = take(5)
    w_q, w_k, w_v, q_gain, k_gain, w_out = take(6)
    p_pre, p_own, heads_out, prefix_v = take(4)
    terms = take(len(rest) - len(names) - 4)
    parts = take(len(names))
    grad_prefix, dhq, dhk, dv = take(4)

    width = cotangent[0].shape[2]
    me = lax.axis_index("mp")
    grad_heads = 0.0
    for blocks, ref in zip(HELD, cotangent):
        for i, block in enumerate(blocks):
            grad_heads += dot_nt(ref[i], w_out[:, features(me ^ block, width)])
    grad_prefix[...] = jnp.zeros_like(grad_prefix)

    count = prefix_v.shape[0]
    window = window_rows(count)
    slot_len = query.shape[0] // slots
    size = q_gain.shape[1]
    kv_heads = key.shape[1] // size
    groups = query.shape[1] // key.shape[1]
    scale = size ** (-0.5)
    for n in range(slots):
        first, _ = prompt_span(prompt_len, resp_prompt[n])
        start = window_start(first, count)
        rows = slice(n * slot_len, (n + 1) * slot_len)
        live = lax.broadcasted_iota(jnp.int32, (slot_len, size), 0) < resp_len[n]
        for h in range(kv_heads):
            heads = range(h * groups, (h + 1) * groups)
            q = stacked(query, rows, heads, size)
            out = stacked(heads_out, rows, heads, size)
            g = jnp.concatenate(
                [
                    jnp.where(live, grad_heads[rows, a * size : (a + 1) * size], 0.0).astype(BF16)
                    for a in heads
                ],
                axis=0,
            )
            k_win = prefix_v[pl.ds(start, window), 2 * h * size : (2 * h + 1) * size]
            v_win = prefix_v[pl.ds(start, window), (2 * h + 1) * size : (2 * h + 2) * size]
            k_own = key[rows, h * size : (h + 1) * size]
            v_own = value[rows, h * size : (h + 1) * size]
            b_pre, b_own = p_pre[n, h], p_own[n, h]
            delta = jnp.sum(g.astype(F32) * out, axis=-1, keepdims=True)
            ds_pre = (b_pre.astype(F32) * (dot_nt(g, v_win) - delta)).astype(BF16)
            ds_own = (b_own.astype(F32) * (dot_nt(g, v_own) - delta)).astype(BF16)
            grad_q = scale * (dot(ds_pre, k_win) + dot(ds_own, k_own))
            for i, a in enumerate(heads):
                cols = slice(a * size, (a + 1) * size)
                one = grad_q[i * slot_len : (i + 1) * slot_len]
                dhq[rows, cols] = norm_back(hq[rows, cols], q_gain[...], one).astype(BF16)
            cols = slice(h * size, (h + 1) * size)
            grad_k = scale * dot_tn(ds_own, q)
            dhk[rows, cols] = norm_back(hk[rows, cols], k_gain[...], grad_k).astype(BF16)
            dv[rows, cols] = dot_tn(b_own, g).astype(BF16)
            k_cols = slice(2 * h * size, (2 * h + 1) * size)
            v_cols = slice((2 * h + 1) * size, (2 * h + 2) * size)
            grad_prefix[pl.ds(start, window), k_cols] += scale * dot_tn(ds_pre, q)
            grad_prefix[pl.ds(start, window), v_cols] += dot_tn(b_pre, g)
    chips = prefix_v.shape[0] // terms[0].shape[1] if len(terms) > 1 else 1
    for ref, steps in zip(terms, TERMS if len(terms) > 1 else ((0,),)):
        for i, step in enumerate(steps):
            ref[i] = grad_prefix[slot_rows(chips, ref.shape[1], step), :]

    def make(cols):
        return (
            dot_nt(dhq[...], w_q[cols, :])
            + dot_nt(dhk[...], w_k[cols, :])
            + dot_nt(dv[...], w_v[cols, :])
        ).astype(BF16)

    make_blocks(make, names, parts)


def backward(names, scalars, cotangent, kept, terms):
    slots = scalars[-1].shape[0]
    query, key, w_out, prefix = kept[0], kept[1], kept[10], kept[14]
    rows, q_width = query.shape
    k_width, depth = key.shape[1], w_out.shape[1]
    count, kv_width = prefix.shape
    results = [(x, F32) for x in terms] + block_shapes(names, rows, cotangent[0].shape[2])
    found = pl.pallas_call(
        functools.partial(backward_kernel, slots, names),
        in_specs=[SMEM] * 3 + [VMEM] * (len(cotangent) + len(kept)),
        out_specs=[VMEM] * len(results),
        out_shape=in_vmem(results),
        scratch_shapes=[
            pltpu.VMEM((count, kv_width), F32),
            pltpu.VMEM((rows, q_width), BF16),
            pltpu.VMEM((rows, k_width), BF16),
            pltpu.VMEM((rows, k_width), BF16),
        ],
        compiler_params=pltpu.CompilerParams(vmem_limit_bytes=vmem_room(count)),
        cost_estimate=lasting(3.5),
    )(*held_in(pltpu.SMEM, scalars), *held_in(pltpu.VMEM, [*cotangent, *kept]))
    return found[: len(terms)], found[len(terms) :]


def last_kernel(counts, *refs):
    take, rest = taker(refs)
    groups = [take(len(count)) for count in counts]
    results = take(len(counts))
    stage = take(len(counts))
    (sems,) = take(1)
    copies = Copies(sems)
    stores = []
    for count, group, result, ref in zip(counts, groups, results, stage):
        whole = 0.0
        for i, term in zip(count, group):
            whole = whole + term[i].astype(F32)
        ref[...] = whole.astype(BF16)
        stores.append(copies.start(ref, result))
    wait(stores)


def last_sums(groups):
    arrays = [array for group in groups for array, _ in group]
    shapes = [jax.ShapeDtypeStruct(group[0][0].shape[1:], BF16) for group in groups]
    return pl.pallas_call(
        functools.partial(last_kernel, [[i for _, i in group] for group in groups]),
        in_specs=[VMEM] * len(arrays),
        out_specs=[HBM] * len(groups),
        out_shape=shapes,
        scratch_shapes=in_vmem(like(shapes)) + [pltpu.SemaphoreType.DMA((len(groups),))],
        compiler_params=pltpu.CompilerParams(vmem_limit_bytes=vmem_room(0)),
        cost_estimate=lasting(0.9),
    )(*held_in(pltpu.VMEM, arrays))


def trade(name, block, axis, step):
    with jax.named_scope(name):
        return lax.ppermute(block, axis, [(i, i ^ step) for i in range(lax.axis_size(axis))])


def after(value, *others):
    return lax.optimization_barrier((value, *others))[0]


def total(*terms):
    whole = terms[0].astype(F32)
    for term in terms[1:]:
        whole = whole + term.astype(F32)
    return whole.astype(BF16)


def per_device(
    hidden_rows,
    w_query,
    w_key,
    w_value,
    w_out,
    q_gain,
    k_gain,
    prefix_kv,
    cotangent,
    prompt_len,
    resp_prompt,
    resp_len,
):
    chips = lax.axis_size("dp")
    scalars = (prompt_len, resp_prompt, resp_len)
    q_gain, k_gain = q_gain[None], k_gain[None]
    own = cotangent[None]
    far = trade("gather_far", own, "mp", 4)
    near = trade("gather_near", own, "mp", 2)
    if chips == 4:
        others = [trade("gather_prefix", prefix_kv, "dp", k) for k in range(1, chips)]
    else:
        prefix_kv, others = lax.all_gather(prefix_kv, "dp", axis=0, tiled=True), []
    far = after(far, *others)
    both = trade("gather_both", far, "mp", 2)
    pair = jnp.concatenate([far, near])
    pair_x = trade("gather_pair_x", pair, "mp", 1)
    own_x = trade("gather_own_x", own, "mp", 1)
    scalars, projected, weights, prefix, own = project(
        scalars, after(hidden_rows, far), w_query, w_key, w_value, q_gain, k_gain, w_out,
        prefix_kv, own,
    )
    both_x = trade("gather_both_x", after(both, projected[0]), "mp", 1)
    probed, parts = forward(
        OUT, cotangent.shape[1], q_gain.shape[1], scalars, *projected[:3], weights[5],
        [prefix, *others],
    )
    back = [own, pair, both, own_x, pair_x, both_x]
    shape = prefix_kv.shape
    terms = [(1, *shape)] if chips != 4 else [(len(steps), *shape) for steps in TERMS]
    terms, grads = backward(IN, scalars, back, [*projected, *weights, *probed], terms)

    out_a, out_b, kept_a, kept_b = parts
    got_a = trade("out_a", out_a, "mp", 2)
    got_b = trade("out_b", after(out_b, pair_x), "mp", 2)
    out_a = total(kept_a, got_a)
    got_out = trade("out_mid", out_a, "mp", 4)
    in_75, in_3, in_1, in_6, in_4, in_2, in_0 = grads
    got_75 = trade("in_75", in_75, "mp", 1)
    got_3 = trade("in_3", in_3, "mp", 1)
    in_6 = total(after(in_6, out_a), got_75[:1])
    got_6 = trade("in_6", in_6, "mp", 2)
    in_2 = total(in_2, got_3)
    got_2 = trade("in_2", in_2, "mp", 2)
    got_1 = trade("in_1", after(in_1, in_2), "mp", 1)
    if chips == 4:
        got = trade("grad_prefix_core", after(terms[0], in_2), "dp", 1)
        last = trade("grad_prefix_y", terms[1][1:] + got[1:], "dp", 2)
    in_4 = total(after(in_4, got_b, got_out, in_2), got_75[1:], got_6)
    got_4 = trade("in_4", in_4, "mp", 4)
    got_x = trade("out_x", total(after(kept_b, in_4)[1:], got_b[1:], got_out[1:]), "mp", 1)
    groups = [
        [(kept_b, 0), (got_b, 0), (got_out, 0), (got_x, 0)],
        [(in_0, 0), (got_1, 0), (got_2, 0), (got_4, 0)],
    ]
    if chips == 4:
        groups.append([(terms[1], 0), (got, 0), (last, 0)])
        return last_sums(groups)
    grad_prefix = lax.psum_scatter(terms[0][0], "dp", scatter_dimension=0, tiled=True)
    return *last_sums(groups), grad_prefix.astype(BF16)


def solution(mesh):
    in_specs = (
        P("dp", None),
        P(None, "mp"),
        P(None, "mp"),
        P(None, "mp"),
        P("mp", None),
        P(),
        P(),
        P("dp", "mp"),
        P("dp", "mp"),
        P(),
        P("dp"),
        P("dp"),
    )
    out_specs = (P("dp", "mp"), P("dp", "mp"), P("dp", "mp"))
    return jax.shard_map(
        per_device, mesh=mesh, in_specs=in_specs, out_specs=out_specs, check_vma=False
    )
```

```python
import functools

import jax
import jax.numpy as jnp
from jax import lax
from jax.experimental import pallas as pl
from jax.experimental.pallas import tpu as pltpu
from jax.sharding import PartitionSpec as P

EPS = 1e-06
NEG = -1e30
ROWS = 16
HELD = ((0,), (4, 2), (6,), (1,), (5, 3), (7,))
OUT = ((6, 7), (2, 3), (4, 5), (0, 1))
TERMS = ((1, 3), (0, 2))
IN = ((7, 5), (3,), (1,), (6,), (4,), (2,), (0,))
F32 = jnp.float32
BF16 = jnp.bfloat16
HBM = pl.BlockSpec(memory_space=pltpu.HBM)
SMEM = pl.BlockSpec(memory_space=pltpu.SMEM)
VMEM = pl.BlockSpec(memory_space=pltpu.VMEM)


def dot(left, right):
    return jnp.dot(left, right, preferred_element_type=F32)


def dot_nt(left, right):
    return lax.dot_general(left, right, (((1,), (1,)), ((), ())), preferred_element_type=F32)


def dot_tn(left, right):
    return lax.dot_general(left, right, (((0,), (0,)), ((), ())), preferred_element_type=F32)


def inverse_root(hidden):
    return lax.rsqrt(jnp.mean(hidden * hidden, axis=-1, keepdims=True) + EPS)


def norm_back(hidden, gain, grad):
    root = inverse_root(hidden)
    unit = hidden * root
    scaled = grad * gain
    return root * (scaled - unit * jnp.mean(scaled * unit, axis=-1, keepdims=True))


class Copies:
    def __init__(self, sems):
        self.sems, self.count = sems, 0

    def start(self, source, target):
        copy = pltpu.make_async_copy(source, target, self.sems.at[self.count])
        self.count += 1
        copy.start()
        return copy


def wait(copies):
    for copy in copies:
        copy.wait()


def prompt_span(prompt_len, prompt):
    first, last = 0, 0
    end = 0
    for p in range(prompt_len.shape[0]):
        begin = end
        end = end + prompt_len[p]
        first = jnp.where(prompt == p, begin, first)
        last = jnp.where(prompt == p, end, last)
    return first, last


def window_rows(count):
    return min(count, count // 3 + ROWS)


def window_start(first, count):
    start = jnp.minimum(first // ROWS * ROWS, count - window_rows(count))
    return pl.multiple_of(start, ROWS)


def slot_rows(slots, rows, step):
    if slots == 1:
        return pl.ds(0, rows)
    return pl.ds(pl.multiple_of((lax.axis_index("dp") ^ step) * rows, ROWS), rows)


def features(block, width):
    return pl.ds(pl.multiple_of(block * width, width), width)


def stacked(ref, rows, heads, size):
    return jnp.concatenate([ref[rows, a * size : (a + 1) * size] for a in heads], axis=0)


def make_blocks(make, names, refs):
    me = lax.axis_index("mp")
    for blocks, ref in zip(names, refs):
        for i, block in enumerate(blocks):
            ref[i] = make(features(me ^ block, ref.shape[-1]))


def taker(refs):
    refs = list(refs)

    def take(count):
        found, refs[:count] = refs[:count], []
        return found

    return take, refs


def project_kernel(*refs):
    take, _ = taker(refs)
    scalars = take(3)
    hidden, w_q, w_k, w_v, q_gain, k_gain, prefix, own = take(8)
    scalars_v = take(3)
    query, key, value, hq, hk = take(5)
    wq_v, wk_v, wv_v, qg_v, kg_v, prefix_v, own_v = take(7)
    hidden_v, sems = take(2)

    copies = Copies(sems)
    depth = hidden.shape[1]
    steps = 4
    part = depth // steps
    loads = []
    for i in range(steps):
        cut = pl.ds(i * part, part)
        loads.append(
            [copies.start(hidden.at[:, cut], hidden_v.at[:, cut])]
            + [
                copies.start(w.at[cut], v.at[cut])
                for w, v in ((w_q, wq_v), (w_k, wk_v), (w_v, wv_v))
            ]
        )
    small = [copies.start(q_gain, qg_v), copies.start(k_gain, kg_v)]
    small += [copies.start(source, target) for source, target in zip(scalars, scalars_v)]
    small += [copies.start(prefix, prefix_v), copies.start(own, own_v)]

    sums = [None] * 3
    for i, load in enumerate(loads):
        wait(load)
        rows = hidden_v[:, i * part : (i + 1) * part]
        for j, v in enumerate((wq_v, wk_v, wv_v)):
            term = dot(rows, v[i * part : (i + 1) * part])
            sums[j] = term if i == 0 else sums[j] + term
    hq[...], hk[...] = sums[0], sums[1]
    value[...] = sums[2].astype(BF16)
    wait(small)
    size = qg_v.shape[1]
    for whole, gain, out in ((sums[0], qg_v, query), (sums[1], kg_v, key)):
        for at in range(0, whole.shape[1], size):
            head = whole[:, at : at + size]
            out[:, at : at + size] = (head * inverse_root(head) * gain[...]).astype(BF16)


def project(scalars, hidden, w_q, w_k, w_v, q_gain, k_gain, prefix, own):
    rows, depth = hidden.shape
    q_width, k_width = w_q.shape[1], w_k.shape[1]
    weights = [w_q, w_k, w_v, q_gain, k_gain, prefix, own]
    operands = [*scalars, hidden, *weights]
    kept = [
        ((rows, q_width), BF16),
        ((rows, k_width), BF16),
        ((rows, k_width), BF16),
        ((rows, q_width), F32),
        ((rows, k_width), F32),
    ] + like(weights)
    found = pl.pallas_call(
        project_kernel,
        in_specs=[HBM] * len(operands),
        out_specs=[SMEM] * 3 + [VMEM] * len(kept),
        out_shape=[pltpu.SMEM(x.shape, jnp.int32) for x in scalars] + in_vmem(kept),
        scratch_shapes=[pltpu.VMEM(hidden.shape, hidden.dtype), pltpu.SemaphoreType.DMA((32,))],
        compiler_params=pltpu.CompilerParams(vmem_limit_bytes=vmem_room(prefix.shape[0])),
        cost_estimate=lasting(2.6),
    )(*held_in(pltpu.HBM, operands))
    return found[:3], found[3:8], found[8:13], found[13], found[14]


def forward_kernel(slots, names, *refs):
    take, rest = taker(refs)
    prompt_len, resp_prompt, resp_len = take(3)
    query, key, value, wo_v = take(4)
    prefix = take(len(rest) - 4 - len(names) - 1)
    p_pre, p_own, heads_out, prefix_v = take(4)
    parts = take(len(names))
    (out_bf,) = take(1)

    held = prefix[0].shape[0]
    for k, ref in enumerate(prefix):
        prefix_v[slot_rows(len(prefix), held, k), :] = ref[...]
    size = heads_out.shape[1] * p_own.shape[3] // p_own.shape[2] // p_own.shape[1]
    count = prefix_v.shape[0]
    window = window_rows(count)
    slot_len = query.shape[0] // slots
    kv_heads = key.shape[1] // size
    groups = query.shape[1] // key.shape[1]
    scale = size ** (-0.5)
    for n in range(slots):
        first, last = prompt_span(prompt_len, resp_prompt[n])
        start = window_start(first, count)
        rows = slice(n * slot_len, (n + 1) * slot_len)
        live = lax.broadcasted_iota(jnp.int32, (slot_len, size), 0) < resp_len[n]
        for h in range(kv_heads):
            heads = range(h * groups, (h + 1) * groups)
            q = stacked(query, rows, heads, size)
            k_win = prefix_v[pl.ds(start, window), 2 * h * size : (2 * h + 1) * size]
            v_win = prefix_v[pl.ds(start, window), (2 * h + 1) * size : (2 * h + 2) * size]
            k_own = key[rows, h * size : (h + 1) * size]
            v_own = value[rows, h * size : (h + 1) * size]
            tall = groups * slot_len
            place = start + lax.broadcasted_iota(jnp.int32, (tall, window), 1)
            s_pre = jnp.where((place >= first) & (place < last), dot_nt(q, k_win) * scale, NEG)
            token = lax.broadcasted_iota(jnp.int32, (groups, slot_len, slot_len), 1)
            token = token.reshape(tall, slot_len)
            other = lax.broadcasted_iota(jnp.int32, (tall, slot_len), 1)
            s_own = jnp.where(
                (other <= token) & (other < resp_len[n]), dot_nt(q, k_own) * scale, NEG
            )
            top = jnp.maximum(
                jnp.max(s_pre, axis=-1, keepdims=True), jnp.max(s_own, axis=-1, keepdims=True)
            )
            e_pre = jnp.exp(s_pre - top)
            e_own = jnp.exp(s_own - top)
            total = jnp.sum(e_pre, axis=-1, keepdims=True) + jnp.sum(e_own, axis=-1, keepdims=True)
            b_pre = (e_pre / total).astype(BF16)
            b_own = (e_own / total).astype(BF16)
            p_pre[n, h] = b_pre
            p_own[n, h] = b_own
            out = dot(b_pre, v_win) + dot(b_own, v_own)
            for i, a in enumerate(heads):
                one = out[i * slot_len : (i + 1) * slot_len]
                heads_out[rows, a * size : (a + 1) * size] = one
                out_bf[rows, a * size : (a + 1) * size] = jnp.where(live, one, 0.0).astype(BF16)

    def make(cols):
        return dot(out_bf[...], wo_v[:, cols]).astype(BF16)

    make_blocks(make, names, parts)


def block_shapes(names, rows, width):
    return [((len(blocks), rows, width), BF16) for blocks in names]


def in_vmem(shapes):
    return [pltpu.VMEM(*x) for x in shapes]


def held_in(space, arrays):
    return [pltpu.with_memory_space_constraint(x, space) for x in arrays]


def lasting(us):
    return pl.CostEstimate(flops=int(us * 1.15e9), bytes_accessed=0, transcendentals=0)


def like(arrays):
    return [(x.shape, x.dtype) for x in arrays]


def vmem_room(prefix_rows):
    return 48 << 20 if prefix_rows > 1024 else 24 << 20


def forward(names, width, size, scalars, query, key, value, w_out, prefix):
    slots = scalars[-1].shape[0]
    rows, q_width = query.shape
    k_width = key.shape[1]
    count = sum(x.shape[0] for x in prefix)
    window = window_rows(count)
    slot_len = rows // slots
    kv_heads, tall = k_width // size, slot_len * q_width // k_width
    results = [
        ((slots, kv_heads, tall, window), BF16),
        ((slots, kv_heads, tall, slot_len), BF16),
        ((rows, q_width), F32),
        ((count, prefix[0].shape[1]), BF16),
    ] + block_shapes(names, rows, width)
    operands = [query, key, value, w_out, *prefix]
    found = pl.pallas_call(
        functools.partial(forward_kernel, slots, names),
        in_specs=[SMEM] * 3 + [VMEM] * len(operands),
        out_specs=[VMEM] * len(results),
        out_shape=in_vmem(results),
        scratch_shapes=[pltpu.VMEM((rows, q_width), BF16)],
        compiler_params=pltpu.CompilerParams(vmem_limit_bytes=vmem_room(count)),
        cost_estimate=lasting(1.7),
    )(*held_in(pltpu.SMEM, scalars), *held_in(pltpu.VMEM, operands))
    return found[:4], found[4:]


def backward_kernel(slots, names, *refs):
    take, rest = taker(refs)
    prompt_len, resp_prompt, resp_len = take(3)
    cotangent = take(len(HELD))
    query, key, value, hq, hk = take(5)
    w_q, w_k, w_v, q_gain, k_gain, w_out = take(6)
    p_pre, p_own, heads_out, prefix_v = take(4)
    terms = take(len(rest) - len(names) - 4)
    parts = take(len(names))
    grad_prefix, dhq, dhk, dv = take(4)

    width = cotangent[0].shape[2]
    me = lax.axis_index("mp")
    grad_heads = 0.0
    for blocks, ref in zip(HELD, cotangent):
        for i, block in enumerate(blocks):
            grad_heads += dot_nt(ref[i], w_out[:, features(me ^ block, width)])
    grad_prefix[...] = jnp.zeros_like(grad_prefix)

    count = prefix_v.shape[0]
    window = window_rows(count)
    slot_len = query.shape[0] // slots
    size = q_gain.shape[1]
    kv_heads = key.shape[1] // size
    groups = query.shape[1] // key.shape[1]
    scale = size ** (-0.5)
    for n in range(slots):
        first, _ = prompt_span(prompt_len, resp_prompt[n])
        start = window_start(first, count)
        rows = slice(n * slot_len, (n + 1) * slot_len)
        live = lax.broadcasted_iota(jnp.int32, (slot_len, size), 0) < resp_len[n]
        for h in range(kv_heads):
            heads = range(h * groups, (h + 1) * groups)
            q = stacked(query, rows, heads, size)
            out = stacked(heads_out, rows, heads, size)
            g = jnp.concatenate(
                [
                    jnp.where(live, grad_heads[rows, a * size : (a + 1) * size], 0.0).astype(BF16)
                    for a in heads
                ],
                axis=0,
            )
            k_win = prefix_v[pl.ds(start, window), 2 * h * size : (2 * h + 1) * size]
            v_win = prefix_v[pl.ds(start, window), (2 * h + 1) * size : (2 * h + 2) * size]
            k_own = key[rows, h * size : (h + 1) * size]
            v_own = value[rows, h * size : (h + 1) * size]
            b_pre, b_own = p_pre[n, h], p_own[n, h]
            delta = jnp.sum(g.astype(F32) * out, axis=-1, keepdims=True)
            ds_pre = (b_pre.astype(F32) * (dot_nt(g, v_win) - delta)).astype(BF16)
            ds_own = (b_own.astype(F32) * (dot_nt(g, v_own) - delta)).astype(BF16)
            grad_q = scale * (dot(ds_pre, k_win) + dot(ds_own, k_own))
            for i, a in enumerate(heads):
                cols = slice(a * size, (a + 1) * size)
                one = grad_q[i * slot_len : (i + 1) * slot_len]
                dhq[rows, cols] = norm_back(hq[rows, cols], q_gain[...], one).astype(BF16)
            cols = slice(h * size, (h + 1) * size)
            grad_k = scale * dot_tn(ds_own, q)
            dhk[rows, cols] = norm_back(hk[rows, cols], k_gain[...], grad_k).astype(BF16)
            dv[rows, cols] = dot_tn(b_own, g).astype(BF16)
            k_cols = slice(2 * h * size, (2 * h + 1) * size)
            v_cols = slice((2 * h + 1) * size, (2 * h + 2) * size)
            grad_prefix[pl.ds(start, window), k_cols] += scale * dot_tn(ds_pre, q)
            grad_prefix[pl.ds(start, window), v_cols] += dot_tn(b_pre, g)
    chips = prefix_v.shape[0] // terms[0].shape[1] if len(terms) > 1 else 1
    for ref, steps in zip(terms, TERMS if len(terms) > 1 else ((0,),)):
        for i, step in enumerate(steps):
            ref[i] = grad_prefix[slot_rows(chips, ref.shape[1], step), :]

    def make(cols):
        return (
            dot_nt(dhq[...], w_q[cols, :])
            + dot_nt(dhk[...], w_k[cols, :])
            + dot_nt(dv[...], w_v[cols, :])
        ).astype(BF16)

    make_blocks(make, names, parts)


def backward(names, scalars, cotangent, kept, terms):
    slots = scalars[-1].shape[0]
    query, key, w_out, prefix = kept[0], kept[1], kept[10], kept[14]
    rows, q_width = query.shape
    k_width, depth = key.shape[1], w_out.shape[1]
    count, kv_width = prefix.shape
    results = [(x, F32) for x in terms] + block_shapes(names, rows, cotangent[0].shape[2])
    found = pl.pallas_call(
        functools.partial(backward_kernel, slots, names),
        in_specs=[SMEM] * 3 + [VMEM] * (len(cotangent) + len(kept)),
        out_specs=[VMEM] * len(results),
        out_shape=in_vmem(results),
        scratch_shapes=[
            pltpu.VMEM((count, kv_width), F32),
            pltpu.VMEM((rows, q_width), BF16),
            pltpu.VMEM((rows, k_width), BF16),
            pltpu.VMEM((rows, k_width), BF16),
        ],
        compiler_params=pltpu.CompilerParams(vmem_limit_bytes=vmem_room(count)),
        cost_estimate=lasting(3.5),
    )(*held_in(pltpu.SMEM, scalars), *held_in(pltpu.VMEM, [*cotangent, *kept]))
    return found[: len(terms)], found[len(terms) :]


def last_kernel(counts, *refs):
    take, rest = taker(refs)
    groups = [take(len(count)) for count in counts]
    results = take(len(counts))
    stage = take(len(counts))
    (sems,) = take(1)
    copies = Copies(sems)
    stores = []
    for count, group, result, ref in zip(counts, groups, results, stage):
        whole = 0.0
        for i, term in zip(count, group):
            whole = whole + term[i].astype(F32)
        ref[...] = whole.astype(BF16)
        stores.append(copies.start(ref, result))
    wait(stores)


def last_sums(groups):
    arrays = [array for group in groups for array, _ in group]
    shapes = [jax.ShapeDtypeStruct(group[0][0].shape[1:], BF16) for group in groups]
    return pl.pallas_call(
        functools.partial(last_kernel, [[i for _, i in group] for group in groups]),
        in_specs=[VMEM] * len(arrays),
        out_specs=[HBM] * len(groups),
        out_shape=shapes,
        scratch_shapes=in_vmem(like(shapes)) + [pltpu.SemaphoreType.DMA((len(groups),))],
        compiler_params=pltpu.CompilerParams(vmem_limit_bytes=vmem_room(0)),
        cost_estimate=lasting(0.9),
    )(*held_in(pltpu.VMEM, arrays))


def trade(name, block, axis, step):
    with jax.named_scope(name):
        return lax.ppermute(block, axis, [(i, i ^ step) for i in range(lax.axis_size(axis))])


def after(value, *others):
    return lax.optimization_barrier((value, *others))[0]


def total(*terms):
    whole = terms[0].astype(F32)
    for term in terms[1:]:
        whole = whole + term.astype(F32)
    return whole.astype(BF16)


def per_device(
    hidden_rows,
    w_query,
    w_key,
    w_value,
    w_out,
    q_gain,
    k_gain,
    prefix_kv,
    cotangent,
    prompt_len,
    resp_prompt,
    resp_len,
):
    chips = lax.axis_size("dp")
    scalars = (prompt_len, resp_prompt, resp_len)
    q_gain, k_gain = q_gain[None], k_gain[None]
    own = cotangent[None]
    far = trade("gather_far", own, "mp", 4)
    near = trade("gather_near", own, "mp", 2)
    if chips == 4:
        others = [trade("gather_prefix", prefix_kv, "dp", k) for k in range(1, chips)]
    else:
        prefix_kv, others = lax.all_gather(prefix_kv, "dp", axis=0, tiled=True), []
    far = after(far, *others)
    both = trade("gather_both", far, "mp", 2)
    pair = jnp.concatenate([far, near])
    pair_x = trade("gather_pair_x", pair, "mp", 1)
    own_x = trade("gather_own_x", own, "mp", 1)
    scalars, projected, weights, prefix, own = project(
        scalars, after(hidden_rows, far), w_query, w_key, w_value, q_gain, k_gain, prefix_kv, own
    )
    both_x = trade("gather_both_x", after(both, projected[0]), "mp", 1)
    probed, parts = forward(
        OUT, cotangent.shape[1], q_gain.shape[1], scalars, *projected[:3], w_out,
        [prefix, *others],
    )
    back = [own, pair, both, own_x, pair_x, both_x]
    shape = prefix_kv.shape
    terms = [(1, *shape)] if chips != 4 else [(len(steps), *shape) for steps in TERMS]
    terms, grads = backward(IN, scalars, back, [*projected, *weights, w_out, *probed], terms)

    out_a, out_b, kept_a, kept_b = parts
    got_a = trade("out_a", out_a, "mp", 2)
    got_b = trade("out_b", after(out_b, pair_x), "mp", 2)
    out_a = total(kept_a, got_a)
    got_out = trade("out_mid", out_a, "mp", 4)
    in_75, in_3, in_1, in_6, in_4, in_2, in_0 = grads
    got_75 = trade("in_75", in_75, "mp", 1)
    got_3 = trade("in_3", in_3, "mp", 1)
    in_6 = total(after(in_6, out_a), got_75[:1])
    got_6 = trade("in_6", in_6, "mp", 2)
    in_2 = total(in_2, got_3)
    got_2 = trade("in_2", in_2, "mp", 2)
    if chips == 4:
        got = trade("grad_prefix_core", after(terms[0], in_2), "dp", 1)
        last = trade("grad_prefix_y", terms[1][1:] + got[1:], "dp", 2)
    in_4 = total(after(in_4, got_b, got_out, in_2), got_75[1:], got_6)
    got_4 = trade("in_4", in_4, "mp", 4)
    got_1 = trade("in_1", after(in_1, in_4), "mp", 1)
    got_x = trade("out_x", total(after(kept_b, in_4)[1:], got_b[1:], got_out[1:]), "mp", 1)
    groups = [
        [(kept_b, 0), (got_b, 0), (got_out, 0), (got_x, 0)],
        [(in_0, 0), (got_1, 0), (got_2, 0), (got_4, 0)],
    ]
    if chips == 4:
        groups.append([(terms[1], 0), (got, 0), (last, 0)])
        return last_sums(groups)
    grad_prefix = lax.psum_scatter(terms[0][0], "dp", scatter_dimension=0, tiled=True)
    return *last_sums(groups), grad_prefix.astype(BF16)


def solution(mesh):
    in_specs = (
        P("dp", None),
        P(None, "mp"),
        P(None, "mp"),
        P(None, "mp"),
        P("mp", None),
        P(),
        P(),
        P("dp", "mp"),
        P("dp", "mp"),
        P(),
        P("dp"),
        P("dp"),
    )
    out_specs = (P("dp", "mp"), P("dp", "mp"), P("dp", "mp"))
    return jax.shard_map(
        per_device, mesh=mesh, in_specs=in_specs, out_specs=out_specs, check_vma=False
    )
```

```python
import functools

import jax
import jax.numpy as jnp
from jax import lax
from jax.experimental import pallas as pl
from jax.experimental.pallas import tpu as pltpu
from jax.sharding import PartitionSpec as P

EPS = 1e-06
NEG = -1e30
ROWS = 16
HELD = ((0,), (4, 2), (6,), (1,), (5, 3), (7,))
OUT = ((6, 7), (2, 3), (4, 5), (0, 1))
TERMS = ((1, 3), (0, 2))
IN = ((7, 5), (3,), (1,), (6,), (4,), (2,), (0,))
F32 = jnp.float32
BF16 = jnp.bfloat16
HBM = pl.BlockSpec(memory_space=pltpu.HBM)
SMEM = pl.BlockSpec(memory_space=pltpu.SMEM)
VMEM = pl.BlockSpec(memory_space=pltpu.VMEM)


def dot(left, right):
    return jnp.dot(left, right, preferred_element_type=F32)


def dot_nt(left, right):
    return lax.dot_general(left, right, (((1,), (1,)), ((), ())), preferred_element_type=F32)


def dot_tn(left, right):
    return lax.dot_general(left, right, (((0,), (0,)), ((), ())), preferred_element_type=F32)


def inverse_root(hidden):
    return lax.rsqrt(jnp.mean(hidden * hidden, axis=-1, keepdims=True) + EPS)


def norm_back(hidden, gain, grad):
    root = inverse_root(hidden)
    unit = hidden * root
    scaled = grad * gain
    return root * (scaled - unit * jnp.mean(scaled * unit, axis=-1, keepdims=True))


class Copies:
    def __init__(self, sems):
        self.sems, self.count = sems, 0

    def start(self, source, target):
        copy = pltpu.make_async_copy(source, target, self.sems.at[self.count])
        self.count += 1
        copy.start()
        return copy


def wait(copies):
    for copy in copies:
        copy.wait()


def prompt_span(prompt_len, prompt):
    first, last = 0, 0
    end = 0
    for p in range(prompt_len.shape[0]):
        begin = end
        end = end + prompt_len[p]
        first = jnp.where(prompt == p, begin, first)
        last = jnp.where(prompt == p, end, last)
    return first, last


def window_rows(count):
    return min(count, count // 3 + ROWS)


def window_start(first, count):
    start = jnp.minimum(first // ROWS * ROWS, count - window_rows(count))
    return pl.multiple_of(start, ROWS)


def slot_rows(slots, rows, step):
    if slots == 1:
        return pl.ds(0, rows)
    return pl.ds(pl.multiple_of((lax.axis_index("dp") ^ step) * rows, ROWS), rows)


def features(block, width):
    return pl.ds(pl.multiple_of(block * width, width), width)


def stacked(ref, rows, heads, size):
    return jnp.concatenate([ref[rows, a * size : (a + 1) * size] for a in heads], axis=0)


def make_blocks(make, names, refs):
    me = lax.axis_index("mp")
    for blocks, ref in zip(names, refs):
        for i, block in enumerate(blocks):
            ref[i] = make(features(me ^ block, ref.shape[-1]))


def taker(refs):
    refs = list(refs)

    def take(count):
        found, refs[:count] = refs[:count], []
        return found

    return take, refs


def project_kernel(*refs):
    take, _ = taker(refs)
    scalars = take(3)
    hidden, w_q, w_k, w_v, q_gain, k_gain, prefix, own = take(8)
    scalars_v = take(3)
    query, key, value, hq, hk = take(5)
    w_all, qg_v, kg_v, prefix_v, own_v = take(5)
    hidden_v, sems = take(2)

    copies = Copies(sems)
    depth = hidden.shape[1]
    steps = 4
    part = depth // steps
    places, end = [], 0
    for w in (w_q, w_k, w_v):
        places.append(slice(end, end + w.shape[1]))
        end += w.shape[1]
    loads = []
    for i in range(steps):
        cut = pl.ds(i * part, part)
        loads.append(
            [copies.start(hidden.at[:, cut], hidden_v.at[:, cut])]
            + [
                copies.start(w.at[cut], w_all.at[cut, place])
                for w, place in zip((w_q, w_k, w_v), places)
            ]
        )
    small = [copies.start(q_gain, qg_v), copies.start(k_gain, kg_v)]
    small += [copies.start(source, target) for source, target in zip(scalars, scalars_v)]
    small += [copies.start(prefix, prefix_v), copies.start(own, own_v)]

    whole = 0.0
    for i, load in enumerate(loads):
        wait(load)
        cut = slice(i * part, (i + 1) * part)
        whole += dot(hidden_v[:, cut], w_all[cut, :])
    hq[...], hk[...] = whole[:, places[0]], whole[:, places[1]]
    value[...] = whole[:, places[2]].astype(BF16)
    wait(small)
    size = qg_v.shape[1]
    for ref, gain, out in ((hq, qg_v, query), (hk, kg_v, key)):
        for at in range(0, ref.shape[1], size):
            head = ref[:, at : at + size]
            out[:, at : at + size] = (head * inverse_root(head) * gain[...]).astype(BF16)


def project(scalars, hidden, w_q, w_k, w_v, q_gain, k_gain, prefix, own):
    rows, depth = hidden.shape
    q_width, k_width = w_q.shape[1], w_k.shape[1]
    small = [q_gain, k_gain, prefix, own]
    operands = [*scalars, hidden, w_q, w_k, w_v, *small]
    kept = [
        ((rows, q_width), BF16),
        ((rows, k_width), BF16),
        ((rows, k_width), BF16),
        ((rows, q_width), F32),
        ((rows, k_width), F32),
        ((depth, q_width + 2 * k_width), BF16),
    ] + like(small)
    found = pl.pallas_call(
        project_kernel,
        in_specs=[HBM] * len(operands),
        out_specs=[SMEM] * 3 + [VMEM] * len(kept),
        out_shape=[pltpu.SMEM(x.shape, jnp.int32) for x in scalars] + in_vmem(kept),
        scratch_shapes=[pltpu.VMEM(hidden.shape, hidden.dtype), pltpu.SemaphoreType.DMA((32,))],
        compiler_params=pltpu.CompilerParams(vmem_limit_bytes=vmem_room(prefix.shape[0])),
        cost_estimate=lasting(2.6),
    )(*held_in(pltpu.HBM, operands))
    return found[:3], found[3:8], found[8:11], found[11], found[12]


def forward_kernel(slots, names, *refs):
    take, rest = taker(refs)
    prompt_len, resp_prompt, resp_len = take(3)
    query, key, value, wo_v = take(4)
    prefix = take(len(rest) - 4 - len(names) - 1)
    p_pre, p_own, heads_out, prefix_v = take(4)
    parts = take(len(names))
    (out_bf,) = take(1)

    held = prefix[0].shape[0]
    for k, ref in enumerate(prefix):
        prefix_v[slot_rows(len(prefix), held, k), :] = ref[...]
    size = heads_out.shape[1] * p_own.shape[3] // p_own.shape[2] // p_own.shape[1]
    count = prefix_v.shape[0]
    window = window_rows(count)
    slot_len = query.shape[0] // slots
    kv_heads = key.shape[1] // size
    groups = query.shape[1] // key.shape[1]
    scale = size ** (-0.5)
    for n in range(slots):
        first, last = prompt_span(prompt_len, resp_prompt[n])
        start = window_start(first, count)
        rows = slice(n * slot_len, (n + 1) * slot_len)
        live = lax.broadcasted_iota(jnp.int32, (slot_len, size), 0) < resp_len[n]
        for h in range(kv_heads):
            heads = range(h * groups, (h + 1) * groups)
            q = stacked(query, rows, heads, size)
            k_win = prefix_v[pl.ds(start, window), 2 * h * size : (2 * h + 1) * size]
            v_win = prefix_v[pl.ds(start, window), (2 * h + 1) * size : (2 * h + 2) * size]
            k_own = key[rows, h * size : (h + 1) * size]
            v_own = value[rows, h * size : (h + 1) * size]
            tall = groups * slot_len
            place = start + lax.broadcasted_iota(jnp.int32, (tall, window), 1)
            s_pre = jnp.where((place >= first) & (place < last), dot_nt(q, k_win) * scale, NEG)
            token = lax.broadcasted_iota(jnp.int32, (groups, slot_len, slot_len), 1)
            token = token.reshape(tall, slot_len)
            other = lax.broadcasted_iota(jnp.int32, (tall, slot_len), 1)
            s_own = jnp.where(
                (other <= token) & (other < resp_len[n]), dot_nt(q, k_own) * scale, NEG
            )
            top = jnp.maximum(
                jnp.max(s_pre, axis=-1, keepdims=True), jnp.max(s_own, axis=-1, keepdims=True)
            )
            e_pre = jnp.exp(s_pre - top)
            e_own = jnp.exp(s_own - top)
            total = jnp.sum(e_pre, axis=-1, keepdims=True) + jnp.sum(e_own, axis=-1, keepdims=True)
            b_pre = (e_pre / total).astype(BF16)
            b_own = (e_own / total).astype(BF16)
            p_pre[n, h] = b_pre
            p_own[n, h] = b_own
            out = dot(b_pre, v_win) + dot(b_own, v_own)
            for i, a in enumerate(heads):
                one = out[i * slot_len : (i + 1) * slot_len]
                heads_out[rows, a * size : (a + 1) * size] = one
                out_bf[rows, a * size : (a + 1) * size] = jnp.where(live, one, 0.0).astype(BF16)

    def make(cols):
        return dot(out_bf[...], wo_v[:, cols]).astype(BF16)

    make_blocks(make, names, parts)


def block_shapes(names, rows, width):
    return [((len(blocks), rows, width), BF16) for blocks in names]


def in_vmem(shapes):
    return [pltpu.VMEM(*x) for x in shapes]


def held_in(space, arrays):
    return [pltpu.with_memory_space_constraint(x, space) for x in arrays]


def lasting(us):
    return pl.CostEstimate(flops=int(us * 1.15e9), bytes_accessed=0, transcendentals=0)


def like(arrays):
    return [(x.shape, x.dtype) for x in arrays]


def vmem_room(prefix_rows):
    return 48 << 20 if prefix_rows > 1024 else 24 << 20


def forward(names, width, size, scalars, query, key, value, w_out, prefix):
    slots = scalars[-1].shape[0]
    rows, q_width = query.shape
    k_width = key.shape[1]
    count = sum(x.shape[0] for x in prefix)
    window = window_rows(count)
    slot_len = rows // slots
    kv_heads, tall = k_width // size, slot_len * q_width // k_width
    results = [
        ((slots, kv_heads, tall, window), BF16),
        ((slots, kv_heads, tall, slot_len), BF16),
        ((rows, q_width), F32),
        ((count, prefix[0].shape[1]), BF16),
    ] + block_shapes(names, rows, width)
    operands = [query, key, value, w_out, *prefix]
    found = pl.pallas_call(
        functools.partial(forward_kernel, slots, names),
        in_specs=[SMEM] * 3 + [VMEM] * len(operands),
        out_specs=[VMEM] * len(results),
        out_shape=in_vmem(results),
        scratch_shapes=[pltpu.VMEM((rows, q_width), BF16)],
        compiler_params=pltpu.CompilerParams(vmem_limit_bytes=vmem_room(count)),
        cost_estimate=lasting(1.7),
    )(*held_in(pltpu.SMEM, scalars), *held_in(pltpu.VMEM, operands))
    return found[:4], found[4:]


def backward_kernel(slots, names, *refs):
    take, rest = taker(refs)
    prompt_len, resp_prompt, resp_len = take(3)
    cotangent = take(len(HELD))
    query, key, value, hq, hk = take(5)
    w_all, q_gain, k_gain, w_out = take(4)
    p_pre, p_own, heads_out, prefix_v = take(4)
    terms = take(len(rest) - len(names) - 2)
    parts = take(len(names))
    grad_prefix, grads = take(2)

    width = cotangent[0].shape[2]
    me = lax.axis_index("mp")
    grad_heads = 0.0
    for blocks, ref in zip(HELD, cotangent):
        for i, block in enumerate(blocks):
            grad_heads += dot_nt(ref[i], w_out[:, features(me ^ block, width)])
    grad_prefix[...] = jnp.zeros_like(grad_prefix)

    count = prefix_v.shape[0]
    window = window_rows(count)
    slot_len = query.shape[0] // slots
    size = q_gain.shape[1]
    kv_heads = key.shape[1] // size
    groups = query.shape[1] // key.shape[1]
    scale = size ** (-0.5)
    for n in range(slots):
        first, _ = prompt_span(prompt_len, resp_prompt[n])
        start = window_start(first, count)
        rows = slice(n * slot_len, (n + 1) * slot_len)
        live = lax.broadcasted_iota(jnp.int32, (slot_len, size), 0) < resp_len[n]
        for h in range(kv_heads):
            heads = range(h * groups, (h + 1) * groups)
            q = stacked(query, rows, heads, size)
            out = stacked(heads_out, rows, heads, size)
            g = jnp.concatenate(
                [
                    jnp.where(live, grad_heads[rows, a * size : (a + 1) * size], 0.0).astype(BF16)
                    for a in heads
                ],
                axis=0,
            )
            k_win = prefix_v[pl.ds(start, window), 2 * h * size : (2 * h + 1) * size]
            v_win = prefix_v[pl.ds(start, window), (2 * h + 1) * size : (2 * h + 2) * size]
            k_own = key[rows, h * size : (h + 1) * size]
            v_own = value[rows, h * size : (h + 1) * size]
            b_pre, b_own = p_pre[n, h], p_own[n, h]
            delta = jnp.sum(g.astype(F32) * out, axis=-1, keepdims=True)
            ds_pre = (b_pre.astype(F32) * (dot_nt(g, v_win) - delta)).astype(BF16)
            ds_own = (b_own.astype(F32) * (dot_nt(g, v_own) - delta)).astype(BF16)
            grad_q = scale * (dot(ds_pre, k_win) + dot(ds_own, k_own))
            for i, a in enumerate(heads):
                cols = slice(a * size, (a + 1) * size)
                one = grad_q[i * slot_len : (i + 1) * slot_len]
                grads[rows, cols] = norm_back(hq[rows, cols], q_gain[...], one).astype(BF16)
            cols = slice(h * size, (h + 1) * size)
            q_width, k_width = query.shape[1], key.shape[1]
            key_cols = slice(q_width + h * size, q_width + (h + 1) * size)
            value_cols = slice(q_width + k_width + h * size, q_width + k_width + (h + 1) * size)
            grad_k = scale * dot_tn(ds_own, q)
            grads[rows, key_cols] = norm_back(hk[rows, cols], k_gain[...], grad_k).astype(BF16)
            grads[rows, value_cols] = dot_tn(b_own, g).astype(BF16)
            k_cols = slice(2 * h * size, (2 * h + 1) * size)
            v_cols = slice((2 * h + 1) * size, (2 * h + 2) * size)
            grad_prefix[pl.ds(start, window), k_cols] += scale * dot_tn(ds_pre, q)
            grad_prefix[pl.ds(start, window), v_cols] += dot_tn(b_pre, g)
    chips = prefix_v.shape[0] // terms[0].shape[1] if len(terms) > 1 else 1
    for ref, steps in zip(terms, TERMS if len(terms) > 1 else ((0,),)):
        for i, step in enumerate(steps):
            ref[i] = grad_prefix[slot_rows(chips, ref.shape[1], step), :]

    def make(cols):
        return dot_nt(grads[...], w_all[cols, :]).astype(BF16)

    make_blocks(make, names, parts)


def backward(names, scalars, cotangent, kept, terms):
    slots = scalars[-1].shape[0]
    query, key, w_out, prefix = kept[0], kept[1], kept[8], kept[12]
    rows, q_width = query.shape
    k_width = key.shape[1]
    count, kv_width = prefix.shape
    results = [(x, F32) for x in terms] + block_shapes(names, rows, cotangent[0].shape[2])
    found = pl.pallas_call(
        functools.partial(backward_kernel, slots, names),
        in_specs=[SMEM] * 3 + [VMEM] * (len(cotangent) + len(kept)),
        out_specs=[VMEM] * len(results),
        out_shape=in_vmem(results),
        scratch_shapes=[
            pltpu.VMEM((count, kv_width), F32),
            pltpu.VMEM((rows, q_width + 2 * k_width), BF16),
        ],
        compiler_params=pltpu.CompilerParams(vmem_limit_bytes=vmem_room(count)),
        cost_estimate=lasting(3.5),
    )(*held_in(pltpu.SMEM, scalars), *held_in(pltpu.VMEM, [*cotangent, *kept]))
    return found[: len(terms)], found[len(terms) :]


def last_kernel(counts, *refs):
    take, rest = taker(refs)
    groups = [take(len(count)) for count in counts]
    results = take(len(counts))
    stage = take(len(counts))
    (sems,) = take(1)
    copies = Copies(sems)
    stores = []
    for count, group, result, ref in zip(counts, groups, results, stage):
        whole = 0.0
        for i, term in zip(count, group):
            whole = whole + term[i].astype(F32)
        ref[...] = whole.astype(BF16)
        stores.append(copies.start(ref, result))
    wait(stores)


def last_sums(groups):
    arrays = [array for group in groups for array, _ in group]
    shapes = [jax.ShapeDtypeStruct(group[0][0].shape[1:], BF16) for group in groups]
    return pl.pallas_call(
        functools.partial(last_kernel, [[i for _, i in group] for group in groups]),
        in_specs=[VMEM] * len(arrays),
        out_specs=[HBM] * len(groups),
        out_shape=shapes,
        scratch_shapes=in_vmem(like(shapes)) + [pltpu.SemaphoreType.DMA((len(groups),))],
        compiler_params=pltpu.CompilerParams(vmem_limit_bytes=vmem_room(0)),
        cost_estimate=lasting(0.9),
    )(*held_in(pltpu.VMEM, arrays))


def trade(name, block, axis, step):
    with jax.named_scope(name):
        return lax.ppermute(block, axis, [(i, i ^ step) for i in range(lax.axis_size(axis))])


def after(value, *others):
    return lax.optimization_barrier((value, *others))[0]


def total(*terms):
    whole = terms[0].astype(F32)
    for term in terms[1:]:
        whole = whole + term.astype(F32)
    return whole.astype(BF16)


def per_device(
    hidden_rows,
    w_query,
    w_key,
    w_value,
    w_out,
    q_gain,
    k_gain,
    prefix_kv,
    cotangent,
    prompt_len,
    resp_prompt,
    resp_len,
):
    chips = lax.axis_size("dp")
    scalars = (prompt_len, resp_prompt, resp_len)
    q_gain, k_gain = q_gain[None], k_gain[None]
    own = cotangent[None]
    far = trade("gather_far", own, "mp", 4)
    near = trade("gather_near", own, "mp", 2)
    if chips == 4:
        others = [trade("gather_prefix", prefix_kv, "dp", k) for k in range(1, chips)]
    else:
        prefix_kv, others = lax.all_gather(prefix_kv, "dp", axis=0, tiled=True), []
    far = after(far, *others)
    both = trade("gather_both", far, "mp", 2)
    pair = jnp.concatenate([far, near])
    pair_x = trade("gather_pair_x", pair, "mp", 1)
    own_x = trade("gather_own_x", own, "mp", 1)
    scalars, projected, weights, prefix, own = project(
        scalars, after(hidden_rows, far), w_query, w_key, w_value, q_gain, k_gain, prefix_kv, own
    )
    both_x = trade("gather_both_x", after(both, projected[0]), "mp", 1)
    probed, parts = forward(
        OUT, cotangent.shape[1], q_gain.shape[1], scalars, *projected[:3], w_out,
        [prefix, *others],
    )
    back = [own, pair, both, own_x, pair_x, both_x]
    shape = prefix_kv.shape
    terms = [(1, *shape)] if chips != 4 else [(len(steps), *shape) for steps in TERMS]
    terms, grads = backward(IN, scalars, back, [*projected, *weights, w_out, *probed], terms)

    out_a, out_b, kept_a, kept_b = parts
    got_a = trade("out_a", out_a, "mp", 2)
    got_b = trade("out_b", after(out_b, pair_x), "mp", 2)
    out_a = total(kept_a, got_a)
    got_out = trade("out_mid", out_a, "mp", 4)
    in_75, in_3, in_1, in_6, in_4, in_2, in_0 = grads
    got_75 = trade("in_75", in_75, "mp", 1)
    got_3 = trade("in_3", in_3, "mp", 1)
    in_6 = total(after(in_6, out_a), got_75[:1])
    got_6 = trade("in_6", in_6, "mp", 2)
    in_2 = total(in_2, got_3)
    got_2 = trade("in_2", in_2, "mp", 2)
    if chips == 4:
        got = trade("grad_prefix_core", after(terms[0], in_2), "dp", 1)
        last = trade("grad_prefix_y", terms[1][1:] + got[1:], "dp", 2)
    in_4 = total(after(in_4, got_b, got_out, in_2), got_75[1:], got_6)
    got_4 = trade("in_4", in_4, "mp", 4)
    got_1 = trade("in_1", after(in_1, in_4), "mp", 1)
    got_x = trade("out_x", total(after(kept_b, in_4)[1:], got_b[1:], got_out[1:]), "mp", 1)
    groups = [
        [(kept_b, 0), (got_b, 0), (got_out, 0), (got_x, 0)],
        [(in_0, 0), (got_1, 0), (got_2, 0), (got_4, 0)],
    ]
    if chips == 4:
        groups.append([(terms[1], 0), (got, 0), (last, 0)])
        return last_sums(groups)
    grad_prefix = lax.psum_scatter(terms[0][0], "dp", scatter_dimension=0, tiled=True)
    return *last_sums(groups), grad_prefix.astype(BF16)


def solution(mesh):
    in_specs = (
        P("dp", None),
        P(None, "mp"),
        P(None, "mp"),
        P(None, "mp"),
        P("mp", None),
        P(),
        P(),
        P("dp", "mp"),
        P("dp", "mp"),
        P(),
        P("dp"),
        P("dp"),
    )
    out_specs = (P("dp", "mp"), P("dp", "mp"), P("dp", "mp"))
    return jax.shard_map(
        per_device, mesh=mesh, in_specs=in_specs, out_specs=out_specs, check_vma=False
    )
```

```python
import functools

import jax
import jax.numpy as jnp
from jax import lax
from jax.experimental import pallas as pl
from jax.experimental.pallas import tpu as pltpu
from jax.sharding import PartitionSpec as P

EPS = 1e-06
NEG = -1e30
ROWS = 16
HELD = ((0,), (4, 2), (6,), (1,), (5, 3), (7,))
OUT = ((6, 7), (2, 3), (4, 5), (0, 1))
TERMS = ((2, 3), (0, 1))
IN = ((7, 5), (3,), (1,), (6,), (4,), (2,), (0,))
F32 = jnp.float32
BF16 = jnp.bfloat16
HBM = pl.BlockSpec(memory_space=pltpu.HBM)
SMEM = pl.BlockSpec(memory_space=pltpu.SMEM)
VMEM = pl.BlockSpec(memory_space=pltpu.VMEM)


def dot(left, right):
    return jnp.dot(left, right, preferred_element_type=F32)


def dot_nt(left, right):
    return lax.dot_general(left, right, (((1,), (1,)), ((), ())), preferred_element_type=F32)


def dot_tn(left, right):
    return lax.dot_general(left, right, (((0,), (0,)), ((), ())), preferred_element_type=F32)


def inverse_root(hidden):
    return lax.rsqrt(jnp.mean(hidden * hidden, axis=-1, keepdims=True) + EPS)


def norm_back(hidden, gain, grad):
    root = inverse_root(hidden)
    unit = hidden * root
    scaled = grad * gain
    return root * (scaled - unit * jnp.mean(scaled * unit, axis=-1, keepdims=True))


class Copies:
    def __init__(self, sems):
        self.sems, self.count = sems, 0

    def start(self, source, target):
        copy = pltpu.make_async_copy(source, target, self.sems.at[self.count])
        self.count += 1
        copy.start()
        return copy


def wait(copies):
    for copy in copies:
        copy.wait()


def prompt_span(prompt_len, prompt):
    first, last = 0, 0
    end = 0
    for p in range(prompt_len.shape[0]):
        begin = end
        end = end + prompt_len[p]
        first = jnp.where(prompt == p, begin, first)
        last = jnp.where(prompt == p, end, last)
    return first, last


def window_rows(count):
    return min(count, count // 3 + ROWS)


def window_start(first, count):
    start = jnp.minimum(first // ROWS * ROWS, count - window_rows(count))
    return pl.multiple_of(start, ROWS)


def slot_rows(slots, rows, step):
    if slots == 1:
        return pl.ds(0, rows)
    return pl.ds(pl.multiple_of((lax.axis_index("dp") ^ step) * rows, ROWS), rows)


def features(block, width):
    return pl.ds(pl.multiple_of(block * width, width), width)


def stacked(ref, rows, heads, size):
    return jnp.concatenate([ref[rows, a * size : (a + 1) * size] for a in heads], axis=0)


def make_blocks(make, names, refs):
    me = lax.axis_index("mp")
    for blocks, ref in zip(names, refs):
        for i, block in enumerate(blocks):
            ref[i] = make(features(me ^ block, ref.shape[-1]))


def taker(refs):
    refs = list(refs)

    def take(count):
        found, refs[:count] = refs[:count], []
        return found

    return take, refs


def project_kernel(*refs):
    take, _ = taker(refs)
    scalars = take(3)
    hidden, w_q, w_k, w_v, q_gain, k_gain, prefix, own = take(8)
    scalars_v = take(3)
    query, key, value, hq, hk = take(5)
    w_all, qg_v, kg_v, prefix_v, own_v = take(5)
    hidden_v, sems = take(2)

    copies = Copies(sems)
    depth = hidden.shape[1]
    steps = 4
    part = depth // steps
    places, end = [], 0
    for w in (w_q, w_k, w_v):
        places.append(slice(end, end + w.shape[1]))
        end += w.shape[1]
    loads = []
    for i in range(steps):
        cut = pl.ds(i * part, part)
        loads.append(
            [copies.start(hidden.at[:, cut], hidden_v.at[:, cut])]
            + [
                copies.start(w.at[cut], w_all.at[cut, place])
                for w, place in zip((w_q, w_k, w_v), places)
            ]
        )
    small = [copies.start(q_gain, qg_v), copies.start(k_gain, kg_v)]
    small += [copies.start(source, target) for source, target in zip(scalars, scalars_v)]
    small += [copies.start(prefix, prefix_v), copies.start(own, own_v)]

    whole = 0.0
    for i, load in enumerate(loads):
        wait(load)
        cut = slice(i * part, (i + 1) * part)
        whole += dot(hidden_v[:, cut], w_all[cut, :])
    hq[...], hk[...] = whole[:, places[0]], whole[:, places[1]]
    value[...] = whole[:, places[2]].astype(BF16)
    wait(small)
    size = qg_v.shape[1]
    for ref, gain, out in ((hq, qg_v, query), (hk, kg_v, key)):
        for at in range(0, ref.shape[1], size):
            head = ref[:, at : at + size]
            out[:, at : at + size] = (head * inverse_root(head) * gain[...]).astype(BF16)


def project(scalars, hidden, w_q, w_k, w_v, q_gain, k_gain, prefix, own):
    rows, depth = hidden.shape
    q_width, k_width = w_q.shape[1], w_k.shape[1]
    small = [q_gain, k_gain, prefix, own]
    operands = [*scalars, hidden, w_q, w_k, w_v, *small]
    kept = [
        ((rows, q_width), BF16),
        ((rows, k_width), BF16),
        ((rows, k_width), BF16),
        ((rows, q_width), F32),
        ((rows, k_width), F32),
        ((depth, q_width + 2 * k_width), BF16),
    ] + like(small)
    found = pl.pallas_call(
        project_kernel,
        in_specs=[HBM] * len(operands),
        out_specs=[SMEM] * 3 + [VMEM] * len(kept),
        out_shape=[pltpu.SMEM(x.shape, jnp.int32) for x in scalars] + in_vmem(kept),
        scratch_shapes=[pltpu.VMEM(hidden.shape, hidden.dtype), pltpu.SemaphoreType.DMA((32,))],
        compiler_params=pltpu.CompilerParams(vmem_limit_bytes=vmem_room(prefix.shape[0])),
        cost_estimate=lasting(2.6),
    )(*held_in(pltpu.HBM, operands))
    return found[:3], found[3:8], found[8:11], found[11], found[12]


def forward_kernel(slots, names, *refs):
    take, rest = taker(refs)
    prompt_len, resp_prompt, resp_len = take(3)
    query, key, value, wo_v = take(4)
    prefix = take(len(rest) - 4 - len(names) - 1)
    p_pre, p_own, heads_out, prefix_v = take(4)
    parts = take(len(names))
    (out_bf,) = take(1)

    held = prefix[0].shape[0]
    for k, ref in enumerate(prefix):
        prefix_v[slot_rows(len(prefix), held, k), :] = ref[...]
    size = heads_out.shape[1] * p_own.shape[3] // p_own.shape[2] // p_own.shape[1]
    count = prefix_v.shape[0]
    window = window_rows(count)
    slot_len = query.shape[0] // slots
    kv_heads = key.shape[1] // size
    groups = query.shape[1] // key.shape[1]
    scale = size ** (-0.5)
    for n in range(slots):
        first, last = prompt_span(prompt_len, resp_prompt[n])
        start = window_start(first, count)
        rows = slice(n * slot_len, (n + 1) * slot_len)
        live = lax.broadcasted_iota(jnp.int32, (slot_len, size), 0) < resp_len[n]
        for h in range(kv_heads):
            heads = range(h * groups, (h + 1) * groups)
            q = stacked(query, rows, heads, size)
            k_win = prefix_v[pl.ds(start, window), 2 * h * size : (2 * h + 1) * size]
            v_win = prefix_v[pl.ds(start, window), (2 * h + 1) * size : (2 * h + 2) * size]
            k_own = key[rows, h * size : (h + 1) * size]
            v_own = value[rows, h * size : (h + 1) * size]
            tall = groups * slot_len
            place = start + lax.broadcasted_iota(jnp.int32, (tall, window), 1)
            s_pre = jnp.where((place >= first) & (place < last), dot_nt(q, k_win) * scale, NEG)
            token = lax.broadcasted_iota(jnp.int32, (groups, slot_len, slot_len), 1)
            token = token.reshape(tall, slot_len)
            other = lax.broadcasted_iota(jnp.int32, (tall, slot_len), 1)
            s_own = jnp.where(
                (other <= token) & (other < resp_len[n]), dot_nt(q, k_own) * scale, NEG
            )
            top = jnp.maximum(
                jnp.max(s_pre, axis=-1, keepdims=True), jnp.max(s_own, axis=-1, keepdims=True)
            )
            e_pre = jnp.exp(s_pre - top)
            e_own = jnp.exp(s_own - top)
            total = jnp.sum(e_pre, axis=-1, keepdims=True) + jnp.sum(e_own, axis=-1, keepdims=True)
            b_pre = (e_pre / total).astype(BF16)
            b_own = (e_own / total).astype(BF16)
            p_pre[n, h] = b_pre
            p_own[n, h] = b_own
            out = dot(b_pre, v_win) + dot(b_own, v_own)
            for i, a in enumerate(heads):
                one = out[i * slot_len : (i + 1) * slot_len]
                heads_out[rows, a * size : (a + 1) * size] = one
                out_bf[rows, a * size : (a + 1) * size] = jnp.where(live, one, 0.0).astype(BF16)

    def make(cols):
        return dot(out_bf[...], wo_v[:, cols]).astype(BF16)

    make_blocks(make, names, parts)


def block_shapes(names, rows, width):
    return [((len(blocks), rows, width), BF16) for blocks in names]


def in_vmem(shapes):
    return [pltpu.VMEM(*x) for x in shapes]


def held_in(space, arrays):
    return [pltpu.with_memory_space_constraint(x, space) for x in arrays]


def lasting(us):
    return pl.CostEstimate(flops=int(us * 1.15e9), bytes_accessed=0, transcendentals=0)


def like(arrays):
    return [(x.shape, x.dtype) for x in arrays]


def vmem_room(prefix_rows):
    return 48 << 20 if prefix_rows > 1024 else 24 << 20


def forward(names, width, size, scalars, query, key, value, w_out, prefix):
    slots = scalars[-1].shape[0]
    rows, q_width = query.shape
    k_width = key.shape[1]
    count = sum(x.shape[0] for x in prefix)
    window = window_rows(count)
    slot_len = rows // slots
    kv_heads, tall = k_width // size, slot_len * q_width // k_width
    results = [
        ((slots, kv_heads, tall, window), BF16),
        ((slots, kv_heads, tall, slot_len), BF16),
        ((rows, q_width), F32),
        ((count, prefix[0].shape[1]), BF16),
    ] + block_shapes(names, rows, width)
    operands = [query, key, value, w_out, *prefix]
    found = pl.pallas_call(
        functools.partial(forward_kernel, slots, names),
        in_specs=[SMEM] * 3 + [VMEM] * len(operands),
        out_specs=[VMEM] * len(results),
        out_shape=in_vmem(results),
        scratch_shapes=[pltpu.VMEM((rows, q_width), BF16)],
        compiler_params=pltpu.CompilerParams(vmem_limit_bytes=vmem_room(count)),
        cost_estimate=lasting(1.7),
    )(*held_in(pltpu.SMEM, scalars), *held_in(pltpu.VMEM, operands))
    return found[:4], found[4:]


def backward_kernel(slots, names, *refs):
    take, rest = taker(refs)
    prompt_len, resp_prompt, resp_len = take(3)
    cotangent = take(len(HELD))
    query, key, value, hq, hk = take(5)
    w_all, q_gain, k_gain, w_out = take(4)
    p_pre, p_own, heads_out, prefix_v = take(4)
    terms = take(len(rest) - len(names) - 2)
    parts = take(len(names))
    grad_prefix, grads = take(2)

    width = cotangent[0].shape[2]
    me = lax.axis_index("mp")
    grad_heads = 0.0
    for blocks, ref in zip(HELD, cotangent):
        for i, block in enumerate(blocks):
            grad_heads += dot_nt(ref[i], w_out[:, features(me ^ block, width)])
    grad_prefix[...] = jnp.zeros_like(grad_prefix)

    count = prefix_v.shape[0]
    window = window_rows(count)
    slot_len = query.shape[0] // slots
    size = q_gain.shape[1]
    kv_heads = key.shape[1] // size
    groups = query.shape[1] // key.shape[1]
    scale = size ** (-0.5)
    for n in range(slots):
        first, _ = prompt_span(prompt_len, resp_prompt[n])
        start = window_start(first, count)
        rows = slice(n * slot_len, (n + 1) * slot_len)
        live = lax.broadcasted_iota(jnp.int32, (slot_len, size), 0) < resp_len[n]
        for h in range(kv_heads):
            heads = range(h * groups, (h + 1) * groups)
            q = stacked(query, rows, heads, size)
            out = stacked(heads_out, rows, heads, size)
            g = jnp.concatenate(
                [
                    jnp.where(live, grad_heads[rows, a * size : (a + 1) * size], 0.0).astype(BF16)
                    for a in heads
                ],
                axis=0,
            )
            k_win = prefix_v[pl.ds(start, window), 2 * h * size : (2 * h + 1) * size]
            v_win = prefix_v[pl.ds(start, window), (2 * h + 1) * size : (2 * h + 2) * size]
            k_own = key[rows, h * size : (h + 1) * size]
            v_own = value[rows, h * size : (h + 1) * size]
            b_pre, b_own = p_pre[n, h], p_own[n, h]
            delta = jnp.sum(g.astype(F32) * out, axis=-1, keepdims=True)
            ds_pre = (b_pre.astype(F32) * (dot_nt(g, v_win) - delta)).astype(BF16)
            ds_own = (b_own.astype(F32) * (dot_nt(g, v_own) - delta)).astype(BF16)
            grad_q = scale * (dot(ds_pre, k_win) + dot(ds_own, k_own))
            for i, a in enumerate(heads):
                cols = slice(a * size, (a + 1) * size)
                one = grad_q[i * slot_len : (i + 1) * slot_len]
                grads[rows, cols] = norm_back(hq[rows, cols], q_gain[...], one).astype(BF16)
            cols = slice(h * size, (h + 1) * size)
            q_width, k_width = query.shape[1], key.shape[1]
            key_cols = slice(q_width + h * size, q_width + (h + 1) * size)
            value_cols = slice(q_width + k_width + h * size, q_width + k_width + (h + 1) * size)
            grad_k = scale * dot_tn(ds_own, q)
            grads[rows, key_cols] = norm_back(hk[rows, cols], k_gain[...], grad_k).astype(BF16)
            grads[rows, value_cols] = dot_tn(b_own, g).astype(BF16)
            k_cols = slice(2 * h * size, (2 * h + 1) * size)
            v_cols = slice((2 * h + 1) * size, (2 * h + 2) * size)
            grad_prefix[pl.ds(start, window), k_cols] += scale * dot_tn(ds_pre, q)
            grad_prefix[pl.ds(start, window), v_cols] += dot_tn(b_pre, g)
    chips = prefix_v.shape[0] // terms[0].shape[1] if len(terms) > 1 else 1
    for ref, steps in zip(terms, TERMS if len(terms) > 1 else ((0,),)):
        for i, step in enumerate(steps):
            ref[i] = grad_prefix[slot_rows(chips, ref.shape[1], step), :]

    def make(cols):
        return dot_nt(grads[...], w_all[cols, :]).astype(BF16)

    make_blocks(make, names, parts)


def backward(names, scalars, cotangent, kept, terms):
    slots = scalars[-1].shape[0]
    query, key, w_out, prefix = kept[0], kept[1], kept[8], kept[12]
    rows, q_width = query.shape
    k_width = key.shape[1]
    count, kv_width = prefix.shape
    results = [(x, F32) for x in terms] + block_shapes(names, rows, cotangent[0].shape[2])
    found = pl.pallas_call(
        functools.partial(backward_kernel, slots, names),
        in_specs=[SMEM] * 3 + [VMEM] * (len(cotangent) + len(kept)),
        out_specs=[VMEM] * len(results),
        out_shape=in_vmem(results),
        scratch_shapes=[
            pltpu.VMEM((count, kv_width), F32),
            pltpu.VMEM((rows, q_width + 2 * k_width), BF16),
        ],
        compiler_params=pltpu.CompilerParams(vmem_limit_bytes=vmem_room(count)),
        cost_estimate=lasting(3.5),
    )(*held_in(pltpu.SMEM, scalars), *held_in(pltpu.VMEM, [*cotangent, *kept]))
    return found[: len(terms)], found[len(terms) :]


def last_kernel(counts, *refs):
    take, rest = taker(refs)
    groups = [take(len(count)) for count in counts]
    results = take(len(counts))
    stage = take(len(counts))
    (sems,) = take(1)
    copies = Copies(sems)
    stores = []
    for count, group, result, ref in zip(counts, groups, results, stage):
        whole = 0.0
        for i, term in zip(count, group):
            whole = whole + term[i].astype(F32)
        ref[...] = whole.astype(BF16)
        stores.append(copies.start(ref, result))
    wait(stores)


def last_sums(groups):
    arrays = [array for group in groups for array, _ in group]
    shapes = [jax.ShapeDtypeStruct(group[0][0].shape[1:], BF16) for group in groups]
    return pl.pallas_call(
        functools.partial(last_kernel, [[i for _, i in group] for group in groups]),
        in_specs=[VMEM] * len(arrays),
        out_specs=[HBM] * len(groups),
        out_shape=shapes,
        scratch_shapes=in_vmem(like(shapes)) + [pltpu.SemaphoreType.DMA((len(groups),))],
        compiler_params=pltpu.CompilerParams(vmem_limit_bytes=vmem_room(0)),
        cost_estimate=lasting(0.9),
    )(*held_in(pltpu.VMEM, arrays))


def trade(name, block, axis, step):
    with jax.named_scope(name):
        return lax.ppermute(block, axis, [(i, i ^ step) for i in range(lax.axis_size(axis))])


def after(value, *others):
    return lax.optimization_barrier((value, *others))[0]


def total(*terms):
    whole = terms[0].astype(F32)
    for term in terms[1:]:
        whole = whole + term.astype(F32)
    return whole.astype(BF16)


def per_device(
    hidden_rows,
    w_query,
    w_key,
    w_value,
    w_out,
    q_gain,
    k_gain,
    prefix_kv,
    cotangent,
    prompt_len,
    resp_prompt,
    resp_len,
):
    chips = lax.axis_size("dp")
    scalars = (prompt_len, resp_prompt, resp_len)
    q_gain, k_gain = q_gain[None], k_gain[None]
    own = cotangent[None]
    far = trade("gather_far", own, "mp", 4)
    near = trade("gather_near", own, "mp", 2)
    if chips == 4:
        others = [trade("gather_prefix", prefix_kv, "dp", k) for k in range(1, chips)]
    else:
        prefix_kv, others = lax.all_gather(prefix_kv, "dp", axis=0, tiled=True), []
    far = after(far, *others)
    both = trade("gather_both", far, "mp", 2)
    pair = jnp.concatenate([far, near])
    pair_x = trade("gather_pair_x", pair, "mp", 1)
    own_x = trade("gather_own_x", own, "mp", 1)
    scalars, projected, weights, prefix, own = project(
        scalars, after(hidden_rows, far), w_query, w_key, w_value, q_gain, k_gain, prefix_kv, own
    )
    both_x = trade("gather_both_x", after(both, projected[0]), "mp", 1)
    probed, parts = forward(
        OUT, cotangent.shape[1], q_gain.shape[1], scalars, *projected[:3], w_out,
        [prefix, *others],
    )
    back = [own, pair, both, own_x, pair_x, both_x]
    shape = prefix_kv.shape
    terms = [(1, *shape)] if chips != 4 else [(len(steps), *shape) for steps in TERMS]
    terms, grads = backward(IN, scalars, back, [*projected, *weights, w_out, *probed], terms)

    out_a, out_b, kept_a, kept_b = parts
    got_a = trade("out_a", out_a, "mp", 2)
    got_b = trade("out_b", after(out_b, pair_x), "mp", 2)
    out_a = total(kept_a, got_a)
    got_out = trade("out_mid", out_a, "mp", 4)
    in_75, in_3, in_1, in_6, in_4, in_2, in_0 = grads
    got_75 = trade("in_75", in_75, "mp", 1)
    got_3 = trade("in_3", in_3, "mp", 1)
    in_6 = total(after(in_6, out_a), got_75[:1])
    got_6 = trade("in_6", in_6, "mp", 2)
    in_2 = total(in_2, got_3)
    got_2 = trade("in_2", in_2, "mp", 2)
    if chips == 4:
        got = trade("grad_prefix_y", after(terms[0], in_2), "dp", 2)
        last = trade("grad_prefix_core", terms[1][1:] + got[1:], "dp", 1)
    in_4 = total(after(in_4, got_b, got_out, in_2), got_75[1:], got_6)
    got_4 = trade("in_4", in_4, "mp", 4)
    got_1 = trade("in_1", after(in_1, in_4), "mp", 1)
    got_x = trade("out_x", total(after(kept_b, in_4)[1:], got_b[1:], got_out[1:]), "mp", 1)
    groups = [
        [(kept_b, 0), (got_b, 0), (got_out, 0), (got_x, 0)],
        [(in_0, 0), (got_1, 0), (got_2, 0), (got_4, 0)],
    ]
    if chips == 4:
        groups.append([(terms[1], 0), (got, 0), (last, 0)])
        return last_sums(groups)
    grad_prefix = lax.psum_scatter(terms[0][0], "dp", scatter_dimension=0, tiled=True)
    return *last_sums(groups), grad_prefix.astype(BF16)


def solution(mesh):
    in_specs = (
        P("dp", None),
        P(None, "mp"),
        P(None, "mp"),
        P(None, "mp"),
        P("mp", None),
        P(),
        P(),
        P("dp", "mp"),
        P("dp", "mp"),
        P(),
        P("dp"),
        P("dp"),
    )
    out_specs = (P("dp", "mp"), P("dp", "mp"), P("dp", "mp"))
    return jax.shard_map(
        per_device, mesh=mesh, in_specs=in_specs, out_specs=out_specs, check_vma=False
    )
```

```python
import functools

import jax
import jax.numpy as jnp
from jax import lax
from jax.experimental import pallas as pl
from jax.experimental.pallas import tpu as pltpu
from jax.sharding import PartitionSpec as P

EPS = 1e-06
NEG = -1e30
ROWS = 16
HELD = ((0,), (4, 2), (6,), (1,), (5, 3), (7,))
OUT = ((6, 7), (2, 3), (4, 5), (0, 1))
TERMS = ((2, 3), (0, 1))
IN = ((7, 5), (3,), (1,), (6,), (4,), (2,), (0,))
F32 = jnp.float32
BF16 = jnp.bfloat16
HBM = pl.BlockSpec(memory_space=pltpu.HBM)
SMEM = pl.BlockSpec(memory_space=pltpu.SMEM)
VMEM = pl.BlockSpec(memory_space=pltpu.VMEM)


def dot(left, right):
    return jnp.dot(left, right, preferred_element_type=F32)


def dot_nt(left, right):
    return lax.dot_general(left, right, (((1,), (1,)), ((), ())), preferred_element_type=F32)


def dot_tn(left, right):
    return lax.dot_general(left, right, (((0,), (0,)), ((), ())), preferred_element_type=F32)


def inverse_root(hidden):
    return lax.rsqrt(jnp.mean(hidden * hidden, axis=-1, keepdims=True) + EPS)


def norm_back(hidden, gain, grad):
    root = inverse_root(hidden)
    unit = hidden * root
    scaled = grad * gain
    return root * (scaled - unit * jnp.mean(scaled * unit, axis=-1, keepdims=True))


class Copies:
    def __init__(self, sems):
        self.sems, self.count = sems, 0

    def start(self, source, target):
        copy = pltpu.make_async_copy(source, target, self.sems.at[self.count])
        self.count += 1
        copy.start()
        return copy


def wait(copies):
    for copy in copies:
        copy.wait()


def prompt_span(prompt_len, prompt):
    first, last = 0, 0
    end = 0
    for p in range(prompt_len.shape[0]):
        begin = end
        end = end + prompt_len[p]
        first = jnp.where(prompt == p, begin, first)
        last = jnp.where(prompt == p, end, last)
    return first, last


def window_rows(count):
    return min(count, count // 3 + ROWS)


def window_start(first, count):
    start = jnp.minimum(first // ROWS * ROWS, count - window_rows(count))
    return pl.multiple_of(start, ROWS)


def slot_rows(slots, rows, step):
    if slots == 1:
        return pl.ds(0, rows)
    return pl.ds(pl.multiple_of((lax.axis_index("dp") ^ step) * rows, ROWS), rows)


def features(block, width):
    return pl.ds(pl.multiple_of(block * width, width), width)


def stacked(ref, rows, heads, size):
    return jnp.concatenate([ref[rows, a * size : (a + 1) * size] for a in heads], axis=0)


def make_blocks(make, names, refs):
    me = lax.axis_index("mp")
    for blocks, ref in zip(names, refs):
        for i, block in enumerate(blocks):
            ref[i] = make(features(me ^ block, ref.shape[-1]))


def taker(refs):
    refs = list(refs)

    def take(count):
        found, refs[:count] = refs[:count], []
        return found

    return take, refs


def project_kernel(*refs):
    take, _ = taker(refs)
    scalars = take(3)
    hidden, w_q, w_k, w_v, q_gain, k_gain, prefix, own = take(8)
    scalars_v = take(3)
    query, key, value, hq, hk = take(5)
    w_all, qg_v, kg_v, prefix_v, own_v = take(5)
    hidden_v, sems = take(2)

    copies = Copies(sems)
    depth = hidden.shape[1]
    steps = 8
    part = depth // steps
    places, end = [], 0
    for w in (w_q, w_k, w_v):
        places.append(slice(end, end + w.shape[1]))
        end += w.shape[1]
    loads = []
    for i in range(steps):
        cut = pl.ds(i * part, part)
        loads.append(
            [copies.start(hidden.at[:, cut], hidden_v.at[:, cut])]
            + [
                copies.start(w.at[cut], w_all.at[cut, place])
                for w, place in zip((w_q, w_k, w_v), places)
            ]
        )
    small = [copies.start(q_gain, qg_v), copies.start(k_gain, kg_v)]
    small += [copies.start(source, target) for source, target in zip(scalars, scalars_v)]
    small += [copies.start(prefix, prefix_v), copies.start(own, own_v)]

    whole = 0.0
    for i, load in enumerate(loads):
        wait(load)
        cut = slice(i * part, (i + 1) * part)
        whole += dot(hidden_v[:, cut], w_all[cut, :])
    hq[...], hk[...] = whole[:, places[0]], whole[:, places[1]]
    value[...] = whole[:, places[2]].astype(BF16)
    wait(small)
    size = qg_v.shape[1]
    for ref, gain, out in ((hq, qg_v, query), (hk, kg_v, key)):
        for at in range(0, ref.shape[1], size):
            head = ref[:, at : at + size]
            out[:, at : at + size] = (head * inverse_root(head) * gain[...]).astype(BF16)


def project(scalars, hidden, w_q, w_k, w_v, q_gain, k_gain, prefix, own):
    rows, depth = hidden.shape
    q_width, k_width = w_q.shape[1], w_k.shape[1]
    small = [q_gain, k_gain, prefix, own]
    operands = [*scalars, hidden, w_q, w_k, w_v, *small]
    kept = [
        ((rows, q_width), BF16),
        ((rows, k_width), BF16),
        ((rows, k_width), BF16),
        ((rows, q_width), F32),
        ((rows, k_width), F32),
        ((depth, q_width + 2 * k_width), BF16),
    ] + like(small)
    found = pl.pallas_call(
        project_kernel,
        in_specs=[HBM] * len(operands),
        out_specs=[SMEM] * 3 + [VMEM] * len(kept),
        out_shape=[pltpu.SMEM(x.shape, jnp.int32) for x in scalars] + in_vmem(kept),
        scratch_shapes=[pltpu.VMEM(hidden.shape, hidden.dtype), pltpu.SemaphoreType.DMA((48,))],
        compiler_params=pltpu.CompilerParams(vmem_limit_bytes=vmem_room(prefix.shape[0])),
        cost_estimate=lasting(2.6),
    )(*held_in(pltpu.HBM, operands))
    return found[:3], found[3:8], found[8:11], found[11], found[12]


def forward_kernel(slots, names, *refs):
    take, rest = taker(refs)
    prompt_len, resp_prompt, resp_len = take(3)
    query, key, value, wo_v = take(4)
    prefix = take(len(rest) - 4 - len(names) - 1)
    p_pre, p_own, heads_out, prefix_v = take(4)
    parts = take(len(names))
    (out_bf,) = take(1)

    held = prefix[0].shape[0]
    for k, ref in enumerate(prefix):
        prefix_v[slot_rows(len(prefix), held, k), :] = ref[...]
    size = heads_out.shape[1] * p_own.shape[3] // p_own.shape[2] // p_own.shape[1]
    count = prefix_v.shape[0]
    window = window_rows(count)
    slot_len = query.shape[0] // slots
    kv_heads = key.shape[1] // size
    groups = query.shape[1] // key.shape[1]
    scale = size ** (-0.5)
    for n in range(slots):
        first, last = prompt_span(prompt_len, resp_prompt[n])
        start = window_start(first, count)
        rows = slice(n * slot_len, (n + 1) * slot_len)
        live = lax.broadcasted_iota(jnp.int32, (slot_len, size), 0) < resp_len[n]
        for h in range(kv_heads):
            heads = range(h * groups, (h + 1) * groups)
            q = stacked(query, rows, heads, size)
            k_win = prefix_v[pl.ds(start, window), 2 * h * size : (2 * h + 1) * size]
            v_win = prefix_v[pl.ds(start, window), (2 * h + 1) * size : (2 * h + 2) * size]
            k_own = key[rows, h * size : (h + 1) * size]
            v_own = value[rows, h * size : (h + 1) * size]
            tall = groups * slot_len
            place = start + lax.broadcasted_iota(jnp.int32, (tall, window), 1)
            s_pre = jnp.where((place >= first) & (place < last), dot_nt(q, k_win) * scale, NEG)
            token = lax.broadcasted_iota(jnp.int32, (groups, slot_len, slot_len), 1)
            token = token.reshape(tall, slot_len)
            other = lax.broadcasted_iota(jnp.int32, (tall, slot_len), 1)
            s_own = jnp.where(
                (other <= token) & (other < resp_len[n]), dot_nt(q, k_own) * scale, NEG
            )
            top = jnp.maximum(
                jnp.max(s_pre, axis=-1, keepdims=True), jnp.max(s_own, axis=-1, keepdims=True)
            )
            e_pre = jnp.exp(s_pre - top)
            e_own = jnp.exp(s_own - top)
            total = jnp.sum(e_pre, axis=-1, keepdims=True) + jnp.sum(e_own, axis=-1, keepdims=True)
            b_pre = (e_pre / total).astype(BF16)
            b_own = (e_own / total).astype(BF16)
            p_pre[n, h] = b_pre
            p_own[n, h] = b_own
            out = dot(b_pre, v_win) + dot(b_own, v_own)
            for i, a in enumerate(heads):
                one = out[i * slot_len : (i + 1) * slot_len]
                heads_out[rows, a * size : (a + 1) * size] = one
                out_bf[rows, a * size : (a + 1) * size] = jnp.where(live, one, 0.0).astype(BF16)

    def make(cols):
        return dot(out_bf[...], wo_v[:, cols]).astype(BF16)

    make_blocks(make, names, parts)


def block_shapes(names, rows, width):
    return [((len(blocks), rows, width), BF16) for blocks in names]


def in_vmem(shapes):
    return [pltpu.VMEM(*x) for x in shapes]


def held_in(space, arrays):
    return [pltpu.with_memory_space_constraint(x, space) for x in arrays]


def lasting(us):
    return pl.CostEstimate(flops=int(us * 1.15e9), bytes_accessed=0, transcendentals=0)


def like(arrays):
    return [(x.shape, x.dtype) for x in arrays]


def vmem_room(prefix_rows):
    return 48 << 20 if prefix_rows > 1024 else 24 << 20


def forward(names, width, size, scalars, query, key, value, w_out, prefix):
    slots = scalars[-1].shape[0]
    rows, q_width = query.shape
    k_width = key.shape[1]
    count = sum(x.shape[0] for x in prefix)
    window = window_rows(count)
    slot_len = rows // slots
    kv_heads, tall = k_width // size, slot_len * q_width // k_width
    results = [
        ((slots, kv_heads, tall, window), BF16),
        ((slots, kv_heads, tall, slot_len), BF16),
        ((rows, q_width), F32),
        ((count, prefix[0].shape[1]), BF16),
    ] + block_shapes(names, rows, width)
    operands = [query, key, value, w_out, *prefix]
    found = pl.pallas_call(
        functools.partial(forward_kernel, slots, names),
        in_specs=[SMEM] * 3 + [VMEM] * len(operands),
        out_specs=[VMEM] * len(results),
        out_shape=in_vmem(results),
        scratch_shapes=[pltpu.VMEM((rows, q_width), BF16)],
        compiler_params=pltpu.CompilerParams(vmem_limit_bytes=vmem_room(count)),
        cost_estimate=lasting(1.7),
    )(*held_in(pltpu.SMEM, scalars), *held_in(pltpu.VMEM, operands))
    return found[:4], found[4:]


def backward_kernel(slots, names, *refs):
    take, rest = taker(refs)
    prompt_len, resp_prompt, resp_len = take(3)
    cotangent = take(len(HELD))
    query, key, value, hq, hk = take(5)
    w_all, q_gain, k_gain, w_out = take(4)
    p_pre, p_own, heads_out, prefix_v = take(4)
    terms = take(len(rest) - len(names) - 2)
    parts = take(len(names))
    grad_prefix, grads = take(2)

    width = cotangent[0].shape[2]
    me = lax.axis_index("mp")
    grad_heads = 0.0
    for blocks, ref in zip(HELD, cotangent):
        for i, block in enumerate(blocks):
            grad_heads += dot_nt(ref[i], w_out[:, features(me ^ block, width)])
    grad_prefix[...] = jnp.zeros_like(grad_prefix)

    count = prefix_v.shape[0]
    window = window_rows(count)
    slot_len = query.shape[0] // slots
    size = q_gain.shape[1]
    kv_heads = key.shape[1] // size
    groups = query.shape[1] // key.shape[1]
    scale = size ** (-0.5)
    for n in range(slots):
        first, _ = prompt_span(prompt_len, resp_prompt[n])
        start = window_start(first, count)
        rows = slice(n * slot_len, (n + 1) * slot_len)
        live = lax.broadcasted_iota(jnp.int32, (slot_len, size), 0) < resp_len[n]
        for h in range(kv_heads):
            heads = range(h * groups, (h + 1) * groups)
            q = stacked(query, rows, heads, size)
            out = stacked(heads_out, rows, heads, size)
            g = jnp.concatenate(
                [
                    jnp.where(live, grad_heads[rows, a * size : (a + 1) * size], 0.0).astype(BF16)
                    for a in heads
                ],
                axis=0,
            )
            k_win = prefix_v[pl.ds(start, window), 2 * h * size : (2 * h + 1) * size]
            v_win = prefix_v[pl.ds(start, window), (2 * h + 1) * size : (2 * h + 2) * size]
            k_own = key[rows, h * size : (h + 1) * size]
            v_own = value[rows, h * size : (h + 1) * size]
            b_pre, b_own = p_pre[n, h], p_own[n, h]
            delta = jnp.sum(g.astype(F32) * out, axis=-1, keepdims=True)
            ds_pre = (b_pre.astype(F32) * (dot_nt(g, v_win) - delta)).astype(BF16)
            ds_own = (b_own.astype(F32) * (dot_nt(g, v_own) - delta)).astype(BF16)
            grad_q = scale * (dot(ds_pre, k_win) + dot(ds_own, k_own))
            for i, a in enumerate(heads):
                cols = slice(a * size, (a + 1) * size)
                one = grad_q[i * slot_len : (i + 1) * slot_len]
                grads[rows, cols] = norm_back(hq[rows, cols], q_gain[...], one).astype(BF16)
            cols = slice(h * size, (h + 1) * size)
            q_width, k_width = query.shape[1], key.shape[1]
            key_cols = slice(q_width + h * size, q_width + (h + 1) * size)
            value_cols = slice(q_width + k_width + h * size, q_width + k_width + (h + 1) * size)
            grad_k = scale * dot_tn(ds_own, q)
            grads[rows, key_cols] = norm_back(hk[rows, cols], k_gain[...], grad_k).astype(BF16)
            grads[rows, value_cols] = dot_tn(b_own, g).astype(BF16)
            k_cols = slice(2 * h * size, (2 * h + 1) * size)
            v_cols = slice((2 * h + 1) * size, (2 * h + 2) * size)
            grad_prefix[pl.ds(start, window), k_cols] += scale * dot_tn(ds_pre, q)
            grad_prefix[pl.ds(start, window), v_cols] += dot_tn(b_pre, g)
    chips = prefix_v.shape[0] // terms[0].shape[1] if len(terms) > 1 else 1
    for ref, steps in zip(terms, TERMS if len(terms) > 1 else ((0,),)):
        for i, step in enumerate(steps):
            ref[i] = grad_prefix[slot_rows(chips, ref.shape[1], step), :]

    def make(cols):
        return dot_nt(grads[...], w_all[cols, :]).astype(BF16)

    make_blocks(make, names, parts)


def backward(names, scalars, cotangent, kept, terms):
    slots = scalars[-1].shape[0]
    query, key, w_out, prefix = kept[0], kept[1], kept[8], kept[12]
    rows, q_width = query.shape
    k_width = key.shape[1]
    count, kv_width = prefix.shape
    results = [(x, F32) for x in terms] + block_shapes(names, rows, cotangent[0].shape[2])
    found = pl.pallas_call(
        functools.partial(backward_kernel, slots, names),
        in_specs=[SMEM] * 3 + [VMEM] * (len(cotangent) + len(kept)),
        out_specs=[VMEM] * len(results),
        out_shape=in_vmem(results),
        scratch_shapes=[
            pltpu.VMEM((count, kv_width), F32),
            pltpu.VMEM((rows, q_width + 2 * k_width), BF16),
        ],
        compiler_params=pltpu.CompilerParams(vmem_limit_bytes=vmem_room(count)),
        cost_estimate=lasting(3.5),
    )(*held_in(pltpu.SMEM, scalars), *held_in(pltpu.VMEM, [*cotangent, *kept]))
    return found[: len(terms)], found[len(terms) :]


def last_kernel(counts, *refs):
    take, rest = taker(refs)
    groups = [take(len(count)) for count in counts]
    results = take(len(counts))
    stage = take(len(counts))
    (sems,) = take(1)
    copies = Copies(sems)
    stores = []
    for count, group, result, ref in zip(counts, groups, results, stage):
        whole = 0.0
        for i, term in zip(count, group):
            whole = whole + term[i].astype(F32)
        ref[...] = whole.astype(BF16)
        stores.append(copies.start(ref, result))
    wait(stores)


def last_sums(groups):
    arrays = [array for group in groups for array, _ in group]
    shapes = [jax.ShapeDtypeStruct(group[0][0].shape[1:], BF16) for group in groups]
    return pl.pallas_call(
        functools.partial(last_kernel, [[i for _, i in group] for group in groups]),
        in_specs=[VMEM] * len(arrays),
        out_specs=[HBM] * len(groups),
        out_shape=shapes,
        scratch_shapes=in_vmem(like(shapes)) + [pltpu.SemaphoreType.DMA((len(groups),))],
        compiler_params=pltpu.CompilerParams(vmem_limit_bytes=vmem_room(0)),
        cost_estimate=lasting(0.9),
    )(*held_in(pltpu.VMEM, arrays))


def trade(name, block, axis, step):
    with jax.named_scope(name):
        return lax.ppermute(block, axis, [(i, i ^ step) for i in range(lax.axis_size(axis))])


def after(value, *others):
    return lax.optimization_barrier((value, *others))[0]


def total(*terms):
    whole = terms[0].astype(F32)
    for term in terms[1:]:
        whole = whole + term.astype(F32)
    return whole.astype(BF16)


def per_device(
    hidden_rows,
    w_query,
    w_key,
    w_value,
    w_out,
    q_gain,
    k_gain,
    prefix_kv,
    cotangent,
    prompt_len,
    resp_prompt,
    resp_len,
):
    chips = lax.axis_size("dp")
    scalars = (prompt_len, resp_prompt, resp_len)
    q_gain, k_gain = q_gain[None], k_gain[None]
    own = cotangent[None]
    far = trade("gather_far", own, "mp", 4)
    near = trade("gather_near", own, "mp", 2)
    if chips == 4:
        others = [trade("gather_prefix", prefix_kv, "dp", k) for k in range(1, chips)]
    else:
        prefix_kv, others = lax.all_gather(prefix_kv, "dp", axis=0, tiled=True), []
    far = after(far, *others)
    both = trade("gather_both", far, "mp", 2)
    pair = jnp.concatenate([far, near])
    pair_x = trade("gather_pair_x", pair, "mp", 1)
    own_x = trade("gather_own_x", own, "mp", 1)
    scalars, projected, weights, prefix, own = project(
        scalars, after(hidden_rows, far), w_query, w_key, w_value, q_gain, k_gain, prefix_kv, own
    )
    both_x = trade("gather_both_x", after(both, projected[0]), "mp", 1)
    probed, parts = forward(
        OUT, cotangent.shape[1], q_gain.shape[1], scalars, *projected[:3], w_out,
        [prefix, *others],
    )
    back = [own, pair, both, own_x, pair_x, both_x]
    shape = prefix_kv.shape
    terms = [(1, *shape)] if chips != 4 else [(len(steps), *shape) for steps in TERMS]
    terms, grads = backward(IN, scalars, back, [*projected, *weights, w_out, *probed], terms)

    out_a, out_b, kept_a, kept_b = parts
    got_a = trade("out_a", out_a, "mp", 2)
    got_b = trade("out_b", after(out_b, pair_x), "mp", 2)
    out_a = total(kept_a, got_a)
    got_out = trade("out_mid", out_a, "mp", 4)
    in_75, in_3, in_1, in_6, in_4, in_2, in_0 = grads
    got_75 = trade("in_75", in_75, "mp", 1)
    got_3 = trade("in_3", in_3, "mp", 1)
    in_6 = total(after(in_6, out_a), got_75[:1])
    got_6 = trade("in_6", in_6, "mp", 2)
    in_2 = total(in_2, got_3)
    got_2 = trade("in_2", in_2, "mp", 2)
    if chips == 4:
        got = trade("grad_prefix_y", after(terms[0], in_2), "dp", 2)
        last = trade("grad_prefix_core", terms[1][1:] + got[1:], "dp", 1)
    in_4 = total(after(in_4, got_b, got_out, in_2), got_75[1:], got_6)
    got_4 = trade("in_4", in_4, "mp", 4)
    got_1 = trade("in_1", after(in_1, in_2), "mp", 1)
    got_x = trade("out_x", total(after(kept_b, in_4)[1:], got_b[1:], got_out[1:]), "mp", 1)
    groups = [
        [(kept_b, 0), (got_b, 0), (got_out, 0), (got_x, 0)],
        [(in_0, 0), (got_1, 0), (got_2, 0), (got_4, 0)],
    ]
    if chips == 4:
        groups.append([(terms[1], 0), (got, 0), (last, 0)])
        return last_sums(groups)
    grad_prefix = lax.psum_scatter(terms[0][0], "dp", scatter_dimension=0, tiled=True)
    return *last_sums(groups), grad_prefix.astype(BF16)


def solution(mesh):
    in_specs = (
        P("dp", None),
        P(None, "mp"),
        P(None, "mp"),
        P(None, "mp"),
        P("mp", None),
        P(),
        P(),
        P("dp", "mp"),
        P("dp", "mp"),
        P(),
        P("dp"),
        P("dp"),
    )
    out_specs = (P("dp", "mp"), P("dp", "mp"), P("dp", "mp"))
    return jax.shard_map(
        per_device, mesh=mesh, in_specs=in_specs, out_specs=out_specs, check_vma=False
    )
```

```python
import functools

import jax
import jax.numpy as jnp
from jax import lax
from jax.experimental import pallas as pl
from jax.experimental.pallas import tpu as pltpu
from jax.sharding import PartitionSpec as P

EPS = 1e-06
NEG = -1e30
ROWS = 16
HELD = ((0,), (4, 2), (6,), (1,), (5, 3), (7,))
OUT = ((6, 7), (2, 3), (4, 5), (0, 1))
TERMS = ((1, 3), (0, 2))
IN_FIRST = ((7, 5),)
IN_REST = ((3,), (1,), (6,), (4,), (2,), (0,))
F32 = jnp.float32
BF16 = jnp.bfloat16
HBM = pl.BlockSpec(memory_space=pltpu.HBM)
SMEM = pl.BlockSpec(memory_space=pltpu.SMEM)
VMEM = pl.BlockSpec(memory_space=pltpu.VMEM)


def dot(left, right):
    return jnp.dot(left, right, preferred_element_type=F32)


def dot_nt(left, right):
    return lax.dot_general(left, right, (((1,), (1,)), ((), ())), preferred_element_type=F32)


def dot_tn(left, right):
    return lax.dot_general(left, right, (((0,), (0,)), ((), ())), preferred_element_type=F32)


def inverse_root(hidden):
    return lax.rsqrt(jnp.mean(hidden * hidden, axis=-1, keepdims=True) + EPS)


def norm_back(hidden, gain, grad):
    root = inverse_root(hidden)
    unit = hidden * root
    scaled = grad * gain
    return root * (scaled - unit * jnp.mean(scaled * unit, axis=-1, keepdims=True))


class Copies:
    def __init__(self, sems):
        self.sems, self.count = sems, 0

    def start(self, source, target):
        copy = pltpu.make_async_copy(source, target, self.sems.at[self.count])
        self.count += 1
        copy.start()
        return copy


def wait(copies):
    for copy in copies:
        copy.wait()


def prompt_span(prompt_len, prompt):
    first, last = 0, 0
    end = 0
    for p in range(prompt_len.shape[0]):
        begin = end
        end = end + prompt_len[p]
        first = jnp.where(prompt == p, begin, first)
        last = jnp.where(prompt == p, end, last)
    return first, last


def window_rows(count):
    return min(count, count // 3 + ROWS)


def window_start(first, count):
    start = jnp.minimum(first // ROWS * ROWS, count - window_rows(count))
    return pl.multiple_of(start, ROWS)


def slot_rows(slots, rows, step):
    if slots == 1:
        return pl.ds(0, rows)
    return pl.ds(pl.multiple_of((lax.axis_index("dp") ^ step) * rows, ROWS), rows)


def features(block, width):
    return pl.ds(pl.multiple_of(block * width, width), width)


def stacked(ref, rows, heads, size):
    return jnp.concatenate([ref[rows, a * size : (a + 1) * size] for a in heads], axis=0)


def make_blocks(make, names, refs):
    me = lax.axis_index("mp")
    for blocks, ref in zip(names, refs):
        for i, block in enumerate(blocks):
            ref[i] = make(features(me ^ block, ref.shape[-1]))


def taker(refs):
    refs = list(refs)

    def take(count):
        found, refs[:count] = refs[:count], []
        return found

    return take, refs


def project_kernel(*refs):
    take, _ = taker(refs)
    scalars = take(3)
    hidden, w_q, w_k, w_v, q_gain, k_gain, prefix, own = take(8)
    scalars_v = take(3)
    query, key, value, hq, hk = take(5)
    w_all, qg_v, kg_v, prefix_v, own_v = take(5)
    hidden_v, sems = take(2)

    copies = Copies(sems)
    depth = hidden.shape[1]
    steps = 4
    part = depth // steps
    places, end = [], 0
    for w in (w_q, w_k, w_v):
        places.append(slice(end, end + w.shape[1]))
        end += w.shape[1]
    loads = []
    for i in range(steps):
        cut = pl.ds(i * part, part)
        loads.append(
            [copies.start(hidden.at[:, cut], hidden_v.at[:, cut])]
            + [
                copies.start(w.at[cut], w_all.at[cut, place])
                for w, place in zip((w_q, w_k, w_v), places)
            ]
        )
    small = [copies.start(q_gain, qg_v), copies.start(k_gain, kg_v)]
    small += [copies.start(source, target) for source, target in zip(scalars, scalars_v)]
    small += [copies.start(prefix, prefix_v), copies.start(own, own_v)]

    whole = 0.0
    for i, load in enumerate(loads):
        wait(load)
        cut = slice(i * part, (i + 1) * part)
        whole += dot(hidden_v[:, cut], w_all[cut, :])
    hq[...], hk[...] = whole[:, places[0]], whole[:, places[1]]
    value[...] = whole[:, places[2]].astype(BF16)
    wait(small)
    size = qg_v.shape[1]
    for ref, gain, out in ((hq, qg_v, query), (hk, kg_v, key)):
        for at in range(0, ref.shape[1], size):
            head = ref[:, at : at + size]
            out[:, at : at + size] = (head * inverse_root(head) * gain[...]).astype(BF16)


def project(scalars, hidden, w_q, w_k, w_v, q_gain, k_gain, prefix, own):
    rows, depth = hidden.shape
    q_width, k_width = w_q.shape[1], w_k.shape[1]
    small = [q_gain, k_gain, prefix, own]
    operands = [*scalars, hidden, w_q, w_k, w_v, *small]
    kept = [
        ((rows, q_width), BF16),
        ((rows, k_width), BF16),
        ((rows, k_width), BF16),
        ((rows, q_width), F32),
        ((rows, k_width), F32),
        ((depth, q_width + 2 * k_width), BF16),
    ] + like(small)
    found = pl.pallas_call(
        project_kernel,
        in_specs=[HBM] * len(operands),
        out_specs=[SMEM] * 3 + [VMEM] * len(kept),
        out_shape=[pltpu.SMEM(x.shape, jnp.int32) for x in scalars] + in_vmem(kept),
        scratch_shapes=[pltpu.VMEM(hidden.shape, hidden.dtype), pltpu.SemaphoreType.DMA((32,))],
        compiler_params=pltpu.CompilerParams(vmem_limit_bytes=vmem_room(prefix.shape[0])),
        cost_estimate=lasting(2.6),
    )(*held_in(pltpu.HBM, operands))
    return found[:3], found[3:8], found[8:11], found[11], found[12]


def forward_kernel(slots, names, *refs):
    take, rest = taker(refs)
    prompt_len, resp_prompt, resp_len = take(3)
    query, key, value, wo_v = take(4)
    prefix = take(len(rest) - 4 - len(names) - 1)
    p_pre, p_own, heads_out, prefix_v = take(4)
    parts = take(len(names))
    (out_bf,) = take(1)

    held = prefix[0].shape[0]
    for k, ref in enumerate(prefix):
        prefix_v[slot_rows(len(prefix), held, k), :] = ref[...]
    size = heads_out.shape[1] * p_own.shape[3] // p_own.shape[2] // p_own.shape[1]
    count = prefix_v.shape[0]
    window = window_rows(count)
    slot_len = query.shape[0] // slots
    kv_heads = key.shape[1] // size
    groups = query.shape[1] // key.shape[1]
    scale = size ** (-0.5)
    for n in range(slots):
        first, last = prompt_span(prompt_len, resp_prompt[n])
        start = window_start(first, count)
        rows = slice(n * slot_len, (n + 1) * slot_len)
        live = lax.broadcasted_iota(jnp.int32, (slot_len, size), 0) < resp_len[n]
        for h in range(kv_heads):
            heads = range(h * groups, (h + 1) * groups)
            q = stacked(query, rows, heads, size)
            k_win = prefix_v[pl.ds(start, window), 2 * h * size : (2 * h + 1) * size]
            v_win = prefix_v[pl.ds(start, window), (2 * h + 1) * size : (2 * h + 2) * size]
            k_own = key[rows, h * size : (h + 1) * size]
            v_own = value[rows, h * size : (h + 1) * size]
            tall = groups * slot_len
            place = start + lax.broadcasted_iota(jnp.int32, (tall, window), 1)
            s_pre = jnp.where((place >= first) & (place < last), dot_nt(q, k_win) * scale, NEG)
            token = lax.broadcasted_iota(jnp.int32, (groups, slot_len, slot_len), 1)
            token = token.reshape(tall, slot_len)
            other = lax.broadcasted_iota(jnp.int32, (tall, slot_len), 1)
            s_own = jnp.where(
                (other <= token) & (other < resp_len[n]), dot_nt(q, k_own) * scale, NEG
            )
            top = jnp.maximum(
                jnp.max(s_pre, axis=-1, keepdims=True), jnp.max(s_own, axis=-1, keepdims=True)
            )
            e_pre = jnp.exp(s_pre - top)
            e_own = jnp.exp(s_own - top)
            total = jnp.sum(e_pre, axis=-1, keepdims=True) + jnp.sum(e_own, axis=-1, keepdims=True)
            b_pre = (e_pre / total).astype(BF16)
            b_own = (e_own / total).astype(BF16)
            p_pre[n, h] = b_pre
            p_own[n, h] = b_own
            out = dot(b_pre, v_win) + dot(b_own, v_own)
            for i, a in enumerate(heads):
                one = out[i * slot_len : (i + 1) * slot_len]
                heads_out[rows, a * size : (a + 1) * size] = one
                out_bf[rows, a * size : (a + 1) * size] = jnp.where(live, one, 0.0).astype(BF16)

    def make(cols):
        return dot(out_bf[...], wo_v[:, cols]).astype(BF16)

    make_blocks(make, names, parts)


def block_shapes(names, rows, width):
    return [((len(blocks), rows, width), BF16) for blocks in names]


def in_vmem(shapes):
    return [pltpu.VMEM(*x) for x in shapes]


def held_in(space, arrays):
    return [pltpu.with_memory_space_constraint(x, space) for x in arrays]


def lasting(us):
    return pl.CostEstimate(flops=int(us * 1.15e9), bytes_accessed=0, transcendentals=0)


def like(arrays):
    return [(x.shape, x.dtype) for x in arrays]


def vmem_room(prefix_rows):
    return 48 << 20 if prefix_rows > 1024 else 24 << 20


def forward(names, width, size, scalars, query, key, value, w_out, prefix):
    slots = scalars[-1].shape[0]
    rows, q_width = query.shape
    k_width = key.shape[1]
    count = sum(x.shape[0] for x in prefix)
    window = window_rows(count)
    slot_len = rows // slots
    kv_heads, tall = k_width // size, slot_len * q_width // k_width
    results = [
        ((slots, kv_heads, tall, window), BF16),
        ((slots, kv_heads, tall, slot_len), BF16),
        ((rows, q_width), F32),
        ((count, prefix[0].shape[1]), BF16),
    ] + block_shapes(names, rows, width)
    operands = [query, key, value, w_out, *prefix]
    found = pl.pallas_call(
        functools.partial(forward_kernel, slots, names),
        in_specs=[SMEM] * 3 + [VMEM] * len(operands),
        out_specs=[VMEM] * len(results),
        out_shape=in_vmem(results),
        scratch_shapes=[pltpu.VMEM((rows, q_width), BF16)],
        compiler_params=pltpu.CompilerParams(vmem_limit_bytes=vmem_room(count)),
        cost_estimate=lasting(1.7),
    )(*held_in(pltpu.SMEM, scalars), *held_in(pltpu.VMEM, operands))
    return found[:4], found[4:]


def backward_kernel(slots, names, *refs):
    take, rest = taker(refs)
    prompt_len, resp_prompt, resp_len = take(3)
    cotangent = take(len(HELD))
    query, key, value, hq, hk = take(5)
    w_all, q_gain, k_gain, w_out = take(4)
    p_pre, p_own, heads_out, prefix_v = take(4)
    terms = take(len(rest) - len(names) - 2)
    parts = take(len(names))
    grads, grad_prefix = take(2)

    width = cotangent[0].shape[2]
    me = lax.axis_index("mp")
    grad_heads = 0.0
    for blocks, ref in zip(HELD, cotangent):
        for i, block in enumerate(blocks):
            grad_heads += dot_nt(ref[i], w_out[:, features(me ^ block, width)])
    grad_prefix[...] = jnp.zeros_like(grad_prefix)

    count = prefix_v.shape[0]
    window = window_rows(count)
    slot_len = query.shape[0] // slots
    size = q_gain.shape[1]
    kv_heads = key.shape[1] // size
    groups = query.shape[1] // key.shape[1]
    scale = size ** (-0.5)
    for n in range(slots):
        first, _ = prompt_span(prompt_len, resp_prompt[n])
        start = window_start(first, count)
        rows = slice(n * slot_len, (n + 1) * slot_len)
        live = lax.broadcasted_iota(jnp.int32, (slot_len, size), 0) < resp_len[n]
        for h in range(kv_heads):
            heads = range(h * groups, (h + 1) * groups)
            q = stacked(query, rows, heads, size)
            out = stacked(heads_out, rows, heads, size)
            g = jnp.concatenate(
                [
                    jnp.where(live, grad_heads[rows, a * size : (a + 1) * size], 0.0).astype(BF16)
                    for a in heads
                ],
                axis=0,
            )
            k_win = prefix_v[pl.ds(start, window), 2 * h * size : (2 * h + 1) * size]
            v_win = prefix_v[pl.ds(start, window), (2 * h + 1) * size : (2 * h + 2) * size]
            k_own = key[rows, h * size : (h + 1) * size]
            v_own = value[rows, h * size : (h + 1) * size]
            b_pre, b_own = p_pre[n, h], p_own[n, h]
            delta = jnp.sum(g.astype(F32) * out, axis=-1, keepdims=True)
            ds_pre = (b_pre.astype(F32) * (dot_nt(g, v_win) - delta)).astype(BF16)
            ds_own = (b_own.astype(F32) * (dot_nt(g, v_own) - delta)).astype(BF16)
            grad_q = scale * (dot(ds_pre, k_win) + dot(ds_own, k_own))
            for i, a in enumerate(heads):
                cols = slice(a * size, (a + 1) * size)
                one = grad_q[i * slot_len : (i + 1) * slot_len]
                grads[rows, cols] = norm_back(hq[rows, cols], q_gain[...], one).astype(BF16)
            cols = slice(h * size, (h + 1) * size)
            q_width, k_width = query.shape[1], key.shape[1]
            key_cols = slice(q_width + h * size, q_width + (h + 1) * size)
            value_cols = slice(q_width + k_width + h * size, q_width + k_width + (h + 1) * size)
            grad_k = scale * dot_tn(ds_own, q)
            grads[rows, key_cols] = norm_back(hk[rows, cols], k_gain[...], grad_k).astype(BF16)
            grads[rows, value_cols] = dot_tn(b_own, g).astype(BF16)
            k_cols = slice(2 * h * size, (2 * h + 1) * size)
            v_cols = slice((2 * h + 1) * size, (2 * h + 2) * size)
            grad_prefix[pl.ds(start, window), k_cols] += scale * dot_tn(ds_pre, q)
            grad_prefix[pl.ds(start, window), v_cols] += dot_tn(b_pre, g)
    chips = prefix_v.shape[0] // terms[0].shape[1] if len(terms) > 1 else 1
    for ref, steps in zip(terms, TERMS if len(terms) > 1 else ((0,),)):
        for i, step in enumerate(steps):
            ref[i] = grad_prefix[slot_rows(chips, ref.shape[1], step), :]

    def make(cols):
        return dot_nt(grads[...], w_all[cols, :]).astype(BF16)

    make_blocks(make, names, parts)


def backward(names, scalars, cotangent, kept, terms):
    slots = scalars[-1].shape[0]
    query, key, w_out, prefix = kept[0], kept[1], kept[8], kept[12]
    rows, q_width = query.shape
    k_width = key.shape[1]
    count, kv_width = prefix.shape
    results = [(x, F32) for x in terms] + block_shapes(names, rows, cotangent[0].shape[2])
    results.append(((rows, q_width + 2 * k_width), BF16))
    found = pl.pallas_call(
        functools.partial(backward_kernel, slots, names),
        in_specs=[SMEM] * 3 + [VMEM] * (len(cotangent) + len(kept)),
        out_specs=[VMEM] * len(results),
        out_shape=in_vmem(results),
        scratch_shapes=[pltpu.VMEM((count, kv_width), F32)],
        compiler_params=pltpu.CompilerParams(vmem_limit_bytes=vmem_room(count)),
        cost_estimate=lasting(2.5),
    )(*held_in(pltpu.SMEM, scalars), *held_in(pltpu.VMEM, [*cotangent, *kept]))
    return found[: len(terms)], found[len(terms) : -1], found[-1]


def rest_kernel(names, *refs):
    grads, w_all, *parts = refs

    def make(cols):
        return dot_nt(grads[...], w_all[cols, :]).astype(BF16)

    make_blocks(make, names, parts)


def rest(names, width, grads, w_all):
    results = block_shapes(names, grads.shape[0], width)
    return pl.pallas_call(
        functools.partial(rest_kernel, names),
        in_specs=[VMEM] * 2,
        out_specs=[VMEM] * len(results),
        out_shape=in_vmem(results),
        compiler_params=pltpu.CompilerParams(vmem_limit_bytes=vmem_room(0)),
        cost_estimate=lasting(0.7),
    )(*held_in(pltpu.VMEM, [grads, w_all]))


def last_kernel(counts, *refs):
    take, rest = taker(refs)
    groups = [take(len(count)) for count in counts]
    results = take(len(counts))
    stage = take(len(counts))
    (sems,) = take(1)
    copies = Copies(sems)
    stores = []
    for count, group, result, ref in zip(counts, groups, results, stage):
        whole = 0.0
        for i, term in zip(count, group):
            whole = whole + term[i].astype(F32)
        ref[...] = whole.astype(BF16)
        stores.append(copies.start(ref, result))
    wait(stores)


def last_sums(groups):
    arrays = [array for group in groups for array, _ in group]
    shapes = [jax.ShapeDtypeStruct(group[0][0].shape[1:], BF16) for group in groups]
    return pl.pallas_call(
        functools.partial(last_kernel, [[i for _, i in group] for group in groups]),
        in_specs=[VMEM] * len(arrays),
        out_specs=[HBM] * len(groups),
        out_shape=shapes,
        scratch_shapes=in_vmem(like(shapes)) + [pltpu.SemaphoreType.DMA((len(groups),))],
        compiler_params=pltpu.CompilerParams(vmem_limit_bytes=vmem_room(0)),
        cost_estimate=lasting(0.9),
    )(*held_in(pltpu.VMEM, arrays))


def trade(name, block, axis, step):
    with jax.named_scope(name):
        return lax.ppermute(block, axis, [(i, i ^ step) for i in range(lax.axis_size(axis))])


def after(value, *others):
    return lax.optimization_barrier((value, *others))[0]


def total(*terms):
    whole = terms[0].astype(F32)
    for term in terms[1:]:
        whole = whole + term.astype(F32)
    return whole.astype(BF16)


def per_device(
    hidden_rows,
    w_query,
    w_key,
    w_value,
    w_out,
    q_gain,
    k_gain,
    prefix_kv,
    cotangent,
    prompt_len,
    resp_prompt,
    resp_len,
):
    chips = lax.axis_size("dp")
    scalars = (prompt_len, resp_prompt, resp_len)
    q_gain, k_gain = q_gain[None], k_gain[None]
    own = cotangent[None]
    far = trade("gather_far", own, "mp", 4)
    near = trade("gather_near", own, "mp", 2)
    if chips == 4:
        others = [trade("gather_prefix", prefix_kv, "dp", k) for k in range(1, chips)]
    else:
        prefix_kv, others = lax.all_gather(prefix_kv, "dp", axis=0, tiled=True), []
    far = after(far, *others)
    both = trade("gather_both", far, "mp", 2)
    pair = jnp.concatenate([far, near])
    pair_x = trade("gather_pair_x", pair, "mp", 1)
    own_x = trade("gather_own_x", own, "mp", 1)
    scalars, projected, weights, prefix, own = project(
        scalars, after(hidden_rows, far), w_query, w_key, w_value, q_gain, k_gain, prefix_kv, own
    )
    both_x = trade("gather_both_x", after(both, projected[0]), "mp", 1)
    probed, parts = forward(
        OUT, cotangent.shape[1], q_gain.shape[1], scalars, *projected[:3], w_out,
        [prefix, *others],
    )
    back = [own, pair, both, own_x, pair_x, both_x]
    shape = prefix_kv.shape
    terms = [(1, *shape)] if chips != 4 else [(len(steps), *shape) for steps in TERMS]
    kept = [*projected, *weights, w_out, *probed]
    terms, (in_75,), grads = backward(IN_FIRST, scalars, back, kept, terms)
    in_3, in_1, in_6, in_4, in_2, in_0 = rest(IN_REST, cotangent.shape[1], grads, weights[0])

    out_a, out_b, kept_a, kept_b = parts
    got_a = trade("out_a", out_a, "mp", 2)
    got_b = trade("out_b", after(out_b, pair_x), "mp", 2)
    out_a = total(kept_a, got_a)
    got_out = trade("out_mid", out_a, "mp", 4)
    got_75 = trade("in_75", in_75, "mp", 1)
    got_3 = trade("in_3", in_3, "mp", 1)
    in_6 = total(after(in_6, out_a), got_75[:1])
    got_6 = trade("in_6", in_6, "mp", 2)
    in_2 = total(in_2, got_3)
    got_2 = trade("in_2", in_2, "mp", 2)
    if chips == 4:
        got = trade("grad_prefix_core", after(terms[0], in_2), "dp", 1)
        last = trade("grad_prefix_y", terms[1][1:] + got[1:], "dp", 2)
    in_4 = total(after(in_4, got_b, got_out, in_2), got_75[1:], got_6)
    got_4 = trade("in_4", in_4, "mp", 4)
    got_1 = trade("in_1", after(in_1, in_4), "mp", 1)
    got_x = trade("out_x", total(after(kept_b, in_4)[1:], got_b[1:], got_out[1:]), "mp", 1)
    groups = [
        [(kept_b, 0), (got_b, 0), (got_out, 0), (got_x, 0)],
        [(in_0, 0), (got_1, 0), (got_2, 0), (got_4, 0)],
    ]
    if chips == 4:
        groups.append([(terms[1], 0), (got, 0), (last, 0)])
        return last_sums(groups)
    grad_prefix = lax.psum_scatter(terms[0][0], "dp", scatter_dimension=0, tiled=True)
    return *last_sums(groups), grad_prefix.astype(BF16)


def solution(mesh):
    in_specs = (
        P("dp", None),
        P(None, "mp"),
        P(None, "mp"),
        P(None, "mp"),
        P("mp", None),
        P(),
        P(),
        P("dp", "mp"),
        P("dp", "mp"),
        P(),
        P("dp"),
        P("dp"),
    )
    out_specs = (P("dp", "mp"), P("dp", "mp"), P("dp", "mp"))
    return jax.shard_map(
        per_device, mesh=mesh, in_specs=in_specs, out_specs=out_specs, check_vma=False
    )
```

```python
import functools

import jax
import jax.numpy as jnp
from jax import lax
from jax.experimental import pallas as pl
from jax.experimental.pallas import tpu as pltpu
from jax.sharding import PartitionSpec as P

EPS = 1e-06
NEG = -1e30
ROWS = 16
HELD = ((0,), (4, 2), (6,), (1,), (5, 3), (7,))
OUT = ((6, 7), (2, 3), (4, 5), (0, 1))
TERMS = ((2, 3), (0, 1))
IN_FIRST = ((7, 5),)
IN_REST = ((3,), (1,), (6,), (4,), (2,), (0,))
F32 = jnp.float32
BF16 = jnp.bfloat16
HBM = pl.BlockSpec(memory_space=pltpu.HBM)
SMEM = pl.BlockSpec(memory_space=pltpu.SMEM)
VMEM = pl.BlockSpec(memory_space=pltpu.VMEM)


def dot(left, right):
    return jnp.dot(left, right, preferred_element_type=F32)


def dot_nt(left, right):
    return lax.dot_general(left, right, (((1,), (1,)), ((), ())), preferred_element_type=F32)


def dot_tn(left, right):
    return lax.dot_general(left, right, (((0,), (0,)), ((), ())), preferred_element_type=F32)


def inverse_root(hidden):
    return lax.rsqrt(jnp.mean(hidden * hidden, axis=-1, keepdims=True) + EPS)


def norm_back(hidden, gain, grad):
    root = inverse_root(hidden)
    unit = hidden * root
    scaled = grad * gain
    return root * (scaled - unit * jnp.mean(scaled * unit, axis=-1, keepdims=True))


class Copies:
    def __init__(self, sems):
        self.sems, self.count = sems, 0

    def start(self, source, target):
        copy = pltpu.make_async_copy(source, target, self.sems.at[self.count])
        self.count += 1
        copy.start()
        return copy


def wait(copies):
    for copy in copies:
        copy.wait()


def prompt_span(prompt_len, prompt):
    first, last = 0, 0
    end = 0
    for p in range(prompt_len.shape[0]):
        begin = end
        end = end + prompt_len[p]
        first = jnp.where(prompt == p, begin, first)
        last = jnp.where(prompt == p, end, last)
    return first, last


def window_rows(count):
    return min(count, count // 3 + ROWS)


def window_start(first, count):
    start = jnp.minimum(first // ROWS * ROWS, count - window_rows(count))
    return pl.multiple_of(start, ROWS)


def slot_rows(slots, rows, step):
    if slots == 1:
        return pl.ds(0, rows)
    return pl.ds(pl.multiple_of((lax.axis_index("dp") ^ step) * rows, ROWS), rows)


def features(block, width):
    return pl.ds(pl.multiple_of(block * width, width), width)


def stacked(ref, rows, heads, size):
    return jnp.concatenate([ref[rows, a * size : (a + 1) * size] for a in heads], axis=0)


def make_blocks(make, names, refs):
    me = lax.axis_index("mp")
    for blocks, ref in zip(names, refs):
        for i, block in enumerate(blocks):
            ref[i] = make(features(me ^ block, ref.shape[-1]))


def taker(refs):
    refs = list(refs)

    def take(count):
        found, refs[:count] = refs[:count], []
        return found

    return take, refs


def project_kernel(*refs):
    take, _ = taker(refs)
    scalars = take(3)
    hidden, w_q, w_k, w_v, q_gain, k_gain, prefix, own = take(8)
    scalars_v = take(3)
    query, key, value, hq, hk = take(5)
    w_all, qg_v, kg_v, prefix_v, own_v = take(5)
    hidden_v, sems = take(2)

    copies = Copies(sems)
    depth = hidden.shape[1]
    steps = 4
    part = depth // steps
    places, end = [], 0
    for w in (w_q, w_k, w_v):
        places.append(slice(end, end + w.shape[1]))
        end += w.shape[1]
    loads = []
    for i in range(steps):
        cut = pl.ds(i * part, part)
        loads.append(
            [copies.start(hidden.at[:, cut], hidden_v.at[:, cut])]
            + [
                copies.start(w.at[cut], w_all.at[cut, place])
                for w, place in zip((w_q, w_k, w_v), places)
            ]
        )
    small = [copies.start(q_gain, qg_v), copies.start(k_gain, kg_v)]
    small += [copies.start(source, target) for source, target in zip(scalars, scalars_v)]
    small += [copies.start(prefix, prefix_v), copies.start(own, own_v)]

    whole = 0.0
    for i, load in enumerate(loads):
        wait(load)
        cut = slice(i * part, (i + 1) * part)
        whole += dot(hidden_v[:, cut], w_all[cut, :])
    hq[...], hk[...] = whole[:, places[0]], whole[:, places[1]]
    value[...] = whole[:, places[2]].astype(BF16)
    wait(small)
    size = qg_v.shape[1]
    for ref, gain, out in ((hq, qg_v, query), (hk, kg_v, key)):
        for at in range(0, ref.shape[1], size):
            head = ref[:, at : at + size]
            out[:, at : at + size] = (head * inverse_root(head) * gain[...]).astype(BF16)


def project(scalars, hidden, w_q, w_k, w_v, q_gain, k_gain, prefix, own):
    rows, depth = hidden.shape
    q_width, k_width = w_q.shape[1], w_k.shape[1]
    small = [q_gain, k_gain, prefix, own]
    operands = [*scalars, hidden, w_q, w_k, w_v, *small]
    kept = [
        ((rows, q_width), BF16),
        ((rows, k_width), BF16),
        ((rows, k_width), BF16),
        ((rows, q_width), F32),
        ((rows, k_width), F32),
        ((depth, q_width + 2 * k_width), BF16),
    ] + like(small)
    found = pl.pallas_call(
        project_kernel,
        in_specs=[HBM] * len(operands),
        out_specs=[SMEM] * 3 + [VMEM] * len(kept),
        out_shape=[pltpu.SMEM(x.shape, jnp.int32) for x in scalars] + in_vmem(kept),
        scratch_shapes=[pltpu.VMEM(hidden.shape, hidden.dtype), pltpu.SemaphoreType.DMA((32,))],
        compiler_params=pltpu.CompilerParams(vmem_limit_bytes=vmem_room(prefix.shape[0])),
        cost_estimate=lasting(2.6),
    )(*held_in(pltpu.HBM, operands))
    return found[:3], found[3:8], found[8:11], found[11], found[12]


def forward_kernel(slots, names, *refs):
    take, rest = taker(refs)
    prompt_len, resp_prompt, resp_len = take(3)
    query, key, value, wo_v = take(4)
    prefix = take(len(rest) - 4 - len(names) - 1)
    p_pre, p_own, heads_out, prefix_v = take(4)
    parts = take(len(names))
    (out_bf,) = take(1)

    held = prefix[0].shape[0]
    for k, ref in enumerate(prefix):
        prefix_v[slot_rows(len(prefix), held, k), :] = ref[...]
    size = heads_out.shape[1] * p_own.shape[3] // p_own.shape[2] // p_own.shape[1]
    count = prefix_v.shape[0]
    window = window_rows(count)
    slot_len = query.shape[0] // slots
    kv_heads = key.shape[1] // size
    groups = query.shape[1] // key.shape[1]
    scale = size ** (-0.5)
    for n in range(slots):
        first, last = prompt_span(prompt_len, resp_prompt[n])
        start = window_start(first, count)
        rows = slice(n * slot_len, (n + 1) * slot_len)
        live = lax.broadcasted_iota(jnp.int32, (slot_len, size), 0) < resp_len[n]
        for h in range(kv_heads):
            heads = range(h * groups, (h + 1) * groups)
            q = stacked(query, rows, heads, size)
            k_win = prefix_v[pl.ds(start, window), 2 * h * size : (2 * h + 1) * size]
            v_win = prefix_v[pl.ds(start, window), (2 * h + 1) * size : (2 * h + 2) * size]
            k_own = key[rows, h * size : (h + 1) * size]
            v_own = value[rows, h * size : (h + 1) * size]
            tall = groups * slot_len
            place = start + lax.broadcasted_iota(jnp.int32, (tall, window), 1)
            s_pre = jnp.where((place >= first) & (place < last), dot_nt(q, k_win) * scale, NEG)
            token = lax.broadcasted_iota(jnp.int32, (groups, slot_len, slot_len), 1)
            token = token.reshape(tall, slot_len)
            other = lax.broadcasted_iota(jnp.int32, (tall, slot_len), 1)
            s_own = jnp.where(
                (other <= token) & (other < resp_len[n]), dot_nt(q, k_own) * scale, NEG
            )
            top = jnp.maximum(
                jnp.max(s_pre, axis=-1, keepdims=True), jnp.max(s_own, axis=-1, keepdims=True)
            )
            e_pre = jnp.exp(s_pre - top)
            e_own = jnp.exp(s_own - top)
            total = jnp.sum(e_pre, axis=-1, keepdims=True) + jnp.sum(e_own, axis=-1, keepdims=True)
            b_pre = (e_pre / total).astype(BF16)
            b_own = (e_own / total).astype(BF16)
            p_pre[n, h] = b_pre
            p_own[n, h] = b_own
            out = dot(b_pre, v_win) + dot(b_own, v_own)
            for i, a in enumerate(heads):
                one = out[i * slot_len : (i + 1) * slot_len]
                heads_out[rows, a * size : (a + 1) * size] = one
                out_bf[rows, a * size : (a + 1) * size] = jnp.where(live, one, 0.0).astype(BF16)

    def make(cols):
        return dot(out_bf[...], wo_v[:, cols]).astype(BF16)

    make_blocks(make, names, parts)


def block_shapes(names, rows, width):
    return [((len(blocks), rows, width), BF16) for blocks in names]


def in_vmem(shapes):
    return [pltpu.VMEM(*x) for x in shapes]


def held_in(space, arrays):
    return [pltpu.with_memory_space_constraint(x, space) for x in arrays]


def lasting(us):
    return pl.CostEstimate(flops=int(us * 1.15e9), bytes_accessed=0, transcendentals=0)


def like(arrays):
    return [(x.shape, x.dtype) for x in arrays]


def vmem_room(prefix_rows):
    return 48 << 20 if prefix_rows > 1024 else 24 << 20


def forward(names, width, size, scalars, query, key, value, w_out, prefix):
    slots = scalars[-1].shape[0]
    rows, q_width = query.shape
    k_width = key.shape[1]
    count = sum(x.shape[0] for x in prefix)
    window = window_rows(count)
    slot_len = rows // slots
    kv_heads, tall = k_width // size, slot_len * q_width // k_width
    results = [
        ((slots, kv_heads, tall, window), BF16),
        ((slots, kv_heads, tall, slot_len), BF16),
        ((rows, q_width), F32),
        ((count, prefix[0].shape[1]), BF16),
    ] + block_shapes(names, rows, width)
    operands = [query, key, value, w_out, *prefix]
    found = pl.pallas_call(
        functools.partial(forward_kernel, slots, names),
        in_specs=[SMEM] * 3 + [VMEM] * len(operands),
        out_specs=[VMEM] * len(results),
        out_shape=in_vmem(results),
        scratch_shapes=[pltpu.VMEM((rows, q_width), BF16)],
        compiler_params=pltpu.CompilerParams(vmem_limit_bytes=vmem_room(count)),
        cost_estimate=lasting(1.7),
    )(*held_in(pltpu.SMEM, scalars), *held_in(pltpu.VMEM, operands))
    return found[:4], found[4:]


def backward_kernel(slots, names, *refs):
    take, rest = taker(refs)
    prompt_len, resp_prompt, resp_len = take(3)
    cotangent = take(len(HELD))
    query, key, value, hq, hk = take(5)
    w_all, q_gain, k_gain, w_out = take(4)
    p_pre, p_own, heads_out, prefix_v = take(4)
    terms = take(len(rest) - len(names) - 2)
    parts = take(len(names))
    grads, grad_prefix = take(2)

    width = cotangent[0].shape[2]
    me = lax.axis_index("mp")
    grad_heads = 0.0
    for blocks, ref in zip(HELD, cotangent):
        for i, block in enumerate(blocks):
            grad_heads += dot_nt(ref[i], w_out[:, features(me ^ block, width)])
    grad_prefix[...] = jnp.zeros_like(grad_prefix)

    count = prefix_v.shape[0]
    window = window_rows(count)
    slot_len = query.shape[0] // slots
    size = q_gain.shape[1]
    kv_heads = key.shape[1] // size
    groups = query.shape[1] // key.shape[1]
    scale = size ** (-0.5)
    for n in range(slots):
        first, _ = prompt_span(prompt_len, resp_prompt[n])
        start = window_start(first, count)
        rows = slice(n * slot_len, (n + 1) * slot_len)
        live = lax.broadcasted_iota(jnp.int32, (slot_len, size), 0) < resp_len[n]
        for h in range(kv_heads):
            heads = range(h * groups, (h + 1) * groups)
            q = stacked(query, rows, heads, size)
            out = stacked(heads_out, rows, heads, size)
            g = jnp.concatenate(
                [
                    jnp.where(live, grad_heads[rows, a * size : (a + 1) * size], 0.0).astype(BF16)
                    for a in heads
                ],
                axis=0,
            )
            k_win = prefix_v[pl.ds(start, window), 2 * h * size : (2 * h + 1) * size]
            v_win = prefix_v[pl.ds(start, window), (2 * h + 1) * size : (2 * h + 2) * size]
            k_own = key[rows, h * size : (h + 1) * size]
            v_own = value[rows, h * size : (h + 1) * size]
            b_pre, b_own = p_pre[n, h], p_own[n, h]
            delta = jnp.sum(g.astype(F32) * out, axis=-1, keepdims=True)
            ds_pre = (b_pre.astype(F32) * (dot_nt(g, v_win) - delta)).astype(BF16)
            ds_own = (b_own.astype(F32) * (dot_nt(g, v_own) - delta)).astype(BF16)
            grad_q = scale * (dot(ds_pre, k_win) + dot(ds_own, k_own))
            for i, a in enumerate(heads):
                cols = slice(a * size, (a + 1) * size)
                one = grad_q[i * slot_len : (i + 1) * slot_len]
                grads[rows, cols] = norm_back(hq[rows, cols], q_gain[...], one).astype(BF16)
            cols = slice(h * size, (h + 1) * size)
            q_width, k_width = query.shape[1], key.shape[1]
            key_cols = slice(q_width + h * size, q_width + (h + 1) * size)
            value_cols = slice(q_width + k_width + h * size, q_width + k_width + (h + 1) * size)
            grad_k = scale * dot_tn(ds_own, q)
            grads[rows, key_cols] = norm_back(hk[rows, cols], k_gain[...], grad_k).astype(BF16)
            grads[rows, value_cols] = dot_tn(b_own, g).astype(BF16)
            k_cols = slice(2 * h * size, (2 * h + 1) * size)
            v_cols = slice((2 * h + 1) * size, (2 * h + 2) * size)
            grad_prefix[pl.ds(start, window), k_cols] += scale * dot_tn(ds_pre, q)
            grad_prefix[pl.ds(start, window), v_cols] += dot_tn(b_pre, g)
    chips = prefix_v.shape[0] // terms[0].shape[1] if len(terms) > 1 else 1
    for ref, steps in zip(terms, TERMS if len(terms) > 1 else ((0,),)):
        for i, step in enumerate(steps):
            ref[i] = grad_prefix[slot_rows(chips, ref.shape[1], step), :]

    def make(cols):
        return dot_nt(grads[...], w_all[cols, :]).astype(BF16)

    make_blocks(make, names, parts)


def backward(names, scalars, cotangent, kept, terms):
    slots = scalars[-1].shape[0]
    query, key, w_out, prefix = kept[0], kept[1], kept[8], kept[12]
    rows, q_width = query.shape
    k_width = key.shape[1]
    count, kv_width = prefix.shape
    results = [(x, F32) for x in terms] + block_shapes(names, rows, cotangent[0].shape[2])
    results.append(((rows, q_width + 2 * k_width), BF16))
    found = pl.pallas_call(
        functools.partial(backward_kernel, slots, names),
        in_specs=[SMEM] * 3 + [VMEM] * (len(cotangent) + len(kept)),
        out_specs=[VMEM] * len(results),
        out_shape=in_vmem(results),
        scratch_shapes=[pltpu.VMEM((count, kv_width), F32)],
        compiler_params=pltpu.CompilerParams(vmem_limit_bytes=vmem_room(count)),
        cost_estimate=lasting(2.5),
    )(*held_in(pltpu.SMEM, scalars), *held_in(pltpu.VMEM, [*cotangent, *kept]))
    return found[: len(terms)], found[len(terms) : -1], found[-1]


def rest_kernel(names, *refs):
    grads, w_all, *parts = refs

    def make(cols):
        return dot_nt(grads[...], w_all[cols, :]).astype(BF16)

    make_blocks(make, names, parts)


def rest(names, width, grads, w_all):
    results = block_shapes(names, grads.shape[0], width)
    return pl.pallas_call(
        functools.partial(rest_kernel, names),
        in_specs=[VMEM] * 2,
        out_specs=[VMEM] * len(results),
        out_shape=in_vmem(results),
        compiler_params=pltpu.CompilerParams(vmem_limit_bytes=vmem_room(0)),
        cost_estimate=lasting(0.7),
    )(*held_in(pltpu.VMEM, [grads, w_all]))


def last_kernel(counts, *refs):
    take, rest = taker(refs)
    groups = [take(len(count)) for count in counts]
    results = take(len(counts))
    stage = take(len(counts))
    (sems,) = take(1)
    copies = Copies(sems)
    stores = []
    for count, group, result, ref in zip(counts, groups, results, stage):
        whole = 0.0
        for i, term in zip(count, group):
            whole = whole + term[i].astype(F32)
        ref[...] = whole.astype(BF16)
        stores.append(copies.start(ref, result))
    wait(stores)


def last_sums(groups):
    arrays = [array for group in groups for array, _ in group]
    shapes = [jax.ShapeDtypeStruct(group[0][0].shape[1:], BF16) for group in groups]
    return pl.pallas_call(
        functools.partial(last_kernel, [[i for _, i in group] for group in groups]),
        in_specs=[VMEM] * len(arrays),
        out_specs=[HBM] * len(groups),
        out_shape=shapes,
        scratch_shapes=in_vmem(like(shapes)) + [pltpu.SemaphoreType.DMA((len(groups),))],
        compiler_params=pltpu.CompilerParams(vmem_limit_bytes=vmem_room(0)),
        cost_estimate=lasting(0.9),
    )(*held_in(pltpu.VMEM, arrays))


def trade(name, block, axis, step):
    with jax.named_scope(name):
        return lax.ppermute(block, axis, [(i, i ^ step) for i in range(lax.axis_size(axis))])


def after(value, *others):
    return lax.optimization_barrier((value, *others))[0]


def total(*terms):
    whole = terms[0].astype(F32)
    for term in terms[1:]:
        whole = whole + term.astype(F32)
    return whole.astype(BF16)


def per_device(
    hidden_rows,
    w_query,
    w_key,
    w_value,
    w_out,
    q_gain,
    k_gain,
    prefix_kv,
    cotangent,
    prompt_len,
    resp_prompt,
    resp_len,
):
    chips = lax.axis_size("dp")
    scalars = (prompt_len, resp_prompt, resp_len)
    q_gain, k_gain = q_gain[None], k_gain[None]
    own = cotangent[None]
    far = trade("gather_far", own, "mp", 4)
    near = trade("gather_near", own, "mp", 2)
    if chips == 4:
        others = [trade("gather_prefix", prefix_kv, "dp", k) for k in range(1, chips)]
    else:
        prefix_kv, others = lax.all_gather(prefix_kv, "dp", axis=0, tiled=True), []
    far = after(far, *others)
    both = trade("gather_both", far, "mp", 2)
    pair = jnp.concatenate([far, near])
    pair_x = trade("gather_pair_x", pair, "mp", 1)
    own_x = trade("gather_own_x", own, "mp", 1)
    scalars, projected, weights, prefix, own = project(
        scalars, after(hidden_rows, far), w_query, w_key, w_value, q_gain, k_gain, prefix_kv, own
    )
    both_x = trade("gather_both_x", after(both, projected[0]), "mp", 1)
    probed, parts = forward(
        OUT, cotangent.shape[1], q_gain.shape[1], scalars, *projected[:3], w_out,
        [prefix, *others],
    )
    back = [own, pair, both, own_x, pair_x, both_x]
    shape = prefix_kv.shape
    terms = [(1, *shape)] if chips != 4 else [(len(steps), *shape) for steps in TERMS]
    kept = [*projected, *weights, w_out, *probed]
    terms, (in_75,), grads = backward(IN_FIRST, scalars, back, kept, terms)
    in_3, in_1, in_6, in_4, in_2, in_0 = rest(IN_REST, cotangent.shape[1], grads, weights[0])

    out_a, out_b, kept_a, kept_b = parts
    got_a = trade("out_a", out_a, "mp", 2)
    got_b = trade("out_b", after(out_b, pair_x), "mp", 2)
    out_a = total(kept_a, got_a)
    got_out = trade("out_mid", out_a, "mp", 4)
    got_75 = trade("in_75", in_75, "mp", 1)
    got_3 = trade("in_3", in_3, "mp", 1)
    in_6 = total(after(in_6, out_a), got_75[:1])
    got_6 = trade("in_6", in_6, "mp", 2)
    in_2 = total(in_2, got_3)
    got_2 = trade("in_2", in_2, "mp", 2)
    if chips == 4:
        got = trade("grad_prefix_y", after(terms[0], in_2), "dp", 2)
        last = trade("grad_prefix_core", terms[1][1:] + got[1:], "dp", 1)
    in_4 = total(after(in_4, got_b, got_out, in_2), got_75[1:], got_6)
    got_4 = trade("in_4", in_4, "mp", 4)
    got_1 = trade("in_1", after(in_1, in_4), "mp", 1)
    got_x = trade("out_x", total(after(kept_b, in_4)[1:], got_b[1:], got_out[1:]), "mp", 1)
    groups = [
        [(kept_b, 0), (got_b, 0), (got_out, 0), (got_x, 0)],
        [(in_0, 0), (got_1, 0), (got_2, 0), (got_4, 0)],
    ]
    if chips == 4:
        groups.append([(terms[1], 0), (got, 0), (last, 0)])
        return last_sums(groups)
    grad_prefix = lax.psum_scatter(terms[0][0], "dp", scatter_dimension=0, tiled=True)
    return *last_sums(groups), grad_prefix.astype(BF16)


def solution(mesh):
    in_specs = (
        P("dp", None),
        P(None, "mp"),
        P(None, "mp"),
        P(None, "mp"),
        P("mp", None),
        P(),
        P(),
        P("dp", "mp"),
        P("dp", "mp"),
        P(),
        P("dp"),
        P("dp"),
    )
    out_specs = (P("dp", "mp"), P("dp", "mp"), P("dp", "mp"))
    return jax.shard_map(
        per_device, mesh=mesh, in_specs=in_specs, out_specs=out_specs, check_vma=False
    )
```
